32 devices in a mesh: pipe: 8 (over z, y), cross: 4 (over x, core).
Axes of the slice: x: 2, y: 2, z: 4, core: 2. Of those that a mesh axis runs over, the one named last changes fastest.
Arguments:
- state: float32 [5, 128, 9216], P(None, 'pipe', 'cross')
- face_diffusion: float32 [128, 9216], P('pipe', 'cross')
- courant: float32 [128, 9216], P('pipe', 'cross'), may hold values from -0.5 to 0.5
- cell_mask: int32 [128, 9216], P('pipe', 'cross'), may hold values from 0 to 1, as said below
- ghost_cell: int32 [4096], P(('pipe', 'cross')), may hold values from 0 to 36863, as said below
- ghost_owner: int32 [4096], P(('pipe', 'cross')), may hold values from 0 to 31, as said below
- ghost_image: int32 [4096], P(('pipe', 'cross')), may hold values from 0 to 255
- image_base: int32 [8192], P(('pipe', 'cross')), may hold values from 0 to 34462, as said below
- image_weight: float32 [8, 8192], P(None, ('pipe', 'cross')), may hold values from 0 to 0.25
Outputs:
- derivative: float32 [5, 128, 9216], P(None, 'pipe', 'cross')
- segment: float32 [5, 128, 9216], P(None, 'pipe', 'cross')
The draws below stay inside these ranges and needn't reach their ends.
Inputs may be any that keep to these rules, and one draw needn't show every extreme that they name: `ghost_cell`: within one device's 128 entries the places are distinct, each a place of that device's block, and cell_mask is 1 at each of them. `ghost_owner`: A device number. Among one device's 128 ghost cells at most 8 name the same owner; one owner, the same for every device, is named by exactly 8 ghost cells of every device. `image_base`: the base row is at most 14, and the base pencil q has q + 97 inside the device's pencils and q + 1 on the same line of 96 pencils. `cell_mask`: 1 marks a solid cell.
All inputs are finite; a program needn't handle non-finite values.
Results may differ from the reference program's by a relative error of at most 0.0003.
Values sent between devices are 32-bit elements; how exact they have to be, the bound alone decides.
No kernel may reach another device: no remote copies, remote signals or barrier semaphores. Data moves between devices by JAX's collectives and lax.ppermute only.
A program may use at most 128 MiB of HBM per device.

```python
import math
import jax
import jax.numpy as jnp
from jax import lax

VARS = 5
L_DEV = 16
PEN_DEV = 2304
LINE = 96
G_DEV = 128
IMG_DEV = 256
AXIAL_ROWS = 128
PEN_TOT = 9216
CAP = 8
GHOSTS = 4096
IMAGES = 8192
N_PIPE = 8
N_CROSS = 4


def ghost_layout(key):
    devices = N_PIPE * N_CROSS
    cell_total = L_DEV * PEN_DEV
    places = jnp.arange(cell_total, dtype=jnp.int32)[None, :]
    priority = jax.random.randint(jax.random.fold_in(key, 101), (devices, cell_total), 0, 1 << 14) * cell_total + places
    edge_place = (places == 0) | (places == cell_total - 1)
    priority = jnp.where(edge_place, places - cell_total, priority)
    ordering = jnp.argsort(priority, axis=1)
    return ordering[:, :G_DEV].astype(jnp.int32)


def draw_ghost_cell(key, part):
    chosen = ghost_layout(key)
    return chosen.reshape(-1)


def draw_cell_mask(key, part):
    chosen = ghost_layout(key)
    key = jax.random.fold_in(key, 5)
    devices = N_PIPE * N_CROSS
    solid_cells = (jax.random.randint(key, (devices, L_DEV * PEN_DEV), 0, 8) == 0).astype(jnp.int32)
    solid_cells = solid_cells.at[jnp.arange(devices)[:, None], chosen].set(1)
    return solid_cells.reshape(N_PIPE, N_CROSS, L_DEV, PEN_DEV).transpose(0, 2, 1, 3).reshape(AXIAL_ROWS, PEN_TOT)


def draw_ghost_owner(key, part):
    key = jax.random.fold_in(key, 7)
    random_subkeys = jax.random.split(key, 5)
    devices = N_PIPE * N_CROSS
    busiest = jax.random.randint(random_subkeys[0], (), 0, devices)
    popular = jax.random.randint(random_subkeys[1], (devices,), 0, 4 * devices)
    jitter = jax.random.randint(random_subkeys[2], (devices, devices), 0, 4 * devices)
    candidates = jnp.arange(devices, dtype=jnp.int32)
    priority = (popular[None, :] + jitter) * (2 * devices) + candidates[None, :] + jnp.where(candidates == busiest, 16 * devices * devices, 0)[None, :]
    ordering = jnp.argsort(priority, axis=1)[:, :devices - 1]
    counts = jax.random.randint(random_subkeys[3], (devices, devices - 1), CAP // 2, CAP + 1)
    count_ends = jnp.cumsum(counts, axis=1)
    positions = jnp.arange(G_DEV - CAP, dtype=jnp.int32)
    picked_rank = jax.vmap(lambda ends_row: jnp.searchsorted(ends_row, positions, side='right'))(count_ends)
    remaining = jnp.take_along_axis(ordering, picked_rank, axis=1)
    owners = jnp.concatenate([jnp.broadcast_to(busiest, (devices, CAP)).astype(jnp.int32), remaining.astype(jnp.int32)], axis=1)
    shuffle = jnp.argsort(jax.random.randint(random_subkeys[4], (devices, G_DEV), 0, 1 << 16) * G_DEV + jnp.arange(G_DEV, dtype=jnp.int32)[None, :], axis=1)
    return jnp.take_along_axis(owners, shuffle, axis=1).reshape(-1).astype(jnp.int32)


def draw_image_base(key, part):
    key = jax.random.fold_in(key, 9)
    random_subkeys = jax.random.split(key, 3)
    devices = N_PIPE * N_CROSS
    base_row = jax.random.randint(random_subkeys[0], (devices, IMG_DEV), 0, L_DEV - 1)
    line_number = jax.random.randint(random_subkeys[1], (devices, IMG_DEV), 0, PEN_DEV // LINE - 1)
    line_spot = jax.random.randint(random_subkeys[2], (devices, IMG_DEV), 0, LINE - 1)
    bases = base_row * PEN_DEV + line_number * LINE + line_spot
    slot = jnp.arange(IMG_DEV, dtype=jnp.int32)[None, :]
    highest = (L_DEV - 1) * PEN_DEV - LINE - 2
    bases = jnp.where(slot == 0, 0, jnp.where(slot == 1, highest, bases))
    return bases.reshape(-1).astype(jnp.int32)


def draw_state(key, part):
    key = jax.random.fold_in(key, 11)
    random_subkeys = jax.random.split(key, 1)
    shape = (VARS, AXIAL_ROWS, PEN_TOT)
    return jax.random.normal(random_subkeys[0], shape, jnp.float32)


def draw_face_diffusion(key, part):
    key = jax.random.fold_in(key, 13)
    random_subkeys = jax.random.split(key, 5)
    lowest = L_DEV / 2.0
    highest = AXIAL_ROWS / 2.0
    pencil_rate = jnp.exp(jax.random.uniform(random_subkeys[0], (1, PEN_TOT), jnp.float32, math.log(lowest), math.log(highest)))
    slab_factor = jnp.exp(jax.random.uniform(random_subkeys[1], (N_PIPE, 1, PEN_TOT), jnp.float32, -0.7, 0.7))
    slab_rows = jnp.broadcast_to(slab_factor, (N_PIPE, L_DEV, PEN_TOT)).reshape(AXIAL_ROWS, PEN_TOT)
    roughness = jnp.exp(jax.random.uniform(random_subkeys[2], (AXIAL_ROWS, PEN_TOT), jnp.float32, -0.7, 0.7))
    cluster_positions = jax.random.randint(random_subkeys[3], (4,), 0, AXIAL_ROWS)
    row_location = lax.broadcasted_iota(jnp.int32, (AXIAL_ROWS, 1), 0)
    cluster_rows = jnp.any(row_location == cluster_positions[None, :], axis=1, keepdims=True)
    split_factor = jnp.where(cluster_rows, jnp.exp(jax.random.uniform(random_subkeys[4], (AXIAL_ROWS, 1), jnp.float32, -6.0, -4.0)), 1.0)
    return pencil_rate * pencil_rate * slab_rows * roughness * split_factor


def with_ends(drawn, key, smallest, top_value):
    index_at = [jax.random.randint(jax.random.fold_in(key, axis), (), 0, length) for axis, length in enumerate(drawn.shape)]
    widest = drawn.shape.index(max(drawn.shape))
    next_to = index_at[:widest] + [(index_at[widest] + 1) % drawn.shape[widest]] + index_at[widest + 1:]
    return drawn.at[tuple(index_at)].set(smallest).at[tuple(next_to)].set(top_value)


def shard_levels(rng, dims, pieces, smallest, largest):
    gain = 1.0
    for axis_at, parts in pieces:
        steps = jax.random.uniform(jax.random.fold_in(jax.random.fold_in(rng, 6), axis_at), (parts,), jnp.float32, smallest / len(pieces), largest / len(pieces))
        gain = gain * jnp.repeat(jnp.exp(steps), dims[axis_at] // parts).reshape((-1,) + (1,) * (len(dims) - 1 - axis_at))
    return gain


def setup_inputs(seed: int = 0) -> dict:
    key_of = jax.random.split(jax.random.key(seed), 10)
    return {
        "state": draw_state(jax.random.fold_in(key_of[9], 71), 0),
        "face_diffusion": draw_face_diffusion(jax.random.fold_in(key_of[9], 71), 0),
        "courant": jnp.clip(jax.random.uniform(key_of[2], (AXIAL_ROWS, PEN_TOT), jnp.float32, -0.5, 0.5) * shard_levels(key_of[2], (AXIAL_ROWS, PEN_TOT), ((0, 8), (1, 4)), -0.4, 0.0), -0.5, 0.5),
        "cell_mask": draw_cell_mask(jax.random.fold_in(key_of[9], 71), 0),
        "ghost_cell": draw_ghost_cell(jax.random.fold_in(key_of[9], 71), 0),
        "ghost_owner": draw_ghost_owner(jax.random.fold_in(key_of[9], 71), 0),
        "ghost_image": with_ends(jax.random.randint(key_of[6], (GHOSTS,), 0, IMG_DEV), jax.random.fold_in(key_of[6], 1), 0, IMG_DEV - 1).astype(jnp.int32),
        "image_base": draw_image_base(jax.random.fold_in(key_of[9], 71), 0),
        "image_weight": jnp.clip(0.25 * jax.random.uniform(key_of[8], (8, IMAGES), jnp.float32) ** shard_levels(key_of[8], (8, IMAGES), ((1, 32),), -0.2, 0.2), 0.0, 0.25),
    }


REFLECT = (1.0, -1.0, -1.0, -1.0, 1.0)


def corner_offsets(pencils):
    return jnp.array([0, 1, LINE, LINE + 1, pencils, pencils + 1, pencils + LINE, pencils + LINE + 1], jnp.int32)


def combine(panels, lower_rows, upper_rows, has_lower, has_upper):
    lower_diag = jnp.where(has_lower, lower_rows[1], 1.0)
    upper_diag = jnp.where(has_upper, upper_rows[1], 1.0)
    lower_ratio = panels[0] / lower_diag
    upper_ratio = panels[2] / upper_diag
    new_lower = -lower_ratio * lower_rows[0]
    new_upper = -upper_ratio * upper_rows[2]
    new_margin = panels[3] - lower_ratio * lower_rows[3] - upper_ratio * upper_rows[3]
    new_diag = new_margin - new_lower - new_upper
    new_rhs = panels[4:] - lower_ratio * lower_rows[4:] - upper_ratio * upper_rows[4:]
    return jnp.concatenate([jnp.stack([new_lower, new_diag, new_upper, new_margin]), new_rhs], axis=0)


def shifted_level(panels, stride, row_index, row_total):
    row_count = panels.shape[1]
    zero_rows = jnp.zeros((panels.shape[0], stride, panels.shape[2]), panels.dtype)
    lower_rows = jnp.concatenate([zero_rows, panels[:, :row_count - stride]], axis=1)
    upper_rows = jnp.concatenate([panels[:, stride:], zero_rows], axis=1)
    return combine(panels, lower_rows, upper_rows, row_index >= stride, row_index < row_total - stride)


def pencil_solve(panels):
    row_total = panels.shape[1]
    row_index = lax.broadcasted_iota(jnp.int32, (row_total, 1), 0)
    stride = 1
    while stride < row_total:
        panels = shifted_level(panels, stride, row_index, row_total)
        stride = stride * 2
    return panels[4:] / panels[1]


def explicit_terms(padded, row_index, row_total):
    centre = padded[:, 2:-2]
    minus_one = padded[:, 1:-3]
    plus_one = padded[:, 3:-1]
    minus_two = padded[:, :-4]
    plus_two = padded[:, 4:]
    inner_terms = (7.0 / 9.0) * (plus_one - minus_one) + (1.0 / 36.0) * (plus_two - minus_two)
    near_terms = 0.75 * (plus_one - minus_one)
    first_terms = -1.5 * centre + 2.0 * plus_one - 0.5 * plus_two
    final_terms = 1.5 * centre - 2.0 * minus_one + 0.5 * minus_two
    edge_rows = (row_index == 1) | (row_index == row_total - 2)
    return jnp.where(row_index == 0, first_terms, jnp.where(row_index == row_total - 1, final_terms, jnp.where(edge_rows, near_terms, inner_terms)))


def derivative_panels(row_index, row_total, pencils, stencil_terms):
    edge_rows = (row_index == 1) | (row_index == row_total - 2)
    end_rows = (row_index == 0) | (row_index == row_total - 1)
    side_coef = jnp.where(end_rows, 0.0, jnp.where(edge_rows, 0.25, 1.0 / 3.0)) * jnp.ones((1, pencils), jnp.float32)
    margin = 1.0 + side_coef + side_coef
    return jnp.concatenate([jnp.stack([side_coef, jnp.ones_like(side_coef), side_coef, margin]), stencil_terms], axis=0)


def diffusion_panels(face_low, face_here, row_index, row_total, right_terms):
    lower_side = -face_low
    upper_side = -jnp.where(row_index == row_total - 1, 0.0, face_here)
    margin = jnp.ones_like(face_here)
    diagonal = margin - lower_side - upper_side
    return jnp.concatenate([jnp.stack([lower_side, diagonal, upper_side, margin]), right_terms], axis=0)


def to_blocks(field):
    depth = field.shape[0]
    return field.reshape(depth, N_PIPE, L_DEV, N_CROSS, PEN_DEV).transpose(1, 3, 0, 2, 4).reshape(N_PIPE * N_CROSS, depth, L_DEV * PEN_DEV)


def from_blocks(blocks):
    depth = blocks.shape[1]
    return blocks.reshape(N_PIPE, N_CROSS, depth, L_DEV, PEN_DEV).transpose(2, 0, 3, 1, 4).reshape(depth, AXIAL_ROWS, PEN_DEV * N_CROSS)


def blockwise_solve(panels):
    depth = panels.shape[0]
    grouped_rows = panels.reshape(depth, AXIAL_ROWS, N_CROSS, PEN_DEV).transpose(2, 0, 1, 3)
    solved = lax.map(pencil_solve, grouped_rows)
    return solved.transpose(1, 2, 0, 3).reshape(depth - 4, AXIAL_ROWS, N_CROSS * PEN_DEV)


def image_terms(block_data, corner_cells, corner_weight):
    picked = block_data[:, corner_cells]
    return jnp.sum(picked * corner_weight[None], axis=1)


def fill_block(block_data, solid_flags, cell_list, cell_values):
    cleared = jnp.where(solid_flags[None] == 1, 0.0, block_data)
    return cleared.at[:, cell_list].set(cell_values)


def reference(state, face_diffusion, courant, cell_mask, ghost_cell, ghost_owner, ghost_image, image_base, image_weight):
    devices = N_PIPE * N_CROSS
    blocks = to_blocks(state)
    corners = image_base.reshape(devices, 1, IMG_DEV) + corner_offsets(PEN_DEV)[None, :, None]
    weights = image_weight.reshape(8, devices, IMG_DEV).transpose(1, 0, 2)
    image_values = jax.vmap(image_terms)(blocks, corners, weights)
    all_images = image_values.transpose(1, 0, 2).reshape(VARS, devices * IMG_DEV)
    reflection = jnp.array(REFLECT, jnp.float32)[:, None]
    ghost_values = reflection * all_images[:, ghost_owner * IMG_DEV + ghost_image]
    solid_blocks = to_blocks(cell_mask[None])[:, 0]
    ghost_blocks = ghost_cell.reshape(devices, G_DEV)
    value_blocks = ghost_values.reshape(VARS, devices, G_DEV).transpose(1, 0, 2)
    filled = from_blocks(jax.vmap(fill_block)(blocks, solid_blocks, ghost_blocks, value_blocks))
    row_index = lax.broadcasted_iota(jnp.int32, (AXIAL_ROWS, 1), 0)
    padded = jnp.pad(filled, ((0, 0), (2, 2), (0, 0)))
    stencil_terms = explicit_terms(padded, row_index, AXIAL_ROWS)
    derivative = blockwise_solve(derivative_panels(row_index, AXIAL_ROWS, PEN_DEV * N_CROSS, stencil_terms))
    rhs_two = filled - courant[None] * derivative
    face_low = jnp.pad(face_diffusion, ((1, 0), (0, 0)))[:-1]
    segment = blockwise_solve(diffusion_panels(face_low, face_diffusion, row_index, AXIAL_ROWS, rhs_two))
    return derivative, segment
```

```python
import functools

import numpy as np
import jax
import jax.numpy as jnp
from jax import lax
from jax.experimental import pallas as pl
from jax.experimental.pallas import tpu as pltpu
from jax.sharding import PartitionSpec as P

LINE = 96
LANES = 128
REFLECT = (1.0, -1.0, -1.0, -1.0, 1.0)

Z_UP, Z_DOWN, ROW_FIRST, ROW_LAST, RIGHT_FIRST, RIGHT_LAST = range(6)
LINK_IN, MARGIN_FIRST, MARGIN_LAST, LINK_UP, FIRST_LO, FIRST_HI, LAST_LO, LAST_HI, FIRST_EDGE, LAST_EDGE = range(10)
COEFFICIENTS = 10
PENCIL, ROW, OWNER, IMAGE, WEIGHT_UP, WEIGHT_DOWN, WEIGHT_FIRST, WEIGHT_LAST = range(8)


def derivative_tables(slabs, rows, var_count):
    total = slabs * rows
    A = np.eye(total)
    B = np.zeros((total, total))
    for i in range(2, total - 2):
        A[i, i - 1] = A[i, i + 1] = 1.0 / 3.0
        B[i, i + 1], B[i, i - 1] = 7.0 / 9.0, -7.0 / 9.0
        B[i, i + 2], B[i, i - 2] = 1.0 / 36.0, -1.0 / 36.0
    for i in (1, total - 2):
        A[i, i - 1] = A[i, i + 1] = 0.25
        B[i, i + 1], B[i, i - 1] = 0.75, -0.75
    B[0, :3] = (-1.5, 2.0, -0.5)
    B[-1, -3:] = (0.5, -2.0, 1.5)
    inverse = np.linalg.inv(A)
    M = inverse @ B

    cells = var_count * rows
    own_at, reduce_at, adjoint_at, profile_at, weight_at = 0, cells, cells + 16, cells + 56, cells + 96
    tables = np.zeros((slabs, cells + 112, LANES))
    carry_up, carry_down = np.zeros(slabs), np.zeros(slabs)
    for p in range(slabs):
        table = tables[p]
        base = p * rows
        here = slice(base, base + rows)
        own = M[here, here]
        lo, hi, lo_edge, hi_edge = (np.zeros(rows) for _ in range(4))
        weight_up, weight_down = np.zeros(rows), np.zeros(rows)
        if p > 0:
            lo = inverse[here, base - 8] / inverse[base + 1, base - 8]
            lo_edge[0] = M[base, base - 1] - lo[0] * M[base + 1, base - 1]
            weight_down = M[base - 2, here]
        if p > 1:
            k = base - rows - 8
            carry_up[p] = inverse[base + 1, k] / inverse[base - rows + 1, k]
        if p < slabs - 1:
            k = base + rows + 8
            hi = inverse[here, k] / inverse[base + rows - 2, k]
            hi_edge[-1] = M[base + rows - 1, base + rows] - hi[-1] * M[base + rows - 2, base + rows]
            weight_up = M[base + rows + 1, here]
        if p < slabs - 2:
            k = base + 2 * rows + 8
            carry_down[p] = inverse[base + rows - 2, k] / inverse[base + 2 * rows - 2, k]
        for v in range(var_count):
            at = slice(v * rows, (v + 1) * rows)
            table[own_at + v * rows : own_at + (v + 1) * rows, at] = own
            table[reduce_at + v, at] = weight_up
            table[reduce_at + var_count + v, at] = weight_down
        table[adjoint_at : adjoint_at + rows, :rows] = own.T
        table[adjoint_at + rows : adjoint_at + 2 * rows, rows : 2 * rows] = own.T
        more = adjoint_at + 2 * rows
        table[more, :rows] = lo
        table[more + 1, :rows] = hi
        table[more + 2, rows : 2 * rows] = lo
        table[more + 3, rows : 2 * rows] = hi
        table[more + 4, 0] = lo_edge[0]
        table[more + 5, 2 * rows - 1] = hi_edge[-1]
        table[profile_at : profile_at + rows] = lo[:, None]
        table[profile_at + rows : profile_at + 2 * rows] = hi[:, None]
        table[profile_at + 2 * rows] = lo_edge[0]
        table[profile_at + 2 * rows + 1] = hi_edge[-1]
        table[weight_at, :rows] = weight_up
        table[weight_at + 1, :rows] = weight_down
    at = (own_at, reduce_at, adjoint_at, profile_at, weight_at)
    return tables.astype(np.float32), at, carry_up, carry_down


def split(x, parts):
    pieces = []
    for _ in range(parts):
        piece = x.astype(jnp.bfloat16)
        pieces.append(piece)
        x = x - piece.astype(jnp.float32)
    return pieces


def exact_dot(x, one_hot, contract):
    found = lax.dot_general(
        jnp.concatenate(split(x, 3), axis=0),
        one_hot,
        (contract, ((), ())),
        preferred_element_type=jnp.float32,
    )
    size = x.shape[0]
    return found[:size] + (found[size : 2 * size] + found[2 * size :])


def full_dot(a, b):
    return jnp.dot(a, b, precision=lax.Precision.HIGHEST, preferred_element_type=jnp.float32)


def marks(shape, axis, values):
    return jnp.where(lax.broadcasted_iota(jnp.int32, shape, axis) == values, 1.0, 0.0).astype(
        jnp.bfloat16
    )


def place_of(cell, rows, pencils):
    row = jnp.zeros_like(cell)
    for k in range(1, rows):
        row += (cell >= k * pencils).astype(jnp.int32)
    return row, cell - row * pencils


def tile(t):
    return slice(t * LANES, (t + 1) * LANES)


def turn(ref, x):
    height, pencils = x.shape
    for t in range(pencils // LANES):
        ref[t * height : (t + 1) * height, :] = x[:, tile(t)]


def slab_at(ref, row, height, count):
    return ref[pl.ds(row, count, stride=height), :]


def put_slab(ref, row, height, count, value):
    ref[pl.ds(row, count, stride=height), :] = value


def kept_at(which, i, rows, count):
    return (which * rows + i) * (-(-count // 8) * 8)


def fetch(sources, targets, sems):
    copies = [
        pltpu.make_async_copy(source, target, sems.at[k])
        for k, (source, target) in enumerate(zip(sources, targets))
    ]
    for copy in copies:
        copy.start()
    return copies


class Slices:
    def __init__(self, slabs, count, var_count):
        rest = count % slabs
        self.slabs, self.count, self.var_count = slabs, count, var_count
        shared = rest > 0 and slabs % rest == 0 and LANES % (slabs // rest) == 0
        self.full = count // slabs if shared else -(-count // slabs)
        self.rest = rest if shared else 0
        self.per = slabs // rest if shared else 1
        self.width = LANES // self.per
        self.chunk = self.full + (1 if shared else 0)
        self.lines, self.back_lines = 6 * var_count + COEFFICIENTS, 4 * var_count
        self.groups, self.back_groups = (self.group_count(n) for n in (self.lines, self.back_lines))
        self.meta_at = self.lines * self.full
        self.packed_at = self.meta_at + 8
        self.height = -(-(self.packed_at + self.groups) // 8) * 8
        self.back_packed_at = self.back_lines * self.full
        self.back_height = -(-(self.back_packed_at + self.back_groups) // 8) * 8

    def group_count(self, lines):
        return -(-lines // self.per) if self.rest else 0

    def tiles_at(self, t):
        return t * self.slabs, min(self.count, (t + 1) * self.slabs)


def lane_block(rows, width):
    return lax.broadcasted_iota(jnp.int32, (rows, LANES), 1) // width


def moved_lanes(x, by):
    by %= LANES
    return x if by == 0 else pltpu.roll(x, by, 1)


def image_kernel(state_hbm, base_hbm, weight_hbm, out_ref, state_ref, base_ref, weight_ref, sems):
    var_count, rows, pencils = state_ref.shape
    images = base_ref.shape[0]
    copies = fetch(
        (state_hbm, base_hbm, weight_hbm), (state_ref, base_ref, weight_ref), sems
    )
    for copy in copies[1:]:
        copy.wait()
    row, pencil = place_of(base_ref[...].reshape(1, images), rows, pencils)
    pick = marks((pencils, images), 0, pencil)
    row_at = lax.broadcasted_iota(jnp.int32, (rows, images), 0)
    lower, upper = row_at == row, row_at == row + 1
    total = [jnp.zeros((rows, images), jnp.float32) for _ in range(var_count)]
    copies[0].wait()
    x = state_ref[...].reshape(var_count * rows, pencils)
    for corner, shift in enumerate((0, 1, LINE, LINE + 1)):
        moved = x if shift == 0 else pltpu.roll(x, pencils - shift, 1)
        pieces = jnp.concatenate(split(moved, 2), axis=0)
        found = jnp.dot(pieces, pick, preferred_element_type=jnp.float32)
        found = found[: var_count * rows] + found[var_count * rows :]
        weight = jnp.where(lower, weight_ref[corner : corner + 1], 0.0) + jnp.where(
            upper, weight_ref[corner + 4 : corner + 5], 0.0
        )
        for v in range(var_count):
            total[v] += found[v * rows : (v + 1) * rows] * weight
    lines = []
    for v in range(var_count):
        value = jnp.sum(total[v], axis=0, keepdims=True)
        lines += [value[:, tile(t)] for t in range(images // LANES)]
    lines = jnp.concatenate(lines, axis=0)
    for k in range(out_ref.shape[0]):
        out_ref[k] = lines


def ghost_values(blocks, owner, image):
    cross = len(blocks)
    slabs, lines, _ = blocks[0].shape
    per = lines // len(REFLECT)
    ghosts = owner.shape[1]
    me = lax.axis_index("cross")
    values = [
        jnp.concatenate(
            [
                jnp.concatenate([block[:, v * per + t, :] for t in range(per)], axis=1)
                for block in blocks
            ],
            axis=0,
        )
        for v in range(len(REFLECT))
    ]
    pick = marks((per * LANES, ghosts), 0, image)
    found = exact_dot(jnp.concatenate(values, axis=0), pick, ((1,), (0,)))
    devices = slabs * cross
    at = lax.broadcasted_iota(jnp.int32, (devices, ghosts), 0)
    mine = (at % slabs) * cross + (me + cross - at // slabs) % cross == owner
    return [
        reflect
        * jnp.sum(
            jnp.where(mine, found[v * devices : (v + 1) * devices], 0.0), axis=0, keepdims=True
        )
        for v, reflect in enumerate(REFLECT)
    ]


def prepare_kernel(
    slices,
    at,
    face_hbm,
    courant_hbm,
    tables_hbm,
    cell_hbm,
    owner_hbm,
    image_hbm,
    mask_hbm,
    state_hbm,
    message_ref,
    kept_ref,
    face_ref,
    courant_ref,
    table_ref,
    cell_ref,
    owner_ref,
    image_ref,
    mask_ref,
    state_ref,
    turned_ref,
    pair_ref,
    matrix_ref,
    adjoint_ref,
    weight_ref,
    cleared_ref,
    rest_ref,
    sems,
):
    var_count, rows, pencils = state_ref.shape
    cells = var_count * rows
    count = pencils // LANES
    ghosts = cell_ref.shape[0]
    padded = -(-count // 8) * 8
    p = lax.axis_index("pipe")
    slabs, height = slices.slabs, slices.height
    lines = slices.groups * slices.per
    _, reduce_at, adjoint_at, profile_at, weight_at = at
    copies = fetch(
        (face_hbm, courant_hbm, tables_hbm.at[p], cell_hbm, owner_hbm, image_hbm, mask_hbm, state_hbm),
        (face_ref, courant_ref, table_ref, cell_ref, owner_ref, image_ref, mask_ref, state_ref),
        sems,
    )

    def send(line, slab):
        for t in range(slices.full):
            start, end = slices.tiles_at(t)
            message_ref[pl.ds(line * slices.full + t, end - start, stride=height), :] = slab[start:end]
        for m in range(slices.rest):
            tail = slices.full * slabs + m
            rest_ref[m * lines + line : m * lines + line + 1, :] = slab[tail : tail + 1]

    def send_value(functional, v, slab):
        send(functional * var_count + v, slab)

    def send_coefficient(which, slab):
        send(6 * var_count + which, slab)

    copies[0].wait()
    turn(turned_ref, face_ref[...])

    def face(i):
        return slab_at(turned_ref, i, rows, count)

    link = face(0)
    margin = jnp.ones_like(link)
    first_margin = margin
    to_up, to_first = [None] * rows, [None] * rows
    for i in range(1, rows - 1):
        above = face(i)
        inverse = 1.0 / (link + margin + above)
        low, up = link * inverse, above * inverse
        to_up[i], to_first[i] = up, low
        for k, part in enumerate((up, low, inverse)):
            start = kept_at(k, i, rows, count)
            kept_ref[start : start + count, :] = part
        first_margin += low * margin
        link = link * up
        margin = 1.0 + margin * up
    send_coefficient(LINK_IN, link)
    send_coefficient(MARGIN_FIRST, first_margin)
    send_coefficient(MARGIN_LAST, margin)
    send_coefficient(LINK_UP, jnp.where(p == slabs - 1, 0.0, face(rows - 1)))

    zero, one = jnp.zeros_like(margin), jnp.ones_like(margin)
    first, last = [None] * rows, [None] * rows
    first[0], first[rows - 1], last[0], last[rows - 1] = one, zero, zero, one
    for i in range(rows - 2, 0, -1):
        first[i] = to_first[i] + to_up[i] * first[i + 1]
        last[i] = to_up[i] * last[i + 1]
    copies[1].wait()
    turn(turned_ref, courant_ref[...])
    for i in range(rows):
        speed = slab_at(turned_ref, i, rows, count)
        start = kept_at(3, i, rows, count)
        kept_ref[start : start + count, :] = speed
        put_slab(pair_ref, i, 2 * rows, count, first[i] * speed)
        put_slab(pair_ref, rows + i, 2 * rows, count, last[i] * speed)
    for t in range(count):
        matrix_ref[:, tile(t)] = pair_ref[t * 2 * rows : (t + 1) * 2 * rows, :]
    copies[2].wait()
    kept_ref[kept_ref.shape[0] - 40 :, :] = table_ref[profile_at : profile_at + 40, :]
    turn(
        adjoint_ref, full_dot(table_ref[adjoint_at : adjoint_at + 40, : 2 * rows], matrix_ref[...])
    )
    for k in range(6):
        send_coefficient(FIRST_LO + k, slab_at(adjoint_ref, 2 * rows + k, 40, count))
    weight_ref[:, padded - 8 :, :] = jnp.zeros((2 * rows, 8, LANES), jnp.float32)
    for i, share in enumerate(first + last):
        weight_ref[i, :count, :] = share - slab_at(adjoint_ref, i, 40, count)

    for copy in copies[3:6]:
        copy.wait()
    row, pencil = place_of(cell_ref[...].reshape(1, ghosts), rows, pencils)
    lane_tile = jnp.right_shift(pencil, 7)
    lane_marks = marks((LANES, ghosts), 0, pencil - lane_tile * LANES)
    picked = exact_dot(
        weight_ref[...].reshape(2 * rows * padded, LANES), lane_marks, ((1,), (0,))
    ).reshape(2, rows, padded, ghosts)
    at_cell = (lax.broadcasted_iota(jnp.int32, (rows, padded, ghosts), 0) == row[None]) & (
        lax.broadcasted_iota(jnp.int32, (rows, padded, ghosts), 1) == lane_tile[None]
    )
    row_marks = jnp.where(lax.broadcasted_iota(jnp.int32, (rows, ghosts), 0) == row, 1.0, 0.0)
    up_down = full_dot(table_ref[weight_at : weight_at + 8, :rows], row_marks)

    def at_ghosts(values):
        return jnp.sum(jnp.sum(jnp.where(at_cell, values, 0.0), axis=0), axis=0, keepdims=True)

    about = jnp.concatenate(
        [
            pencil.astype(jnp.float32),
            row.astype(jnp.float32),
            owner_ref[...].reshape(1, ghosts).astype(jnp.float32),
            image_ref[...].reshape(1, ghosts).astype(jnp.float32),
            up_down[0:2],
            at_ghosts(picked[0]),
            at_ghosts(picked[1]),
        ],
        axis=0,
    )
    for j in range(slabs):
        start = j * height + slices.meta_at
        message_ref[start : start + 8, :] = about

    copies[6].wait()
    copies[7].wait()
    solid = mask_ref[...] == 1
    for v in range(var_count):
        here = slice(v * rows, (v + 1) * rows)
        cleared_ref[here, :] = jnp.where(solid, 0.0, state_ref[v])
    turn(turned_ref, cleared_ref[...])
    turn(pair_ref, full_dot(table_ref[reduce_at : reduce_at + 16, :cells], cleared_ref[...]))
    for k in range(2 * var_count):
        send(k, slab_at(pair_ref, k, 16, count))
    for v in range(var_count):
        low = high = zero
        for i in range(rows):
            cell = slab_at(turned_ref, v * rows + i, cells, count)
            if i == 0:
                send_value(ROW_FIRST, v, cell)
            if i == rows - 1:
                send_value(ROW_LAST, v, cell)
            low += weight_ref[i, :count, :] * cell
            high += weight_ref[rows + i, :count, :] * cell
        send_value(RIGHT_FIRST, v, low)
        send_value(RIGHT_LAST, v, high)

    block = lane_block(max(slices.groups, 1), slices.width)
    for m in range(slices.rest):
        lined = [
            rest_ref[pl.ds(m * lines + k, slices.groups, stride=slices.per), :]
            for k in range(slices.per)
        ]
        for i in range(slices.per):
            packed = lined[0]
            for k in range(slices.per):
                moved = moved_lanes(lined[k], (k - i) * slices.width)
                packed = moved if k == 0 else jnp.where(block == k, moved, packed)
            start = (m * slices.per + i) * height + slices.packed_at
            message_ref[start : start + slices.groups, :] = packed


def solve_kernel(slices, carry_up, carry_down, message_ref, *refs):
    *blocks, back_ref, ghost_ref, rest_ref, back_rest_ref = refs
    slabs, var_count, chunk, full = slices.slabs, slices.var_count, slices.chunk, slices.full
    height, per, width = slices.height, slices.per, slices.width
    me = lax.axis_index("pipe")

    def meta(p, k):
        start = p * height + slices.meta_at + k
        return message_ref[start : start + 1, :]

    def meta_all(k):
        return jnp.concatenate([meta(p, k) for p in range(slabs)], axis=1).astype(jnp.int32)

    values = ghost_values(blocks, meta_all(OWNER), meta_all(IMAGE))
    ghost_lines = 6 * var_count + 2
    ghosts = LANES
    place = lax.broadcasted_iota(jnp.int32, (chunk * LANES, ghosts), 0)
    slot, lane = place // LANES, place % LANES
    pencil_at = jnp.where(
        slot < full,
        (me + slot * slabs) * LANES + lane,
        (full * slabs + me // per) * LANES + (me % per) * width + lane,
    )
    for p in range(slabs):
        row = meta(p, ROW)
        weights = (
            meta(p, WEIGHT_UP),
            meta(p, WEIGHT_DOWN),
            jnp.where(row == 0.0, 1.0, 0.0),
            jnp.where(row == 15.0, 1.0, 0.0),
            meta(p, WEIGHT_FIRST),
            meta(p, WEIGHT_LAST),
        )
        here = jnp.concatenate([value[:, tile(p)] for value in values], axis=0)
        shares = jnp.concatenate(
            [here * weight for weight in weights] + [jnp.zeros((2, ghosts), jnp.float32)], axis=0
        )
        spots = jnp.where(pencil_at == meta(p, PENCIL).astype(jnp.int32), 1.0, 0.0)
        share = exact_dot(shares, spots.astype(jnp.bfloat16), ((1,), (1,)))
        for t in range(chunk):
            start = (p * chunk + t) * ghost_lines
            ghost_ref[start : start + ghost_lines, :] = share[:, tile(t)]
        if slices.rest:
            start = p * height + slices.packed_at
            packed = message_ref[start : start + slices.groups, :]
            for k in range(per):
                rest_ref[pl.ds(p * slices.groups * per + k, slices.groups, stride=per), :] = (
                    moved_lanes(packed, -k * width)
                )

    def sent(p, line):
        start = p * height + line * full
        slab = message_ref[start : start + full, :]
        if slices.rest:
            start = p * slices.groups * per + line
            slab = jnp.concatenate([slab, rest_ref[start : start + 1, :]], axis=0)
        return slab

    def value(p, functional, v):
        line = functional * var_count + v
        start = p * chunk * ghost_lines + line
        return sent(p, line) + ghost_ref[pl.ds(start, chunk, stride=ghost_lines), :]

    def give(p, functional, v, slab):
        line = functional * var_count + v
        start = p * slices.back_height + line * full
        back_ref[start : start + full, :] = slab[:full]
        if slices.rest:
            start = p * slices.back_groups * per + line
            back_rest_ref[start : start + 1, :] = slab[full:]

    coefficients = [
        [sent(p, 6 * var_count + k) for k in range(COEFFICIENTS)] for p in range(slabs)
    ]
    nodes = 2 * slabs
    ratio, scale = [], []
    margin = coefficients[0][MARGIN_FIRST]
    for k in range(nodes):
        link = coefficients[k // 2][LINK_UP if k % 2 else LINK_IN]
        inverse = 1.0 / (margin + link)
        ratio.append(link * inverse)
        scale.append(inverse)
        if k < nodes - 1:
            following = coefficients[(k + 1) // 2][MARGIN_FIRST if k % 2 else MARGIN_LAST]
            margin = following + margin * ratio[k]

    zero = jnp.zeros((chunk, LANES), jnp.float32)
    for v in range(var_count):
        lo, hi = [zero] * slabs, [zero] * slabs
        below, above = [zero] * slabs, [zero] * slabs
        for p in range(1, slabs):
            lo[p] = value(p - 1, Z_UP, v) + float(carry_up[p]) * lo[p - 1]
            below[p] = value(p - 1, ROW_LAST, v)
        for p in range(slabs - 2, -1, -1):
            hi[p] = value(p + 1, Z_DOWN, v) + float(carry_down[p]) * hi[p + 1]
            above[p] = value(p + 1, ROW_FIRST, v)
        right = []
        for p in range(slabs):
            coefficient = coefficients[p]
            right.append(
                value(p, RIGHT_FIRST, v)
                - coefficient[FIRST_LO] * lo[p]
                - coefficient[FIRST_HI] * hi[p]
                - coefficient[FIRST_EDGE] * below[p]
            )
            right.append(
                value(p, RIGHT_LAST, v)
                - coefficient[LAST_LO] * lo[p]
                - coefficient[LAST_HI] * hi[p]
                - coefficient[LAST_EDGE] * above[p]
            )
            give(p, 2, v, lo[p])
            give(p, 3, v, hi[p])
        for k in range(1, nodes):
            right[k] = right[k] + ratio[k - 1] * right[k - 1]
        x = right[nodes - 1] * scale[nodes - 1]
        give(slabs - 1, 1, v, x)
        for k in range(nodes - 2, -1, -1):
            x = right[k] * scale[k] + ratio[k] * x
            give(k // 2, k % 2, v, x)
    if slices.rest:
        groups = slices.back_groups
        block = lane_block(groups, width)
        for p in range(slabs):
            for k in range(per):
                lined = back_rest_ref[pl.ds(p * groups * per + k, groups, stride=per), :]
                moved = moved_lanes(lined, k * width)
                packed = moved if k == 0 else jnp.where(block == k, moved, packed)
            start = p * slices.back_height + slices.back_packed_at
            back_ref[start : start + groups, :] = packed


def fill_kernel(at, owner_hbm, image_hbm, cell_hbm, courant_hbm, tables_hbm, mask_hbm, state_hbm, *refs):
    *blocks, turned_ref, up_ref, down_ref = refs[:-9]
    owner_ref, image_ref, cell_ref, courant_ref, table_ref, mask_ref, state_ref = refs[-9:-2]
    filled_ref, sems = refs[-2:]
    var_count, rows, pencils = state_ref.shape
    cells = var_count * rows
    count = pencils // LANES
    ghosts = cell_ref.shape[0]
    copies = fetch(
        (
            owner_hbm,
            image_hbm,
            cell_hbm,
            courant_hbm,
            tables_hbm.at[lax.axis_index("pipe")],
            mask_hbm,
            state_hbm,
        ),
        (owner_ref, image_ref, cell_ref, courant_ref, table_ref, mask_ref, state_ref),
        sems,
    )
    for copy in copies[:3]:
        copy.wait()
    owner, image = (ref[...].reshape(1, ghosts) for ref in (owner_ref, image_ref))
    values = ghost_values(blocks, owner, image)
    row, pencil = place_of(cell_ref[...].reshape(1, ghosts), rows, pencils)
    spots = marks((pencils, ghosts), 0, pencil)
    at_row = lax.broadcasted_iota(jnp.int32, (rows, ghosts), 0) == row
    spread = jnp.concatenate([jnp.where(at_row, value, 0.0) for value in values], axis=0)
    placed = exact_dot(spread, spots, ((1,), (1,)))
    for copy in copies[3:]:
        copy.wait()
    solid = mask_ref[...] == 1
    for v in range(var_count):
        here = slice(v * rows, (v + 1) * rows)
        filled_ref[here, :] = jnp.where(solid, 0.0, state_ref[v]) + placed[here]
    for v in range(var_count):
        for t in range(count):
            line = slice(v * count + t, v * count + t + 1)
            down_ref[line, :] = filled_ref[v * rows : v * rows + 1, tile(t)]
            up_ref[line, :] = filled_ref[(v + 1) * rows - 1 : (v + 1) * rows, tile(t)]
    own = full_dot(table_ref[at[0] : at[0] + cells, :cells], filled_ref[...])
    turn(turned_ref.at[: cells * count, :], own)
    courant = courant_ref[...]
    for v in range(var_count):
        here = slice(v * rows, (v + 1) * rows)
        right = filled_ref[here, :] - courant * own[here]
        for t in range(count):
            start = (count + t) * cells + v * rows
            turned_ref[start : start + rows, :] = right[:, tile(t)]


def finish_kernel(
    slices,
    back_ref,
    turned_ref,
    kept_ref,
    below_ref,
    above_ref,
    derivative_hbm,
    segment_hbm,
    derivative_ref,
    segment_ref,
    derivative_turned_ref,
    segment_turned_ref,
    tail_ref,
    sems,
):
    var_count, rows, pencils = segment_ref.shape
    count = pencils // LANES
    cells = var_count * rows
    variables = range(var_count)
    profile_at = kept_ref.shape[0] - 40
    back_height, groups, per = slices.back_height, slices.back_groups, slices.per
    block = lane_block(max(groups, 1), slices.width)
    for m in range(slices.rest):
        packed = []
        for i in range(per):
            start = (m * per + i) * back_height + slices.back_packed_at
            packed.append(back_ref[start : start + groups, :])
        for k in range(per):
            for i in range(per):
                moved = moved_lanes(packed[i], (i - k) * slices.width)
                joined = moved if i == 0 else jnp.where(block == i, moved, joined)
            tail_ref[pl.ds(m * groups * per + k, groups, stride=per), :] = joined

    def got(functional, v):
        line = functional * var_count + v
        parts = []
        for t in range(slices.full):
            start, end = slices.tiles_at(t)
            parts.append(
                back_ref[pl.ds(line * slices.full + t, end - start, stride=back_height), :]
            )
        for m in range(slices.rest):
            start = m * groups * per + line
            parts.append(tail_ref[start : start + 1, :])
        return jnp.concatenate(parts, axis=0)

    def profile(k):
        return kept_ref[profile_at + k : profile_at + k + 1, :]

    def kept(which, i):
        start = kept_at(which, i, rows, count)
        return kept_ref[start : start + count, :]

    def give(turned, straight, hbm, which):
        copies = []
        for v in variables:
            for t in range(count):
                start = t * cells + v * rows
                straight[v, :, tile(t)] = turned[start : start + rows, :]
            copies.append(
                pltpu.make_async_copy(straight.at[v], hbm.at[v], sems.at[which * var_count + v])
            )
            copies[-1].start()
        return copies

    lo, hi = [got(2, v) for v in variables], [got(3, v) for v in variables]
    swept = [[None] * rows for _ in variables]
    for i in range(rows):
        for v in variables:
            row = v * rows + i
            edge = slice(v * count, (v + 1) * count)
            far = profile(i) * lo[v] + profile(rows + i) * hi[v]
            if i == 0:
                far += profile(2 * rows) * below_ref[edge, :]
            if i == rows - 1:
                far += profile(2 * rows + 1) * above_ref[edge, :]
            value = slab_at(turned_ref, row, cells, count) + far
            put_slab(derivative_turned_ref, row, cells, count, value)
            if 0 < i < rows - 1:
                right = slab_at(turned_ref, cells * count + row, cells, count)
                right -= kept(3, i) * far
                if i > 1:
                    right += kept(0, i - 1) * swept[v][i - 1]
                swept[v][i] = right
    copies = give(derivative_turned_ref, derivative_ref, derivative_hbm, 0)
    first, last = [got(0, v) for v in variables], [got(1, v) for v in variables]
    x = list(last)
    for v in variables:
        put_slab(segment_turned_ref, v * rows, cells, count, first[v])
        put_slab(segment_turned_ref, (v + 1) * rows - 1, cells, count, last[v])
    for i in range(rows - 2, 0, -1):
        for v in variables:
            x[v] = kept(2, i) * swept[v][i] + kept(1, i) * first[v] + kept(0, i) * x[v]
            put_slab(segment_turned_ref, v * rows + i, cells, count, x[v])
    copies += give(segment_turned_ref, segment_ref, segment_hbm, 1)
    for copy in copies:
        copy.wait()


def call(kernel, outs, scratch, sems, args, near=(), far_out=False, limit=62):
    whole = pl.BlockSpec(memory_space=pltpu.VMEM)
    far = pl.BlockSpec(memory_space=pltpu.HBM)
    buffers = [
        pltpu.VMEM(s.shape, s.dtype) if hasattr(s, "dtype") else pltpu.VMEM(s, jnp.float32)
        for s in scratch
    ]
    buffers += [pltpu.SemaphoreType.DMA((size,)) for size in sems]
    return pl.pallas_call(
        kernel,
        out_shape=[jax.ShapeDtypeStruct(shape, jnp.float32) for shape in outs],
        in_specs=[whole if k in near else far for k in range(len(args))],
        out_specs=[far if far_out else whole] * len(outs),
        scratch_shapes=buffers,
        compiler_params=pltpu.CompilerParams(vmem_limit_bytes=limit * 2**20),
    )(*args)


def exchange(message, axes):
    return lax.all_to_all(message, axes, 0, 0, tiled=True)


def local(
    state,
    face_diffusion,
    courant,
    cell_mask,
    ghost_cell,
    ghost_owner,
    ghost_image,
    image_base,
    image_weight,
):
    var_count, rows, pencils = state.shape
    slabs, cross = lax.axis_size("pipe"), lax.axis_size("cross")
    count = pencils // LANES
    cells = var_count * rows
    images = image_base.shape[0]
    tables, at, carry_up, carry_down = derivative_tables(slabs, rows, var_count)
    slices = Slices(slabs, count, var_count)
    tables = jnp.asarray(tables)
    table = jax.ShapeDtypeStruct(tables.shape[1:], jnp.float32)
    turned = (cells * count, LANES)
    edge = (var_count * count, LANES)
    kept = (kept_at(4, 0, rows, count) + 40, LANES)

    (image_values,) = call(
        image_kernel,
        [(slabs, var_count * images // LANES, LANES)],
        [state, image_base, image_weight],
        [3],
        (state, image_base, image_weight),
    )
    image_values = exchange(image_values, "pipe")

    arguments = (
        face_diffusion,
        courant,
        tables,
        ghost_cell,
        ghost_owner,
        ghost_image,
        cell_mask,
        state,
    )
    message, kept_here = call(
        functools.partial(prepare_kernel, slices, at),
        [(slabs * slices.height, LANES), kept],
        [face_diffusion, courant, table, ghost_cell, ghost_owner, ghost_image, cell_mask, state]
        + [
            turned,
            (2 * rows * count, LANES),
            (2 * rows, pencils),
            (40 * count, LANES),
            (2 * rows, -(-count // 8) * 8, LANES),
            (cells, pencils),
            (max(slices.rest, 1) * max(slices.groups, 1) * slices.per, LANES),
        ],
        [len(arguments)],
        arguments,
    )
    image_values, message = lax.optimization_barrier((image_values, message))
    message = exchange(message, "pipe")
    blocks = [image_values] + [
        lax.ppermute(image_values, "cross", [(i, (i + s) % cross) for i in range(cross)])
        for s in range(1, cross)
    ]
    arguments = (ghost_owner, ghost_image, ghost_cell, courant, tables, cell_mask, state, *blocks)
    turned_here, up, down = call(
        functools.partial(fill_kernel, at),
        [(2 * cells * count, LANES), edge, edge],
        [ghost_owner, ghost_image, ghost_cell, courant, table, cell_mask, state, (cells, pencils)],
        [7],
        arguments,
        near=range(7, 7 + cross),
        limit=48,
    )
    forward = [(i, i + 1) for i in range(slabs - 1)]
    below = lax.ppermute(up, "pipe", forward)
    above = lax.ppermute(down, "pipe", [(j, i) for i, j in forward])

    spare = slabs * slices.per
    (back,) = call(
        functools.partial(solve_kernel, slices, carry_up, carry_down),
        [(slabs * slices.back_height, LANES)],
        [
            (slabs * slices.chunk * (6 * var_count + 2), LANES),
            (max(slices.groups, 1) * spare, LANES),
            (max(slices.back_groups, 1) * spare, LANES),
        ],
        [],
        (message, *blocks),
        near=range(1 + cross),
        limit=24,
    )
    back = exchange(back, "pipe")
    arguments = (back, turned_here, kept_here, below, above)
    return tuple(
        call(
            functools.partial(finish_kernel, slices),
            [state.shape, state.shape],
            [
                state.shape,
                state.shape,
                turned,
                turned,
                (max(slices.rest, 1) * max(slices.back_groups, 1) * slices.per, LANES),
            ],
            [2 * var_count],
            arguments,
            near=range(len(arguments)),
            far_out=True,
            limit=48,
        )
    )


def solution(mesh):
    in_specs = (
        P(None, "pipe", "cross"),
        P("pipe", "cross"),
        P("pipe", "cross"),
        P("pipe", "cross"),
        P(("pipe", "cross")),
        P(("pipe", "cross")),
        P(("pipe", "cross")),
        P(("pipe", "cross")),
        P(None, ("pipe", "cross")),
    )
    out_specs = (P(None, "pipe", "cross"), P(None, "pipe", "cross"))
    return jax.shard_map(local, mesh=mesh, in_specs=in_specs, out_specs=out_specs, check_vma=False)
```

```python
import functools

import numpy as np
import jax
import jax.numpy as jnp
from jax import lax
from jax.experimental import pallas as pl
from jax.experimental.pallas import tpu as pltpu
from jax.sharding import PartitionSpec as P

LINE = 96
LANES = 128
REFLECT = (1.0, -1.0, -1.0, -1.0, 1.0)

Z_UP, Z_DOWN, ROW_FIRST, ROW_LAST, RIGHT_FIRST, RIGHT_LAST = range(6)
LINK_IN, MARGIN_FIRST, MARGIN_LAST, LINK_UP, FIRST_LO, FIRST_HI, LAST_LO, LAST_HI, FIRST_EDGE, LAST_EDGE = range(10)
COEFFICIENTS = 10
PENCIL, ROW, OWNER, IMAGE, WEIGHT_UP, WEIGHT_DOWN, WEIGHT_FIRST, WEIGHT_LAST = range(8)


def derivative_tables(slabs, rows, var_count):
    total = slabs * rows
    A = np.eye(total)
    B = np.zeros((total, total))
    for i in range(2, total - 2):
        A[i, i - 1] = A[i, i + 1] = 1.0 / 3.0
        B[i, i + 1], B[i, i - 1] = 7.0 / 9.0, -7.0 / 9.0
        B[i, i + 2], B[i, i - 2] = 1.0 / 36.0, -1.0 / 36.0
    for i in (1, total - 2):
        A[i, i - 1] = A[i, i + 1] = 0.25
        B[i, i + 1], B[i, i - 1] = 0.75, -0.75
    B[0, :3] = (-1.5, 2.0, -0.5)
    B[-1, -3:] = (0.5, -2.0, 1.5)
    inverse = np.linalg.inv(A)
    M = inverse @ B

    cells = var_count * rows
    own_at, reduce_at, adjoint_at, profile_at, weight_at = 0, cells, cells + 16, cells + 56, cells + 96
    tables = np.zeros((slabs, cells + 112, LANES))
    carry_up, carry_down = np.zeros(slabs), np.zeros(slabs)
    for p in range(slabs):
        table = tables[p]
        base = p * rows
        here = slice(base, base + rows)
        own = M[here, here]
        lo, hi, lo_edge, hi_edge = (np.zeros(rows) for _ in range(4))
        weight_up, weight_down = np.zeros(rows), np.zeros(rows)
        if p > 0:
            lo = inverse[here, base - 8] / inverse[base + 1, base - 8]
            lo_edge[0] = M[base, base - 1] - lo[0] * M[base + 1, base - 1]
            weight_down = M[base - 2, here]
        if p > 1:
            k = base - rows - 8
            carry_up[p] = inverse[base + 1, k] / inverse[base - rows + 1, k]
        if p < slabs - 1:
            k = base + rows + 8
            hi = inverse[here, k] / inverse[base + rows - 2, k]
            hi_edge[-1] = M[base + rows - 1, base + rows] - hi[-1] * M[base + rows - 2, base + rows]
            weight_up = M[base + rows + 1, here]
        if p < slabs - 2:
            k = base + 2 * rows + 8
            carry_down[p] = inverse[base + rows - 2, k] / inverse[base + 2 * rows - 2, k]
        for v in range(var_count):
            at = slice(v * rows, (v + 1) * rows)
            table[own_at + v * rows : own_at + (v + 1) * rows, at] = own
            table[reduce_at + v, at] = weight_up
            table[reduce_at + var_count + v, at] = weight_down
        table[adjoint_at : adjoint_at + rows, :rows] = own.T
        table[adjoint_at + rows : adjoint_at + 2 * rows, rows : 2 * rows] = own.T
        more = adjoint_at + 2 * rows
        table[more, :rows] = lo
        table[more + 1, :rows] = hi
        table[more + 2, rows : 2 * rows] = lo
        table[more + 3, rows : 2 * rows] = hi
        table[more + 4, 0] = lo_edge[0]
        table[more + 5, 2 * rows - 1] = hi_edge[-1]
        table[profile_at : profile_at + rows] = lo[:, None]
        table[profile_at + rows : profile_at + 2 * rows] = hi[:, None]
        table[profile_at + 2 * rows] = lo_edge[0]
        table[profile_at + 2 * rows + 1] = hi_edge[-1]
        table[weight_at, :rows] = weight_up
        table[weight_at + 1, :rows] = weight_down
    at = (own_at, reduce_at, adjoint_at, profile_at, weight_at)
    return tables.astype(np.float32), at, carry_up, carry_down


def split(x, parts):
    pieces = []
    for _ in range(parts):
        piece = x.astype(jnp.bfloat16)
        pieces.append(piece)
        x = x - piece.astype(jnp.float32)
    return pieces


def exact_dot(x, one_hot, contract):
    found = lax.dot_general(
        jnp.concatenate(split(x, 3), axis=0),
        one_hot,
        (contract, ((), ())),
        preferred_element_type=jnp.float32,
    )
    size = x.shape[0]
    return found[:size] + (found[size : 2 * size] + found[2 * size :])


def full_dot(a, b):
    return jnp.dot(a, b, precision=lax.Precision.HIGHEST, preferred_element_type=jnp.float32)


def marks(shape, axis, values):
    return jnp.where(lax.broadcasted_iota(jnp.int32, shape, axis) == values, 1.0, 0.0).astype(
        jnp.bfloat16
    )


def place_of(cell, rows, pencils):
    row = jnp.zeros_like(cell)
    for k in range(1, rows):
        row += (cell >= k * pencils).astype(jnp.int32)
    return row, cell - row * pencils


def tile(t):
    return slice(t * LANES, (t + 1) * LANES)


def turn(ref, x):
    height, pencils = x.shape
    for t in range(pencils // LANES):
        ref[t * height : (t + 1) * height, :] = x[:, tile(t)]


def slab_at(ref, row, height, count):
    return ref[pl.ds(row, count, stride=height), :]


def put_slab(ref, row, height, count, value):
    ref[pl.ds(row, count, stride=height), :] = value


def kept_at(which, i, rows, count):
    return (which * rows + i) * (-(-count // 8) * 8)


def stay_at(rows, count, cells):
    kept = kept_at(4, 0, rows, count) + 40
    return kept, kept, kept + cells, kept + cells + 8


def ready_at(rows, count, cells):
    kept = 2 * cells * count
    return cells * count, kept, kept + stay_at(rows, count, cells)[3]


def fetch(sources, targets, sems):
    copies = [
        pltpu.make_async_copy(source, target, sems.at[k])
        for k, (source, target) in enumerate(zip(sources, targets))
    ]
    for copy in copies:
        copy.start()
    return copies


class Slices:
    def __init__(self, slabs, count, cross, var_count, images):
        rest = count % slabs
        self.slabs, self.count, self.cross, self.var_count = slabs, count, cross, var_count
        self.image_rows = var_count * images // LANES
        shared = rest > 0 and slabs % rest == 0 and LANES % (slabs // rest) == 0
        self.full = count // slabs if shared else -(-count // slabs)
        self.rest = rest if shared else 0
        self.per = slabs // rest if shared else 1
        self.width = LANES // self.per
        self.chunk = self.full + (1 if shared else 0)
        self.lines, self.back_lines = 6 * var_count + COEFFICIENTS, 6 * var_count
        self.groups, self.back_groups = (self.group_count(n) for n in (self.lines, self.back_lines))
        self.meta_at = self.lines * self.full
        self.packed_at = self.meta_at + 8
        self.images_at = self.packed_at + self.groups
        self.height = -(-(self.images_at + self.image_rows) // 8) * 8
        self.back_packed_at = self.back_lines * self.full
        self.back_height = -(-(self.back_packed_at + self.back_groups) // 8) * 8

    def group_count(self, lines):
        return -(-lines // self.per) if self.rest else 0

    def tiles_at(self, t):
        return t * self.slabs, min(self.count, (t + 1) * self.slabs)


def lane_block(rows, width):
    return lax.broadcasted_iota(jnp.int32, (rows, LANES), 1) // width


def moved_lanes(x, by):
    by %= LANES
    return x if by == 0 else pltpu.roll(x, by, 1)


def image_lines(x, base, weight_ref, rows, var_count):
    pencils = x.shape[1]
    images = base.shape[1]
    row, pencil = place_of(base, rows, pencils)
    pick = marks((pencils, images), 0, pencil)
    row_at = lax.broadcasted_iota(jnp.int32, (rows, images), 0)
    lower, upper = row_at == row, row_at == row + 1
    total = [jnp.zeros((rows, images), jnp.float32) for _ in range(var_count)]
    for corner, shift in enumerate((0, 1, LINE, LINE + 1)):
        moved = x if shift == 0 else pltpu.roll(x, pencils - shift, 1)
        pieces = jnp.concatenate(split(moved, 2), axis=0)
        found = jnp.dot(pieces, pick, preferred_element_type=jnp.float32)
        found = found[: var_count * rows] + found[var_count * rows :]
        weight = jnp.where(lower, weight_ref[corner : corner + 1], 0.0) + jnp.where(
            upper, weight_ref[corner + 4 : corner + 5], 0.0
        )
        for v in range(var_count):
            total[v] += found[v * rows : (v + 1) * rows] * weight
    lines = []
    for v in range(var_count):
        value = jnp.sum(total[v], axis=0, keepdims=True)
        lines += [value[:, tile(t)] for t in range(images // LANES)]
    return jnp.concatenate(lines, axis=0)


def ghost_values(slices, blocks, owner, image):
    per = slices.image_rows // slices.var_count
    slabs, cross = slices.slabs, slices.cross
    ghosts = owner.shape[1]
    across = lax.axis_index("cross")
    values = [
        jnp.concatenate(
            [
                jnp.concatenate(
                    [
                        block[pl.ds(v * per + t, slabs, stride=slices.image_rows), :]
                        for t in range(per)
                    ],
                    axis=1,
                )
                for block in blocks
            ],
            axis=0,
        )
        for v in range(slices.var_count)
    ]
    pick = marks((per * LANES, ghosts), 0, image)
    found = exact_dot(jnp.concatenate(values, axis=0), pick, ((1,), (0,)))
    devices = slabs * cross
    at = lax.broadcasted_iota(jnp.int32, (devices, ghosts), 0)
    mine = (at % slabs) * cross + (across + cross - at // slabs) % cross == owner
    return [
        reflect
        * jnp.sum(
            jnp.where(mine, found[v * devices : (v + 1) * devices], 0.0), axis=0, keepdims=True
        )
        for v, reflect in enumerate(REFLECT)
    ]


def prepare_kernel(
    slices,
    at,
    face_hbm,
    courant_hbm,
    tables_hbm,
    cell_hbm,
    owner_hbm,
    image_hbm,
    mask_hbm,
    base_hbm,
    corner_hbm,
    state_hbm,
    message_ref,
    stay_ref,
    face_ref,
    courant_ref,
    table_ref,
    cell_ref,
    owner_ref,
    image_ref,
    mask_ref,
    base_ref,
    corner_ref,
    state_ref,
    turned_ref,
    pair_ref,
    matrix_ref,
    adjoint_ref,
    weight_ref,
    cleared_ref,
    rest_ref,
    sems,
):
    var_count, rows, pencils = state_ref.shape
    cells = var_count * rows
    count = pencils // LANES
    ghosts = cell_ref.shape[0]
    padded = -(-count // 8) * 8
    p = lax.axis_index("pipe")
    slabs, height = slices.slabs, slices.height
    lines = slices.groups * slices.per
    own_at, reduce_at, adjoint_at, profile_at, weight_at = at
    copies = fetch(
        (
            face_hbm,
            courant_hbm,
            tables_hbm.at[p],
            cell_hbm,
            owner_hbm,
            image_hbm,
            mask_hbm,
            base_hbm,
            corner_hbm,
            state_hbm,
        ),
        (
            face_ref,
            courant_ref,
            table_ref,
            cell_ref,
            owner_ref,
            image_ref,
            mask_ref,
            base_ref,
            corner_ref,
            state_ref,
        ),
        sems,
    )
    kept, own, about_at, cleared_at = stay_at(rows, count, cells)

    def send(line, slab):
        for t in range(slices.full):
            start, end = slices.tiles_at(t)
            message_ref[pl.ds(line * slices.full + t, end - start, stride=height), :] = slab[start:end]
        for m in range(slices.rest):
            tail = slices.full * slabs + m
            rest_ref[m * lines + line : m * lines + line + 1, :] = slab[tail : tail + 1]

    def send_value(functional, v, slab):
        send(functional * var_count + v, slab)

    def send_coefficient(which, slab):
        send(6 * var_count + which, slab)

    copies[0].wait()
    turn(turned_ref, face_ref[...])

    def face(i):
        return slab_at(turned_ref, i, rows, count)

    link = face(0)
    margin = jnp.ones_like(link)
    first_margin = margin
    to_up, to_first = [None] * rows, [None] * rows
    for i in range(1, rows - 1):
        above = face(i)
        inverse = 1.0 / (link + margin + above)
        low, up = link * inverse, above * inverse
        to_up[i], to_first[i] = up, low
        for k, part in enumerate((up, low, inverse)):
            start = kept_at(k, i, rows, count)
            stay_ref[start : start + count, :] = part
        first_margin += low * margin
        link = link * up
        margin = 1.0 + margin * up
    send_coefficient(LINK_IN, link)
    send_coefficient(MARGIN_FIRST, first_margin)
    send_coefficient(MARGIN_LAST, margin)
    send_coefficient(LINK_UP, jnp.where(p == slabs - 1, 0.0, face(rows - 1)))

    zero, one = jnp.zeros_like(margin), jnp.ones_like(margin)
    first, last = [None] * rows, [None] * rows
    first[0], first[rows - 1], last[0], last[rows - 1] = one, zero, zero, one
    for i in range(rows - 2, 0, -1):
        first[i] = to_first[i] + to_up[i] * first[i + 1]
        last[i] = to_up[i] * last[i + 1]
    copies[1].wait()
    turn(turned_ref, courant_ref[...])
    for i in range(rows):
        speed = slab_at(turned_ref, i, rows, count)
        start = kept_at(3, i, rows, count)
        stay_ref[start : start + count, :] = speed
        put_slab(pair_ref, i, 2 * rows, count, first[i] * speed)
        put_slab(pair_ref, rows + i, 2 * rows, count, last[i] * speed)
    for t in range(count):
        matrix_ref[:, tile(t)] = pair_ref[t * 2 * rows : (t + 1) * 2 * rows, :]
    copies[2].wait()
    stay_ref[kept - 40 : kept, :] = table_ref[profile_at : profile_at + 40, :]
    stay_ref[own : own + cells, :] = table_ref[own_at : own_at + cells, :]
    turn(
        adjoint_ref, full_dot(table_ref[adjoint_at : adjoint_at + 40, : 2 * rows], matrix_ref[...])
    )
    for k in range(6):
        send_coefficient(FIRST_LO + k, slab_at(adjoint_ref, 2 * rows + k, 40, count))
    weight_ref[:, padded - 8 :, :] = jnp.zeros((2 * rows, 8, LANES), jnp.float32)
    for i, share in enumerate(first + last):
        weight_ref[i, :count, :] = share - slab_at(adjoint_ref, i, 40, count)

    for copy in copies[3:6]:
        copy.wait()
    row, pencil = place_of(cell_ref[...].reshape(1, ghosts), rows, pencils)
    lane_tile = jnp.right_shift(pencil, 7)
    lane_marks = marks((LANES, ghosts), 0, pencil - lane_tile * LANES)
    picked = exact_dot(
        weight_ref[...].reshape(2 * rows * padded, LANES), lane_marks, ((1,), (0,))
    ).reshape(2, rows, padded, ghosts)
    at_cell = (lax.broadcasted_iota(jnp.int32, (rows, padded, ghosts), 0) == row[None]) & (
        lax.broadcasted_iota(jnp.int32, (rows, padded, ghosts), 1) == lane_tile[None]
    )
    row_marks = jnp.where(lax.broadcasted_iota(jnp.int32, (rows, ghosts), 0) == row, 1.0, 0.0)
    up_down = full_dot(table_ref[weight_at : weight_at + 8, :rows], row_marks)

    def at_ghosts(values):
        return jnp.sum(jnp.sum(jnp.where(at_cell, values, 0.0), axis=0), axis=0, keepdims=True)

    about = jnp.concatenate(
        [
            pencil.astype(jnp.float32),
            row.astype(jnp.float32),
            owner_ref[...].reshape(1, ghosts).astype(jnp.float32),
            image_ref[...].reshape(1, ghosts).astype(jnp.float32),
            up_down[0:2],
            at_ghosts(picked[0]),
            at_ghosts(picked[1]),
        ],
        axis=0,
    )
    for j in range(slabs):
        start = j * height + slices.meta_at
        message_ref[start : start + 8, :] = about
    stay_ref[about_at : about_at + 8, :] = about
    for copy in copies[6:]:
        copy.wait()
    values = image_lines(
        state_ref[...].reshape(cells, pencils),
        base_ref[...].reshape(1, base_ref.shape[0]),
        corner_ref,
        rows,
        var_count,
    )
    for j in range(slabs):
        start = j * height + slices.images_at
        message_ref[start : start + slices.image_rows, :] = values
    solid = mask_ref[...] == 1
    for v in range(var_count):
        here = slice(v * rows, (v + 1) * rows)
        cleared_ref[here, :] = jnp.where(solid, 0.0, state_ref[v])
    turned = stay_ref.at[cleared_at : cleared_at + cells * count, :]
    turn(turned, cleared_ref[...])
    turn(pair_ref, full_dot(table_ref[reduce_at : reduce_at + 16, :cells], cleared_ref[...]))
    for k in range(2 * var_count):
        send(k, slab_at(pair_ref, k, 16, count))
    for v in range(var_count):
        low = high = zero
        for i in range(rows):
            cell = slab_at(stay_ref, cleared_at + v * rows + i, cells, count)
            if i == 0:
                send_value(ROW_FIRST, v, cell)
            if i == rows - 1:
                send_value(ROW_LAST, v, cell)
            low += weight_ref[i, :count, :] * cell
            high += weight_ref[rows + i, :count, :] * cell
        send_value(RIGHT_FIRST, v, low)
        send_value(RIGHT_LAST, v, high)

    block = lane_block(max(slices.groups, 1), slices.width)
    for m in range(slices.rest):
        lined = [
            rest_ref[pl.ds(m * lines + k, slices.groups, stride=slices.per), :]
            for k in range(slices.per)
        ]
        for i in range(slices.per):
            packed = lined[0]
            for k in range(slices.per):
                moved = moved_lanes(lined[k], (k - i) * slices.width)
                packed = moved if k == 0 else jnp.where(block == k, moved, packed)
            start = (m * slices.per + i) * height + slices.packed_at
            message_ref[start : start + slices.groups, :] = packed


def solve_kernel(slices, carry_up, carry_down, message_ref, *refs):
    *blocks, back_ref, ghost_ref, rest_ref, back_rest_ref = refs
    slabs, var_count, chunk, full = slices.slabs, slices.var_count, slices.chunk, slices.full
    height, per, width = slices.height, slices.per, slices.width
    me = lax.axis_index("pipe")

    def meta(p, k):
        start = p * height + slices.meta_at + k
        return message_ref[start : start + 1, :]

    def meta_all(k):
        return jnp.concatenate([meta(p, k) for p in range(slabs)], axis=1).astype(jnp.int32)

    values = ghost_values(slices, blocks, meta_all(OWNER), meta_all(IMAGE))
    ghost_lines = 6 * var_count + 2
    ghosts = LANES
    place = lax.broadcasted_iota(jnp.int32, (chunk * LANES, ghosts), 0)
    slot, lane = place // LANES, place % LANES
    pencil_at = jnp.where(
        slot < full,
        (me + slot * slabs) * LANES + lane,
        (full * slabs + me // per) * LANES + (me % per) * width + lane,
    )
    for p in range(slabs):
        row = meta(p, ROW)
        weights = (
            meta(p, WEIGHT_UP),
            meta(p, WEIGHT_DOWN),
            jnp.where(row == 0.0, 1.0, 0.0),
            jnp.where(row == 15.0, 1.0, 0.0),
            meta(p, WEIGHT_FIRST),
            meta(p, WEIGHT_LAST),
        )
        here = jnp.concatenate([value[:, tile(p)] for value in values], axis=0)
        shares = jnp.concatenate(
            [here * weight for weight in weights] + [jnp.zeros((2, ghosts), jnp.float32)], axis=0
        )
        spots = jnp.where(pencil_at == meta(p, PENCIL).astype(jnp.int32), 1.0, 0.0)
        share = exact_dot(shares, spots.astype(jnp.bfloat16), ((1,), (1,)))
        for t in range(chunk):
            start = (p * chunk + t) * ghost_lines
            ghost_ref[start : start + ghost_lines, :] = share[:, tile(t)]
        if slices.rest:
            start = p * height + slices.packed_at
            packed = message_ref[start : start + slices.groups, :]
            for k in range(per):
                rest_ref[pl.ds(p * slices.groups * per + k, slices.groups, stride=per), :] = (
                    moved_lanes(packed, -k * width)
                )

    def sent(p, line):
        start = p * height + line * full
        slab = message_ref[start : start + full, :]
        if slices.rest:
            start = p * slices.groups * per + line
            slab = jnp.concatenate([slab, rest_ref[start : start + 1, :]], axis=0)
        return slab

    def value(p, functional, v):
        line = functional * var_count + v
        start = p * chunk * ghost_lines + line
        return sent(p, line) + ghost_ref[pl.ds(start, chunk, stride=ghost_lines), :]

    def give(p, functional, v, slab):
        line = functional * var_count + v
        start = p * slices.back_height + line * full
        back_ref[start : start + full, :] = slab[:full]
        if slices.rest:
            start = p * slices.back_groups * per + line
            back_rest_ref[start : start + 1, :] = slab[full:]

    coefficients = [
        [sent(p, 6 * var_count + k) for k in range(COEFFICIENTS)] for p in range(slabs)
    ]
    nodes = 2 * slabs
    ratio, scale = [], []
    margin = coefficients[0][MARGIN_FIRST]
    for k in range(nodes):
        link = coefficients[k // 2][LINK_UP if k % 2 else LINK_IN]
        inverse = 1.0 / (margin + link)
        ratio.append(link * inverse)
        scale.append(inverse)
        if k < nodes - 1:
            following = coefficients[(k + 1) // 2][MARGIN_FIRST if k % 2 else MARGIN_LAST]
            margin = following + margin * ratio[k]

    zero = jnp.zeros((chunk, LANES), jnp.float32)
    for v in range(var_count):
        lo, hi = [zero] * slabs, [zero] * slabs
        below, above = [zero] * slabs, [zero] * slabs
        for p in range(1, slabs):
            lo[p] = value(p - 1, Z_UP, v) + float(carry_up[p]) * lo[p - 1]
            below[p] = value(p - 1, ROW_LAST, v)
        for p in range(slabs - 2, -1, -1):
            hi[p] = value(p + 1, Z_DOWN, v) + float(carry_down[p]) * hi[p + 1]
            above[p] = value(p + 1, ROW_FIRST, v)
        right = []
        for p in range(slabs):
            coefficient = coefficients[p]
            right.append(
                value(p, RIGHT_FIRST, v)
                - coefficient[FIRST_LO] * lo[p]
                - coefficient[FIRST_HI] * hi[p]
                - coefficient[FIRST_EDGE] * below[p]
            )
            right.append(
                value(p, RIGHT_LAST, v)
                - coefficient[LAST_LO] * lo[p]
                - coefficient[LAST_HI] * hi[p]
                - coefficient[LAST_EDGE] * above[p]
            )
            give(p, 2, v, lo[p])
            give(p, 3, v, hi[p])
            give(p, 4, v, below[p])
            give(p, 5, v, above[p])
        for k in range(1, nodes):
            right[k] = right[k] + ratio[k - 1] * right[k - 1]
        x = right[nodes - 1] * scale[nodes - 1]
        give(slabs - 1, 1, v, x)
        for k in range(nodes - 2, -1, -1):
            x = right[k] * scale[k] + ratio[k] * x
            give(k // 2, k % 2, v, x)
    if slices.rest:
        groups = slices.back_groups
        block = lane_block(groups, width)
        for p in range(slabs):
            for k in range(per):
                lined = back_rest_ref[pl.ds(p * groups * per + k, groups, stride=per), :]
                moved = moved_lanes(lined, k * width)
                packed = moved if k == 0 else jnp.where(block == k, moved, packed)
            start = p * slices.back_height + slices.back_packed_at
            back_ref[start : start + groups, :] = packed


def pick_kernel(slices, message_ref, values_ref):
    size = slices.image_rows
    for p in range(slices.slabs):
        start = p * slices.height + slices.images_at
        values_ref[p * size : (p + 1) * size, :] = message_ref[start : start + size, :]


def own_kernel(shape, stay_ref, ready_ref):
    var_count, rows, pencils = shape
    cells = var_count * rows
    count = pencils // LANES
    _, own_at, _, cleared_at = stay_at(rows, count, cells)
    cells_at, kept_start, end = ready_at(rows, count, cells)
    cleared = [
        stay_ref[cleared_at + t * cells : cleared_at + (t + 1) * cells, :] for t in range(count)
    ]
    for t in range(count):
        ready_ref[cells_at + t * cells : cells_at + (t + 1) * cells, :] = cleared[t]
    turn(
        ready_ref.at[: cells * count, :],
        full_dot(stay_ref[own_at : own_at + cells, :cells], jnp.concatenate(cleared, axis=1)),
    )
    ready_ref[kept_start:end, :] = stay_ref[:cleared_at, :]


def fill_kernel(slices, shape, ready_ref, *refs):
    *blocks, filled_ref = refs
    var_count, rows, pencils = shape
    cells = var_count * rows
    count = pencils // LANES
    _, own_at, about_at, _ = stay_at(rows, count, cells)
    _, kept_start, end = ready_at(rows, count, cells)

    def known(k):
        start = kept_start + about_at + k
        return ready_ref[start : start + 1, :].astype(jnp.int32)

    values = ghost_values(slices, blocks, known(OWNER), known(IMAGE))
    ghosts = LANES
    at_row = lax.broadcasted_iota(jnp.int32, (rows, ghosts), 0) == known(ROW)
    spread = jnp.concatenate([jnp.where(at_row, value, 0.0) for value in values], axis=0)
    own = ready_ref[kept_start + own_at : kept_start + own_at + cells, :cells]
    both = jnp.concatenate([full_dot(own, spread), spread], axis=0)
    spots = marks((pencils, ghosts), 0, known(PENCIL))
    added = exact_dot(both, spots, ((1,), (1,)))
    for t in range(count):
        for k in range(2):
            here = slice((k * count + t) * cells, (k * count + t + 1) * cells)
            filled_ref[here, :] = ready_ref[here, :] + added[k * cells : (k + 1) * cells, tile(t)]
    filled_ref[kept_start:end, :] = ready_ref[kept_start:end, :]


def finish_kernel(
    slices,
    back_ref,
    ready_ref,
    derivative_hbm,
    segment_hbm,
    derivative_ref,
    segment_ref,
    derivative_turned_ref,
    segment_turned_ref,
    tail_ref,
    sems,
):
    var_count, rows, pencils = segment_ref.shape
    count = pencils // LANES
    cells = var_count * rows
    variables = range(var_count)
    filled_start, kept_start, _ = ready_at(rows, count, cells)
    profile_at = kept_start + stay_at(rows, count, cells)[0] - 40
    back_height, groups, per = slices.back_height, slices.back_groups, slices.per
    block = lane_block(max(groups, 1), slices.width)
    for m in range(slices.rest):
        packed = []
        for i in range(per):
            start = (m * per + i) * back_height + slices.back_packed_at
            packed.append(back_ref[start : start + groups, :])
        for k in range(per):
            for i in range(per):
                moved = moved_lanes(packed[i], (i - k) * slices.width)
                joined = moved if i == 0 else jnp.where(block == i, moved, joined)
            tail_ref[pl.ds(m * groups * per + k, groups, stride=per), :] = joined

    def got(functional, v):
        line = functional * var_count + v
        parts = []
        for t in range(slices.full):
            start, end = slices.tiles_at(t)
            parts.append(
                back_ref[pl.ds(line * slices.full + t, end - start, stride=back_height), :]
            )
        for m in range(slices.rest):
            start = m * groups * per + line
            parts.append(tail_ref[start : start + 1, :])
        return jnp.concatenate(parts, axis=0)

    def profile(k):
        return ready_ref[profile_at + k : profile_at + k + 1, :]

    def kept(which, i):
        start = kept_start + kept_at(which, i, rows, count)
        return ready_ref[start : start + count, :]

    def give(turned, straight, hbm, which):
        copies = []
        for v in variables:
            for t in range(count):
                start = t * cells + v * rows
                straight[v, :, tile(t)] = turned[start : start + rows, :]
            copies.append(
                pltpu.make_async_copy(straight.at[v], hbm.at[v], sems.at[which * var_count + v])
            )
            copies[-1].start()
        return copies

    lo, hi = [got(2, v) for v in variables], [got(3, v) for v in variables]
    swept = [[None] * rows for _ in variables]
    for i in range(rows):
        for v in variables:
            row = v * rows + i
            far = profile(i) * lo[v] + profile(rows + i) * hi[v]
            if i == 0:
                far += profile(2 * rows) * got(4, v)
            if i == rows - 1:
                far += profile(2 * rows + 1) * got(5, v)
            value = slab_at(ready_ref, row, cells, count) + far
            put_slab(derivative_turned_ref, row, cells, count, value)
            if 0 < i < rows - 1:
                right = slab_at(ready_ref, filled_start + row, cells, count) - kept(3, i) * value
                if i > 1:
                    right += kept(0, i - 1) * swept[v][i - 1]
                swept[v][i] = right
    copies = give(derivative_turned_ref, derivative_ref, derivative_hbm, 0)
    first, last = [got(0, v) for v in variables], [got(1, v) for v in variables]
    x = list(last)
    for v in variables:
        put_slab(segment_turned_ref, v * rows, cells, count, first[v])
        put_slab(segment_turned_ref, (v + 1) * rows - 1, cells, count, last[v])
    for i in range(rows - 2, 0, -1):
        for v in variables:
            x[v] = kept(2, i) * swept[v][i] + kept(1, i) * first[v] + kept(0, i) * x[v]
            put_slab(segment_turned_ref, v * rows + i, cells, count, x[v])
    copies += give(segment_turned_ref, segment_ref, segment_hbm, 1)
    for copy in copies:
        copy.wait()


def call(kernel, outs, scratch, sems, args, near=(), far_out=False, limit=62):
    whole = pl.BlockSpec(memory_space=pltpu.VMEM)
    far = pl.BlockSpec(memory_space=pltpu.HBM)
    buffers = [
        pltpu.VMEM(s.shape, s.dtype) if hasattr(s, "dtype") else pltpu.VMEM(s, jnp.float32)
        for s in scratch
    ]
    buffers += [pltpu.SemaphoreType.DMA((size,)) for size in sems]
    return pl.pallas_call(
        kernel,
        out_shape=[jax.ShapeDtypeStruct(shape, jnp.float32) for shape in outs],
        in_specs=[whole if k in near else far for k in range(len(args))],
        out_specs=[far if far_out else whole] * len(outs),
        scratch_shapes=buffers,
        compiler_params=pltpu.CompilerParams(vmem_limit_bytes=limit * 2**20),
    )(*args)


def exchange(message, axes):
    return lax.all_to_all(message, axes, 0, 0, tiled=True)


def local(
    state,
    face_diffusion,
    courant,
    cell_mask,
    ghost_cell,
    ghost_owner,
    ghost_image,
    image_base,
    image_weight,
):
    var_count, rows, pencils = state.shape
    slabs, cross = lax.axis_size("pipe"), lax.axis_size("cross")
    count = pencils // LANES
    cells = var_count * rows
    images = image_base.shape[0]
    tables, at, carry_up, carry_down = derivative_tables(slabs, rows, var_count)
    slices = Slices(slabs, count, cross, var_count, images)
    tables = jnp.asarray(tables)
    turned = (cells * count, LANES)
    stay = stay_at(rows, count, cells)[3] + cells * count
    ready = (ready_at(rows, count, cells)[2], LANES)

    arguments = (
        face_diffusion,
        courant,
        tables,
        ghost_cell,
        ghost_owner,
        ghost_image,
        cell_mask,
        image_base,
        image_weight,
        state,
    )
    buffers = list(arguments)
    buffers[2] = jax.ShapeDtypeStruct(tables.shape[1:], jnp.float32)
    message, stay = call(
        functools.partial(prepare_kernel, slices, at),
        [(slabs * slices.height, LANES), (stay, LANES)],
        buffers
        + [
            (rows * count, LANES),
            (2 * rows * count, LANES),
            (2 * rows, pencils),
            (40 * count, LANES),
            (2 * rows, -(-count // 8) * 8, LANES),
            (cells, pencils),
            (max(slices.rest, 1) * max(slices.groups, 1) * slices.per, LANES),
        ],
        [len(arguments)],
        arguments,
    )
    message = exchange(message, "pipe")
    (ready,) = call(
        functools.partial(own_kernel, state.shape), [ready], [], [], (stay,), near=(0,), limit=48
    )
    (image_values,) = call(
        functools.partial(pick_kernel, slices),
        [(slabs * slices.image_rows, LANES)],
        [],
        [],
        (message,),
        near=(0,),
        limit=24,
    )
    blocks = [image_values] + [
        lax.ppermute(image_values, "cross", [(i, (i + u) % cross) for i in range(cross)])
        for u in range(1, cross)
    ]

    spare = slabs * slices.per
    (back,) = call(
        functools.partial(solve_kernel, slices, carry_up, carry_down),
        [(slabs * slices.back_height, LANES)],
        [
            (slabs * slices.chunk * (6 * var_count + 2), LANES),
            (max(slices.groups, 1) * spare, LANES),
            (max(slices.back_groups, 1) * spare, LANES),
        ],
        [],
        (message, *blocks),
        near=range(1 + cross),
        limit=24,
    )
    back = exchange(back, "pipe")
    (ready,) = call(
        functools.partial(fill_kernel, slices, state.shape),
        [ready.shape],
        [],
        [],
        (ready, *blocks),
        near=range(1 + cross),
        limit=48,
    )
    return tuple(
        call(
            functools.partial(finish_kernel, slices),
            [state.shape, state.shape],
            [
                state.shape,
                state.shape,
                turned,
                turned,
                (max(slices.rest, 1) * max(slices.back_groups, 1) * slices.per, LANES),
            ],
            [2 * var_count],
            (back, ready),
            near=range(2),
            far_out=True,
            limit=48,
        )
    )


def solution(mesh):
    in_specs = (
        P(None, "pipe", "cross"),
        P("pipe", "cross"),
        P("pipe", "cross"),
        P("pipe", "cross"),
        P(("pipe", "cross")),
        P(("pipe", "cross")),
        P(("pipe", "cross")),
        P(("pipe", "cross")),
        P(None, ("pipe", "cross")),
    )
    out_specs = (P(None, "pipe", "cross"), P(None, "pipe", "cross"))
    return jax.shard_map(local, mesh=mesh, in_specs=in_specs, out_specs=out_specs, check_vma=False)
```

```python
import functools

import numpy as np
import jax
import jax.numpy as jnp
from jax import lax
from jax.experimental import pallas as pl
from jax.experimental.pallas import tpu as pltpu
from jax.sharding import PartitionSpec as P

LINE = 96
LANES = 128
REFLECT = (1.0, -1.0, -1.0, -1.0, 1.0)

Z_UP, Z_DOWN, ROW_FIRST, ROW_LAST, RIGHT_FIRST, RIGHT_LAST = range(6)
LINK_IN, MARGIN_FIRST, MARGIN_LAST, LINK_UP, FIRST_LO, FIRST_HI, LAST_LO, LAST_HI, FIRST_EDGE, LAST_EDGE = range(10)
COEFFICIENTS = 10
PENCIL, ROW, OWNER, IMAGE, WEIGHT_UP, WEIGHT_DOWN, WEIGHT_FIRST, WEIGHT_LAST = range(8)


def derivative_tables(slabs, rows, var_count):
    total = slabs * rows
    A = np.eye(total)
    B = np.zeros((total, total))
    for i in range(2, total - 2):
        A[i, i - 1] = A[i, i + 1] = 1.0 / 3.0
        B[i, i + 1], B[i, i - 1] = 7.0 / 9.0, -7.0 / 9.0
        B[i, i + 2], B[i, i - 2] = 1.0 / 36.0, -1.0 / 36.0
    for i in (1, total - 2):
        A[i, i - 1] = A[i, i + 1] = 0.25
        B[i, i + 1], B[i, i - 1] = 0.75, -0.75
    B[0, :3] = (-1.5, 2.0, -0.5)
    B[-1, -3:] = (0.5, -2.0, 1.5)
    inverse = np.linalg.inv(A)
    M = inverse @ B

    cells = var_count * rows
    own_at, reduce_at, adjoint_at, profile_at, weight_at = 0, cells, cells + 16, cells + 56, cells + 96
    tables = np.zeros((slabs, cells + 112, LANES))
    carry_up, carry_down = np.zeros(slabs), np.zeros(slabs)
    for p in range(slabs):
        table = tables[p]
        base = p * rows
        here = slice(base, base + rows)
        own = M[here, here]
        lo, hi, lo_edge, hi_edge = (np.zeros(rows) for _ in range(4))
        weight_up, weight_down = np.zeros(rows), np.zeros(rows)
        if p > 0:
            lo = inverse[here, base - 8] / inverse[base + 1, base - 8]
            lo_edge[0] = M[base, base - 1] - lo[0] * M[base + 1, base - 1]
            weight_down = M[base - 2, here]
        if p > 1:
            k = base - rows - 8
            carry_up[p] = inverse[base + 1, k] / inverse[base - rows + 1, k]
        if p < slabs - 1:
            k = base + rows + 8
            hi = inverse[here, k] / inverse[base + rows - 2, k]
            hi_edge[-1] = M[base + rows - 1, base + rows] - hi[-1] * M[base + rows - 2, base + rows]
            weight_up = M[base + rows + 1, here]
        if p < slabs - 2:
            k = base + 2 * rows + 8
            carry_down[p] = inverse[base + rows - 2, k] / inverse[base + 2 * rows - 2, k]
        for v in range(var_count):
            at = slice(v * rows, (v + 1) * rows)
            table[own_at + v * rows : own_at + (v + 1) * rows, at] = own
            table[reduce_at + v, at] = weight_up
            table[reduce_at + var_count + v, at] = weight_down
        table[adjoint_at : adjoint_at + rows, :rows] = own.T
        table[adjoint_at + rows : adjoint_at + 2 * rows, rows : 2 * rows] = own.T
        more = adjoint_at + 2 * rows
        table[more, :rows] = lo
        table[more + 1, :rows] = hi
        table[more + 2, rows : 2 * rows] = lo
        table[more + 3, rows : 2 * rows] = hi
        table[more + 4, 0] = lo_edge[0]
        table[more + 5, 2 * rows - 1] = hi_edge[-1]
        table[profile_at : profile_at + rows] = lo[:, None]
        table[profile_at + rows : profile_at + 2 * rows] = hi[:, None]
        table[profile_at + 2 * rows] = lo_edge[0]
        table[profile_at + 2 * rows + 1] = hi_edge[-1]
        table[weight_at, :rows] = weight_up
        table[weight_at + 1, :rows] = weight_down
    at = (own_at, reduce_at, adjoint_at, profile_at, weight_at)
    return tables.astype(np.float32), at, carry_up, carry_down


def split(x, parts):
    pieces = []
    for _ in range(parts):
        piece = x.astype(jnp.bfloat16)
        pieces.append(piece)
        x = x - piece.astype(jnp.float32)
    return pieces


def exact_dot(x, one_hot, contract):
    found = lax.dot_general(
        jnp.concatenate(split(x, 3), axis=0),
        one_hot,
        (contract, ((), ())),
        preferred_element_type=jnp.float32,
    )
    size = x.shape[0]
    return found[:size] + (found[size : 2 * size] + found[2 * size :])


def full_dot(a, b):
    return jnp.dot(a, b, precision=lax.Precision.HIGHEST, preferred_element_type=jnp.float32)


def marks(shape, axis, values):
    return jnp.where(lax.broadcasted_iota(jnp.int32, shape, axis) == values, 1.0, 0.0).astype(
        jnp.bfloat16
    )


def place_of(cell, rows, pencils):
    row = jnp.zeros_like(cell)
    for k in range(1, rows):
        row += (cell >= k * pencils).astype(jnp.int32)
    return row, cell - row * pencils


def tile(t):
    return slice(t * LANES, (t + 1) * LANES)


def turn(ref, x):
    height, pencils = x.shape
    for t in range(pencils // LANES):
        ref[t * height : (t + 1) * height, :] = x[:, tile(t)]


def slab_at(ref, row, height, count):
    return ref[pl.ds(row, count, stride=height), :]


def put_slab(ref, row, height, count, value):
    ref[pl.ds(row, count, stride=height), :] = value


def kept_at(which, i, rows, count):
    return (which * rows + i) * (-(-count // 8) * 8)


def stay_at(rows, count, cells):
    kept = kept_at(4, 0, rows, count) + 40
    return kept, kept, kept + cells, kept + cells + 8


def ready_at(rows, count, cells):
    kept = 2 * cells * count
    return cells * count, kept, kept + stay_at(rows, count, cells)[3]


def done_at(rows, count, cells):
    x = cells * count
    response = 2 * x
    profile = response + 4 * rows * count
    return x, response, profile, profile + 40


def fetch(sources, targets, sems):
    copies = [
        pltpu.make_async_copy(source, target, sems.at[k])
        for k, (source, target) in enumerate(zip(sources, targets))
    ]
    for copy in copies:
        copy.start()
    return copies


class Slices:
    def __init__(self, slabs, count, cross, var_count, images):
        rest = count % slabs
        self.slabs, self.count, self.cross, self.var_count = slabs, count, cross, var_count
        self.image_rows = var_count * images // LANES
        shared = rest > 0 and slabs % rest == 0 and LANES % (slabs // rest) == 0
        self.full = count // slabs if shared else -(-count // slabs)
        self.rest = rest if shared else 0
        self.per = slabs // rest if shared else 1
        self.width = LANES // self.per
        self.chunk = self.full + (1 if shared else 0)
        self.lines, self.back_lines = 6 * var_count + COEFFICIENTS, 6 * var_count
        self.groups, self.back_groups = (self.group_count(n) for n in (self.lines, self.back_lines))
        self.meta_at = self.lines * self.full
        self.packed_at = self.meta_at + 8
        self.images_at = self.packed_at + self.groups
        self.height = -(-(self.images_at + self.image_rows) // 8) * 8
        self.back_packed_at = self.back_lines * self.full
        self.back_height = -(-(self.back_packed_at + self.back_groups) // 8) * 8

    def group_count(self, lines):
        return -(-lines // self.per) if self.rest else 0

    def row(self, functional, t):
        return (functional * self.full + t) * self.var_count

    def coefficient_row(self, which, t):
        return 6 * self.full * self.var_count + which * self.full + t

    def tiles_at(self, t):
        return t * self.slabs, min(self.count, (t + 1) * self.slabs)


def lane_block(rows, width):
    return lax.broadcasted_iota(jnp.int32, (rows, LANES), 1) // width


def moved_lanes(x, by):
    by %= LANES
    return x if by == 0 else pltpu.roll(x, by, 1)


def image_lines(x, base, weight_ref, rows, var_count):
    pencils = x.shape[1]
    images = base.shape[1]
    row, pencil = place_of(base, rows, pencils)
    pick = marks((pencils, images), 0, pencil)
    row_at = lax.broadcasted_iota(jnp.int32, (rows, images), 0)
    lower, upper = row_at == row, row_at == row + 1
    total = [jnp.zeros((rows, images), jnp.float32) for _ in range(var_count)]
    for corner, shift in enumerate((0, 1, LINE, LINE + 1)):
        moved = x if shift == 0 else pltpu.roll(x, pencils - shift, 1)
        pieces = jnp.concatenate(split(moved, 2), axis=0)
        found = jnp.dot(pieces, pick, preferred_element_type=jnp.float32)
        found = found[: var_count * rows] + found[var_count * rows :]
        weight = jnp.where(lower, weight_ref[corner : corner + 1], 0.0) + jnp.where(
            upper, weight_ref[corner + 4 : corner + 5], 0.0
        )
        for v in range(var_count):
            total[v] += found[v * rows : (v + 1) * rows] * weight
    lines = []
    for v in range(var_count):
        value = jnp.sum(total[v], axis=0, keepdims=True)
        lines += [value[:, tile(t)] for t in range(images // LANES)]
    return jnp.concatenate(lines, axis=0)


def ghost_values(slices, blocks, owner, image):
    per = slices.image_rows // slices.var_count
    slabs, cross = slices.slabs, slices.cross
    ghosts = owner.shape[1]
    across = lax.axis_index("cross")
    values = [
        jnp.concatenate(
            [
                jnp.concatenate(
                    [
                        block[pl.ds(v * per + t, slabs, stride=slices.image_rows), :]
                        for t in range(per)
                    ],
                    axis=1,
                )
                for block in blocks
            ],
            axis=0,
        )
        for v in range(slices.var_count)
    ]
    pick = marks((per * LANES, ghosts), 0, image)
    found = exact_dot(jnp.concatenate(values, axis=0), pick, ((1,), (0,)))
    devices = slabs * cross
    at = lax.broadcasted_iota(jnp.int32, (devices, ghosts), 0)
    mine = (at % slabs) * cross + (across + cross - at // slabs) % cross == owner
    return [
        reflect
        * jnp.sum(
            jnp.where(mine, found[v * devices : (v + 1) * devices], 0.0), axis=0, keepdims=True
        )
        for v, reflect in enumerate(REFLECT)
    ]


def prepare_kernel(
    slices,
    at,
    face_hbm,
    courant_hbm,
    tables_hbm,
    cell_hbm,
    owner_hbm,
    image_hbm,
    mask_hbm,
    base_hbm,
    corner_hbm,
    state_hbm,
    message_ref,
    stay_hbm,
    face_ref,
    courant_ref,
    table_ref,
    cell_ref,
    owner_ref,
    image_ref,
    mask_ref,
    base_ref,
    corner_ref,
    state_ref,
    stay_ref,
    face_turned_ref,
    courant_turned_ref,
    pair_ref,
    z_ref,
    matrix_ref,
    adjoint_ref,
    weight_ref,
    cleared_ref,
    rest_ref,
    sems,
    stay_sem,
):
    var_count, rows, pencils = state_ref.shape
    cells = var_count * rows
    count = pencils // LANES
    ghosts = cell_ref.shape[0]
    padded = -(-count // 8) * 8
    p = lax.axis_index("pipe")
    slabs, height = slices.slabs, slices.height
    lines = slices.groups * slices.per
    own_at, reduce_at, adjoint_at, profile_at, weight_at = at
    copies = fetch(
        (
            face_hbm,
            courant_hbm,
            tables_hbm.at[p],
            cell_hbm,
            owner_hbm,
            image_hbm,
            mask_hbm,
            base_hbm,
            corner_hbm,
            state_hbm,
        ),
        (
            face_ref,
            courant_ref,
            table_ref,
            cell_ref,
            owner_ref,
            image_ref,
            mask_ref,
            base_ref,
            corner_ref,
            state_ref,
        ),
        sems,
    )
    kept, own, about_at, cleared_at = stay_at(rows, count, cells)

    def send(line, rows_at, slab):
        for t, row_at in enumerate(rows_at):
            start, end = slices.tiles_at(t)
            message_ref[pl.ds(row_at, end - start, stride=height), :] = slab[start:end]
        for m in range(slices.rest):
            tail = slices.full * slabs + m
            rest_ref[m * lines + line : m * lines + line + 1, :] = slab[tail : tail + 1]

    def send_value(functional, v, slab):
        rows_at = [slices.row(functional, t) + v for t in range(slices.full)]
        send(functional * var_count + v, rows_at, slab)

    def send_coefficient(which, slab):
        rows_at = [slices.coefficient_row(which, t) for t in range(slices.full)]
        send(6 * var_count + which, rows_at, slab)

    copies[0].wait()
    turn(face_turned_ref, face_ref[...])

    def face(i):
        return slab_at(face_turned_ref, i, rows, count)

    link = face(0)
    margin = jnp.ones_like(link)
    first_margin = margin
    to_up, to_first = [None] * rows, [None] * rows
    for i in range(1, rows - 1):
        above = face(i)
        inverse = 1.0 / (link + margin + above)
        low, up = link * inverse, above * inverse
        to_up[i], to_first[i] = up, low
        for k, part in enumerate((up, low, inverse)):
            start = kept_at(k, i, rows, count)
            stay_ref[start : start + count, :] = part
        first_margin += low * margin
        link = link * up
        margin = 1.0 + margin * up
    send_coefficient(LINK_IN, link)
    send_coefficient(MARGIN_FIRST, first_margin)
    send_coefficient(MARGIN_LAST, margin)
    send_coefficient(LINK_UP, jnp.where(p == slabs - 1, 0.0, face(rows - 1)))

    zero, one = jnp.zeros_like(margin), jnp.ones_like(margin)
    first, last = [None] * rows, [None] * rows
    first[0], first[rows - 1], last[0], last[rows - 1] = one, zero, zero, one
    for i in range(rows - 2, 0, -1):
        first[i] = to_first[i] + to_up[i] * first[i + 1]
        last[i] = to_up[i] * last[i + 1]
    copies[1].wait()
    turn(courant_turned_ref, courant_ref[...])
    for i in range(rows):
        speed = slab_at(courant_turned_ref, i, rows, count)
        start = kept_at(3, i, rows, count)
        stay_ref[start : start + count, :] = speed
        put_slab(pair_ref, i, 2 * rows, count, first[i] * speed)
        put_slab(pair_ref, rows + i, 2 * rows, count, last[i] * speed)
    for t in range(count):
        matrix_ref[:, tile(t)] = pair_ref[t * 2 * rows : (t + 1) * 2 * rows, :]
    copies[2].wait()
    stay_ref[kept - 40 : kept, :] = table_ref[profile_at : profile_at + 40, :]
    stay_ref[own : own + cells, :] = table_ref[own_at : own_at + cells, :]
    turn(
        adjoint_ref, full_dot(table_ref[adjoint_at : adjoint_at + 40, : 2 * rows], matrix_ref[...])
    )
    for k in range(6):
        send_coefficient(FIRST_LO + k, slab_at(adjoint_ref, 2 * rows + k, 40, count))
    weight_ref[:, padded - 8 :, :] = jnp.zeros((2 * rows, 8, LANES), jnp.float32)
    for i, share in enumerate(first + last):
        weight_ref[i, :count, :] = share - slab_at(adjoint_ref, i, 40, count)

    for copy in copies[3:6]:
        copy.wait()
    row, pencil = place_of(cell_ref[...].reshape(1, ghosts), rows, pencils)
    lane_tile = jnp.right_shift(pencil, 7)
    lane_marks = marks((LANES, ghosts), 0, pencil - lane_tile * LANES)
    picked = exact_dot(
        weight_ref[...].reshape(2 * rows * padded, LANES), lane_marks, ((1,), (0,))
    ).reshape(2, rows, padded, ghosts)
    at_cell = (lax.broadcasted_iota(jnp.int32, (rows, padded, ghosts), 0) == row[None]) & (
        lax.broadcasted_iota(jnp.int32, (rows, padded, ghosts), 1) == lane_tile[None]
    )
    row_marks = jnp.where(lax.broadcasted_iota(jnp.int32, (rows, ghosts), 0) == row, 1.0, 0.0)
    up_down = full_dot(table_ref[weight_at : weight_at + 8, :rows], row_marks)

    def at_ghosts(values):
        return jnp.sum(jnp.sum(jnp.where(at_cell, values, 0.0), axis=0), axis=0, keepdims=True)

    about = jnp.concatenate(
        [
            pencil.astype(jnp.float32),
            row.astype(jnp.float32),
            owner_ref[...].reshape(1, ghosts).astype(jnp.float32),
            image_ref[...].reshape(1, ghosts).astype(jnp.float32),
            up_down[0:2],
            at_ghosts(picked[0]),
            at_ghosts(picked[1]),
        ],
        axis=0,
    )
    for j in range(slabs):
        start = j * height + slices.meta_at
        message_ref[start : start + 8, :] = about
    stay_ref[about_at : about_at + 8, :] = about
    for copy in copies[6:]:
        copy.wait()
    values = image_lines(
        state_ref[...].reshape(cells, pencils),
        base_ref[...].reshape(1, base_ref.shape[0]),
        corner_ref,
        rows,
        var_count,
    )
    for j in range(slabs):
        start = j * height + slices.images_at
        message_ref[start : start + slices.image_rows, :] = values
    solid = mask_ref[...] == 1
    for v in range(var_count):
        here = slice(v * rows, (v + 1) * rows)
        cleared_ref[here, :] = jnp.where(solid, 0.0, state_ref[v])
    turn(stay_ref.at[cleared_at : cleared_at + cells * count, :], cleared_ref[...])
    turn(z_ref, full_dot(table_ref[reduce_at : reduce_at + 16, :cells], cleared_ref[...]))
    for v in range(var_count):
        send_value(Z_UP, v, slab_at(z_ref, v, 16, count))
        send_value(Z_DOWN, v, slab_at(z_ref, var_count + v, 16, count))
    staying = pltpu.make_async_copy(stay_ref, stay_hbm, stay_sem.at[0])
    staying.start()
    low, high = ([jnp.zeros((count, LANES), jnp.float32)] * var_count for _ in range(2))
    for i in range(rows):
        to_low, to_high = weight_ref[i, :count, :], weight_ref[rows + i, :count, :]
        for v in range(var_count):
            cell = slab_at(stay_ref, cleared_at + v * rows + i, cells, count)
            if i == 0:
                send_value(ROW_FIRST, v, cell)
            if i == rows - 1:
                send_value(ROW_LAST, v, cell)
            low[v] = low[v] + to_low * cell
            high[v] = high[v] + to_high * cell
    for v in range(var_count):
        send_value(RIGHT_FIRST, v, low[v])
        send_value(RIGHT_LAST, v, high[v])

    block = lane_block(max(slices.groups, 1), slices.width)
    for m in range(slices.rest):
        lined = [
            rest_ref[pl.ds(m * lines + k, slices.groups, stride=slices.per), :]
            for k in range(slices.per)
        ]
        for i in range(slices.per):
            packed = lined[0]
            for k in range(slices.per):
                moved = moved_lanes(lined[k], (k - i) * slices.width)
                packed = moved if k == 0 else jnp.where(block == k, moved, packed)
            start = (m * slices.per + i) * height + slices.packed_at
            message_ref[start : start + slices.groups, :] = packed
    staying.wait()


def chain_kernel(slices, message_ref, rest_ref, chain_ref):
    slabs, chunk, full = slices.slabs, slices.chunk, slices.full
    height, per, width = slices.height, slices.per, slices.width
    if slices.rest:
        for p in range(slabs):
            start = p * height + slices.packed_at
            packed = message_ref[start : start + slices.groups, :]
            for k in range(per):
                rest_ref[pl.ds(p * slices.groups * per + k, slices.groups, stride=per), :] = (
                    moved_lanes(packed, -k * width)
                )
    else:
        rest_ref[...] = jnp.zeros_like(rest_ref)

    def sent(p, which):
        start = p * height + slices.coefficient_row(which, 0)
        slab = message_ref[start : start + full, :]
        if slices.rest:
            start = p * slices.groups * per + 6 * slices.var_count + which
            slab = jnp.concatenate([slab, rest_ref[start : start + 1, :]], axis=0)
        return slab

    nodes = 2 * slabs
    margin = sent(0, MARGIN_FIRST)
    for k in range(nodes):
        link = sent(k // 2, LINK_UP if k % 2 else LINK_IN)
        inverse = 1.0 / (margin + link)
        ratio = link * inverse
        chain_ref[16 * k : 16 * k + chunk, :] = ratio
        chain_ref[16 * k + 8 : 16 * k + 8 + chunk, :] = inverse
        if k < nodes - 1:
            following = sent((k + 1) // 2, MARGIN_FIRST if k % 2 else MARGIN_LAST)
            margin = following + margin * ratio


def solve_kernel(slices, carry_up, carry_down, message_ref, rest_ref, chain_ref, *refs):
    *blocks, back_ref, ghost_ref, back_rest_ref = refs
    slabs, var_count, chunk, full = slices.slabs, slices.var_count, slices.chunk, slices.full
    height, per, width = slices.height, slices.per, slices.width
    me = lax.axis_index("pipe")

    def meta(p, k):
        start = p * height + slices.meta_at + k
        return message_ref[start : start + 1, :]

    def meta_all(k):
        return jnp.concatenate([meta(p, k) for p in range(slabs)], axis=1).astype(jnp.int32)

    values = ghost_values(slices, blocks, meta_all(OWNER), meta_all(IMAGE))
    ghosts = LANES
    place = lax.broadcasted_iota(jnp.int32, (chunk * LANES, ghosts), 0)
    slot, lane = place // LANES, place % LANES
    pencil_at = jnp.where(
        slot < full,
        (me + slot * slabs) * LANES + lane,
        (full * slabs + me // per) * LANES + (me % per) * width + lane,
    )
    none = jnp.zeros((8 - var_count, ghosts), jnp.float32)
    for p in range(slabs):
        row = meta(p, ROW)
        weights = (
            meta(p, WEIGHT_UP),
            meta(p, WEIGHT_DOWN),
            jnp.where(row == 0.0, 1.0, 0.0),
            jnp.where(row == 15.0, 1.0, 0.0),
            meta(p, WEIGHT_FIRST),
            meta(p, WEIGHT_LAST),
        )
        here = jnp.concatenate([value[:, tile(p)] for value in values] + [none], axis=0)
        shares = jnp.concatenate([here * weight for weight in weights], axis=0)
        spots = jnp.where(pencil_at == meta(p, PENCIL).astype(jnp.int32), 1.0, 0.0)
        share = exact_dot(shares, spots.astype(jnp.bfloat16), ((1,), (1,)))
        for t in range(chunk):
            start = (p * chunk + t) * 48
            ghost_ref[start : start + 48, :] = share[:, tile(t)]

    nodes = 2 * slabs
    zero = jnp.zeros((var_count, LANES), jnp.float32)
    for t in range(chunk):

        def value(p, functional):
            if t < full:
                start = p * height + slices.row(functional, t)
                sent = message_ref[start : start + var_count, :]
            else:
                start = p * slices.groups * per + functional * var_count
                sent = rest_ref[start : start + var_count, :]
            start = (p * chunk + t) * 48 + functional * 8
            return sent + ghost_ref[start : start + var_count, :]

        def coefficient(p, which):
            if t < full:
                start = p * height + slices.coefficient_row(which, t)
                return message_ref[start : start + 1, :]
            start = p * slices.groups * per + 6 * var_count + which
            return rest_ref[start : start + 1, :]

        def give(p, functional, block):
            if t < full:
                start = p * slices.back_height + slices.row(functional, t)
                back_ref[start : start + var_count, :] = block
            else:
                start = p * slices.back_groups * per + functional * var_count
                back_rest_ref[start : start + var_count, :] = block

        def ratio(k):
            return chain_ref[16 * k + t : 16 * k + t + 1, :]

        def scale(k):
            return chain_ref[16 * k + 8 + t : 16 * k + 9 + t, :]

        lo, hi, below, above = ([zero] * slabs for _ in range(4))
        for p in range(1, slabs):
            lo[p] = value(p - 1, Z_UP) + float(carry_up[p]) * lo[p - 1]
            below[p] = value(p - 1, ROW_LAST)
        for p in range(slabs - 2, -1, -1):
            hi[p] = value(p + 1, Z_DOWN) + float(carry_down[p]) * hi[p + 1]
            above[p] = value(p + 1, ROW_FIRST)
        right = []
        for p in range(slabs):
            right.append(
                value(p, RIGHT_FIRST)
                - coefficient(p, FIRST_LO) * lo[p]
                - coefficient(p, FIRST_HI) * hi[p]
                - coefficient(p, FIRST_EDGE) * below[p]
            )
            right.append(
                value(p, RIGHT_LAST)
                - coefficient(p, LAST_LO) * lo[p]
                - coefficient(p, LAST_HI) * hi[p]
                - coefficient(p, LAST_EDGE) * above[p]
            )
            for functional, block in enumerate((lo[p], hi[p], below[p], above[p])):
                give(p, 2 + functional, block)
        for k in range(1, nodes):
            right[k] = right[k] + ratio(k - 1) * right[k - 1]
        x = right[nodes - 1] * scale(nodes - 1)
        give(slabs - 1, 1, x)
        for k in range(nodes - 2, -1, -1):
            x = right[k] * scale(k) + ratio(k) * x
            give(k // 2, k % 2, x)
    if slices.rest:
        groups = slices.back_groups
        block = lane_block(groups, width)
        for p in range(slabs):
            for k in range(per):
                lined = back_rest_ref[pl.ds(p * groups * per + k, groups, stride=per), :]
                moved = moved_lanes(lined, k * width)
                packed = moved if k == 0 else jnp.where(block == k, moved, packed)
            start = p * slices.back_height + slices.back_packed_at
            back_ref[start : start + groups, :] = packed


def pick_kernel(slices, message_ref, values_ref):
    size = slices.image_rows
    for p in range(slices.slabs):
        start = p * slices.height + slices.images_at
        values_ref[p * size : (p + 1) * size, :] = message_ref[start : start + size, :]


def own_kernel(shape, stay_ref, ready_ref):
    var_count, rows, pencils = shape
    cells = var_count * rows
    count = pencils // LANES
    _, own_at, _, cleared_at = stay_at(rows, count, cells)
    cells_at, kept_start, end = ready_at(rows, count, cells)
    cleared = [
        stay_ref[cleared_at + t * cells : cleared_at + (t + 1) * cells, :] for t in range(count)
    ]
    for t in range(count):
        ready_ref[cells_at + t * cells : cells_at + (t + 1) * cells, :] = cleared[t]
    turn(
        ready_ref.at[: cells * count, :],
        full_dot(stay_ref[own_at : own_at + cells, :cells], jnp.concatenate(cleared, axis=1)),
    )
    ready_ref[kept_start:end, :] = stay_ref[:cleared_at, :]


def fill_kernel(slices, shape, ready_ref, *refs):
    *blocks, done_ref, filled_ref = refs
    var_count, rows, pencils = shape
    cells = var_count * rows
    count = pencils // LANES
    _, own_at, about_at, _ = stay_at(rows, count, cells)
    cells_at, kept_start, _ = ready_at(rows, count, cells)

    def known(k):
        start = kept_start + about_at + k
        return ready_ref[start : start + 1, :].astype(jnp.int32)

    values = ghost_values(slices, blocks, known(OWNER), known(IMAGE))
    ghosts = LANES
    at_row = lax.broadcasted_iota(jnp.int32, (rows, ghosts), 0) == known(ROW)
    spread = jnp.concatenate([jnp.where(at_row, value, 0.0) for value in values], axis=0)
    own = ready_ref[kept_start + own_at : kept_start + own_at + cells, :cells]
    both = jnp.concatenate([full_dot(own, spread), spread], axis=0)
    spots = marks((pencils, ghosts), 0, known(PENCIL))
    added = exact_dot(both, spots, ((1,), (1,)))
    for t in range(count):
        here = slice(t * cells, (t + 1) * cells)
        there = slice(cells_at + t * cells, cells_at + (t + 1) * cells)
        done_ref[here, :] = ready_ref[here, :] + added[:cells, tile(t)]
        filled_ref[here, :] = ready_ref[there, :] + added[cells:, tile(t)]
    x_at, response_at, profile_at, _ = done_at(rows, count, cells)

    def kept(which, i):
        start = kept_start + kept_at(which, i, rows, count)
        return ready_ref[start : start + count, :]

    def profile(k):
        start = kept_start + own_at - 40 + k
        return ready_ref[start : start + 1, :]

    def put(at, i, height, value):
        done_ref[pl.ds(at + i, count, stride=height), :] = value

    swept = []
    for i in range(1, rows - 1):
        speed = kept(3, i)
        here = [-speed * profile(i), -speed * profile(rows + i)]
        for v in range(var_count):
            row = v * rows + i
            own_slab = slab_at(done_ref, row, cells, count)
            here.append(slab_at(filled_ref, row, cells, count) - speed * own_slab)
        if swept:
            ratio = kept(0, i - 1)
            here = [x + ratio * y for x, y in zip(here, swept[-1])]
        swept.append(here)
    zero = jnp.zeros((count, LANES), jnp.float32)
    one = jnp.ones((count, LANES), jnp.float32)
    x = [zero] * (2 + var_count)
    first, last = zero, one
    for i in range(rows - 1, -1, -1):
        if 0 < i < rows - 1:
            ratio, inverse = kept(0, i), kept(2, i)
            first, last = kept(1, i) + ratio * first, ratio * last
            x = [inverse * y + ratio * z for y, z in zip(swept[i - 1], x)]
        if i == 0:
            first, last, x = one, zero, [zero] * (2 + var_count)
        for k, value in enumerate([first, last] + x[:2]):
            put(response_at + k * rows * count, i, rows, value)
        for v in range(var_count):
            put(x_at, v * rows + i, cells, x[2 + v])
    done_ref[profile_at : profile_at + 40, :] = ready_ref[
        kept_start + own_at - 40 : kept_start + own_at, :
    ]


def finish_kernel(
    slices, back_ref, done_ref, derivative_hbm, segment_hbm, derivative_ref, segment_ref, tail_ref, sems
):
    var_count, rows, pencils = segment_ref.shape
    count = pencils // LANES
    cells = var_count * rows
    x_at, response_at, profile_at, _ = done_at(rows, count, cells)
    back_height, groups, per = slices.back_height, slices.back_groups, slices.per
    block = lane_block(max(groups, 1), slices.width)
    for m in range(slices.rest):
        packed = []
        for i in range(per):
            start = (m * per + i) * back_height + slices.back_packed_at
            packed.append(back_ref[start : start + groups, :])
        for k in range(per):
            for i in range(per):
                moved = moved_lanes(packed[i], (i - k) * slices.width)
                joined = moved if i == 0 else jnp.where(block == i, moved, joined)
            tail_ref[pl.ds(m * groups * per + k, groups, stride=per), :] = joined

    def got(functional, v, t):
        step, j = t // slices.slabs, t % slices.slabs
        if step < slices.full:
            start = j * back_height + slices.row(functional, step) + v
            return back_ref[start : start + 1, :]
        start = j * groups * per + functional * var_count + v
        return tail_ref[start : start + 1, :]

    lo_profile = done_ref[profile_at : profile_at + rows, :]
    hi_profile = done_ref[profile_at + rows : profile_at + 2 * rows, :]
    row_at = lax.broadcasted_iota(jnp.int32, (rows, LANES), 0)
    edges = profile_at + 2 * rows
    lo_edge = jnp.where(row_at == 0, done_ref[edges : edges + 1, :], 0.0)
    hi_edge = jnp.where(row_at == rows - 1, done_ref[edges + 1 : edges + 2, :], 0.0)

    def response(k, t):
        start = response_at + (k * count + t) * rows
        return done_ref[start : start + rows, :]

    copies = []
    for v in range(var_count):
        for t in range(count):
            start = t * cells + v * rows
            lo, hi = got(2, v, t), got(3, v, t)
            derivative_ref[v, :, tile(t)] = (
                done_ref[start : start + rows, :]
                + (lo_profile * lo + hi_profile * hi)
                + (lo_edge * got(4, v, t) + hi_edge * got(5, v, t))
            )
            segment_ref[v, :, tile(t)] = (
                done_ref[x_at + start : x_at + start + rows, :]
                + (response(0, t) * got(0, v, t) + response(1, t) * got(1, v, t))
                + (response(2, t) * lo + response(3, t) * hi)
            )
        for which, (ref, hbm) in enumerate(
            ((derivative_ref, derivative_hbm), (segment_ref, segment_hbm))
        ):
            copies.append(
                pltpu.make_async_copy(ref.at[v], hbm.at[v], sems.at[which * var_count + v])
            )
            copies[-1].start()
    for copy in copies:
        copy.wait()


def call(kernel, outs, scratch, sems, args, near=(), far_out=(), limit=62):
    whole = pl.BlockSpec(memory_space=pltpu.VMEM)
    far = pl.BlockSpec(memory_space=pltpu.HBM)
    buffers = [
        pltpu.VMEM(s.shape, s.dtype) if hasattr(s, "dtype") else pltpu.VMEM(s, jnp.float32)
        for s in scratch
    ]
    buffers += [pltpu.SemaphoreType.DMA((size,)) for size in sems]
    return pl.pallas_call(
        kernel,
        out_shape=[jax.ShapeDtypeStruct(shape, jnp.float32) for shape in outs],
        in_specs=[whole if k in near else far for k in range(len(args))],
        out_specs=[far if k in far_out else whole for k in range(len(outs))],
        scratch_shapes=buffers,
        compiler_params=pltpu.CompilerParams(vmem_limit_bytes=limit * 2**20),
    )(*args)


def exchange(message, axes):
    return lax.all_to_all(message, axes, 0, 0, tiled=True)


def local(
    state,
    face_diffusion,
    courant,
    cell_mask,
    ghost_cell,
    ghost_owner,
    ghost_image,
    image_base,
    image_weight,
):
    var_count, rows, pencils = state.shape
    slabs, cross = lax.axis_size("pipe"), lax.axis_size("cross")
    count = pencils // LANES
    cells = var_count * rows
    images = image_base.shape[0]
    tables, at, carry_up, carry_down = derivative_tables(slabs, rows, var_count)
    slices = Slices(slabs, count, cross, var_count, images)
    tables = jnp.asarray(tables)
    turned = (cells * count, LANES)
    stay = stay_at(rows, count, cells)[3] + cells * count
    ready = (ready_at(rows, count, cells)[2], LANES)

    arguments = (
        face_diffusion,
        courant,
        tables,
        ghost_cell,
        ghost_owner,
        ghost_image,
        cell_mask,
        image_base,
        image_weight,
        state,
    )
    buffers = list(arguments)
    buffers[2] = jax.ShapeDtypeStruct(tables.shape[1:], jnp.float32)
    message, stay = call(
        functools.partial(prepare_kernel, slices, at),
        [(slabs * slices.height, LANES), (stay, LANES)],
        buffers
        + [
            (stay, LANES),
            (rows * count, LANES),
            (rows * count, LANES),
            (2 * rows * count, LANES),
            (16 * count, LANES),
            (2 * rows, pencils),
            (40 * count, LANES),
            (2 * rows, -(-count // 8) * 8, LANES),
            (cells, pencils),
            (max(slices.rest, 1) * max(slices.groups, 1) * slices.per, LANES),
        ],
        [len(arguments), 1],
        arguments,
        far_out=(1,),
    )
    message = exchange(message, "pipe")
    (ready,) = call(
        functools.partial(own_kernel, state.shape), [ready], [], [], (stay,), near=(0,), limit=48
    )
    (image_values,) = call(
        functools.partial(pick_kernel, slices),
        [(slabs * slices.image_rows, LANES)],
        [],
        [],
        (message,),
        near=(0,),
        limit=24,
    )
    blocks = [image_values] + [
        lax.ppermute(image_values, "cross", [(i, (i + u) % cross) for i in range(cross)])
        for u in range(1, cross)
    ]

    rest, chain = call(
        functools.partial(chain_kernel, slices),
        [(slabs * max(slices.groups, 1) * slices.per, LANES), (2 * slabs * 16, LANES)],
        [],
        [],
        (message,),
        near=(0,),
        limit=24,
    )
    (back,) = call(
        functools.partial(solve_kernel, slices, carry_up, carry_down),
        [(slabs * slices.back_height, LANES)],
        [
            (slabs * slices.chunk * 48, LANES),
            (slabs * max(slices.back_groups, 1) * slices.per, LANES),
        ],
        [],
        (message, rest, chain, *blocks),
        near=range(3 + cross),
        limit=24,
    )
    back = exchange(back, "pipe")
    (done,) = call(
        functools.partial(fill_kernel, slices, state.shape),
        [(done_at(rows, count, cells)[3], LANES)],
        [turned],
        [],
        (ready, *blocks),
        near=range(1 + cross),
        limit=48,
    )
    return tuple(
        call(
            functools.partial(finish_kernel, slices),
            [state.shape, state.shape],
            [
                state.shape,
                state.shape,
                (max(slices.rest, 1) * max(slices.back_groups, 1) * slices.per, LANES),
            ],
            [2 * var_count],
            (back, done),
            near=range(2),
            far_out=(0, 1),
            limit=48,
        )
    )


def solution(mesh):
    in_specs = (
        P(None, "pipe", "cross"),
        P("pipe", "cross"),
        P("pipe", "cross"),
        P("pipe", "cross"),
        P(("pipe", "cross")),
        P(("pipe", "cross")),
        P(("pipe", "cross")),
        P(("pipe", "cross")),
        P(None, ("pipe", "cross")),
    )
    out_specs = (P(None, "pipe", "cross"), P(None, "pipe", "cross"))
    return jax.shard_map(local, mesh=mesh, in_specs=in_specs, out_specs=out_specs, check_vma=False)
```

```python
import functools

import numpy as np
import jax
import jax.numpy as jnp
from jax import lax
from jax.experimental import pallas as pl
from jax.experimental.pallas import tpu as pltpu
from jax.sharding import PartitionSpec as P

LINE = 96
LANES = 128
REFLECT = (1.0, -1.0, -1.0, -1.0, 1.0)

Z_UP, Z_DOWN, ROW_FIRST, ROW_LAST, RIGHT_FIRST, RIGHT_LAST = range(6)
LINK_IN, MARGIN_FIRST, MARGIN_LAST, LINK_UP, FIRST_LO, FIRST_HI, LAST_LO, LAST_HI, FIRST_EDGE, LAST_EDGE = range(10)
COEFFICIENTS = 10
PENCIL, ROW, OWNER, IMAGE, WEIGHT_UP, WEIGHT_DOWN, WEIGHT_FIRST, WEIGHT_LAST = range(8)


def derivative_tables(slabs, rows, var_count):
    total = slabs * rows
    A = np.eye(total)
    B = np.zeros((total, total))
    for i in range(2, total - 2):
        A[i, i - 1] = A[i, i + 1] = 1.0 / 3.0
        B[i, i + 1], B[i, i - 1] = 7.0 / 9.0, -7.0 / 9.0
        B[i, i + 2], B[i, i - 2] = 1.0 / 36.0, -1.0 / 36.0
    for i in (1, total - 2):
        A[i, i - 1] = A[i, i + 1] = 0.25
        B[i, i + 1], B[i, i - 1] = 0.75, -0.75
    B[0, :3] = (-1.5, 2.0, -0.5)
    B[-1, -3:] = (0.5, -2.0, 1.5)
    inverse = np.linalg.inv(A)
    M = inverse @ B

    cells = var_count * rows
    own_at, reduce_at, adjoint_at, profile_at, weight_at = 0, cells, cells + 16, cells + 56, cells + 96
    tables = np.zeros((slabs, cells + 112, LANES))
    carry_up, carry_down = np.zeros(slabs), np.zeros(slabs)
    for p in range(slabs):
        table = tables[p]
        base = p * rows
        here = slice(base, base + rows)
        own = M[here, here]
        lo, hi, lo_edge, hi_edge = (np.zeros(rows) for _ in range(4))
        weight_up, weight_down = np.zeros(rows), np.zeros(rows)
        if p > 0:
            lo = inverse[here, base - 8] / inverse[base + 1, base - 8]
            lo_edge[0] = M[base, base - 1] - lo[0] * M[base + 1, base - 1]
            weight_down = M[base - 2, here]
        if p > 1:
            k = base - rows - 8
            carry_up[p] = inverse[base + 1, k] / inverse[base - rows + 1, k]
        if p < slabs - 1:
            k = base + rows + 8
            hi = inverse[here, k] / inverse[base + rows - 2, k]
            hi_edge[-1] = M[base + rows - 1, base + rows] - hi[-1] * M[base + rows - 2, base + rows]
            weight_up = M[base + rows + 1, here]
        if p < slabs - 2:
            k = base + 2 * rows + 8
            carry_down[p] = inverse[base + rows - 2, k] / inverse[base + 2 * rows - 2, k]
        for v in range(var_count):
            at = slice(v * rows, (v + 1) * rows)
            table[own_at + v * rows : own_at + (v + 1) * rows, at] = own
            table[reduce_at + v, at] = weight_up
            table[reduce_at + var_count + v, at] = weight_down
        table[adjoint_at : adjoint_at + rows, :rows] = own.T
        table[adjoint_at + rows : adjoint_at + 2 * rows, rows : 2 * rows] = own.T
        more = adjoint_at + 2 * rows
        table[more, :rows] = lo
        table[more + 1, :rows] = hi
        table[more + 2, rows : 2 * rows] = lo
        table[more + 3, rows : 2 * rows] = hi
        table[more + 4, 0] = lo_edge[0]
        table[more + 5, 2 * rows - 1] = hi_edge[-1]
        table[profile_at : profile_at + rows] = lo[:, None]
        table[profile_at + rows : profile_at + 2 * rows] = hi[:, None]
        table[profile_at + 2 * rows] = lo_edge[0]
        table[profile_at + 2 * rows + 1] = hi_edge[-1]
        table[weight_at, :rows] = weight_up
        table[weight_at + 1, :rows] = weight_down
    at = (own_at, reduce_at, adjoint_at, profile_at, weight_at)
    return tables.astype(np.float32), at, carry_up, carry_down


def split(x, parts):
    pieces = []
    for _ in range(parts):
        piece = x.astype(jnp.bfloat16)
        pieces.append(piece)
        x = x - piece.astype(jnp.float32)
    return pieces


def exact_dot(x, one_hot, contract):
    found = lax.dot_general(
        jnp.concatenate(split(x, 3), axis=0),
        one_hot,
        (contract, ((), ())),
        preferred_element_type=jnp.float32,
    )
    size = x.shape[0]
    return found[:size] + (found[size : 2 * size] + found[2 * size :])


def full_dot(a, b):
    return jnp.dot(a, b, precision=lax.Precision.HIGHEST, preferred_element_type=jnp.float32)


def marks(shape, axis, values):
    return jnp.where(lax.broadcasted_iota(jnp.int32, shape, axis) == values, 1.0, 0.0).astype(
        jnp.bfloat16
    )


def place_of(cell, rows, pencils):
    row = jnp.zeros_like(cell)
    for k in range(1, rows):
        row += (cell >= k * pencils).astype(jnp.int32)
    return row, cell - row * pencils


def tile(t):
    return slice(t * LANES, (t + 1) * LANES)


def turn(ref, x):
    height, pencils = x.shape
    for t in range(pencils // LANES):
        ref[t * height : (t + 1) * height, :] = x[:, tile(t)]


def slab_at(ref, row, height, count):
    return ref[pl.ds(row, count, stride=height), :]


def put_slab(ref, row, height, count, value):
    ref[pl.ds(row, count, stride=height), :] = value


def kept_at(which, i, rows, count):
    return (which * rows + i) * (-(-count // 8) * 8)


def stay_at(rows, count, cells):
    kept = kept_at(4, 0, rows, count) + 40
    return kept, kept, kept + cells, kept + cells + 8


def ready_at(rows, count, cells):
    kept = 2 * cells * count
    return cells * count, kept, kept + stay_at(rows, count, cells)[3]


def done_at(rows, count, cells, var_count):
    x = cells * count
    response = 2 * x
    profile = response + 4 * rows * count
    return x, response, profile, profile + 40, profile + 40 + 2 * var_count * count


def fetch(sources, targets, sems):
    copies = [
        pltpu.make_async_copy(source, target, sems.at[k])
        for k, (source, target) in enumerate(zip(sources, targets))
    ]
    for copy in copies:
        copy.start()
    return copies


class Slices:
    def __init__(self, slabs, count, cross, var_count, images):
        rest = count % slabs
        self.slabs, self.count, self.cross, self.var_count = slabs, count, cross, var_count
        self.image_rows = var_count * images // LANES
        shared = rest > 0 and slabs % rest == 0 and LANES % (slabs // rest) == 0
        self.full = count // slabs if shared else -(-count // slabs)
        self.rest = rest if shared else 0
        self.per = slabs // rest if shared else 1
        self.width = LANES // self.per
        self.chunk = self.full + (1 if shared else 0)
        self.lines, self.back_lines = 6 * var_count + COEFFICIENTS, 4 * var_count
        self.groups, self.back_groups = (self.group_count(n) for n in (self.lines, self.back_lines))
        self.meta_at = self.lines * self.full
        self.packed_at = self.meta_at + 8
        self.images_at = self.packed_at + self.groups
        self.height = -(-(self.images_at + self.image_rows) // 8) * 8
        self.back_packed_at = self.back_lines * self.full
        self.back_height = -(-(self.back_packed_at + self.back_groups) // 8) * 8

    def group_count(self, lines):
        return -(-lines // self.per) if self.rest else 0

    def row(self, functional, t):
        return (functional * self.full + t) * self.var_count

    def coefficient_row(self, which, t):
        return 6 * self.full * self.var_count + which * self.full + t

    def tiles_at(self, t):
        return t * self.slabs, min(self.count, (t + 1) * self.slabs)


def lane_block(rows, width):
    return lax.broadcasted_iota(jnp.int32, (rows, LANES), 1) // width


def moved_lanes(x, by):
    by %= LANES
    return x if by == 0 else pltpu.roll(x, by, 1)


def image_lines(x, base, weight_ref, rows, var_count):
    pencils = x.shape[1]
    images = base.shape[1]
    row, pencil = place_of(base, rows, pencils)
    pick = marks((pencils, images), 0, pencil)
    row_at = lax.broadcasted_iota(jnp.int32, (rows, images), 0)
    lower, upper = row_at == row, row_at == row + 1
    total = [jnp.zeros((rows, images), jnp.float32) for _ in range(var_count)]
    pieces = jnp.concatenate(split(x, 2), axis=0)
    for corner, shift in enumerate((0, 1, LINE, LINE + 1)):
        moved = pieces if shift == 0 else pltpu.roll(pieces, pencils - shift, 1)
        found = jnp.dot(moved, pick, preferred_element_type=jnp.float32)
        found = found[: var_count * rows] + found[var_count * rows :]
        weight = jnp.where(lower, weight_ref[corner : corner + 1], 0.0) + jnp.where(
            upper, weight_ref[corner + 4 : corner + 5], 0.0
        )
        for v in range(var_count):
            total[v] += found[v * rows : (v + 1) * rows] * weight
    lines = []
    for v in range(var_count):
        value = jnp.sum(total[v], axis=0, keepdims=True)
        lines += [value[:, tile(t)] for t in range(images // LANES)]
    return jnp.concatenate(lines, axis=0)


def ghost_values(slices, blocks, owner, image):
    per = slices.image_rows // slices.var_count
    slabs, cross = slices.slabs, slices.cross
    ghosts = owner.shape[1]
    across = lax.axis_index("cross")
    values = [
        jnp.concatenate(
            [
                jnp.concatenate(
                    [
                        block[pl.ds(v * per + t, slabs, stride=slices.image_rows), :]
                        for t in range(per)
                    ],
                    axis=1,
                )
                for block in blocks
            ],
            axis=0,
        )
        for v in range(slices.var_count)
    ]
    pick = marks((per * LANES, ghosts), 0, image)
    found = exact_dot(jnp.concatenate(values, axis=0), pick, ((1,), (0,)))
    devices = slabs * cross
    at = lax.broadcasted_iota(jnp.int32, (devices, ghosts), 0)
    mine = (at % slabs) * cross + (across + cross - at // slabs) % cross == owner
    return [
        reflect
        * jnp.sum(
            jnp.where(mine, found[v * devices : (v + 1) * devices], 0.0), axis=0, keepdims=True
        )
        for v, reflect in enumerate(REFLECT)
    ]


def prepare_kernel(
    slices,
    at,
    face_hbm,
    courant_hbm,
    tables_hbm,
    cell_hbm,
    owner_hbm,
    image_hbm,
    mask_hbm,
    base_hbm,
    corner_hbm,
    state_hbm,
    message_ref,
    stay_hbm,
    up_ref,
    down_ref,
    face_ref,
    courant_ref,
    table_ref,
    cell_ref,
    owner_ref,
    image_ref,
    mask_ref,
    base_ref,
    corner_ref,
    state_ref,
    stay_ref,
    turned_ref,
    face_turned_ref,
    courant_turned_ref,
    pair_ref,
    z_ref,
    matrix_ref,
    adjoint_ref,
    weight_ref,
    cleared_ref,
    rest_ref,
    sems,
    stay_sem,
):
    var_count, rows, pencils = state_ref.shape
    cells = var_count * rows
    count = pencils // LANES
    ghosts = cell_ref.shape[0]
    padded = -(-count // 8) * 8
    p = lax.axis_index("pipe")
    slabs, height = slices.slabs, slices.height
    lines = slices.groups * slices.per
    own_at, reduce_at, adjoint_at, profile_at, weight_at = at
    copies = fetch(
        (
            face_hbm,
            courant_hbm,
            tables_hbm.at[p],
            cell_hbm,
            owner_hbm,
            image_hbm,
            mask_hbm,
            base_hbm,
            corner_hbm,
            state_hbm,
        ),
        (
            face_ref,
            courant_ref,
            table_ref,
            cell_ref,
            owner_ref,
            image_ref,
            mask_ref,
            base_ref,
            corner_ref,
            state_ref,
        ),
        sems,
    )
    kept, own, about_at, _ = stay_at(rows, count, cells)

    def send(line, rows_at, slab):
        for t, row_at in enumerate(rows_at):
            start, end = slices.tiles_at(t)
            message_ref[pl.ds(row_at, end - start, stride=height), :] = slab[start:end]
        for m in range(slices.rest):
            tail = slices.full * slabs + m
            rest_ref[m * lines + line : m * lines + line + 1, :] = slab[tail : tail + 1]

    def send_value(functional, v, slab):
        rows_at = [slices.row(functional, t) + v for t in range(slices.full)]
        send(functional * var_count + v, rows_at, slab)

    def send_coefficient(which, slab):
        rows_at = [slices.coefficient_row(which, t) for t in range(slices.full)]
        send(6 * var_count + which, rows_at, slab)

    copies[0].wait()
    turn(face_turned_ref, face_ref[...])

    def face(i):
        return slab_at(face_turned_ref, i, rows, count)

    link = face(0)
    margin = jnp.ones_like(link)
    first_margin = margin
    to_up, to_first = [None] * rows, [None] * rows
    for i in range(1, rows - 1):
        above = face(i)
        inverse = 1.0 / (link + margin + above)
        low, up = link * inverse, above * inverse
        to_up[i], to_first[i] = up, low
        for k, part in enumerate((up, low, inverse)):
            start = kept_at(k, i, rows, count)
            stay_ref[start : start + count, :] = part
        first_margin += low * margin
        link = link * up
        margin = 1.0 + margin * up
    send_coefficient(LINK_IN, link)
    send_coefficient(MARGIN_FIRST, first_margin)
    send_coefficient(MARGIN_LAST, margin)
    send_coefficient(LINK_UP, jnp.where(p == slabs - 1, 0.0, face(rows - 1)))

    zero, one = jnp.zeros_like(margin), jnp.ones_like(margin)
    first, last = [None] * rows, [None] * rows
    first[0], first[rows - 1], last[0], last[rows - 1] = one, zero, zero, one
    for i in range(rows - 2, 0, -1):
        first[i] = to_first[i] + to_up[i] * first[i + 1]
        last[i] = to_up[i] * last[i + 1]
    copies[1].wait()
    turn(courant_turned_ref, courant_ref[...])
    for i in range(rows):
        speed = slab_at(courant_turned_ref, i, rows, count)
        start = kept_at(3, i, rows, count)
        stay_ref[start : start + count, :] = speed
        put_slab(pair_ref, i, 2 * rows, count, first[i] * speed)
        put_slab(pair_ref, rows + i, 2 * rows, count, last[i] * speed)
    for t in range(count):
        matrix_ref[:, tile(t)] = pair_ref[t * 2 * rows : (t + 1) * 2 * rows, :]
    copies[2].wait()
    stay_ref[kept - 40 : kept, :] = table_ref[profile_at : profile_at + 40, :]
    stay_ref[own : own + cells, :] = table_ref[own_at : own_at + cells, :]
    turn(
        adjoint_ref, full_dot(table_ref[adjoint_at : adjoint_at + 40, : 2 * rows], matrix_ref[...])
    )
    for k in range(6):
        send_coefficient(FIRST_LO + k, slab_at(adjoint_ref, 2 * rows + k, 40, count))
    weight_ref[:, padded - 8 :, :] = jnp.zeros((2 * rows, 8, LANES), jnp.float32)
    for i, share in enumerate(first + last):
        weight_ref[i, :count, :] = share - slab_at(adjoint_ref, i, 40, count)

    for copy in copies[3:6]:
        copy.wait()
    row, pencil = place_of(cell_ref[...].reshape(1, ghosts), rows, pencils)
    lane_tile = jnp.right_shift(pencil, 7)
    lane_marks = marks((LANES, ghosts), 0, pencil - lane_tile * LANES)
    picked = exact_dot(
        weight_ref[...].reshape(2 * rows * padded, LANES), lane_marks, ((1,), (0,))
    ).reshape(2, rows, padded, ghosts)
    at_cell = (lax.broadcasted_iota(jnp.int32, (rows, padded, ghosts), 0) == row[None]) & (
        lax.broadcasted_iota(jnp.int32, (rows, padded, ghosts), 1) == lane_tile[None]
    )
    row_marks = jnp.where(lax.broadcasted_iota(jnp.int32, (rows, ghosts), 0) == row, 1.0, 0.0)
    up_down = full_dot(table_ref[weight_at : weight_at + 8, :rows], row_marks)

    def at_ghosts(values):
        return jnp.sum(jnp.sum(jnp.where(at_cell, values, 0.0), axis=0), axis=0, keepdims=True)

    about = jnp.concatenate(
        [
            pencil.astype(jnp.float32),
            row.astype(jnp.float32),
            owner_ref[...].reshape(1, ghosts).astype(jnp.float32),
            image_ref[...].reshape(1, ghosts).astype(jnp.float32),
            up_down[0:2],
            at_ghosts(picked[0]),
            at_ghosts(picked[1]),
        ],
        axis=0,
    )
    for j in range(slabs):
        start = j * height + slices.meta_at
        message_ref[start : start + 8, :] = about
    stay_ref[about_at : about_at + 8, :] = about
    edge = var_count * count
    for ref in (up_ref, down_ref):
        ref[edge : ref.shape[0] - 8, :] = jnp.zeros((ref.shape[0] - 8 - edge, LANES), jnp.float32)
        ref[ref.shape[0] - 8 :, :] = about
    staying = pltpu.make_async_copy(stay_ref, stay_hbm, stay_sem.at[0])
    staying.start()
    for copy in copies[6:]:
        copy.wait()
    values = image_lines(
        state_ref[...].reshape(cells, pencils),
        base_ref[...].reshape(1, base_ref.shape[0]),
        corner_ref,
        rows,
        var_count,
    )
    for j in range(slabs):
        start = j * height + slices.images_at
        message_ref[start : start + slices.image_rows, :] = values
    solid = mask_ref[...] == 1
    for v in range(var_count):
        here = slice(v * rows, (v + 1) * rows)
        cleared_ref[here, :] = jnp.where(solid, 0.0, state_ref[v])
    turn(turned_ref, cleared_ref[...])
    turn(z_ref, full_dot(table_ref[reduce_at : reduce_at + 16, :cells], cleared_ref[...]))
    for v in range(var_count):
        send_value(Z_UP, v, slab_at(z_ref, v, 16, count))
        send_value(Z_DOWN, v, slab_at(z_ref, var_count + v, 16, count))
    low, high = ([jnp.zeros((count, LANES), jnp.float32)] * var_count for _ in range(2))
    for i in range(rows):
        to_low, to_high = weight_ref[i, :count, :], weight_ref[rows + i, :count, :]
        for v in range(var_count):
            cell = slab_at(turned_ref, v * rows + i, cells, count)
            if i == 0:
                send_value(ROW_FIRST, v, cell)
                down_ref[v * count : (v + 1) * count, :] = cell
            if i == rows - 1:
                send_value(ROW_LAST, v, cell)
                up_ref[v * count : (v + 1) * count, :] = cell
            low[v] = low[v] + to_low * cell
            high[v] = high[v] + to_high * cell
    for v in range(var_count):
        send_value(RIGHT_FIRST, v, low[v])
        send_value(RIGHT_LAST, v, high[v])

    block = lane_block(max(slices.groups, 1), slices.width)
    for m in range(slices.rest):
        lined = [
            rest_ref[pl.ds(m * lines + k, slices.groups, stride=slices.per), :]
            for k in range(slices.per)
        ]
        for i in range(slices.per):
            packed = lined[0]
            for k in range(slices.per):
                moved = moved_lanes(lined[k], (k - i) * slices.width)
                packed = moved if k == 0 else jnp.where(block == k, moved, packed)
            start = (m * slices.per + i) * height + slices.packed_at
            message_ref[start : start + slices.groups, :] = packed
    staying.wait()


def chain_kernel(slices, message_ref, rest_ref, chain_ref):
    slabs, chunk, full = slices.slabs, slices.chunk, slices.full
    height, per, width = slices.height, slices.per, slices.width
    if slices.rest:
        for p in range(slabs):
            start = p * height + slices.packed_at
            packed = message_ref[start : start + slices.groups, :]
            for k in range(per):
                rest_ref[pl.ds(p * slices.groups * per + k, slices.groups, stride=per), :] = (
                    moved_lanes(packed, -k * width)
                )
    else:
        rest_ref[...] = jnp.zeros_like(rest_ref)

    def sent(p, which):
        start = p * height + slices.coefficient_row(which, 0)
        slab = message_ref[start : start + full, :]
        if slices.rest:
            start = p * slices.groups * per + 6 * slices.var_count + which
            slab = jnp.concatenate([slab, rest_ref[start : start + 1, :]], axis=0)
        return slab

    nodes = 2 * slabs
    margin = sent(0, MARGIN_FIRST)
    for k in range(nodes):
        link = sent(k // 2, LINK_UP if k % 2 else LINK_IN)
        inverse = 1.0 / (margin + link)
        ratio = link * inverse
        chain_ref[16 * k : 16 * k + chunk, :] = ratio
        chain_ref[16 * k + 8 : 16 * k + 8 + chunk, :] = inverse
        if k < nodes - 1:
            following = sent((k + 1) // 2, MARGIN_FIRST if k % 2 else MARGIN_LAST)
            margin = following + margin * ratio


def solve_kernel(slices, carry_up, carry_down, message_ref, rest_ref, chain_ref, *refs):
    *blocks, back_ref, ghost_ref, back_rest_ref = refs
    slabs, var_count, chunk, full = slices.slabs, slices.var_count, slices.chunk, slices.full
    height, per, width = slices.height, slices.per, slices.width
    me = lax.axis_index("pipe")

    def meta(p, k):
        start = p * height + slices.meta_at + k
        return message_ref[start : start + 1, :]

    def meta_all(k):
        return jnp.concatenate([meta(p, k) for p in range(slabs)], axis=1).astype(jnp.int32)

    values = ghost_values(slices, blocks, meta_all(OWNER), meta_all(IMAGE))
    ghosts = LANES
    place = lax.broadcasted_iota(jnp.int32, (chunk * LANES, ghosts), 0)
    slot, lane = place // LANES, place % LANES
    pencil_at = jnp.where(
        slot < full,
        (me + slot * slabs) * LANES + lane,
        (full * slabs + me // per) * LANES + (me % per) * width + lane,
    )
    none = jnp.zeros((8 - var_count, ghosts), jnp.float32)
    for p in range(slabs):
        row = meta(p, ROW)
        weights = (
            meta(p, WEIGHT_UP),
            meta(p, WEIGHT_DOWN),
            jnp.where(row == 0.0, 1.0, 0.0),
            jnp.where(row == 15.0, 1.0, 0.0),
            meta(p, WEIGHT_FIRST),
            meta(p, WEIGHT_LAST),
        )
        here = jnp.concatenate([value[:, tile(p)] for value in values] + [none], axis=0)
        shares = jnp.concatenate([here * weight for weight in weights], axis=0)
        spots = jnp.where(pencil_at == meta(p, PENCIL).astype(jnp.int32), 1.0, 0.0)
        share = exact_dot(shares, spots.astype(jnp.bfloat16), ((1,), (1,)))
        for t in range(chunk):
            start = (p * chunk + t) * 48
            ghost_ref[start : start + 48, :] = share[:, tile(t)]

    nodes = 2 * slabs
    zero = jnp.zeros((var_count, LANES), jnp.float32)
    for t in range(chunk):

        def value(p, functional):
            if t < full:
                start = p * height + slices.row(functional, t)
                sent = message_ref[start : start + var_count, :]
            else:
                start = p * slices.groups * per + functional * var_count
                sent = rest_ref[start : start + var_count, :]
            start = (p * chunk + t) * 48 + functional * 8
            return sent + ghost_ref[start : start + var_count, :]

        def coefficient(p, which):
            if t < full:
                start = p * height + slices.coefficient_row(which, t)
                return message_ref[start : start + 1, :]
            start = p * slices.groups * per + 6 * var_count + which
            return rest_ref[start : start + 1, :]

        def give(p, functional, block):
            if t < full:
                start = p * slices.back_height + slices.row(functional, t)
                back_ref[start : start + var_count, :] = block
            else:
                start = p * slices.back_groups * per + functional * var_count
                back_rest_ref[start : start + var_count, :] = block

        def ratio(k):
            return chain_ref[16 * k + t : 16 * k + t + 1, :]

        def scale(k):
            return chain_ref[16 * k + 8 + t : 16 * k + 9 + t, :]

        lo, hi, below, above = ([zero] * slabs for _ in range(4))
        for p in range(1, slabs):
            lo[p] = value(p - 1, Z_UP) + float(carry_up[p]) * lo[p - 1]
            below[p] = value(p - 1, ROW_LAST)
        for p in range(slabs - 2, -1, -1):
            hi[p] = value(p + 1, Z_DOWN) + float(carry_down[p]) * hi[p + 1]
            above[p] = value(p + 1, ROW_FIRST)
        right = []
        for p in range(slabs):
            right.append(
                value(p, RIGHT_FIRST)
                - coefficient(p, FIRST_LO) * lo[p]
                - coefficient(p, FIRST_HI) * hi[p]
                - coefficient(p, FIRST_EDGE) * below[p]
            )
            right.append(
                value(p, RIGHT_LAST)
                - coefficient(p, LAST_LO) * lo[p]
                - coefficient(p, LAST_HI) * hi[p]
                - coefficient(p, LAST_EDGE) * above[p]
            )
            give(p, 2, lo[p])
            give(p, 3, hi[p])
        for k in range(1, nodes):
            right[k] = right[k] + ratio(k - 1) * right[k - 1]
        x = right[nodes - 1] * scale(nodes - 1)
        give(slabs - 1, 1, x)
        for k in range(nodes - 2, -1, -1):
            x = right[k] * scale(k) + ratio(k) * x
            give(k // 2, k % 2, x)
    if slices.rest:
        groups = slices.back_groups
        block = lane_block(groups, width)
        for p in range(slabs):
            for k in range(per):
                lined = back_rest_ref[pl.ds(p * groups * per + k, groups, stride=per), :]
                moved = moved_lanes(lined, k * width)
                packed = moved if k == 0 else jnp.where(block == k, moved, packed)
            start = p * slices.back_height + slices.back_packed_at
            back_ref[start : start + groups, :] = packed


def pick_kernel(slices, message_ref, values_ref):
    size = slices.image_rows
    for p in range(slices.slabs):
        start = p * slices.height + slices.images_at
        values_ref[p * size : (p + 1) * size, :] = message_ref[start : start + size, :]


def own_kernel(stay_ref, mask_ref, state_ref, ready_ref, cleared_ref):
    var_count, rows, pencils = state_ref.shape
    cells = var_count * rows
    count = pencils // LANES
    own_at = stay_at(rows, count, cells)[1]
    cells_at, kept_start, end = ready_at(rows, count, cells)
    solid = mask_ref[...] == 1
    for v in range(var_count):
        cleared_ref[v * rows : (v + 1) * rows, :] = jnp.where(solid, 0.0, state_ref[v])
    turn(ready_ref.at[cells_at:kept_start, :], cleared_ref[...])
    turn(
        ready_ref.at[:cells_at, :],
        full_dot(stay_ref[own_at : own_at + cells, :cells], cleared_ref[...]),
    )
    ready_ref[kept_start:end, :] = stay_ref[...]


def fill_kernel(slices, shape, ready_ref, below_ref, above_ref, *refs):
    *blocks, done_ref, filled_ref, edge_ref = refs
    var_count, rows, pencils = shape
    cells = var_count * rows
    count = pencils // LANES
    _, own_at, about_at, _ = stay_at(rows, count, cells)
    cells_at, kept_start, _ = ready_at(rows, count, cells)

    ghosts = LANES
    about = [ready_ref[kept_start + about_at : kept_start + about_at + 8, :]]
    about += [ref[ref.shape[0] - 8 :, :] for ref in (below_ref, above_ref)]

    def known(k):
        return jnp.concatenate([x[k : k + 1] for x in about], axis=1).astype(jnp.int32)

    values = ghost_values(slices, blocks, known(OWNER), known(IMAGE))
    row, pencil = known(ROW), known(PENCIL)
    at_row = lax.broadcasted_iota(jnp.int32, (rows, ghosts), 0) == row[:, :ghosts]
    spread = jnp.concatenate([jnp.where(at_row, value[:, :ghosts], 0.0) for value in values], axis=0)
    own = ready_ref[kept_start + own_at : kept_start + own_at + cells, :cells]
    both = jnp.concatenate([full_dot(own, spread), spread], axis=0)
    spots = marks((pencils, ghosts), 0, pencil[:, :ghosts])
    added = exact_dot(both, spots, ((1,), (1,)))
    for t in range(count):
        here = slice(t * cells, (t + 1) * cells)
        there = slice(cells_at + t * cells, cells_at + (t + 1) * cells)
        done_ref[here, :] = ready_ref[here, :] + added[:cells, tile(t)]
        filled_ref[here, :] = ready_ref[there, :] + added[cells:, tile(t)]
    x_at, response_at, profile_at, edge_at, _ = done_at(rows, count, cells, var_count)
    none = jnp.zeros((8 - var_count, ghosts), jnp.float32)
    for k, (ref, wanted) in enumerate(((below_ref, rows - 1), (above_ref, 0))):
        here = slice((k + 1) * ghosts, (k + 2) * ghosts)
        at_edge = row[:, here] == wanted
        spread = [jnp.where(at_edge, value[:, here], 0.0) for value in values] + [none]
        spots = marks((pencils, ghosts), 0, pencil[:, here])
        turn(edge_ref, exact_dot(jnp.concatenate(spread, axis=0), spots, ((1,), (1,))))
        for v in range(var_count):
            start = edge_at + (k * var_count + v) * count
            done_ref[start : start + count, :] = ref[v * count : (v + 1) * count, :] + slab_at(
                edge_ref, v, 8, count
            )

    def kept(which, i):
        start = kept_start + kept_at(which, i, rows, count)
        return ready_ref[start : start + count, :]

    def profile(k):
        start = kept_start + own_at - 40 + k
        return ready_ref[start : start + 1, :]

    def put(at, i, height, value):
        done_ref[pl.ds(at + i, count, stride=height), :] = value

    swept = []
    for i in range(1, rows - 1):
        speed = kept(3, i)
        here = [-speed * profile(i), -speed * profile(rows + i)]
        for v in range(var_count):
            row = v * rows + i
            own_slab = slab_at(done_ref, row, cells, count)
            here.append(slab_at(filled_ref, row, cells, count) - speed * own_slab)
        if swept:
            ratio = kept(0, i - 1)
            here = [x + ratio * y for x, y in zip(here, swept[-1])]
        swept.append(here)
    zero = jnp.zeros((count, LANES), jnp.float32)
    one = jnp.ones((count, LANES), jnp.float32)
    x = [zero] * (2 + var_count)
    first, last = zero, one
    for i in range(rows - 1, -1, -1):
        if 0 < i < rows - 1:
            ratio, inverse = kept(0, i), kept(2, i)
            first, last = kept(1, i) + ratio * first, ratio * last
            x = [inverse * y + ratio * z for y, z in zip(swept[i - 1], x)]
        if i == 0:
            first, last, x = one, zero, [zero] * (2 + var_count)
        for k, value in enumerate([first, last] + x[:2]):
            put(response_at + k * rows * count, i, rows, value)
        for v in range(var_count):
            put(x_at, v * rows + i, cells, x[2 + v])
    done_ref[profile_at : profile_at + 40, :] = ready_ref[
        kept_start + own_at - 40 : kept_start + own_at, :
    ]


def finish_kernel(
    slices, back_ref, done_ref, derivative_hbm, segment_hbm, derivative_ref, segment_ref, tail_ref, sems
):
    var_count, rows, pencils = segment_ref.shape
    count = pencils // LANES
    cells = var_count * rows
    x_at, response_at, profile_at, edge_at, _ = done_at(rows, count, cells, var_count)
    back_height, groups, per = slices.back_height, slices.back_groups, slices.per
    block = lane_block(max(groups, 1), slices.width)
    for m in range(slices.rest):
        packed = []
        for i in range(per):
            start = (m * per + i) * back_height + slices.back_packed_at
            packed.append(back_ref[start : start + groups, :])
        for k in range(per):
            for i in range(per):
                moved = moved_lanes(packed[i], (i - k) * slices.width)
                joined = moved if i == 0 else jnp.where(block == i, moved, joined)
            tail_ref[pl.ds(m * groups * per + k, groups, stride=per), :] = joined

    def got(functional, v, t):
        step, j = t // slices.slabs, t % slices.slabs
        if step < slices.full:
            start = j * back_height + slices.row(functional, step) + v
            return back_ref[start : start + 1, :]
        start = j * groups * per + functional * var_count + v
        return tail_ref[start : start + 1, :]

    lo_profile = done_ref[profile_at : profile_at + rows, :]
    hi_profile = done_ref[profile_at + rows : profile_at + 2 * rows, :]
    row_at = lax.broadcasted_iota(jnp.int32, (rows, LANES), 0)
    edges = profile_at + 2 * rows
    lo_edge = jnp.where(row_at == 0, done_ref[edges : edges + 1, :], 0.0)
    hi_edge = jnp.where(row_at == rows - 1, done_ref[edges + 1 : edges + 2, :], 0.0)

    def edge(k, v, t):
        start = edge_at + (k * var_count + v) * count + t
        return done_ref[start : start + 1, :]

    def response(k, t):
        start = response_at + (k * count + t) * rows
        return done_ref[start : start + rows, :]

    copies = []
    for v in range(var_count):
        for t in range(count):
            start = t * cells + v * rows
            lo, hi = got(2, v, t), got(3, v, t)
            derivative_ref[v, :, tile(t)] = (
                done_ref[start : start + rows, :]
                + (lo_profile * lo + hi_profile * hi)
                + (lo_edge * edge(0, v, t) + hi_edge * edge(1, v, t))
            )
            segment_ref[v, :, tile(t)] = (
                done_ref[x_at + start : x_at + start + rows, :]
                + (response(0, t) * got(0, v, t) + response(1, t) * got(1, v, t))
                + (response(2, t) * lo + response(3, t) * hi)
            )
        for which, (ref, hbm) in enumerate(
            ((derivative_ref, derivative_hbm), (segment_ref, segment_hbm))
        ):
            copies.append(
                pltpu.make_async_copy(ref.at[v], hbm.at[v], sems.at[which * var_count + v])
            )
            copies[-1].start()
    for copy in copies:
        copy.wait()


def call(kernel, outs, scratch, sems, args, near=(), far_out=(), limit=62):
    whole = pl.BlockSpec(memory_space=pltpu.VMEM)
    far = pl.BlockSpec(memory_space=pltpu.HBM)
    buffers = [
        pltpu.VMEM(s.shape, s.dtype) if hasattr(s, "dtype") else pltpu.VMEM(s, jnp.float32)
        for s in scratch
    ]
    buffers += [pltpu.SemaphoreType.DMA((size,)) for size in sems]
    return pl.pallas_call(
        kernel,
        out_shape=[jax.ShapeDtypeStruct(shape, jnp.float32) for shape in outs],
        in_specs=[whole if k in near else far for k in range(len(args))],
        out_specs=[far if k in far_out else whole for k in range(len(outs))],
        scratch_shapes=buffers,
        compiler_params=pltpu.CompilerParams(vmem_limit_bytes=limit * 2**20),
    )(*args)


def exchange(message, axes):
    return lax.all_to_all(message, axes, 0, 0, tiled=True)


def local(
    state,
    face_diffusion,
    courant,
    cell_mask,
    ghost_cell,
    ghost_owner,
    ghost_image,
    image_base,
    image_weight,
):
    var_count, rows, pencils = state.shape
    slabs, cross = lax.axis_size("pipe"), lax.axis_size("cross")
    count = pencils // LANES
    cells = var_count * rows
    images = image_base.shape[0]
    tables, at, carry_up, carry_down = derivative_tables(slabs, rows, var_count)
    slices = Slices(slabs, count, cross, var_count, images)
    tables = jnp.asarray(tables)
    turned = (cells * count, LANES)
    stay = stay_at(rows, count, cells)[3]
    ready = (ready_at(rows, count, cells)[2], LANES)

    arguments = (
        face_diffusion,
        courant,
        tables,
        ghost_cell,
        ghost_owner,
        ghost_image,
        cell_mask,
        image_base,
        image_weight,
        state,
    )
    buffers = list(arguments)
    buffers[2] = jax.ShapeDtypeStruct(tables.shape[1:], jnp.float32)
    edge = (-(-var_count * count // 8) * 8 + 8, LANES)
    message, stay, up, down = call(
        functools.partial(prepare_kernel, slices, at),
        [(slabs * slices.height, LANES), (stay, LANES), edge, edge],
        buffers
        + [
            (stay, LANES),
            turned,
            (rows * count, LANES),
            (rows * count, LANES),
            (2 * rows * count, LANES),
            (16 * count, LANES),
            (2 * rows, pencils),
            (40 * count, LANES),
            (2 * rows, -(-count // 8) * 8, LANES),
            (cells, pencils),
            (max(slices.rest, 1) * max(slices.groups, 1) * slices.per, LANES),
        ],
        [len(arguments), 1],
        arguments,
        far_out=(1,),
    )
    message = exchange(message, "pipe")
    forward = [(i, i + 1) for i in range(slabs - 1)]
    below = lax.ppermute(up, "pipe", forward)
    above = lax.ppermute(down, "pipe", [(j, i) for i, j in forward])
    message, below, above = lax.optimization_barrier((message, below, above))
    (ready,) = call(
        own_kernel,
        [ready],
        [(cells, pencils)],
        [],
        (stay, cell_mask, state),
        near=range(3),
        limit=48,
    )
    (image_values,) = call(
        functools.partial(pick_kernel, slices),
        [(slabs * slices.image_rows, LANES)],
        [],
        [],
        (message,),
        near=(0,),
        limit=24,
    )
    blocks = [image_values] + [
        lax.ppermute(image_values, "cross", [(i, (i + u) % cross) for i in range(cross)])
        for u in range(1, cross)
    ]

    rest, chain = call(
        functools.partial(chain_kernel, slices),
        [(slabs * max(slices.groups, 1) * slices.per, LANES), (2 * slabs * 16, LANES)],
        [],
        [],
        (message,),
        near=(0,),
        limit=24,
    )
    (back,) = call(
        functools.partial(solve_kernel, slices, carry_up, carry_down),
        [(slabs * slices.back_height, LANES)],
        [
            (slabs * slices.chunk * 48, LANES),
            (slabs * max(slices.back_groups, 1) * slices.per, LANES),
        ],
        [],
        (message, rest, chain, *blocks),
        near=range(3 + cross),
        limit=24,
    )
    back = exchange(back, "pipe")
    (done,) = call(
        functools.partial(fill_kernel, slices, state.shape),
        [(done_at(rows, count, cells, var_count)[4], LANES)],
        [turned, (8 * count, LANES)],
        [],
        (ready, below, above, *blocks),
        near=range(3 + cross),
        limit=48,
    )
    return tuple(
        call(
            functools.partial(finish_kernel, slices),
            [state.shape, state.shape],
            [
                state.shape,
                state.shape,
                (max(slices.rest, 1) * max(slices.back_groups, 1) * slices.per, LANES),
            ],
            [2 * var_count],
            (back, done),
            near=range(2),
            far_out=(0, 1),
            limit=48,
        )
    )


def solution(mesh):
    in_specs = (
        P(None, "pipe", "cross"),
        P("pipe", "cross"),
        P("pipe", "cross"),
        P("pipe", "cross"),
        P(("pipe", "cross")),
        P(("pipe", "cross")),
        P(("pipe", "cross")),
        P(("pipe", "cross")),
        P(None, ("pipe", "cross")),
    )
    out_specs = (P(None, "pipe", "cross"), P(None, "pipe", "cross"))
    return jax.shard_map(local, mesh=mesh, in_specs=in_specs, out_specs=out_specs, check_vma=False)
```

```python
import functools

import numpy as np
import jax
import jax.numpy as jnp
from jax import lax
from jax.experimental import pallas as pl
from jax.experimental.pallas import tpu as pltpu
from jax.sharding import PartitionSpec as P

LINE = 96
LANES = 128
REFLECT = (1.0, -1.0, -1.0, -1.0, 1.0)

Z_UP, Z_DOWN, ROW_FIRST, ROW_LAST, RIGHT_FIRST, RIGHT_LAST = range(6)
LINK_IN, MARGIN_FIRST, MARGIN_LAST, LINK_UP, FIRST_LO, FIRST_HI, LAST_LO, LAST_HI, FIRST_EDGE, LAST_EDGE = range(10)
COEFFICIENTS = 10
CELL, COLUMN, WEIGHT_FIRST, WEIGHT_LAST = range(4)
ABOUT = 4


def derivative_tables(slabs, rows, var_count):
    total = slabs * rows
    A = np.eye(total)
    B = np.zeros((total, total))
    for i in range(2, total - 2):
        A[i, i - 1] = A[i, i + 1] = 1.0 / 3.0
        B[i, i + 1], B[i, i - 1] = 7.0 / 9.0, -7.0 / 9.0
        B[i, i + 2], B[i, i - 2] = 1.0 / 36.0, -1.0 / 36.0
    for i in (1, total - 2):
        A[i, i - 1] = A[i, i + 1] = 0.25
        B[i, i + 1], B[i, i - 1] = 0.75, -0.75
    B[0, :3] = (-1.5, 2.0, -0.5)
    B[-1, -3:] = (0.5, -2.0, 1.5)
    inverse = np.linalg.inv(A)
    M = inverse @ B

    cells = var_count * rows
    own_at, reduce_at, adjoint_at, profile_at = 0, cells, cells + 32, cells + 72
    tables = np.zeros((slabs, cells + 112, LANES))
    carry_up, carry_down = np.zeros(slabs), np.zeros(slabs)
    ups, downs = np.zeros((slabs, rows)), np.zeros((slabs, rows))
    for p in range(slabs):
        table = tables[p]
        base = p * rows
        here = slice(base, base + rows)
        own = M[here, here]
        lo, hi, lo_edge, hi_edge = (np.zeros(rows) for _ in range(4))
        weight_up, weight_down = np.zeros(rows), np.zeros(rows)
        if p > 0:
            lo = inverse[here, base - 8] / inverse[base + 1, base - 8]
            lo_edge[0] = M[base, base - 1] - lo[0] * M[base + 1, base - 1]
            weight_down = M[base - 2, here]
        if p > 1:
            k = base - rows - 8
            carry_up[p] = inverse[base + 1, k] / inverse[base - rows + 1, k]
        if p < slabs - 1:
            k = base + rows + 8
            hi = inverse[here, k] / inverse[base + rows - 2, k]
            hi_edge[-1] = M[base + rows - 1, base + rows] - hi[-1] * M[base + rows - 2, base + rows]
            weight_up = M[base + rows + 1, here]
        if p < slabs - 2:
            k = base + 2 * rows + 8
            carry_down[p] = inverse[base + rows - 2, k] / inverse[base + 2 * rows - 2, k]
        for v in range(var_count):
            at = slice(v * rows, (v + 1) * rows)
            table[own_at + v * rows : own_at + (v + 1) * rows, at] = own
        table[reduce_at : reduce_at + rows] = weight_up[:, None]
        table[reduce_at + rows : reduce_at + 2 * rows] = weight_down[:, None]
        table[adjoint_at : adjoint_at + rows, :rows] = own.T
        table[adjoint_at + rows : adjoint_at + 2 * rows, rows : 2 * rows] = own.T
        more = adjoint_at + 2 * rows
        table[more, :rows] = lo
        table[more + 1, :rows] = hi
        table[more + 2, rows : 2 * rows] = lo
        table[more + 3, rows : 2 * rows] = hi
        table[more + 4, 0] = lo_edge[0]
        table[more + 5, 2 * rows - 1] = hi_edge[-1]
        table[profile_at : profile_at + rows] = lo[:, None]
        table[profile_at + rows : profile_at + 2 * rows] = hi[:, None]
        table[profile_at + 2 * rows] = lo_edge[0]
        table[profile_at + 2 * rows + 1] = hi_edge[-1]
        ups[p], downs[p] = weight_up, weight_down
    at = (own_at, reduce_at, adjoint_at, profile_at)
    return tables.astype(np.float32), at, (carry_up, carry_down, ups, downs)


def split(x, parts):
    pieces = []
    for _ in range(parts):
        piece = x.astype(jnp.bfloat16)
        pieces.append(piece)
        x = x - piece.astype(jnp.float32)
    return pieces


def exact_dot(x, one_hot, contract):
    found = lax.dot_general(
        jnp.concatenate(split(x, 3), axis=0),
        one_hot,
        (contract, ((), ())),
        preferred_element_type=jnp.float32,
    )
    size = x.shape[0]
    return found[:size] + (found[size : 2 * size] + found[2 * size :])


def full_dot(a, b):
    return jnp.dot(a, b, precision=lax.Precision.HIGHEST, preferred_element_type=jnp.float32)


def marks(shape, axis, values):
    return jnp.where(lax.broadcasted_iota(jnp.int32, shape, axis) == values, 1.0, 0.0).astype(
        jnp.bfloat16
    )


def place_of(cell, rows, pencils):
    row = jnp.zeros_like(cell)
    for k in range(1, rows):
        row += (cell >= k * pencils).astype(jnp.int32)
    return row, cell - row * pencils


def tile(t):
    return slice(t * LANES, (t + 1) * LANES)


def turn(ref, x):
    height, pencils = x.shape
    for t in range(pencils // LANES):
        ref[t * height : (t + 1) * height, :] = x[:, tile(t)]


def slab_at(ref, row, height, count):
    return ref[pl.ds(row, count, stride=height), :]


def put_slab(ref, row, height, count, value):
    ref[pl.ds(row, count, stride=height), :] = value


def kept_at(which, i, rows, count):
    return (which * rows + i) * (-(-count // 8) * 8)


def stay_at(rows, count, cells):
    kept = kept_at(4, 0, rows, count) + 40
    return kept, kept, kept + cells, kept + cells + 8


def ready_at(rows, count, cells):
    kept = 2 * cells * count
    return cells * count, kept, kept + stay_at(rows, count, cells)[3]


def done_at(rows, count, cells, var_count):
    x = cells * count
    response = 2 * x
    profile = response + 4 * rows * count
    return x, response, profile, profile + 40, profile + 40 + 2 * var_count * count


def fetch(sources, targets, sems):
    copies = [
        pltpu.make_async_copy(source, target, sems.at[k])
        for k, (source, target) in enumerate(zip(sources, targets))
    ]
    for copy in copies:
        copy.start()
    return copies


class Slices:
    def __init__(self, slabs, count, cross, var_count, images):
        rest = count % slabs
        self.slabs, self.count, self.cross, self.var_count = slabs, count, cross, var_count
        self.image_rows = var_count * images // LANES
        shared = rest > 0 and slabs % rest == 0 and LANES % (slabs // rest) == 0
        self.full = count // slabs if shared else -(-count // slabs)
        self.rest = rest if shared else 0
        self.per = slabs // rest if shared else 1
        self.width = LANES // self.per
        self.chunk = self.full + (1 if shared else 0)
        self.lines, self.back_lines = 6 * var_count + COEFFICIENTS, 4 * var_count
        self.groups, self.back_groups = (self.group_count(n) for n in (self.lines, self.back_lines))
        self.meta_at = self.lines * self.full
        self.packed_at = self.meta_at + ABOUT
        self.images_at = self.packed_at + self.groups
        self.height = -(-(self.images_at + self.image_rows) // 8) * 8
        self.back_packed_at = self.back_lines * self.full
        self.back_height = -(-(self.back_packed_at + self.back_groups) // 8) * 8

    def group_count(self, lines):
        return -(-lines // self.per) if self.rest else 0

    def row(self, functional, t):
        return (functional * self.full + t) * self.var_count

    def coefficient_row(self, which, t):
        return 6 * self.full * self.var_count + which * self.full + t

    def tiles_at(self, t):
        return t * self.slabs, min(self.count, (t + 1) * self.slabs)


def lane_block(rows, width):
    return lax.broadcasted_iota(jnp.int32, (rows, LANES), 1) // width


def moved_lanes(x, by):
    by %= LANES
    return x if by == 0 else pltpu.roll(x, by, 1)


def image_lines(x, row, pick_ref, weight_ref, rows, var_count):
    pencils, images = pick_ref.shape
    row_at = lax.broadcasted_iota(jnp.int32, (rows, images), 0)
    lower, upper = row_at == row, row_at == row + 1
    total = [jnp.zeros((rows, images), jnp.float32) for _ in range(var_count)]
    pieces = jnp.concatenate(split(x, 2), axis=0)
    for corner, shift in enumerate((0, 1, LINE, LINE + 1)):
        moved = pieces if shift == 0 else pltpu.roll(pieces, pencils - shift, 1)
        found = jnp.dot(moved, pick_ref[...], preferred_element_type=jnp.float32)
        found = found[: var_count * rows] + found[var_count * rows :]
        weight = jnp.where(lower, weight_ref[corner : corner + 1], 0.0) + jnp.where(
            upper, weight_ref[corner + 4 : corner + 5], 0.0
        )
        for v in range(var_count):
            total[v] += found[v * rows : (v + 1) * rows] * weight
    lines = []
    for v in range(var_count):
        value = jnp.sum(total[v], axis=0, keepdims=True)
        lines += [value[:, tile(t)] for t in range(images // LANES)]
    return jnp.concatenate(lines, axis=0)


def ghost_values(slices, blocks, column):
    per = slices.image_rows // slices.var_count
    slabs, cross = slices.slabs, slices.cross
    ghosts = column.shape[1]
    images = per * LANES
    owner = ((column + 0.5) * (1.0 / images)).astype(jnp.int32)
    image = column.astype(jnp.int32) - owner * images
    across = lax.axis_index("cross")
    values = [
        jnp.concatenate(
            [
                jnp.concatenate(
                    [
                        block[pl.ds(v * per + t, slabs, stride=slices.image_rows), :]
                        for t in range(per)
                    ],
                    axis=1,
                )
                for block in blocks
            ],
            axis=0,
        )
        for v in range(slices.var_count)
    ]
    pick = marks((per * LANES, ghosts), 0, image)
    found = exact_dot(jnp.concatenate(values, axis=0), pick, ((1,), (0,)))
    devices = slabs * cross
    at = lax.broadcasted_iota(jnp.int32, (devices, ghosts), 0)
    mine = (at % slabs) * cross + (across ^ (at // slabs)) == owner
    return [
        reflect
        * jnp.sum(
            jnp.where(mine, found[v * devices : (v + 1) * devices], 0.0), axis=0, keepdims=True
        )
        for v, reflect in enumerate(REFLECT)
    ]


def prepare_kernel(
    slices,
    at,
    face_hbm,
    courant_hbm,
    tables_hbm,
    cell_hbm,
    owner_hbm,
    image_hbm,
    mask_hbm,
    base_hbm,
    corner_hbm,
    state_hbm,
    message_ref,
    stay_hbm,
    up_ref,
    down_ref,
    face_ref,
    courant_ref,
    table_ref,
    cell_ref,
    owner_ref,
    image_ref,
    mask_ref,
    base_ref,
    corner_ref,
    state_ref,
    stay_ref,
    turned_ref,
    face_turned_ref,
    courant_turned_ref,
    pair_ref,
    pick_ref,
    matrix_ref,
    adjoint_ref,
    weight_ref,
    cleared_ref,
    rest_ref,
    sems,
    stay_sem,
):
    var_count, rows, pencils = state_ref.shape
    cells = var_count * rows
    count = pencils // LANES
    ghosts = cell_ref.shape[0]
    padded = -(-count // 8) * 8
    p = lax.axis_index("pipe")
    slabs, height = slices.slabs, slices.height
    lines = slices.groups * slices.per
    own_at, reduce_at, adjoint_at, profile_at = at
    copies = fetch(
        (
            face_hbm,
            courant_hbm,
            tables_hbm.at[p],
            cell_hbm,
            owner_hbm,
            image_hbm,
            base_hbm,
            corner_hbm,
            mask_hbm,
            state_hbm,
        ),
        (
            face_ref,
            courant_ref,
            table_ref,
            cell_ref,
            owner_ref,
            image_ref,
            base_ref,
            corner_ref,
            mask_ref,
            state_ref,
        ),
        sems,
    )
    kept, own, about_at, _ = stay_at(rows, count, cells)

    def send(line, rows_at, slab):
        for t, row_at in enumerate(rows_at):
            start, end = slices.tiles_at(t)
            message_ref[pl.ds(row_at, end - start, stride=height), :] = slab[start:end]
        for m in range(slices.rest):
            tail = slices.full * slabs + m
            rest_ref[m * lines + line : m * lines + line + 1, :] = slab[tail : tail + 1]

    def send_value(functional, v, slab):
        rows_at = [slices.row(functional, t) + v for t in range(slices.full)]
        send(functional * var_count + v, rows_at, slab)

    def send_coefficient(which, slab):
        rows_at = [slices.coefficient_row(which, t) for t in range(slices.full)]
        send(6 * var_count + which, rows_at, slab)

    for copy in copies[:8]:
        copy.wait()
    image_row, image_pencil = place_of(base_ref[...].reshape(1, -1), rows, pencils)
    pick_ref[...] = marks(pick_ref.shape, 0, image_pencil)
    turn(face_turned_ref, face_ref[...])

    def face(i):
        return slab_at(face_turned_ref, i, rows, count)

    link = face(0)
    margin = jnp.ones_like(link)
    first_margin = margin
    to_up, to_first = [None] * rows, [None] * rows
    for i in range(1, rows - 1):
        above = face(i)
        inverse = 1.0 / (link + margin + above)
        low, up = link * inverse, above * inverse
        to_up[i], to_first[i] = up, low
        for k, part in enumerate((up, low, inverse)):
            start = kept_at(k, i, rows, count)
            stay_ref[start : start + count, :] = part
        first_margin += low * margin
        link = link * up
        margin = 1.0 + margin * up
    send_coefficient(LINK_IN, link)
    send_coefficient(MARGIN_FIRST, first_margin)
    send_coefficient(MARGIN_LAST, margin)
    send_coefficient(LINK_UP, jnp.where(p == slabs - 1, 0.0, face(rows - 1)))

    zero, one = jnp.zeros_like(margin), jnp.ones_like(margin)
    first, last = [None] * rows, [None] * rows
    first[0], first[rows - 1], last[0], last[rows - 1] = one, zero, zero, one
    for i in range(rows - 2, 0, -1):
        first[i] = to_first[i] + to_up[i] * first[i + 1]
        last[i] = to_up[i] * last[i + 1]
    turn(courant_turned_ref, courant_ref[...])
    for i in range(rows):
        speed = slab_at(courant_turned_ref, i, rows, count)
        start = kept_at(3, i, rows, count)
        stay_ref[start : start + count, :] = speed
        put_slab(pair_ref, i, 2 * rows, count, first[i] * speed)
        put_slab(pair_ref, rows + i, 2 * rows, count, last[i] * speed)
    for t in range(count):
        matrix_ref[:, tile(t)] = pair_ref[t * 2 * rows : (t + 1) * 2 * rows, :]
    stay_ref[kept - 40 : kept, :] = table_ref[profile_at : profile_at + 40, :]
    stay_ref[own : own + cells, :] = table_ref[own_at : own_at + cells, :]
    turn(
        adjoint_ref, full_dot(table_ref[adjoint_at : adjoint_at + 40, : 2 * rows], matrix_ref[...])
    )
    for k in range(6):
        send_coefficient(FIRST_LO + k, slab_at(adjoint_ref, 2 * rows + k, 40, count))
    weight_ref[:, padded - 8 :, :] = jnp.zeros((2 * rows, 8, LANES), jnp.float32)
    for i, share in enumerate(first + last):
        weight_ref[i, :count, :] = share - slab_at(adjoint_ref, i, 40, count)

    row, pencil = place_of(cell_ref[...].reshape(1, ghosts), rows, pencils)
    lane_tile = jnp.right_shift(pencil, 7)
    lane_marks = marks((LANES, ghosts), 0, pencil - lane_tile * LANES)
    picked = exact_dot(
        weight_ref[...].reshape(2 * rows * padded, LANES), lane_marks, ((1,), (0,))
    ).reshape(2, rows, padded, ghosts)
    at_cell = (lax.broadcasted_iota(jnp.int32, (rows, padded, ghosts), 0) == row[None]) & (
        lax.broadcasted_iota(jnp.int32, (rows, padded, ghosts), 1) == lane_tile[None]
    )

    def at_ghosts(values):
        return jnp.sum(jnp.sum(jnp.where(at_cell, values, 0.0), axis=0), axis=0, keepdims=True)

    about = jnp.concatenate(
        [
            cell_ref[...].reshape(1, ghosts).astype(jnp.float32),
            (owner_ref[...] * base_ref.shape[0] + image_ref[...])
            .reshape(1, ghosts)
            .astype(jnp.float32),
            at_ghosts(picked[0]),
            at_ghosts(picked[1]),
        ],
        axis=0,
    )
    for j in range(slabs):
        start = j * height + slices.meta_at
        message_ref[start : start + ABOUT, :] = about
    stay_ref[about_at : about_at + ABOUT, :] = about
    edge = var_count * count
    for ref in (up_ref, down_ref):
        ref[edge : edge + ABOUT, :] = about
    staying = pltpu.make_async_copy(stay_ref, stay_hbm, stay_sem.at[0])
    staying.start()
    for copy in copies[8:]:
        copy.wait()
    values = image_lines(
        state_ref[...].reshape(cells, pencils),
        image_row,
        pick_ref,
        corner_ref,
        rows,
        var_count,
    )
    for j in range(slabs):
        start = j * height + slices.images_at
        message_ref[start : start + slices.image_rows, :] = values
    solid = mask_ref[...] == 1
    for v in range(var_count):
        here = slice(v * rows, (v + 1) * rows)
        cleared_ref[here, :] = jnp.where(solid, 0.0, state_ref[v])
    turn(turned_ref, cleared_ref[...])
    for group in (range(0, 3), range(3, var_count)):
        sums = {v: [zero] * 4 for v in group}
        for i in range(rows):
            up, down = reduce_at + i, reduce_at + rows + i
            weights = (
                table_ref[up : up + 1, :],
                table_ref[down : down + 1, :],
                weight_ref[i, :count, :],
                weight_ref[rows + i, :count, :],
            )
            for v in group:
                cell = slab_at(turned_ref, v * rows + i, cells, count)
                if i == 0:
                    send_value(ROW_FIRST, v, cell)
                    down_ref[v * count : (v + 1) * count, :] = cell
                if i == rows - 1:
                    send_value(ROW_LAST, v, cell)
                    up_ref[v * count : (v + 1) * count, :] = cell
                sums[v] = [x + weight * cell for x, weight in zip(sums[v], weights)]
        for v in group:
            for functional, total in zip((Z_UP, Z_DOWN, RIGHT_FIRST, RIGHT_LAST), sums[v]):
                send_value(functional, v, total)

    block = lane_block(max(slices.groups, 1), slices.width)
    for m in range(slices.rest):
        lined = [
            rest_ref[pl.ds(m * lines + k, slices.groups, stride=slices.per), :]
            for k in range(slices.per)
        ]
        for i in range(slices.per):
            packed = lined[0]
            for k in range(slices.per):
                moved = moved_lanes(lined[k], (k - i) * slices.width)
                packed = moved if k == 0 else jnp.where(block == k, moved, packed)
            start = (m * slices.per + i) * height + slices.packed_at
            message_ref[start : start + slices.groups, :] = packed
    staying.wait()


def chain_kernel(slices, message_ref, rest_ref, chain_ref):
    slabs, chunk, full = slices.slabs, slices.chunk, slices.full
    height, per, width = slices.height, slices.per, slices.width
    if slices.rest:
        for p in range(slabs):
            start = p * height + slices.packed_at
            packed = message_ref[start : start + slices.groups, :]
            for k in range(per):
                rest_ref[pl.ds(p * slices.groups * per + k, slices.groups, stride=per), :] = (
                    moved_lanes(packed, -k * width)
                )
    else:
        rest_ref[...] = jnp.zeros_like(rest_ref)

    def sent(p, which):
        start = p * height + slices.coefficient_row(which, 0)
        slab = message_ref[start : start + full, :]
        if slices.rest:
            start = p * slices.groups * per + 6 * slices.var_count + which
            slab = jnp.concatenate([slab, rest_ref[start : start + 1, :]], axis=0)
        return slab

    nodes = 2 * slabs
    margin = sent(0, MARGIN_FIRST)
    for k in range(nodes):
        link = sent(k // 2, LINK_UP if k % 2 else LINK_IN)
        inverse = 1.0 / (margin + link)
        ratio = link * inverse
        chain_ref[16 * k : 16 * k + chunk, :] = ratio
        chain_ref[16 * k + 8 : 16 * k + 8 + chunk, :] = inverse
        if k < nodes - 1:
            following = sent((k + 1) // 2, MARGIN_FIRST if k % 2 else MARGIN_LAST)
            margin = following + margin * ratio


def solve_kernel(slices, pencils, constants, message_ref, rest_ref, chain_ref, *refs):
    *blocks, back_ref, ghost_ref, back_rest_ref = refs
    slabs, var_count, chunk, full = slices.slabs, slices.var_count, slices.chunk, slices.full
    height, per, width = slices.height, slices.per, slices.width
    me = lax.axis_index("pipe")

    def meta(p, k):
        start = p * height + slices.meta_at + k
        return message_ref[start : start + 1, :]

    def meta_all(k):
        return jnp.concatenate([meta(p, k) for p in range(slabs)], axis=1)

    carry_up, carry_down, ups, downs = constants
    values = ghost_values(slices, blocks, meta_all(COLUMN))
    rows = ups.shape[1]
    row_of, pencil_of = place_of(meta_all(CELL).astype(jnp.int32), rows, pencils)
    ghosts = LANES
    place = lax.broadcasted_iota(jnp.int32, (chunk * LANES, ghosts), 0)
    slot, lane = place // LANES, place % LANES
    pencil_at = jnp.where(
        slot < full,
        (me + slot * slabs) * LANES + lane,
        (full * slabs + me // per) * LANES + (me % per) * width + lane,
    )
    none = jnp.zeros((8 - var_count, ghosts), jnp.float32)
    for p in range(slabs):
        row = row_of[:, tile(p)]
        up = down = jnp.zeros((1, ghosts), jnp.float32)
        for i in range(rows):
            up = jnp.where(row == i, float(ups[p, i]), up)
            down = jnp.where(row == i, float(downs[p, i]), down)
        weights = (
            up,
            down,
            jnp.where(row == 0, 1.0, 0.0),
            jnp.where(row == rows - 1, 1.0, 0.0),
            meta(p, WEIGHT_FIRST),
            meta(p, WEIGHT_LAST),
        )
        here = jnp.concatenate([value[:, tile(p)] for value in values] + [none], axis=0)
        shares = jnp.concatenate([here * weight for weight in weights], axis=0)
        spots = jnp.where(pencil_at == pencil_of[:, tile(p)], 1.0, 0.0)
        share = exact_dot(shares, spots.astype(jnp.bfloat16), ((1,), (1,)))
        for t in range(chunk):
            start = (p * chunk + t) * 48
            ghost_ref[start : start + 48, :] = share[:, tile(t)]

    nodes = 2 * slabs
    zero = jnp.zeros((var_count, LANES), jnp.float32)
    for t in range(chunk):

        def value(p, functional):
            if t < full:
                start = p * height + slices.row(functional, t)
                sent = message_ref[start : start + var_count, :]
            else:
                start = p * slices.groups * per + functional * var_count
                sent = rest_ref[start : start + var_count, :]
            start = (p * chunk + t) * 48 + functional * 8
            return sent + ghost_ref[start : start + var_count, :]

        def coefficient(p, which):
            if t < full:
                start = p * height + slices.coefficient_row(which, t)
                return message_ref[start : start + 1, :]
            start = p * slices.groups * per + 6 * var_count + which
            return rest_ref[start : start + 1, :]

        def give(p, functional, block):
            if t < full:
                start = p * slices.back_height + slices.row(functional, t)
                back_ref[start : start + var_count, :] = block
            else:
                start = p * slices.back_groups * per + functional * var_count
                back_rest_ref[start : start + var_count, :] = block

        def ratio(k):
            return chain_ref[16 * k + t : 16 * k + t + 1, :]

        def scale(k):
            return chain_ref[16 * k + 8 + t : 16 * k + 9 + t, :]

        lo, hi, below, above = ([zero] * slabs for _ in range(4))
        for p in range(1, slabs):
            lo[p] = value(p - 1, Z_UP) + float(carry_up[p]) * lo[p - 1]
            below[p] = value(p - 1, ROW_LAST)
        for p in range(slabs - 2, -1, -1):
            hi[p] = value(p + 1, Z_DOWN) + float(carry_down[p]) * hi[p + 1]
            above[p] = value(p + 1, ROW_FIRST)
        right = []
        for p in range(slabs):
            right.append(
                value(p, RIGHT_FIRST)
                - coefficient(p, FIRST_LO) * lo[p]
                - coefficient(p, FIRST_HI) * hi[p]
                - coefficient(p, FIRST_EDGE) * below[p]
            )
            right.append(
                value(p, RIGHT_LAST)
                - coefficient(p, LAST_LO) * lo[p]
                - coefficient(p, LAST_HI) * hi[p]
                - coefficient(p, LAST_EDGE) * above[p]
            )
            give(p, 2, lo[p])
            give(p, 3, hi[p])
        for k in range(1, nodes):
            right[k] = right[k] + ratio(k - 1) * right[k - 1]
        x = right[nodes - 1] * scale(nodes - 1)
        give(slabs - 1, 1, x)
        for k in range(nodes - 2, -1, -1):
            x = right[k] * scale(k) + ratio(k) * x
            give(k // 2, k % 2, x)
    if slices.rest:
        groups = slices.back_groups
        block = lane_block(groups, width)
        for p in range(slabs):
            for k in range(per):
                lined = back_rest_ref[pl.ds(p * groups * per + k, groups, stride=per), :]
                moved = moved_lanes(lined, k * width)
                packed = moved if k == 0 else jnp.where(block == k, moved, packed)
            start = p * slices.back_height + slices.back_packed_at
            back_ref[start : start + groups, :] = packed


def pick_kernel(slices, message_ref, values_ref):
    size = slices.image_rows
    for p in range(slices.slabs):
        start = p * slices.height + slices.images_at
        values_ref[p * size : (p + 1) * size, :] = message_ref[start : start + size, :]


def own_kernel(stay_ref, mask_ref, state_ref, ready_ref, cleared_ref):
    var_count, rows, pencils = state_ref.shape
    cells = var_count * rows
    count = pencils // LANES
    own_at = stay_at(rows, count, cells)[1]
    cells_at, kept_start, end = ready_at(rows, count, cells)
    solid = mask_ref[...] == 1
    for v in range(var_count):
        cleared_ref[v * rows : (v + 1) * rows, :] = jnp.where(solid, 0.0, state_ref[v])
    turn(ready_ref.at[cells_at:kept_start, :], cleared_ref[...])
    turn(
        ready_ref.at[:cells_at, :],
        full_dot(stay_ref[own_at : own_at + cells, :cells], cleared_ref[...]),
    )
    ready_ref[kept_start:end, :] = stay_ref[...]


def fill_kernel(slices, shape, ready_ref, below_ref, above_ref, *refs):
    *blocks, done_ref, filled_ref, edge_ref = refs
    var_count, rows, pencils = shape
    cells = var_count * rows
    count = pencils // LANES
    _, own_at, about_at, _ = stay_at(rows, count, cells)
    cells_at, kept_start, _ = ready_at(rows, count, cells)

    ghosts = LANES
    about = [ready_ref[kept_start + about_at : kept_start + about_at + ABOUT, :]]
    edge = var_count * count
    about += [ref[edge : edge + ABOUT, :] for ref in (below_ref, above_ref)]

    def known(k):
        return jnp.concatenate([x[k : k + 1] for x in about], axis=1)

    values = ghost_values(slices, blocks, known(COLUMN))
    row, pencil = place_of(known(CELL).astype(jnp.int32), rows, pencils)
    at_row = lax.broadcasted_iota(jnp.int32, (rows, ghosts), 0) == row[:, :ghosts]
    spread = jnp.concatenate([jnp.where(at_row, value[:, :ghosts], 0.0) for value in values], axis=0)
    own = ready_ref[kept_start + own_at : kept_start + own_at + cells, :cells]
    both = jnp.concatenate([full_dot(own, spread), spread], axis=0)
    spots = marks((pencils, ghosts), 0, pencil[:, :ghosts])
    added = exact_dot(both, spots, ((1,), (1,)))
    for t in range(count):
        here = slice(t * cells, (t + 1) * cells)
        there = slice(cells_at + t * cells, cells_at + (t + 1) * cells)
        done_ref[here, :] = ready_ref[here, :] + added[:cells, tile(t)]
        filled_ref[here, :] = ready_ref[there, :] + added[cells:, tile(t)]
    x_at, response_at, profile_at, edge_at, _ = done_at(rows, count, cells, var_count)
    none = jnp.zeros((8 - var_count, ghosts), jnp.float32)
    for k, (ref, wanted) in enumerate(((below_ref, rows - 1), (above_ref, 0))):
        here = slice((k + 1) * ghosts, (k + 2) * ghosts)
        at_edge = row[:, here] == wanted
        spread = [jnp.where(at_edge, value[:, here], 0.0) for value in values] + [none]
        spots = marks((pencils, ghosts), 0, pencil[:, here])
        turn(edge_ref, exact_dot(jnp.concatenate(spread, axis=0), spots, ((1,), (1,))))
        for v in range(var_count):
            start = edge_at + (k * var_count + v) * count
            done_ref[start : start + count, :] = ref[v * count : (v + 1) * count, :] + slab_at(
                edge_ref, v, 8, count
            )

    def kept(which, i):
        start = kept_start + kept_at(which, i, rows, count)
        return ready_ref[start : start + count, :]

    def profile(k):
        start = kept_start + own_at - 40 + k
        return ready_ref[start : start + 1, :]

    def put(at, i, height, value):
        done_ref[pl.ds(at + i, count, stride=height), :] = value

    swept = []
    for i in range(1, rows - 1):
        speed = kept(3, i)
        here = [-speed * profile(i), -speed * profile(rows + i)]
        for v in range(var_count):
            row = v * rows + i
            own_slab = slab_at(done_ref, row, cells, count)
            here.append(slab_at(filled_ref, row, cells, count) - speed * own_slab)
        if swept:
            ratio = kept(0, i - 1)
            here = [x + ratio * y for x, y in zip(here, swept[-1])]
        swept.append(here)
    zero = jnp.zeros((count, LANES), jnp.float32)
    one = jnp.ones((count, LANES), jnp.float32)
    x = [zero] * (2 + var_count)
    first, last = zero, one
    for i in range(rows - 1, -1, -1):
        if 0 < i < rows - 1:
            ratio, inverse = kept(0, i), kept(2, i)
            first, last = kept(1, i) + ratio * first, ratio * last
            x = [inverse * y + ratio * z for y, z in zip(swept[i - 1], x)]
        if i == 0:
            first, last, x = one, zero, [zero] * (2 + var_count)
        for k, value in enumerate([first, last] + x[:2]):
            put(response_at + k * rows * count, i, rows, value)
        for v in range(var_count):
            put(x_at, v * rows + i, cells, x[2 + v])
    done_ref[profile_at : profile_at + 40, :] = ready_ref[
        kept_start + own_at - 40 : kept_start + own_at, :
    ]


def finish_kernel(
    slices, back_ref, done_ref, derivative_hbm, segment_hbm, derivative_ref, segment_ref, tail_ref, sems
):
    var_count, rows, pencils = segment_ref.shape
    count = pencils // LANES
    cells = var_count * rows
    x_at, response_at, profile_at, edge_at, _ = done_at(rows, count, cells, var_count)
    back_height, groups, per = slices.back_height, slices.back_groups, slices.per
    block = lane_block(max(groups, 1), slices.width)
    for m in range(slices.rest):
        packed = []
        for i in range(per):
            start = (m * per + i) * back_height + slices.back_packed_at
            packed.append(back_ref[start : start + groups, :])
        for k in range(per):
            for i in range(per):
                moved = moved_lanes(packed[i], (i - k) * slices.width)
                joined = moved if i == 0 else jnp.where(block == i, moved, joined)
            tail_ref[pl.ds(m * groups * per + k, groups, stride=per), :] = joined

    def got(functional, v, t):
        step, j = t // slices.slabs, t % slices.slabs
        if step < slices.full:
            start = j * back_height + slices.row(functional, step) + v
            return back_ref[start : start + 1, :]
        start = j * groups * per + functional * var_count + v
        return tail_ref[start : start + 1, :]

    lo_profile = done_ref[profile_at : profile_at + rows, :]
    hi_profile = done_ref[profile_at + rows : profile_at + 2 * rows, :]
    row_at = lax.broadcasted_iota(jnp.int32, (rows, LANES), 0)
    edges = profile_at + 2 * rows
    lo_edge = jnp.where(row_at == 0, done_ref[edges : edges + 1, :], 0.0)
    hi_edge = jnp.where(row_at == rows - 1, done_ref[edges + 1 : edges + 2, :], 0.0)

    def edge(k, v, t):
        start = edge_at + (k * var_count + v) * count + t
        return done_ref[start : start + 1, :]

    def response(k, t):
        start = response_at + (k * count + t) * rows
        return done_ref[start : start + rows, :]

    copies = []
    for v in range(var_count):
        for t in range(count):
            start = t * cells + v * rows
            lo, hi = got(2, v, t), got(3, v, t)
            derivative_ref[v, :, tile(t)] = (
                done_ref[start : start + rows, :]
                + (lo_profile * lo + hi_profile * hi)
                + (lo_edge * edge(0, v, t) + hi_edge * edge(1, v, t))
            )
            segment_ref[v, :, tile(t)] = (
                done_ref[x_at + start : x_at + start + rows, :]
                + (response(0, t) * got(0, v, t) + response(1, t) * got(1, v, t))
                + (response(2, t) * lo + response(3, t) * hi)
            )
        for which, (ref, hbm) in enumerate(
            ((derivative_ref, derivative_hbm), (segment_ref, segment_hbm))
        ):
            copies.append(
                pltpu.make_async_copy(ref.at[v], hbm.at[v], sems.at[which * var_count + v])
            )
            copies[-1].start()
    for copy in copies:
        copy.wait()


def call(kernel, outs, scratch, sems, args, near=(), far_out=(), limit=62):
    whole = pl.BlockSpec(memory_space=pltpu.VMEM)
    far = pl.BlockSpec(memory_space=pltpu.HBM)
    buffers = [
        pltpu.VMEM(s.shape, s.dtype) if hasattr(s, "dtype") else pltpu.VMEM(s, jnp.float32)
        for s in scratch
    ]
    buffers += [pltpu.SemaphoreType.DMA((size,)) for size in sems]
    return pl.pallas_call(
        kernel,
        out_shape=[jax.ShapeDtypeStruct(shape, jnp.float32) for shape in outs],
        in_specs=[whole if k in near else far for k in range(len(args))],
        out_specs=[far if k in far_out else whole for k in range(len(outs))],
        scratch_shapes=buffers,
        compiler_params=pltpu.CompilerParams(vmem_limit_bytes=limit * 2**20),
    )(*args)


def exchange(message, axes):
    return lax.all_to_all(message, axes, 0, 0, tiled=True)


def local(
    state,
    face_diffusion,
    courant,
    cell_mask,
    ghost_cell,
    ghost_owner,
    ghost_image,
    image_base,
    image_weight,
):
    var_count, rows, pencils = state.shape
    slabs, cross = lax.axis_size("pipe"), lax.axis_size("cross")
    count = pencils // LANES
    cells = var_count * rows
    images = image_base.shape[0]
    tables, at, constants = derivative_tables(slabs, rows, var_count)
    slices = Slices(slabs, count, cross, var_count, images)
    tables = jnp.asarray(tables)
    turned = (cells * count, LANES)
    stay = stay_at(rows, count, cells)[3]
    ready = (ready_at(rows, count, cells)[2], LANES)

    arguments = (
        face_diffusion,
        courant,
        tables,
        ghost_cell,
        ghost_owner,
        ghost_image,
        cell_mask,
        image_base,
        image_weight,
        state,
    )
    buffers = list(arguments)
    buffers[2] = jax.ShapeDtypeStruct(tables.shape[1:], jnp.float32)
    edge = (-(-(var_count * count + ABOUT) // 8) * 8, LANES)
    message, stay, up, down = call(
        functools.partial(prepare_kernel, slices, at),
        [(slabs * slices.height, LANES), (stay, LANES), edge, edge],
        buffers
        + [
            (stay, LANES),
            turned,
            (rows * count, LANES),
            (rows * count, LANES),
            (2 * rows * count, LANES),
            jax.ShapeDtypeStruct((pencils, images), jnp.bfloat16),
            (2 * rows, pencils),
            (40 * count, LANES),
            (2 * rows, -(-count // 8) * 8, LANES),
            (cells, pencils),
            (max(slices.rest, 1) * max(slices.groups, 1) * slices.per, LANES),
        ],
        [len(arguments), 1],
        arguments,
        far_out=(1,),
    )
    message = exchange(message, "pipe")
    forward = [(i, i + 1) for i in range(slabs - 1)]
    below = lax.ppermute(up, "pipe", forward)
    above = lax.ppermute(down, "pipe", [(j, i) for i, j in forward])
    message, below, above = lax.optimization_barrier((message, below, above))
    (ready,) = call(
        own_kernel,
        [ready],
        [(cells, pencils)],
        [],
        (stay, cell_mask, state),
        near=range(3),
        limit=48,
    )
    (image_values,) = call(
        functools.partial(pick_kernel, slices),
        [(slabs * slices.image_rows, LANES)],
        [],
        [],
        (message,),
        near=(0,),
        limit=24,
    )
    blocks = [image_values] + [
        lax.ppermute(image_values, "cross", [(i, i ^ u) for i in range(cross)])
        for u in range(1, cross)
    ]

    rest, chain = call(
        functools.partial(chain_kernel, slices),
        [(slabs * max(slices.groups, 1) * slices.per, LANES), (2 * slabs * 16, LANES)],
        [],
        [],
        (message,),
        near=(0,),
        limit=24,
    )
    (back,) = call(
        functools.partial(solve_kernel, slices, pencils, constants),
        [(slabs * slices.back_height, LANES)],
        [
            (slabs * slices.chunk * 48, LANES),
            (slabs * max(slices.back_groups, 1) * slices.per, LANES),
        ],
        [],
        (message, rest, chain, *blocks),
        near=range(3 + cross),
        limit=24,
    )
    back = exchange(back, "pipe")
    (done,) = call(
        functools.partial(fill_kernel, slices, state.shape),
        [(done_at(rows, count, cells, var_count)[4], LANES)],
        [turned, (8 * count, LANES)],
        [],
        (ready, below, above, *blocks),
        near=range(3 + cross),
        limit=48,
    )
    return tuple(
        call(
            functools.partial(finish_kernel, slices),
            [state.shape, state.shape],
            [
                state.shape,
                state.shape,
                (max(slices.rest, 1) * max(slices.back_groups, 1) * slices.per, LANES),
            ],
            [2 * var_count],
            (back, done),
            near=range(2),
            far_out=(0, 1),
            limit=48,
        )
    )


def solution(mesh):
    in_specs = (
        P(None, "pipe", "cross"),
        P("pipe", "cross"),
        P("pipe", "cross"),
        P("pipe", "cross"),
        P(("pipe", "cross")),
        P(("pipe", "cross")),
        P(("pipe", "cross")),
        P(("pipe", "cross")),
        P(None, ("pipe", "cross")),
    )
    out_specs = (P(None, "pipe", "cross"), P(None, "pipe", "cross"))
    return jax.shard_map(local, mesh=mesh, in_specs=in_specs, out_specs=out_specs, check_vma=False)
```

```python
import functools

import numpy as np
import jax
import jax.numpy as jnp
from jax import lax
from jax.experimental import pallas as pl
from jax.experimental.pallas import tpu as pltpu
from jax.sharding import PartitionSpec as P

LINE = 96
LANES = 128
REFLECT = (1.0, -1.0, -1.0, -1.0, 1.0)

Z_UP, Z_DOWN, ROW_FIRST, ROW_LAST, RIGHT_FIRST, RIGHT_LAST = range(6)
LINK_IN, MARGIN_FIRST, MARGIN_LAST, LINK_UP, FIRST_LO, FIRST_HI, LAST_LO, LAST_HI, FIRST_EDGE, LAST_EDGE = range(10)
COEFFICIENTS = 10
CELL, COLUMN, WEIGHT_FIRST, WEIGHT_LAST = range(4)
ABOUT = 4


def derivative_tables(slabs, rows, var_count):
    total = slabs * rows
    A = np.eye(total)
    B = np.zeros((total, total))
    for i in range(2, total - 2):
        A[i, i - 1] = A[i, i + 1] = 1.0 / 3.0
        B[i, i + 1], B[i, i - 1] = 7.0 / 9.0, -7.0 / 9.0
        B[i, i + 2], B[i, i - 2] = 1.0 / 36.0, -1.0 / 36.0
    for i in (1, total - 2):
        A[i, i - 1] = A[i, i + 1] = 0.25
        B[i, i + 1], B[i, i - 1] = 0.75, -0.75
    B[0, :3] = (-1.5, 2.0, -0.5)
    B[-1, -3:] = (0.5, -2.0, 1.5)
    inverse = np.linalg.inv(A)
    M = inverse @ B

    cells = var_count * rows
    own_at, reduce_at, adjoint_at, profile_at = 0, cells, cells + 32, cells + 72
    tables = np.zeros((slabs, cells + 112, LANES))
    carry_up, carry_down = np.zeros(slabs), np.zeros(slabs)
    ups, downs = np.zeros((slabs, rows)), np.zeros((slabs, rows))
    for p in range(slabs):
        table = tables[p]
        base = p * rows
        here = slice(base, base + rows)
        own = M[here, here]
        lo, hi, lo_edge, hi_edge = (np.zeros(rows) for _ in range(4))
        weight_up, weight_down = np.zeros(rows), np.zeros(rows)
        if p > 0:
            lo = inverse[here, base - 8] / inverse[base + 1, base - 8]
            lo_edge[0] = M[base, base - 1] - lo[0] * M[base + 1, base - 1]
            weight_down = M[base - 2, here]
        if p > 1:
            k = base - rows - 8
            carry_up[p] = inverse[base + 1, k] / inverse[base - rows + 1, k]
        if p < slabs - 1:
            k = base + rows + 8
            hi = inverse[here, k] / inverse[base + rows - 2, k]
            hi_edge[-1] = M[base + rows - 1, base + rows] - hi[-1] * M[base + rows - 2, base + rows]
            weight_up = M[base + rows + 1, here]
        if p < slabs - 2:
            k = base + 2 * rows + 8
            carry_down[p] = inverse[base + rows - 2, k] / inverse[base + 2 * rows - 2, k]
        for v in range(var_count):
            at = slice(v * rows, (v + 1) * rows)
            table[own_at + v * rows : own_at + (v + 1) * rows, at] = own
        table[reduce_at : reduce_at + rows] = weight_up[:, None]
        table[reduce_at + rows : reduce_at + 2 * rows] = weight_down[:, None]
        table[adjoint_at : adjoint_at + rows, :rows] = own.T
        table[adjoint_at + rows : adjoint_at + 2 * rows, rows : 2 * rows] = own.T
        more = adjoint_at + 2 * rows
        table[more, :rows] = lo
        table[more + 1, :rows] = hi
        table[more + 2, rows : 2 * rows] = lo
        table[more + 3, rows : 2 * rows] = hi
        table[more + 4, 0] = lo_edge[0]
        table[more + 5, 2 * rows - 1] = hi_edge[-1]
        table[profile_at : profile_at + rows] = lo[:, None]
        table[profile_at + rows : profile_at + 2 * rows] = hi[:, None]
        table[profile_at + 2 * rows] = lo_edge[0]
        table[profile_at + 2 * rows + 1] = hi_edge[-1]
        ups[p], downs[p] = weight_up, weight_down
    at = (own_at, reduce_at, adjoint_at, profile_at)
    return tables.astype(np.float32), at, (carry_up, carry_down, ups, downs)


def split(x, parts):
    pieces = []
    for _ in range(parts):
        piece = x.astype(jnp.bfloat16)
        pieces.append(piece)
        x = x - piece.astype(jnp.float32)
    return pieces


def exact_dot(x, one_hot, contract):
    found = lax.dot_general(
        jnp.concatenate(split(x, 3), axis=0),
        one_hot,
        (contract, ((), ())),
        preferred_element_type=jnp.float32,
    )
    size = x.shape[0]
    return found[:size] + (found[size : 2 * size] + found[2 * size :])


def full_dot(a, b):
    return jnp.dot(a, b, precision=lax.Precision.HIGHEST, preferred_element_type=jnp.float32)


def marks(shape, axis, values):
    return jnp.where(lax.broadcasted_iota(jnp.int32, shape, axis) == values, 1.0, 0.0).astype(
        jnp.bfloat16
    )


def place_of(cell, rows, pencils):
    row = jnp.zeros_like(cell)
    for k in range(1, rows):
        row += (cell >= k * pencils).astype(jnp.int32)
    return row, cell - row * pencils


def tile(t):
    return slice(t * LANES, (t + 1) * LANES)


def turn(ref, x):
    height, pencils = x.shape
    for t in range(pencils // LANES):
        ref[t * height : (t + 1) * height, :] = x[:, tile(t)]


def slab_at(ref, row, height, count):
    return ref[pl.ds(row, count, stride=height), :]


def put_slab(ref, row, height, count, value):
    ref[pl.ds(row, count, stride=height), :] = value


def kept_at(which, i, rows, count):
    return (which * rows + i) * (-(-count // 8) * 8)


def stay_at(rows, count, cells):
    kept = kept_at(4, 0, rows, count) + 40
    return kept, kept, kept + cells, kept + cells + 8


def ready_at(rows, count, cells):
    kept = 2 * cells * count
    return cells * count, kept, kept + stay_at(rows, count, cells)[3]


def done_at(rows, count, cells, var_count):
    x = cells * count
    response = 2 * x
    profile = response + 4 * rows * count
    return x, response, profile, profile + 40, profile + 40 + 2 * var_count * count


def fetch(sources, targets, sems):
    copies = [
        pltpu.make_async_copy(source, target, sems.at[k])
        for k, (source, target) in enumerate(zip(sources, targets))
    ]
    for copy in copies:
        copy.start()
    return copies


class Slices:
    def __init__(self, slabs, count, cross, var_count, images):
        rest = count % slabs
        self.slabs, self.count, self.cross, self.var_count = slabs, count, cross, var_count
        self.image_rows = var_count * images // LANES
        shared = rest > 0 and slabs % rest == 0 and LANES % (slabs // rest) == 0
        self.full = count // slabs if shared else -(-count // slabs)
        self.rest = rest if shared else 0
        self.per = slabs // rest if shared else 1
        self.width = LANES // self.per
        self.chunk = self.full + (1 if shared else 0)
        self.lines, self.back_lines = 6 * var_count + COEFFICIENTS, 4 * var_count
        self.groups, self.back_groups = (self.group_count(n) for n in (self.lines, self.back_lines))
        self.meta_at = self.lines * self.full
        self.packed_at = self.meta_at + ABOUT
        self.images_at = self.packed_at + self.groups
        self.height = -(-(self.images_at + self.image_rows) // 8) * 8
        self.back_packed_at = self.back_lines * self.full
        self.back_height = -(-(self.back_packed_at + self.back_groups) // 8) * 8

    def group_count(self, lines):
        return -(-lines // self.per) if self.rest else 0

    def row(self, functional, t):
        return (functional * self.full + t) * self.var_count

    def coefficient_row(self, which, t):
        return 6 * self.full * self.var_count + which * self.full + t

    def tiles_at(self, t):
        return t * self.slabs, min(self.count, (t + 1) * self.slabs)


def lane_block(rows, width):
    return lax.broadcasted_iota(jnp.int32, (rows, LANES), 1) // width


def moved_lanes(x, by):
    by %= LANES
    return x if by == 0 else pltpu.roll(x, by, 1)


def image_lines(x, row, pick_ref, weight_ref, rows, var_count):
    pencils, images = pick_ref.shape
    row_at = lax.broadcasted_iota(jnp.int32, (rows, images), 0)
    lower, upper = row_at == row, row_at == row + 1
    total = [jnp.zeros((rows, images), jnp.float32) for _ in range(var_count)]
    pieces = jnp.concatenate(split(x, 2), axis=0)
    for corner, shift in enumerate((0, 1, LINE, LINE + 1)):
        moved = pieces if shift == 0 else pltpu.roll(pieces, pencils - shift, 1)
        found = jnp.dot(moved, pick_ref[...], preferred_element_type=jnp.float32)
        found = found[: var_count * rows] + found[var_count * rows :]
        weight = jnp.where(lower, weight_ref[corner : corner + 1], 0.0) + jnp.where(
            upper, weight_ref[corner + 4 : corner + 5], 0.0
        )
        for v in range(var_count):
            total[v] += found[v * rows : (v + 1) * rows] * weight
    lines = []
    for v in range(var_count):
        value = jnp.sum(total[v], axis=0, keepdims=True)
        lines += [value[:, tile(t)] for t in range(images // LANES)]
    return jnp.concatenate(lines, axis=0)


def ghost_values(slices, blocks, column):
    per = slices.image_rows // slices.var_count
    slabs, cross = slices.slabs, slices.cross
    ghosts = column.shape[1]
    images = per * LANES
    owner = ((column + 0.5) * (1.0 / images)).astype(jnp.int32)
    image = column.astype(jnp.int32) - owner * images
    across = lax.axis_index("cross")
    values = [
        jnp.concatenate(
            [
                jnp.concatenate(
                    [
                        block[pl.ds(v * per + t, slabs, stride=slices.image_rows), :]
                        for t in range(per)
                    ],
                    axis=1,
                )
                for block in blocks
            ],
            axis=0,
        )
        for v in range(slices.var_count)
    ]
    pick = marks((per * LANES, ghosts), 0, image)
    found = exact_dot(jnp.concatenate(values, axis=0), pick, ((1,), (0,)))
    devices = slabs * cross
    at = lax.broadcasted_iota(jnp.int32, (devices, ghosts), 0)
    mine = (at % slabs) * cross + (across ^ (at // slabs)) == owner
    return [
        reflect
        * jnp.sum(
            jnp.where(mine, found[v * devices : (v + 1) * devices], 0.0), axis=0, keepdims=True
        )
        for v, reflect in enumerate(REFLECT)
    ]


def prepare_kernel(
    slices,
    at,
    face_hbm,
    courant_hbm,
    tables_hbm,
    cell_hbm,
    owner_hbm,
    image_hbm,
    mask_hbm,
    base_hbm,
    corner_hbm,
    state_hbm,
    message_ref,
    stay_hbm,
    up_ref,
    down_ref,
    face_ref,
    courant_ref,
    table_ref,
    cell_ref,
    owner_ref,
    image_ref,
    mask_ref,
    base_ref,
    corner_ref,
    state_ref,
    stay_ref,
    turned_ref,
    face_turned_ref,
    courant_turned_ref,
    pair_ref,
    pick_ref,
    matrix_ref,
    adjoint_ref,
    weight_ref,
    cleared_ref,
    rest_ref,
    sems,
    stay_sem,
):
    var_count, rows, pencils = state_ref.shape
    cells = var_count * rows
    count = pencils // LANES
    ghosts = cell_ref.shape[0]
    padded = -(-count // 8) * 8
    p = lax.axis_index("pipe")
    slabs, height = slices.slabs, slices.height
    lines = slices.groups * slices.per
    own_at, reduce_at, adjoint_at, profile_at = at
    copies = fetch(
        (
            face_hbm,
            courant_hbm,
            tables_hbm.at[p],
            cell_hbm,
            owner_hbm,
            image_hbm,
            base_hbm,
            corner_hbm,
            mask_hbm,
            state_hbm,
        ),
        (
            face_ref,
            courant_ref,
            table_ref,
            cell_ref,
            owner_ref,
            image_ref,
            base_ref,
            corner_ref,
            mask_ref,
            state_ref,
        ),
        sems,
    )
    kept, own, about_at, _ = stay_at(rows, count, cells)

    def send(line, rows_at, slab):
        for t, row_at in enumerate(rows_at):
            start, end = slices.tiles_at(t)
            message_ref[pl.ds(row_at, end - start, stride=height), :] = slab[start:end]
        for m in range(slices.rest):
            tail = slices.full * slabs + m
            rest_ref[m * lines + line : m * lines + line + 1, :] = slab[tail : tail + 1]

    def send_value(functional, v, slab):
        rows_at = [slices.row(functional, t) + v for t in range(slices.full)]
        send(functional * var_count + v, rows_at, slab)

    def send_coefficient(which, slab):
        rows_at = [slices.coefficient_row(which, t) for t in range(slices.full)]
        send(6 * var_count + which, rows_at, slab)

    for copy in copies[:8]:
        copy.wait()
    image_row, image_pencil = place_of(base_ref[...].reshape(1, -1), rows, pencils)
    pick_ref[...] = marks(pick_ref.shape, 0, image_pencil)
    turn(face_turned_ref, face_ref[...])

    def face(i):
        return slab_at(face_turned_ref, i, rows, count)

    link = face(0)
    margin = jnp.ones_like(link)
    first_margin = margin
    to_up, to_first = [None] * rows, [None] * rows
    for i in range(1, rows - 1):
        above = face(i)
        inverse = 1.0 / (link + margin + above)
        low, up = link * inverse, above * inverse
        to_up[i], to_first[i] = up, low
        for k, part in enumerate((up, low, inverse)):
            start = kept_at(k, i, rows, count)
            stay_ref[start : start + count, :] = part
        first_margin += low * margin
        link = link * up
        margin = 1.0 + margin * up
    send_coefficient(LINK_IN, link)
    send_coefficient(MARGIN_FIRST, first_margin)
    send_coefficient(MARGIN_LAST, margin)
    send_coefficient(LINK_UP, jnp.where(p == slabs - 1, 0.0, face(rows - 1)))

    zero, one = jnp.zeros_like(margin), jnp.ones_like(margin)
    first, last = [None] * rows, [None] * rows
    first[0], first[rows - 1], last[0], last[rows - 1] = one, zero, zero, one
    for i in range(rows - 2, 0, -1):
        first[i] = to_first[i] + to_up[i] * first[i + 1]
        last[i] = to_up[i] * last[i + 1]
    turn(courant_turned_ref, courant_ref[...])
    for i in range(rows):
        speed = slab_at(courant_turned_ref, i, rows, count)
        start = kept_at(3, i, rows, count)
        stay_ref[start : start + count, :] = speed
        put_slab(pair_ref, i, 2 * rows, count, first[i] * speed)
        put_slab(pair_ref, rows + i, 2 * rows, count, last[i] * speed)
    for t in range(count):
        matrix_ref[:, tile(t)] = pair_ref[t * 2 * rows : (t + 1) * 2 * rows, :]
    stay_ref[kept - 40 : kept, :] = table_ref[profile_at : profile_at + 40, :]
    stay_ref[own : own + cells, :] = table_ref[own_at : own_at + cells, :]
    turn(
        adjoint_ref, full_dot(table_ref[adjoint_at : adjoint_at + 40, : 2 * rows], matrix_ref[...])
    )
    for k in range(6):
        send_coefficient(FIRST_LO + k, slab_at(adjoint_ref, 2 * rows + k, 40, count))
    weight_ref[:, padded - 8 :, :] = jnp.zeros((2 * rows, 8, LANES), jnp.float32)
    for i, share in enumerate(first + last):
        weight_ref[i, :count, :] = share - slab_at(adjoint_ref, i, 40, count)

    row, pencil = place_of(cell_ref[...].reshape(1, ghosts), rows, pencils)
    lane_tile = jnp.right_shift(pencil, 7)
    lane_marks = marks((LANES, ghosts), 0, pencil - lane_tile * LANES)
    picked = exact_dot(
        weight_ref[...].reshape(2 * rows * padded, LANES), lane_marks, ((1,), (0,))
    ).reshape(2, rows, padded, ghosts)
    at_cell = (lax.broadcasted_iota(jnp.int32, (rows, padded, ghosts), 0) == row[None]) & (
        lax.broadcasted_iota(jnp.int32, (rows, padded, ghosts), 1) == lane_tile[None]
    )

    def at_ghosts(values):
        return jnp.sum(jnp.sum(jnp.where(at_cell, values, 0.0), axis=0), axis=0, keepdims=True)

    about = jnp.concatenate(
        [
            cell_ref[...].reshape(1, ghosts).astype(jnp.float32),
            (owner_ref[...] * base_ref.shape[0] + image_ref[...])
            .reshape(1, ghosts)
            .astype(jnp.float32),
            at_ghosts(picked[0]),
            at_ghosts(picked[1]),
        ],
        axis=0,
    )
    for j in range(slabs):
        start = j * height + slices.meta_at
        message_ref[start : start + ABOUT, :] = about
    stay_ref[about_at : about_at + ABOUT, :] = about
    edge = var_count * count
    for ref in (up_ref, down_ref):
        ref[edge : edge + ABOUT, :] = about
    staying = pltpu.make_async_copy(stay_ref, stay_hbm, stay_sem.at[0])
    staying.start()
    for copy in copies[8:]:
        copy.wait()
    values = image_lines(
        state_ref[...].reshape(cells, pencils),
        image_row,
        pick_ref,
        corner_ref,
        rows,
        var_count,
    )
    for j in range(slabs):
        start = j * height + slices.images_at
        message_ref[start : start + slices.image_rows, :] = values
    solid = mask_ref[...] == 1
    for v in range(var_count):
        here = slice(v * rows, (v + 1) * rows)
        cleared_ref[here, :] = jnp.where(solid, 0.0, state_ref[v])
    turn(turned_ref, cleared_ref[...])
    for group in (range(0, 3), range(3, var_count)):
        sums = {v: [zero] * 4 for v in group}
        for i in range(rows):
            up, down = reduce_at + i, reduce_at + rows + i
            weights = (
                table_ref[up : up + 1, :],
                table_ref[down : down + 1, :],
                weight_ref[i, :count, :],
                weight_ref[rows + i, :count, :],
            )
            for v in group:
                cell = slab_at(turned_ref, v * rows + i, cells, count)
                if i == 0:
                    send_value(ROW_FIRST, v, cell)
                    down_ref[v * count : (v + 1) * count, :] = cell
                if i == rows - 1:
                    send_value(ROW_LAST, v, cell)
                    up_ref[v * count : (v + 1) * count, :] = cell
                sums[v] = [x + weight * cell for x, weight in zip(sums[v], weights)]
        for v in group:
            for functional, total in zip((Z_UP, Z_DOWN, RIGHT_FIRST, RIGHT_LAST), sums[v]):
                send_value(functional, v, total)

    block = lane_block(max(slices.groups, 1), slices.width)
    for m in range(slices.rest):
        lined = [
            rest_ref[pl.ds(m * lines + k, slices.groups, stride=slices.per), :]
            for k in range(slices.per)
        ]
        for i in range(slices.per):
            packed = lined[0]
            for k in range(slices.per):
                moved = moved_lanes(lined[k], (k - i) * slices.width)
                packed = moved if k == 0 else jnp.where(block == k, moved, packed)
            start = (m * slices.per + i) * height + slices.packed_at
            message_ref[start : start + slices.groups, :] = packed
    staying.wait()


def chain_kernel(slices, message_ref, rest_ref, chain_ref):
    slabs, chunk, full = slices.slabs, slices.chunk, slices.full
    height, per, width = slices.height, slices.per, slices.width
    if slices.rest:
        for p in range(slabs):
            start = p * height + slices.packed_at
            packed = message_ref[start : start + slices.groups, :]
            for k in range(per):
                rest_ref[pl.ds(p * slices.groups * per + k, slices.groups, stride=per), :] = (
                    moved_lanes(packed, -k * width)
                )
    else:
        rest_ref[...] = jnp.zeros_like(rest_ref)

    def sent(p, which):
        start = p * height + slices.coefficient_row(which, 0)
        slab = message_ref[start : start + full, :]
        if slices.rest:
            start = p * slices.groups * per + 6 * slices.var_count + which
            slab = jnp.concatenate([slab, rest_ref[start : start + 1, :]], axis=0)
        return slab

    nodes = 2 * slabs
    margin = sent(0, MARGIN_FIRST)
    for k in range(nodes):
        link = sent(k // 2, LINK_UP if k % 2 else LINK_IN)
        inverse = 1.0 / (margin + link)
        ratio = link * inverse
        chain_ref[16 * k : 16 * k + chunk, :] = ratio
        chain_ref[16 * k + 8 : 16 * k + 8 + chunk, :] = inverse
        if k < nodes - 1:
            following = sent((k + 1) // 2, MARGIN_FIRST if k % 2 else MARGIN_LAST)
            margin = following + margin * ratio


def solve_kernel(slices, pencils, constants, message_ref, rest_ref, chain_ref, *refs):
    *blocks, back_ref, ghost_ref, back_rest_ref = refs
    slabs, var_count, chunk, full = slices.slabs, slices.var_count, slices.chunk, slices.full
    height, per, width = slices.height, slices.per, slices.width
    me = lax.axis_index("pipe")

    def meta(p, k):
        start = p * height + slices.meta_at + k
        return message_ref[start : start + 1, :]

    def meta_all(k):
        return jnp.concatenate([meta(p, k) for p in range(slabs)], axis=1)

    carry_up, carry_down, ups, downs = constants
    values = ghost_values(slices, blocks, meta_all(COLUMN))
    rows = ups.shape[1]
    row_of, pencil_of = place_of(meta_all(CELL).astype(jnp.int32), rows, pencils)
    ghosts = LANES
    place = lax.broadcasted_iota(jnp.int32, (chunk * LANES, ghosts), 0)
    slot, lane = place // LANES, place % LANES
    pencil_at = jnp.where(
        slot < full,
        (me + slot * slabs) * LANES + lane,
        (full * slabs + me // per) * LANES + (me % per) * width + lane,
    )
    none = jnp.zeros((8 - var_count, ghosts), jnp.float32)
    for p in range(slabs):
        row = row_of[:, tile(p)]
        up = down = jnp.zeros((1, ghosts), jnp.float32)
        for i in range(rows):
            up = jnp.where(row == i, float(ups[p, i]), up)
            down = jnp.where(row == i, float(downs[p, i]), down)
        weights = (
            up,
            down,
            jnp.where(row == 0, 1.0, 0.0),
            jnp.where(row == rows - 1, 1.0, 0.0),
            meta(p, WEIGHT_FIRST),
            meta(p, WEIGHT_LAST),
        )
        here = jnp.concatenate([value[:, tile(p)] for value in values] + [none], axis=0)
        shares = jnp.concatenate([here * weight for weight in weights], axis=0)
        spots = jnp.where(pencil_at == pencil_of[:, tile(p)], 1.0, 0.0)
        share = exact_dot(shares, spots.astype(jnp.bfloat16), ((1,), (1,)))
        for t in range(chunk):
            start = (p * chunk + t) * 48
            ghost_ref[start : start + 48, :] = share[:, tile(t)]

    nodes = 2 * slabs
    zero = jnp.zeros((var_count, LANES), jnp.float32)
    for t in range(chunk):

        def value(p, functional):
            if t < full:
                start = p * height + slices.row(functional, t)
                sent = message_ref[start : start + var_count, :]
            else:
                start = p * slices.groups * per + functional * var_count
                sent = rest_ref[start : start + var_count, :]
            start = (p * chunk + t) * 48 + functional * 8
            return sent + ghost_ref[start : start + var_count, :]

        def coefficient(p, which):
            if t < full:
                start = p * height + slices.coefficient_row(which, t)
                return message_ref[start : start + 1, :]
            start = p * slices.groups * per + 6 * var_count + which
            return rest_ref[start : start + 1, :]

        def give(p, functional, block):
            if t < full:
                start = p * slices.back_height + slices.row(functional, t)
                back_ref[start : start + var_count, :] = block
            else:
                start = p * slices.back_groups * per + functional * var_count
                back_rest_ref[start : start + var_count, :] = block

        def ratio(k):
            return chain_ref[16 * k + t : 16 * k + t + 1, :]

        def scale(k):
            return chain_ref[16 * k + 8 + t : 16 * k + 9 + t, :]

        lo, hi, below, above = ([zero] * slabs for _ in range(4))
        for p in range(1, slabs):
            lo[p] = value(p - 1, Z_UP) + float(carry_up[p]) * lo[p - 1]
            below[p] = value(p - 1, ROW_LAST)
        for p in range(slabs - 2, -1, -1):
            hi[p] = value(p + 1, Z_DOWN) + float(carry_down[p]) * hi[p + 1]
            above[p] = value(p + 1, ROW_FIRST)
        right = []
        for p in range(slabs):
            right.append(
                value(p, RIGHT_FIRST)
                - coefficient(p, FIRST_LO) * lo[p]
                - coefficient(p, FIRST_HI) * hi[p]
                - coefficient(p, FIRST_EDGE) * below[p]
            )
            right.append(
                value(p, RIGHT_LAST)
                - coefficient(p, LAST_LO) * lo[p]
                - coefficient(p, LAST_HI) * hi[p]
                - coefficient(p, LAST_EDGE) * above[p]
            )
            give(p, 2, lo[p])
            give(p, 3, hi[p])
        for k in range(1, nodes):
            right[k] = right[k] + ratio(k - 1) * right[k - 1]
        x = right[nodes - 1] * scale(nodes - 1)
        give(slabs - 1, 1, x)
        for k in range(nodes - 2, -1, -1):
            x = right[k] * scale(k) + ratio(k) * x
            give(k // 2, k % 2, x)
    if slices.rest:
        groups = slices.back_groups
        block = lane_block(groups, width)
        for p in range(slabs):
            for k in range(per):
                lined = back_rest_ref[pl.ds(p * groups * per + k, groups, stride=per), :]
                moved = moved_lanes(lined, k * width)
                packed = moved if k == 0 else jnp.where(block == k, moved, packed)
            start = p * slices.back_height + slices.back_packed_at
            back_ref[start : start + groups, :] = packed


def pick_kernel(slices, message_ref, values_ref):
    size = slices.image_rows
    for p in range(slices.slabs):
        start = p * slices.height + slices.images_at
        values_ref[p * size : (p + 1) * size, :] = message_ref[start : start + size, :]


def own_kernel(stay_ref, mask_ref, state_ref, ready_ref, cleared_ref):
    var_count, rows, pencils = state_ref.shape
    cells = var_count * rows
    count = pencils // LANES
    own_at = stay_at(rows, count, cells)[1]
    cells_at, kept_start, end = ready_at(rows, count, cells)
    solid = mask_ref[...] == 1
    for v in range(var_count):
        cleared_ref[v * rows : (v + 1) * rows, :] = jnp.where(solid, 0.0, state_ref[v])
    turn(ready_ref.at[cells_at:kept_start, :], cleared_ref[...])
    turn(
        ready_ref.at[:cells_at, :],
        full_dot(stay_ref[own_at : own_at + cells, :cells], cleared_ref[...]),
    )
    ready_ref[kept_start:end, :] = stay_ref[...]


def fill_kernel(slices, shape, ready_ref, below_ref, above_ref, *refs):
    *blocks, done_ref, filled_ref, edge_ref = refs
    var_count, rows, pencils = shape
    cells = var_count * rows
    count = pencils // LANES
    _, own_at, about_at, _ = stay_at(rows, count, cells)
    cells_at, kept_start, _ = ready_at(rows, count, cells)

    ghosts = LANES
    about = [ready_ref[kept_start + about_at : kept_start + about_at + ABOUT, :]]
    edge = var_count * count
    about += [ref[edge : edge + ABOUT, :] for ref in (below_ref, above_ref)]

    def known(k):
        return jnp.concatenate([x[k : k + 1] for x in about], axis=1)

    values = ghost_values(slices, blocks, known(COLUMN))
    row, pencil = place_of(known(CELL).astype(jnp.int32), rows, pencils)
    at_row = lax.broadcasted_iota(jnp.int32, (rows, ghosts), 0) == row[:, :ghosts]
    spread = jnp.concatenate([jnp.where(at_row, value[:, :ghosts], 0.0) for value in values], axis=0)
    own = ready_ref[kept_start + own_at : kept_start + own_at + cells, :cells]
    both = jnp.concatenate([full_dot(own, spread), spread], axis=0)
    spots = marks((pencils, ghosts), 0, pencil[:, :ghosts])
    added = exact_dot(both, spots, ((1,), (1,)))
    for t in range(count):
        here = slice(t * cells, (t + 1) * cells)
        there = slice(cells_at + t * cells, cells_at + (t + 1) * cells)
        done_ref[here, :] = ready_ref[here, :] + added[:cells, tile(t)]
        filled_ref[here, :] = ready_ref[there, :] + added[cells:, tile(t)]
    x_at, response_at, profile_at, edge_at, _ = done_at(rows, count, cells, var_count)
    none = jnp.zeros((8 - var_count, ghosts), jnp.float32)
    for k, (ref, wanted) in enumerate(((below_ref, rows - 1), (above_ref, 0))):
        here = slice((k + 1) * ghosts, (k + 2) * ghosts)
        at_edge = row[:, here] == wanted
        spread = [jnp.where(at_edge, value[:, here], 0.0) for value in values] + [none]
        spots = marks((pencils, ghosts), 0, pencil[:, here])
        turn(edge_ref, exact_dot(jnp.concatenate(spread, axis=0), spots, ((1,), (1,))))
        for v in range(var_count):
            start = edge_at + (k * var_count + v) * count
            done_ref[start : start + count, :] = ref[v * count : (v + 1) * count, :] + slab_at(
                edge_ref, v, 8, count
            )

    def kept(which, i):
        start = kept_start + kept_at(which, i, rows, count)
        return ready_ref[start : start + count, :]

    def profile(k):
        start = kept_start + own_at - 40 + k
        return ready_ref[start : start + 1, :]

    def put(at, i, height, value):
        done_ref[pl.ds(at + i, count, stride=height), :] = value

    swept = []
    for i in range(1, rows - 1):
        speed = kept(3, i)
        here = [-speed * profile(i), -speed * profile(rows + i)]
        for v in range(var_count):
            row = v * rows + i
            own_slab = slab_at(done_ref, row, cells, count)
            here.append(slab_at(filled_ref, row, cells, count) - speed * own_slab)
        if swept:
            ratio = kept(0, i - 1)
            here = [x + ratio * y for x, y in zip(here, swept[-1])]
        swept.append(here)
    zero = jnp.zeros((count, LANES), jnp.float32)
    one = jnp.ones((count, LANES), jnp.float32)
    x = [zero] * (2 + var_count)
    first, last = zero, one
    for i in range(rows - 1, -1, -1):
        if 0 < i < rows - 1:
            ratio, inverse = kept(0, i), kept(2, i)
            first, last = kept(1, i) + ratio * first, ratio * last
            x = [inverse * y + ratio * z for y, z in zip(swept[i - 1], x)]
        if i == 0:
            first, last, x = one, zero, [zero] * (2 + var_count)
        for k, value in enumerate([first, last] + x[:2]):
            put(response_at + k * rows * count, i, rows, value)
        for v in range(var_count):
            put(x_at, v * rows + i, cells, x[2 + v])
    done_ref[profile_at : profile_at + 40, :] = ready_ref[
        kept_start + own_at - 40 : kept_start + own_at, :
    ]


def finish_kernel(
    slices, back_ref, done_ref, derivative_hbm, segment_hbm, derivative_ref, segment_ref, tail_ref, sems
):
    var_count, rows, pencils = segment_ref.shape
    count = pencils // LANES
    cells = var_count * rows
    x_at, response_at, profile_at, edge_at, _ = done_at(rows, count, cells, var_count)
    back_height, groups, per = slices.back_height, slices.back_groups, slices.per
    block = lane_block(max(groups, 1), slices.width)
    for m in range(slices.rest):
        packed = []
        for i in range(per):
            start = (m * per + i) * back_height + slices.back_packed_at
            packed.append(back_ref[start : start + groups, :])
        for k in range(per):
            for i in range(per):
                moved = moved_lanes(packed[i], (i - k) * slices.width)
                joined = moved if i == 0 else jnp.where(block == i, moved, joined)
            tail_ref[pl.ds(m * groups * per + k, groups, stride=per), :] = joined

    def got(functional, v, t):
        step, j = t // slices.slabs, t % slices.slabs
        if step < slices.full:
            start = j * back_height + slices.row(functional, step) + v
            return back_ref[start : start + 1, :]
        start = j * groups * per + functional * var_count + v
        return tail_ref[start : start + 1, :]

    lo_profile = done_ref[profile_at : profile_at + rows, :]
    hi_profile = done_ref[profile_at + rows : profile_at + 2 * rows, :]
    row_at = lax.broadcasted_iota(jnp.int32, (rows, LANES), 0)
    edges = profile_at + 2 * rows
    lo_edge = jnp.where(row_at == 0, done_ref[edges : edges + 1, :], 0.0)
    hi_edge = jnp.where(row_at == rows - 1, done_ref[edges + 1 : edges + 2, :], 0.0)

    def edge(k, v, t):
        start = edge_at + (k * var_count + v) * count + t
        return done_ref[start : start + 1, :]

    def response(k, t):
        start = response_at + (k * count + t) * rows
        return done_ref[start : start + rows, :]

    copies = []
    for v in range(var_count):
        for t in range(count):
            start = t * cells + v * rows
            lo, hi = got(2, v, t), got(3, v, t)
            derivative_ref[v, :, tile(t)] = (
                done_ref[start : start + rows, :]
                + (lo_profile * lo + hi_profile * hi)
                + (lo_edge * edge(0, v, t) + hi_edge * edge(1, v, t))
            )
            segment_ref[v, :, tile(t)] = (
                done_ref[x_at + start : x_at + start + rows, :]
                + (response(0, t) * got(0, v, t) + response(1, t) * got(1, v, t))
                + (response(2, t) * lo + response(3, t) * hi)
            )
        for which, (ref, hbm) in enumerate(
            ((derivative_ref, derivative_hbm), (segment_ref, segment_hbm))
        ):
            copies.append(
                pltpu.make_async_copy(ref.at[v], hbm.at[v], sems.at[which * var_count + v])
            )
            copies[-1].start()
    for copy in copies:
        copy.wait()


def call(kernel, outs, scratch, sems, args, near=(), far_out=(), limit=62):
    whole = pl.BlockSpec(memory_space=pltpu.VMEM)
    far = pl.BlockSpec(memory_space=pltpu.HBM)
    buffers = [
        pltpu.VMEM(s.shape, s.dtype) if hasattr(s, "dtype") else pltpu.VMEM(s, jnp.float32)
        for s in scratch
    ]
    buffers += [pltpu.SemaphoreType.DMA((size,)) for size in sems]
    return pl.pallas_call(
        kernel,
        out_shape=[jax.ShapeDtypeStruct(shape, jnp.float32) for shape in outs],
        in_specs=[whole if k in near else far for k in range(len(args))],
        out_specs=[far if k in far_out else whole for k in range(len(outs))],
        scratch_shapes=buffers,
        compiler_params=pltpu.CompilerParams(vmem_limit_bytes=limit * 2**20),
    )(*args)


def exchange(message, axes):
    return lax.all_to_all(message, axes, 0, 0, tiled=True)


def local(
    state,
    face_diffusion,
    courant,
    cell_mask,
    ghost_cell,
    ghost_owner,
    ghost_image,
    image_base,
    image_weight,
):
    var_count, rows, pencils = state.shape
    slabs, cross = lax.axis_size("pipe"), lax.axis_size("cross")
    count = pencils // LANES
    cells = var_count * rows
    images = image_base.shape[0]
    tables, at, constants = derivative_tables(slabs, rows, var_count)
    slices = Slices(slabs, count, cross, var_count, images)
    tables = jnp.asarray(tables)
    turned = (cells * count, LANES)
    stay = stay_at(rows, count, cells)[3]
    ready = (ready_at(rows, count, cells)[2], LANES)

    arguments = (
        face_diffusion,
        courant,
        tables,
        ghost_cell,
        ghost_owner,
        ghost_image,
        cell_mask,
        image_base,
        image_weight,
        state,
    )
    buffers = list(arguments)
    buffers[2] = jax.ShapeDtypeStruct(tables.shape[1:], jnp.float32)
    edge = (-(-(var_count * count + ABOUT) // 8) * 8, LANES)
    message, stay, up, down = call(
        functools.partial(prepare_kernel, slices, at),
        [(slabs * slices.height, LANES), (stay, LANES), edge, edge],
        buffers
        + [
            (stay, LANES),
            turned,
            (rows * count, LANES),
            (rows * count, LANES),
            (2 * rows * count, LANES),
            jax.ShapeDtypeStruct((pencils, images), jnp.bfloat16),
            (2 * rows, pencils),
            (40 * count, LANES),
            (2 * rows, -(-count // 8) * 8, LANES),
            (cells, pencils),
            (max(slices.rest, 1) * max(slices.groups, 1) * slices.per, LANES),
        ],
        [len(arguments), 1],
        arguments,
        far_out=(1,),
    )
    message = exchange(message, "pipe")
    forward = [(i, i + 1) for i in range(slabs - 1)]
    below = lax.ppermute(up, "pipe", forward)
    above = lax.ppermute(down, "pipe", [(j, i) for i, j in forward])
    (ready,) = call(
        own_kernel,
        [ready],
        [(cells, pencils)],
        [],
        (stay, cell_mask, state),
        near=range(3),
        limit=48,
    )
    (image_values,) = call(
        functools.partial(pick_kernel, slices),
        [(slabs * slices.image_rows, LANES)],
        [],
        [],
        (message,),
        near=(0,),
        limit=24,
    )
    blocks = [image_values] + [
        lax.ppermute(image_values, "cross", [(i, i ^ u) for i in range(cross)])
        for u in range(1, cross)
    ]

    factored, below, above = lax.optimization_barrier((message, below, above))
    rest, chain = call(
        functools.partial(chain_kernel, slices),
        [(slabs * max(slices.groups, 1) * slices.per, LANES), (2 * slabs * 16, LANES)],
        [],
        [],
        (factored,),
        near=(0,),
        limit=24,
    )
    (back,) = call(
        functools.partial(solve_kernel, slices, pencils, constants),
        [(slabs * slices.back_height, LANES)],
        [
            (slabs * slices.chunk * 48, LANES),
            (slabs * max(slices.back_groups, 1) * slices.per, LANES),
        ],
        [],
        (message, rest, chain, *blocks),
        near=range(3 + cross),
        limit=24,
    )
    back = exchange(back, "pipe")
    (done,) = call(
        functools.partial(fill_kernel, slices, state.shape),
        [(done_at(rows, count, cells, var_count)[4], LANES)],
        [turned, (8 * count, LANES)],
        [],
        (ready, below, above, *blocks),
        near=range(3 + cross),
        limit=48,
    )
    return tuple(
        call(
            functools.partial(finish_kernel, slices),
            [state.shape, state.shape],
            [
                state.shape,
                state.shape,
                (max(slices.rest, 1) * max(slices.back_groups, 1) * slices.per, LANES),
            ],
            [2 * var_count],
            (back, done),
            near=range(2),
            far_out=(0, 1),
            limit=48,
        )
    )


def solution(mesh):
    in_specs = (
        P(None, "pipe", "cross"),
        P("pipe", "cross"),
        P("pipe", "cross"),
        P("pipe", "cross"),
        P(("pipe", "cross")),
        P(("pipe", "cross")),
        P(("pipe", "cross")),
        P(("pipe", "cross")),
        P(None, ("pipe", "cross")),
    )
    out_specs = (P(None, "pipe", "cross"), P(None, "pipe", "cross"))
    return jax.shard_map(local, mesh=mesh, in_specs=in_specs, out_specs=out_specs, check_vma=False)
```

```python
import functools

import numpy as np
import jax
import jax.numpy as jnp
from jax import lax
from jax.experimental import pallas as pl
from jax.experimental.pallas import tpu as pltpu
from jax.sharding import PartitionSpec as P

LINE = 96
LANES = 128
REFLECT = (1.0, -1.0, -1.0, -1.0, 1.0)

Z_UP, Z_DOWN, ROW_FIRST, ROW_LAST, RIGHT_FIRST, RIGHT_LAST = range(6)
LINK_IN, MARGIN_FIRST, MARGIN_LAST, LINK_UP, FIRST_LO, FIRST_HI, LAST_LO, LAST_HI, FIRST_EDGE, LAST_EDGE = range(10)
COEFFICIENTS = 10
CELL, COLUMN, WEIGHT_FIRST, WEIGHT_LAST = range(4)
ABOUT = 4


def derivative_tables(slabs, rows, var_count):
    total = slabs * rows
    A = np.eye(total)
    B = np.zeros((total, total))
    for i in range(2, total - 2):
        A[i, i - 1] = A[i, i + 1] = 1.0 / 3.0
        B[i, i + 1], B[i, i - 1] = 7.0 / 9.0, -7.0 / 9.0
        B[i, i + 2], B[i, i - 2] = 1.0 / 36.0, -1.0 / 36.0
    for i in (1, total - 2):
        A[i, i - 1] = A[i, i + 1] = 0.25
        B[i, i + 1], B[i, i - 1] = 0.75, -0.75
    B[0, :3] = (-1.5, 2.0, -0.5)
    B[-1, -3:] = (0.5, -2.0, 1.5)
    inverse = np.linalg.inv(A)
    M = inverse @ B

    cells = var_count * rows
    own_at, reduce_at, adjoint_at, profile_at = 0, cells, cells + 32, cells + 72
    tables = np.zeros((slabs, cells + 112, LANES))
    carry_up, carry_down = np.zeros(slabs), np.zeros(slabs)
    ups, downs = np.zeros((slabs, rows)), np.zeros((slabs, rows))
    for p in range(slabs):
        table = tables[p]
        base = p * rows
        here = slice(base, base + rows)
        own = M[here, here]
        lo, hi, lo_edge, hi_edge = (np.zeros(rows) for _ in range(4))
        weight_up, weight_down = np.zeros(rows), np.zeros(rows)
        if p > 0:
            lo = inverse[here, base - 8] / inverse[base + 1, base - 8]
            lo_edge[0] = M[base, base - 1] - lo[0] * M[base + 1, base - 1]
            weight_down = M[base - 2, here]
        if p > 1:
            k = base - rows - 8
            carry_up[p] = inverse[base + 1, k] / inverse[base - rows + 1, k]
        if p < slabs - 1:
            k = base + rows + 8
            hi = inverse[here, k] / inverse[base + rows - 2, k]
            hi_edge[-1] = M[base + rows - 1, base + rows] - hi[-1] * M[base + rows - 2, base + rows]
            weight_up = M[base + rows + 1, here]
        if p < slabs - 2:
            k = base + 2 * rows + 8
            carry_down[p] = inverse[base + rows - 2, k] / inverse[base + 2 * rows - 2, k]
        for v in range(var_count):
            at = slice(v * rows, (v + 1) * rows)
            table[own_at + v * rows : own_at + (v + 1) * rows, at] = own
        table[reduce_at : reduce_at + rows] = weight_up[:, None]
        table[reduce_at + rows : reduce_at + 2 * rows] = weight_down[:, None]
        table[adjoint_at : adjoint_at + rows, :rows] = own.T
        table[adjoint_at + rows : adjoint_at + 2 * rows, rows : 2 * rows] = own.T
        more = adjoint_at + 2 * rows
        table[more, :rows] = lo
        table[more + 1, :rows] = hi
        table[more + 2, rows : 2 * rows] = lo
        table[more + 3, rows : 2 * rows] = hi
        table[more + 4, 0] = lo_edge[0]
        table[more + 5, 2 * rows - 1] = hi_edge[-1]
        table[profile_at : profile_at + rows] = lo[:, None]
        table[profile_at + rows : profile_at + 2 * rows] = hi[:, None]
        table[profile_at + 2 * rows] = lo_edge[0]
        table[profile_at + 2 * rows + 1] = hi_edge[-1]
        ups[p], downs[p] = weight_up, weight_down
    at = (own_at, reduce_at, adjoint_at, profile_at)
    return tables.astype(np.float32), at, (carry_up, carry_down, ups, downs)


def split(x, parts):
    pieces = []
    for _ in range(parts):
        piece = x.astype(jnp.bfloat16)
        pieces.append(piece)
        x = x - piece.astype(jnp.float32)
    return pieces


def exact_dot(x, one_hot, contract):
    found = lax.dot_general(
        jnp.concatenate(split(x, 3), axis=0),
        one_hot,
        (contract, ((), ())),
        preferred_element_type=jnp.float32,
    )
    size = x.shape[0]
    return found[:size] + (found[size : 2 * size] + found[2 * size :])


def full_dot(a, b):
    return jnp.dot(a, b, precision=lax.Precision.HIGHEST, preferred_element_type=jnp.float32)


def marks(shape, axis, values):
    return jnp.where(lax.broadcasted_iota(jnp.int32, shape, axis) == values, 1.0, 0.0).astype(
        jnp.bfloat16
    )


def place_of(cell, rows, pencils):
    row = jnp.zeros_like(cell)
    for k in range(1, rows):
        row += (cell >= k * pencils).astype(jnp.int32)
    return row, cell - row * pencils


def tile(t):
    return slice(t * LANES, (t + 1) * LANES)


def turn(ref, x):
    height, pencils = x.shape
    for t in range(pencils // LANES):
        ref[t * height : (t + 1) * height, :] = x[:, tile(t)]


def slab_at(ref, row, height, count):
    return ref[pl.ds(row, count, stride=height), :]


def put_slab(ref, row, height, count, value):
    ref[pl.ds(row, count, stride=height), :] = value


def kept_at(which, i, rows, count):
    return (which * rows + i) * (-(-count // 8) * 8)


def stay_at(rows, count, cells):
    kept = kept_at(4, 0, rows, count) + 40
    return kept, kept, kept + cells, kept + cells + 8


def ready_at(rows, count, cells):
    kept = 2 * cells * count
    return cells * count, kept, kept + stay_at(rows, count, cells)[3]


def done_at(rows, count, cells, var_count):
    x = cells * count
    response = 2 * x
    profile = response + 4 * rows * count
    return x, response, profile, profile + 40, profile + 40 + 2 * var_count * count


def fetch(sources, targets, sems):
    copies = [
        pltpu.make_async_copy(source, target, sems.at[k])
        for k, (source, target) in enumerate(zip(sources, targets))
    ]
    for copy in copies:
        copy.start()
    return copies


def middle_first(slabs):
    return sorted(range(slabs), key=lambda p: (abs(2 * p - slabs + 1), p))


class Slices:
    def __init__(self, slabs, count, cross, var_count, images):
        rest = count % slabs
        order = middle_first(slabs)
        self.place = [order.index(p) for p in range(slabs)]
        self.slabs, self.count, self.cross, self.var_count = slabs, count, cross, var_count
        self.image_rows = var_count * images // LANES
        shared = rest > 0 and slabs % rest == 0 and LANES % (slabs // rest) == 0
        self.full = count // slabs if shared else -(-count // slabs)
        self.rest = rest if shared else 0
        self.per = slabs // rest if shared else 1
        self.width = LANES // self.per
        self.chunk = self.full + (1 if shared else 0)
        self.lines, self.back_lines = 6 * var_count + COEFFICIENTS, 4 * var_count
        self.groups, self.back_groups = (self.group_count(n) for n in (self.lines, self.back_lines))
        self.meta_at = self.lines * self.full
        self.packed_at = self.meta_at + ABOUT
        self.images_at = self.packed_at + self.groups
        self.height = -(-(self.images_at + self.image_rows) // 8) * 8
        self.back_packed_at = self.back_lines * self.full
        self.back_height = -(-(self.back_packed_at + self.back_groups) // 8) * 8

    def group_count(self, lines):
        return -(-lines // self.per) if self.rest else 0

    def row(self, functional, t):
        return (functional * self.full + t) * self.var_count

    def coefficient_row(self, which, t):
        return 6 * self.full * self.var_count + which * self.full + t

    def tiles_at(self, t):
        return t * self.slabs, min(self.count, (t + 1) * self.slabs)


def lane_block(rows, width):
    return lax.broadcasted_iota(jnp.int32, (rows, LANES), 1) // width


def moved_lanes(x, by):
    by %= LANES
    return x if by == 0 else pltpu.roll(x, by, 1)


def image_lines(x, row, pick_ref, weight_ref, rows, var_count):
    pencils, images = pick_ref.shape
    row_at = lax.broadcasted_iota(jnp.int32, (rows, images), 0)
    lower, upper = row_at == row, row_at == row + 1
    total = [jnp.zeros((rows, images), jnp.float32) for _ in range(var_count)]
    pieces = jnp.concatenate(split(x, 2), axis=0)
    for corner, shift in enumerate((0, 1, LINE, LINE + 1)):
        moved = pieces if shift == 0 else pltpu.roll(pieces, pencils - shift, 1)
        found = jnp.dot(moved, pick_ref[...], preferred_element_type=jnp.float32)
        found = found[: var_count * rows] + found[var_count * rows :]
        weight = jnp.where(lower, weight_ref[corner : corner + 1], 0.0) + jnp.where(
            upper, weight_ref[corner + 4 : corner + 5], 0.0
        )
        for v in range(var_count):
            total[v] += found[v * rows : (v + 1) * rows] * weight
    lines = []
    for v in range(var_count):
        value = jnp.sum(total[v], axis=0, keepdims=True)
        lines += [value[:, tile(t)] for t in range(images // LANES)]
    return jnp.concatenate(lines, axis=0)


def ghost_values(slices, blocks, column):
    per = slices.image_rows // slices.var_count
    slabs, cross = slices.slabs, slices.cross
    ghosts = column.shape[1]
    images = per * LANES
    owner = ((column + 0.5) * (1.0 / images)).astype(jnp.int32)
    image = column.astype(jnp.int32) - owner * images
    across = lax.axis_index("cross")
    values = [
        jnp.concatenate(
            [
                jnp.concatenate(
                    [
                        block[pl.ds(v * per + t, slabs, stride=slices.image_rows), :]
                        for t in range(per)
                    ],
                    axis=1,
                )
                for block in blocks
            ],
            axis=0,
        )
        for v in range(slices.var_count)
    ]
    pick = marks((per * LANES, ghosts), 0, image)
    found = exact_dot(jnp.concatenate(values, axis=0), pick, ((1,), (0,)))
    devices = slabs * cross
    at = lax.broadcasted_iota(jnp.int32, (devices, ghosts), 0)
    mine = (at % slabs) * cross + (across ^ (at // slabs)) == owner
    return [
        reflect
        * jnp.sum(
            jnp.where(mine, found[v * devices : (v + 1) * devices], 0.0), axis=0, keepdims=True
        )
        for v, reflect in enumerate(REFLECT)
    ]


def prepare_kernel(
    slices,
    at,
    face_hbm,
    courant_hbm,
    tables_hbm,
    cell_hbm,
    owner_hbm,
    image_hbm,
    mask_hbm,
    base_hbm,
    corner_hbm,
    state_hbm,
    message_ref,
    stay_hbm,
    up_ref,
    down_ref,
    face_ref,
    courant_ref,
    table_ref,
    cell_ref,
    owner_ref,
    image_ref,
    mask_ref,
    base_ref,
    corner_ref,
    state_ref,
    stay_ref,
    turned_ref,
    face_turned_ref,
    courant_turned_ref,
    pair_ref,
    pick_ref,
    matrix_ref,
    adjoint_ref,
    weight_ref,
    cleared_ref,
    rest_ref,
    sems,
    stay_sem,
):
    var_count, rows, pencils = state_ref.shape
    cells = var_count * rows
    count = pencils // LANES
    ghosts = cell_ref.shape[0]
    padded = -(-count // 8) * 8
    p = lax.axis_index("pipe")
    slabs, height = slices.slabs, slices.height
    lines = slices.groups * slices.per
    own_at, reduce_at, adjoint_at, profile_at = at
    copies = fetch(
        (
            face_hbm,
            courant_hbm,
            tables_hbm.at[p],
            cell_hbm,
            owner_hbm,
            image_hbm,
            base_hbm,
            corner_hbm,
            mask_hbm,
            state_hbm,
        ),
        (
            face_ref,
            courant_ref,
            table_ref,
            cell_ref,
            owner_ref,
            image_ref,
            base_ref,
            corner_ref,
            mask_ref,
            state_ref,
        ),
        sems,
    )
    kept, own, about_at, _ = stay_at(rows, count, cells)

    def send(line, rows_at, slab):
        for t, row_at in enumerate(rows_at):
            start, end = slices.tiles_at(t)
            message_ref[pl.ds(row_at, end - start, stride=height), :] = slab[start:end]
        for m in range(slices.rest):
            tail = slices.full * slabs + m
            rest_ref[m * lines + line : m * lines + line + 1, :] = slab[tail : tail + 1]

    def send_value(functional, v, slab):
        rows_at = [slices.row(functional, t) + v for t in range(slices.full)]
        send(functional * var_count + v, rows_at, slab)

    def send_coefficient(which, slab):
        rows_at = [slices.coefficient_row(which, t) for t in range(slices.full)]
        send(6 * var_count + which, rows_at, slab)

    for copy in copies[:8]:
        copy.wait()
    image_row, image_pencil = place_of(base_ref[...].reshape(1, -1), rows, pencils)
    pick_ref[...] = marks(pick_ref.shape, 0, image_pencil)
    turn(face_turned_ref, face_ref[...])

    def face(i):
        return slab_at(face_turned_ref, i, rows, count)

    link = face(0)
    margin = jnp.ones_like(link)
    first_margin = margin
    to_up, to_first = [None] * rows, [None] * rows
    for i in range(1, rows - 1):
        above = face(i)
        inverse = 1.0 / (link + margin + above)
        low, up = link * inverse, above * inverse
        to_up[i], to_first[i] = up, low
        for k, part in enumerate((up, low, inverse)):
            start = kept_at(k, i, rows, count)
            stay_ref[start : start + count, :] = part
        first_margin += low * margin
        link = link * up
        margin = 1.0 + margin * up
    send_coefficient(LINK_IN, link)
    send_coefficient(MARGIN_FIRST, first_margin)
    send_coefficient(MARGIN_LAST, margin)
    send_coefficient(LINK_UP, jnp.where(p == slabs - 1, 0.0, face(rows - 1)))

    zero, one = jnp.zeros_like(margin), jnp.ones_like(margin)
    first, last = [None] * rows, [None] * rows
    first[0], first[rows - 1], last[0], last[rows - 1] = one, zero, zero, one
    for i in range(rows - 2, 0, -1):
        first[i] = to_first[i] + to_up[i] * first[i + 1]
        last[i] = to_up[i] * last[i + 1]
    turn(courant_turned_ref, courant_ref[...])
    for i in range(rows):
        speed = slab_at(courant_turned_ref, i, rows, count)
        start = kept_at(3, i, rows, count)
        stay_ref[start : start + count, :] = speed
        put_slab(pair_ref, i, 2 * rows, count, first[i] * speed)
        put_slab(pair_ref, rows + i, 2 * rows, count, last[i] * speed)
    for t in range(count):
        matrix_ref[:, tile(t)] = pair_ref[t * 2 * rows : (t + 1) * 2 * rows, :]
    stay_ref[kept - 40 : kept, :] = table_ref[profile_at : profile_at + 40, :]
    stay_ref[own : own + cells, :] = table_ref[own_at : own_at + cells, :]
    turn(
        adjoint_ref, full_dot(table_ref[adjoint_at : adjoint_at + 40, : 2 * rows], matrix_ref[...])
    )
    for k in range(6):
        send_coefficient(FIRST_LO + k, slab_at(adjoint_ref, 2 * rows + k, 40, count))
    weight_ref[:, padded - 8 :, :] = jnp.zeros((2 * rows, 8, LANES), jnp.float32)
    for i, share in enumerate(first + last):
        weight_ref[i, :count, :] = share - slab_at(adjoint_ref, i, 40, count)

    row, pencil = place_of(cell_ref[...].reshape(1, ghosts), rows, pencils)
    lane_tile = jnp.right_shift(pencil, 7)
    lane_marks = marks((LANES, ghosts), 0, pencil - lane_tile * LANES)
    picked = exact_dot(
        weight_ref[...].reshape(2 * rows * padded, LANES), lane_marks, ((1,), (0,))
    ).reshape(2, rows, padded, ghosts)
    at_cell = (lax.broadcasted_iota(jnp.int32, (rows, padded, ghosts), 0) == row[None]) & (
        lax.broadcasted_iota(jnp.int32, (rows, padded, ghosts), 1) == lane_tile[None]
    )

    def at_ghosts(values):
        return jnp.sum(jnp.sum(jnp.where(at_cell, values, 0.0), axis=0), axis=0, keepdims=True)

    about = jnp.concatenate(
        [
            cell_ref[...].reshape(1, ghosts).astype(jnp.float32),
            (owner_ref[...] * base_ref.shape[0] + image_ref[...])
            .reshape(1, ghosts)
            .astype(jnp.float32),
            at_ghosts(picked[0]),
            at_ghosts(picked[1]),
        ],
        axis=0,
    )
    for j in range(slabs):
        start = j * height + slices.meta_at
        message_ref[start : start + ABOUT, :] = about
    stay_ref[about_at : about_at + ABOUT, :] = about
    edge = var_count * count
    for ref in (up_ref, down_ref):
        ref[edge : edge + ABOUT, :] = about
    staying = pltpu.make_async_copy(stay_ref, stay_hbm, stay_sem.at[0])
    staying.start()
    for copy in copies[8:]:
        copy.wait()
    values = image_lines(
        state_ref[...].reshape(cells, pencils),
        image_row,
        pick_ref,
        corner_ref,
        rows,
        var_count,
    )
    for j in range(slabs):
        start = j * height + slices.images_at
        message_ref[start : start + slices.image_rows, :] = values
    solid = mask_ref[...] == 1
    for v in range(var_count):
        here = slice(v * rows, (v + 1) * rows)
        cleared_ref[here, :] = jnp.where(solid, 0.0, state_ref[v])
    turn(turned_ref, cleared_ref[...])
    for group in (range(0, 3), range(3, var_count)):
        sums = {v: [zero] * 4 for v in group}
        for i in range(rows):
            up, down = reduce_at + i, reduce_at + rows + i
            weights = (
                table_ref[up : up + 1, :],
                table_ref[down : down + 1, :],
                weight_ref[i, :count, :],
                weight_ref[rows + i, :count, :],
            )
            for v in group:
                cell = slab_at(turned_ref, v * rows + i, cells, count)
                if i == 0:
                    send_value(ROW_FIRST, v, cell)
                    down_ref[v * count : (v + 1) * count, :] = cell
                if i == rows - 1:
                    send_value(ROW_LAST, v, cell)
                    up_ref[v * count : (v + 1) * count, :] = cell
                sums[v] = [x + weight * cell for x, weight in zip(sums[v], weights)]
        for v in group:
            for functional, total in zip((Z_UP, Z_DOWN, RIGHT_FIRST, RIGHT_LAST), sums[v]):
                send_value(functional, v, total)

    block = lane_block(max(slices.groups, 1), slices.width)
    for m in range(slices.rest):
        lined = [
            rest_ref[pl.ds(m * lines + k, slices.groups, stride=slices.per), :]
            for k in range(slices.per)
        ]
        for i in range(slices.per):
            packed = lined[0]
            for k in range(slices.per):
                moved = moved_lanes(lined[k], (k - i) * slices.width)
                packed = moved if k == 0 else jnp.where(block == k, moved, packed)
            start = (m * slices.per + i) * height + slices.packed_at
            message_ref[start : start + slices.groups, :] = packed
    staying.wait()


def chain_kernel(slices, message_ref, rest_ref, chain_ref):
    slabs, chunk, full = slices.slabs, slices.chunk, slices.full
    height, per, width = slices.height, slices.per, slices.width
    if slices.rest:
        for p in range(slabs):
            start = slices.place[p] * height + slices.packed_at
            packed = message_ref[start : start + slices.groups, :]
            for k in range(per):
                rest_ref[pl.ds(p * slices.groups * per + k, slices.groups, stride=per), :] = (
                    moved_lanes(packed, -k * width)
                )
    else:
        rest_ref[...] = jnp.zeros_like(rest_ref)

    def sent(p, which):
        start = slices.place[p] * height + slices.coefficient_row(which, 0)
        slab = message_ref[start : start + full, :]
        if slices.rest:
            start = p * slices.groups * per + 6 * slices.var_count + which
            slab = jnp.concatenate([slab, rest_ref[start : start + 1, :]], axis=0)
        return slab

    nodes = 2 * slabs
    margin = sent(0, MARGIN_FIRST)
    for k in range(nodes):
        link = sent(k // 2, LINK_UP if k % 2 else LINK_IN)
        inverse = 1.0 / (margin + link)
        ratio = link * inverse
        chain_ref[16 * k : 16 * k + chunk, :] = ratio
        chain_ref[16 * k + 8 : 16 * k + 8 + chunk, :] = inverse
        if k < nodes - 1:
            following = sent((k + 1) // 2, MARGIN_FIRST if k % 2 else MARGIN_LAST)
            margin = following + margin * ratio


def solve_kernel(slices, pencils, constants, message_ref, rest_ref, chain_ref, *refs):
    *blocks, back_ref, ghost_ref, back_rest_ref = refs
    slabs, var_count, chunk, full = slices.slabs, slices.var_count, slices.chunk, slices.full
    height, per, width = slices.height, slices.per, slices.width
    along = lax.axis_index("pipe")
    me = sum(jnp.where(along == p, slices.place[p], 0) for p in range(slabs))

    def meta(p, k):
        start = slices.place[p] * height + slices.meta_at + k
        return message_ref[start : start + 1, :]

    def meta_all(k):
        return jnp.concatenate([meta(p, k) for p in range(slabs)], axis=1)

    carry_up, carry_down, ups, downs = constants
    values = ghost_values(slices, blocks, meta_all(COLUMN))
    rows = ups.shape[1]
    row_of, pencil_of = place_of(meta_all(CELL).astype(jnp.int32), rows, pencils)
    ghosts = LANES
    place = lax.broadcasted_iota(jnp.int32, (chunk * LANES, ghosts), 0)
    slot, lane = place // LANES, place % LANES
    pencil_at = jnp.where(
        slot < full,
        (me + slot * slabs) * LANES + lane,
        (full * slabs + me // per) * LANES + (me % per) * width + lane,
    )
    none = jnp.zeros((8 - var_count, ghosts), jnp.float32)
    for p in range(slabs):
        row = row_of[:, tile(p)]
        up = down = jnp.zeros((1, ghosts), jnp.float32)
        for i in range(rows):
            up = jnp.where(row == i, float(ups[p, i]), up)
            down = jnp.where(row == i, float(downs[p, i]), down)
        weights = (
            up,
            down,
            jnp.where(row == 0, 1.0, 0.0),
            jnp.where(row == rows - 1, 1.0, 0.0),
            meta(p, WEIGHT_FIRST),
            meta(p, WEIGHT_LAST),
        )
        here = jnp.concatenate([value[:, tile(p)] for value in values] + [none], axis=0)
        shares = jnp.concatenate([here * weight for weight in weights], axis=0)
        spots = jnp.where(pencil_at == pencil_of[:, tile(p)], 1.0, 0.0)
        share = exact_dot(shares, spots.astype(jnp.bfloat16), ((1,), (1,)))
        for t in range(chunk):
            start = (p * chunk + t) * 48
            ghost_ref[start : start + 48, :] = share[:, tile(t)]

    nodes = 2 * slabs
    zero = jnp.zeros((var_count, LANES), jnp.float32)
    for t in range(chunk):

        def value(p, functional):
            if t < full:
                start = slices.place[p] * height + slices.row(functional, t)
                sent = message_ref[start : start + var_count, :]
            else:
                start = p * slices.groups * per + functional * var_count
                sent = rest_ref[start : start + var_count, :]
            start = (p * chunk + t) * 48 + functional * 8
            return sent + ghost_ref[start : start + var_count, :]

        def coefficient(p, which):
            if t < full:
                start = slices.place[p] * height + slices.coefficient_row(which, t)
                return message_ref[start : start + 1, :]
            start = p * slices.groups * per + 6 * var_count + which
            return rest_ref[start : start + 1, :]

        def give(p, functional, block):
            if t < full:
                start = slices.place[p] * slices.back_height + slices.row(functional, t)
                back_ref[start : start + var_count, :] = block
            else:
                start = p * slices.back_groups * per + functional * var_count
                back_rest_ref[start : start + var_count, :] = block

        def ratio(k):
            return chain_ref[16 * k + t : 16 * k + t + 1, :]

        def scale(k):
            return chain_ref[16 * k + 8 + t : 16 * k + 9 + t, :]

        lo, hi, below, above = ([zero] * slabs for _ in range(4))
        for p in range(1, slabs):
            lo[p] = value(p - 1, Z_UP) + float(carry_up[p]) * lo[p - 1]
            below[p] = value(p - 1, ROW_LAST)
        for p in range(slabs - 2, -1, -1):
            hi[p] = value(p + 1, Z_DOWN) + float(carry_down[p]) * hi[p + 1]
            above[p] = value(p + 1, ROW_FIRST)
        right = []
        for p in range(slabs):
            right.append(
                value(p, RIGHT_FIRST)
                - coefficient(p, FIRST_LO) * lo[p]
                - coefficient(p, FIRST_HI) * hi[p]
                - coefficient(p, FIRST_EDGE) * below[p]
            )
            right.append(
                value(p, RIGHT_LAST)
                - coefficient(p, LAST_LO) * lo[p]
                - coefficient(p, LAST_HI) * hi[p]
                - coefficient(p, LAST_EDGE) * above[p]
            )
            give(p, 2, lo[p])
            give(p, 3, hi[p])
        for k in range(1, nodes):
            right[k] = right[k] + ratio(k - 1) * right[k - 1]
        x = right[nodes - 1] * scale(nodes - 1)
        give(slabs - 1, 1, x)
        for k in range(nodes - 2, -1, -1):
            x = right[k] * scale(k) + ratio(k) * x
            give(k // 2, k % 2, x)
    if slices.rest:
        groups = slices.back_groups
        block = lane_block(groups, width)
        for p in range(slabs):
            for k in range(per):
                lined = back_rest_ref[pl.ds(p * groups * per + k, groups, stride=per), :]
                moved = moved_lanes(lined, k * width)
                packed = moved if k == 0 else jnp.where(block == k, moved, packed)
            start = slices.place[p] * slices.back_height + slices.back_packed_at
            back_ref[start : start + groups, :] = packed


def pick_kernel(slices, message_ref, values_ref):
    size = slices.image_rows
    for p in range(slices.slabs):
        start = slices.place[p] * slices.height + slices.images_at
        values_ref[p * size : (p + 1) * size, :] = message_ref[start : start + size, :]


def own_kernel(stay_ref, mask_ref, state_ref, ready_ref, cleared_ref):
    var_count, rows, pencils = state_ref.shape
    cells = var_count * rows
    count = pencils // LANES
    own_at = stay_at(rows, count, cells)[1]
    cells_at, kept_start, end = ready_at(rows, count, cells)
    solid = mask_ref[...] == 1
    for v in range(var_count):
        cleared_ref[v * rows : (v + 1) * rows, :] = jnp.where(solid, 0.0, state_ref[v])
    turn(ready_ref.at[cells_at:kept_start, :], cleared_ref[...])
    turn(
        ready_ref.at[:cells_at, :],
        full_dot(stay_ref[own_at : own_at + cells, :cells], cleared_ref[...]),
    )
    ready_ref[kept_start:end, :] = stay_ref[...]


def fill_kernel(slices, shape, ready_ref, below_ref, above_ref, *refs):
    *blocks, done_ref, filled_ref, edge_ref = refs
    var_count, rows, pencils = shape
    cells = var_count * rows
    count = pencils // LANES
    _, own_at, about_at, _ = stay_at(rows, count, cells)
    cells_at, kept_start, _ = ready_at(rows, count, cells)

    ghosts = LANES
    about = [ready_ref[kept_start + about_at : kept_start + about_at + ABOUT, :]]
    edge = var_count * count
    about += [ref[edge : edge + ABOUT, :] for ref in (below_ref, above_ref)]

    def known(k):
        return jnp.concatenate([x[k : k + 1] for x in about], axis=1)

    values = ghost_values(slices, blocks, known(COLUMN))
    row, pencil = place_of(known(CELL).astype(jnp.int32), rows, pencils)
    at_row = lax.broadcasted_iota(jnp.int32, (rows, ghosts), 0) == row[:, :ghosts]
    spread = jnp.concatenate([jnp.where(at_row, value[:, :ghosts], 0.0) for value in values], axis=0)
    own = ready_ref[kept_start + own_at : kept_start + own_at + cells, :cells]
    both = jnp.concatenate([full_dot(own, spread), spread], axis=0)
    spots = marks((pencils, ghosts), 0, pencil[:, :ghosts])
    added = exact_dot(both, spots, ((1,), (1,)))
    for t in range(count):
        here = slice(t * cells, (t + 1) * cells)
        there = slice(cells_at + t * cells, cells_at + (t + 1) * cells)
        done_ref[here, :] = ready_ref[here, :] + added[:cells, tile(t)]
        filled_ref[here, :] = ready_ref[there, :] + added[cells:, tile(t)]
    x_at, response_at, profile_at, edge_at, _ = done_at(rows, count, cells, var_count)
    none = jnp.zeros((8 - var_count, ghosts), jnp.float32)
    for k, (ref, wanted) in enumerate(((below_ref, rows - 1), (above_ref, 0))):
        here = slice((k + 1) * ghosts, (k + 2) * ghosts)
        at_edge = row[:, here] == wanted
        spread = [jnp.where(at_edge, value[:, here], 0.0) for value in values] + [none]
        spots = marks((pencils, ghosts), 0, pencil[:, here])
        turn(edge_ref, exact_dot(jnp.concatenate(spread, axis=0), spots, ((1,), (1,))))
        for v in range(var_count):
            start = edge_at + (k * var_count + v) * count
            done_ref[start : start + count, :] = ref[v * count : (v + 1) * count, :] + slab_at(
                edge_ref, v, 8, count
            )

    def kept(which, i):
        start = kept_start + kept_at(which, i, rows, count)
        return ready_ref[start : start + count, :]

    def profile(k):
        start = kept_start + own_at - 40 + k
        return ready_ref[start : start + 1, :]

    def put(at, i, height, value):
        done_ref[pl.ds(at + i, count, stride=height), :] = value

    swept = []
    for i in range(1, rows - 1):
        speed = kept(3, i)
        here = [-speed * profile(i), -speed * profile(rows + i)]
        for v in range(var_count):
            row = v * rows + i
            own_slab = slab_at(done_ref, row, cells, count)
            here.append(slab_at(filled_ref, row, cells, count) - speed * own_slab)
        if swept:
            ratio = kept(0, i - 1)
            here = [x + ratio * y for x, y in zip(here, swept[-1])]
        swept.append(here)
    zero = jnp.zeros((count, LANES), jnp.float32)
    one = jnp.ones((count, LANES), jnp.float32)
    x = [zero] * (2 + var_count)
    first, last = zero, one
    for i in range(rows - 1, -1, -1):
        if 0 < i < rows - 1:
            ratio, inverse = kept(0, i), kept(2, i)
            first, last = kept(1, i) + ratio * first, ratio * last
            x = [inverse * y + ratio * z for y, z in zip(swept[i - 1], x)]
        if i == 0:
            first, last, x = one, zero, [zero] * (2 + var_count)
        for k, value in enumerate([first, last] + x[:2]):
            put(response_at + k * rows * count, i, rows, value)
        for v in range(var_count):
            put(x_at, v * rows + i, cells, x[2 + v])
    done_ref[profile_at : profile_at + 40, :] = ready_ref[
        kept_start + own_at - 40 : kept_start + own_at, :
    ]


def finish_kernel(
    slices, back_ref, done_ref, derivative_hbm, segment_hbm, derivative_ref, segment_ref, tail_ref, sems
):
    var_count, rows, pencils = segment_ref.shape
    count = pencils // LANES
    cells = var_count * rows
    x_at, response_at, profile_at, edge_at, _ = done_at(rows, count, cells, var_count)
    back_height, groups, per = slices.back_height, slices.back_groups, slices.per
    block = lane_block(max(groups, 1), slices.width)
    for m in range(slices.rest):
        packed = []
        for i in range(per):
            start = (m * per + i) * back_height + slices.back_packed_at
            packed.append(back_ref[start : start + groups, :])
        for k in range(per):
            for i in range(per):
                moved = moved_lanes(packed[i], (i - k) * slices.width)
                joined = moved if i == 0 else jnp.where(block == i, moved, joined)
            tail_ref[pl.ds(m * groups * per + k, groups, stride=per), :] = joined

    def got(functional, v, t):
        step, j = t // slices.slabs, t % slices.slabs
        if step < slices.full:
            start = j * back_height + slices.row(functional, step) + v
            return back_ref[start : start + 1, :]
        start = j * groups * per + functional * var_count + v
        return tail_ref[start : start + 1, :]

    lo_profile = done_ref[profile_at : profile_at + rows, :]
    hi_profile = done_ref[profile_at + rows : profile_at + 2 * rows, :]
    row_at = lax.broadcasted_iota(jnp.int32, (rows, LANES), 0)
    edges = profile_at + 2 * rows
    lo_edge = jnp.where(row_at == 0, done_ref[edges : edges + 1, :], 0.0)
    hi_edge = jnp.where(row_at == rows - 1, done_ref[edges + 1 : edges + 2, :], 0.0)

    def edge(k, v, t):
        start = edge_at + (k * var_count + v) * count + t
        return done_ref[start : start + 1, :]

    def response(k, t):
        start = response_at + (k * count + t) * rows
        return done_ref[start : start + rows, :]

    copies = []
    for v in range(var_count):
        for t in range(count):
            start = t * cells + v * rows
            lo, hi = got(2, v, t), got(3, v, t)
            derivative_ref[v, :, tile(t)] = (
                done_ref[start : start + rows, :]
                + (lo_profile * lo + hi_profile * hi)
                + (lo_edge * edge(0, v, t) + hi_edge * edge(1, v, t))
            )
            segment_ref[v, :, tile(t)] = (
                done_ref[x_at + start : x_at + start + rows, :]
                + (response(0, t) * got(0, v, t) + response(1, t) * got(1, v, t))
                + (response(2, t) * lo + response(3, t) * hi)
            )
        for which, (ref, hbm) in enumerate(
            ((derivative_ref, derivative_hbm), (segment_ref, segment_hbm))
        ):
            copies.append(
                pltpu.make_async_copy(ref.at[v], hbm.at[v], sems.at[which * var_count + v])
            )
            copies[-1].start()
    for copy in copies:
        copy.wait()


def call(kernel, outs, scratch, sems, args, near=(), far_out=(), limit=62):
    whole = pl.BlockSpec(memory_space=pltpu.VMEM)
    far = pl.BlockSpec(memory_space=pltpu.HBM)
    buffers = [
        pltpu.VMEM(s.shape, s.dtype) if hasattr(s, "dtype") else pltpu.VMEM(s, jnp.float32)
        for s in scratch
    ]
    buffers += [pltpu.SemaphoreType.DMA((size,)) for size in sems]
    return pl.pallas_call(
        kernel,
        out_shape=[jax.ShapeDtypeStruct(shape, jnp.float32) for shape in outs],
        in_specs=[whole if k in near else far for k in range(len(args))],
        out_specs=[far if k in far_out else whole for k in range(len(outs))],
        scratch_shapes=buffers,
        compiler_params=pltpu.CompilerParams(vmem_limit_bytes=limit * 2**20),
    )(*args)


def exchange(message, axis):
    groups = [middle_first(lax.axis_size(axis))]
    return lax.all_to_all(message, axis, 0, 0, axis_index_groups=groups, tiled=True)


def local(
    state,
    face_diffusion,
    courant,
    cell_mask,
    ghost_cell,
    ghost_owner,
    ghost_image,
    image_base,
    image_weight,
):
    var_count, rows, pencils = state.shape
    slabs, cross = lax.axis_size("pipe"), lax.axis_size("cross")
    count = pencils // LANES
    cells = var_count * rows
    images = image_base.shape[0]
    tables, at, constants = derivative_tables(slabs, rows, var_count)
    slices = Slices(slabs, count, cross, var_count, images)
    tables = jnp.asarray(tables)
    turned = (cells * count, LANES)
    stay = stay_at(rows, count, cells)[3]
    ready = (ready_at(rows, count, cells)[2], LANES)

    arguments = (
        face_diffusion,
        courant,
        tables,
        ghost_cell,
        ghost_owner,
        ghost_image,
        cell_mask,
        image_base,
        image_weight,
        state,
    )
    buffers = list(arguments)
    buffers[2] = jax.ShapeDtypeStruct(tables.shape[1:], jnp.float32)
    edge = (-(-(var_count * count + ABOUT) // 8) * 8, LANES)
    message, stay, up, down = call(
        functools.partial(prepare_kernel, slices, at),
        [(slabs * slices.height, LANES), (stay, LANES), edge, edge],
        buffers
        + [
            (stay, LANES),
            turned,
            (rows * count, LANES),
            (rows * count, LANES),
            (2 * rows * count, LANES),
            jax.ShapeDtypeStruct((pencils, images), jnp.bfloat16),
            (2 * rows, pencils),
            (40 * count, LANES),
            (2 * rows, -(-count // 8) * 8, LANES),
            (cells, pencils),
            (max(slices.rest, 1) * max(slices.groups, 1) * slices.per, LANES),
        ],
        [len(arguments), 1],
        arguments,
        far_out=(1,),
    )
    message = exchange(message, "pipe")
    forward = [(i, i + 1) for i in range(slabs - 1)]
    below = lax.ppermute(up, "pipe", forward)
    above = lax.ppermute(down, "pipe", [(j, i) for i, j in forward])
    (ready,) = call(
        own_kernel,
        [ready],
        [(cells, pencils)],
        [],
        (stay, cell_mask, state),
        near=range(3),
        limit=48,
    )
    (image_values,) = call(
        functools.partial(pick_kernel, slices),
        [(slabs * slices.image_rows, LANES)],
        [],
        [],
        (message,),
        near=(0,),
        limit=24,
    )
    blocks = [image_values] + [
        lax.ppermute(image_values, "cross", [(i, i ^ u) for i in range(cross)])
        for u in range(1, cross)
    ]

    factored, below, above = lax.optimization_barrier((message, below, above))
    rest, chain = call(
        functools.partial(chain_kernel, slices),
        [(slabs * max(slices.groups, 1) * slices.per, LANES), (2 * slabs * 16, LANES)],
        [],
        [],
        (factored,),
        near=(0,),
        limit=24,
    )
    (back,) = call(
        functools.partial(solve_kernel, slices, pencils, constants),
        [(slabs * slices.back_height, LANES)],
        [
            (slabs * slices.chunk * 48, LANES),
            (slabs * max(slices.back_groups, 1) * slices.per, LANES),
        ],
        [],
        (message, rest, chain, *blocks),
        near=range(3 + cross),
        limit=24,
    )
    back = exchange(back, "pipe")
    (done,) = call(
        functools.partial(fill_kernel, slices, state.shape),
        [(done_at(rows, count, cells, var_count)[4], LANES)],
        [turned, (8 * count, LANES)],
        [],
        (ready, below, above, *blocks),
        near=range(3 + cross),
        limit=48,
    )
    return tuple(
        call(
            functools.partial(finish_kernel, slices),
            [state.shape, state.shape],
            [
                state.shape,
                state.shape,
                (max(slices.rest, 1) * max(slices.back_groups, 1) * slices.per, LANES),
            ],
            [2 * var_count],
            (back, done),
            near=range(2),
            far_out=(0, 1),
            limit=48,
        )
    )


def solution(mesh):
    in_specs = (
        P(None, "pipe", "cross"),
        P("pipe", "cross"),
        P("pipe", "cross"),
        P("pipe", "cross"),
        P(("pipe", "cross")),
        P(("pipe", "cross")),
        P(("pipe", "cross")),
        P(("pipe", "cross")),
        P(None, ("pipe", "cross")),
    )
    out_specs = (P(None, "pipe", "cross"), P(None, "pipe", "cross"))
    return jax.shard_map(local, mesh=mesh, in_specs=in_specs, out_specs=out_specs, check_vma=False)
```

```python
import functools

import numpy as np
import jax
import jax.numpy as jnp
from jax import lax
from jax.experimental import pallas as pl
from jax.experimental.pallas import tpu as pltpu
from jax.sharding import PartitionSpec as P

LINE = 96
LANES = 128
REFLECT = (1.0, -1.0, -1.0, -1.0, 1.0)

Z_UP, Z_DOWN, ROW_FIRST, ROW_LAST, RIGHT_FIRST, RIGHT_LAST = range(6)
LINK_IN, MARGIN_FIRST, MARGIN_LAST, LINK_UP, FIRST_LO, FIRST_HI, LAST_LO, LAST_HI, FIRST_EDGE, LAST_EDGE = range(10)
COEFFICIENTS = 10
CELL, COLUMN, WEIGHT_FIRST, WEIGHT_LAST = range(4)
ABOUT = 4


def derivative_tables(slabs, rows, var_count):
    total = slabs * rows
    A = np.eye(total)
    B = np.zeros((total, total))
    for i in range(2, total - 2):
        A[i, i - 1] = A[i, i + 1] = 1.0 / 3.0
        B[i, i + 1], B[i, i - 1] = 7.0 / 9.0, -7.0 / 9.0
        B[i, i + 2], B[i, i - 2] = 1.0 / 36.0, -1.0 / 36.0
    for i in (1, total - 2):
        A[i, i - 1] = A[i, i + 1] = 0.25
        B[i, i + 1], B[i, i - 1] = 0.75, -0.75
    B[0, :3] = (-1.5, 2.0, -0.5)
    B[-1, -3:] = (0.5, -2.0, 1.5)
    inverse = np.linalg.inv(A)
    M = inverse @ B

    cells = var_count * rows
    own_at, reduce_at, adjoint_at, profile_at = 0, cells, cells + 32, cells + 72
    tables = np.zeros((slabs, cells + 112, LANES))
    carry_up, carry_down = np.zeros(slabs), np.zeros(slabs)
    ups, downs = np.zeros((slabs, rows)), np.zeros((slabs, rows))
    for p in range(slabs):
        table = tables[p]
        base = p * rows
        here = slice(base, base + rows)
        own = M[here, here]
        lo, hi, lo_edge, hi_edge = (np.zeros(rows) for _ in range(4))
        weight_up, weight_down = np.zeros(rows), np.zeros(rows)
        if p > 0:
            lo = inverse[here, base - 8] / inverse[base + 1, base - 8]
            lo_edge[0] = M[base, base - 1] - lo[0] * M[base + 1, base - 1]
            weight_down = M[base - 2, here]
        if p > 1:
            k = base - rows - 8
            carry_up[p] = inverse[base + 1, k] / inverse[base - rows + 1, k]
        if p < slabs - 1:
            k = base + rows + 8
            hi = inverse[here, k] / inverse[base + rows - 2, k]
            hi_edge[-1] = M[base + rows - 1, base + rows] - hi[-1] * M[base + rows - 2, base + rows]
            weight_up = M[base + rows + 1, here]
        if p < slabs - 2:
            k = base + 2 * rows + 8
            carry_down[p] = inverse[base + rows - 2, k] / inverse[base + 2 * rows - 2, k]
        for v in range(var_count):
            at = slice(v * rows, (v + 1) * rows)
            table[own_at + v * rows : own_at + (v + 1) * rows, at] = own
        table[reduce_at : reduce_at + rows] = weight_up[:, None]
        table[reduce_at + rows : reduce_at + 2 * rows] = weight_down[:, None]
        table[adjoint_at : adjoint_at + rows, :rows] = own.T
        table[adjoint_at + rows : adjoint_at + 2 * rows, rows : 2 * rows] = own.T
        more = adjoint_at + 2 * rows
        table[more, :rows] = lo
        table[more + 1, :rows] = hi
        table[more + 2, rows : 2 * rows] = lo
        table[more + 3, rows : 2 * rows] = hi
        table[more + 4, 0] = lo_edge[0]
        table[more + 5, 2 * rows - 1] = hi_edge[-1]
        table[profile_at : profile_at + rows] = lo[:, None]
        table[profile_at + rows : profile_at + 2 * rows] = hi[:, None]
        table[profile_at + 2 * rows] = lo_edge[0]
        table[profile_at + 2 * rows + 1] = hi_edge[-1]
        ups[p], downs[p] = weight_up, weight_down
    at = (own_at, reduce_at, adjoint_at, profile_at)
    return tables.astype(np.float32), at, (carry_up, carry_down, ups, downs)


def split(x, parts):
    pieces = []
    for _ in range(parts):
        piece = x.astype(jnp.bfloat16)
        pieces.append(piece)
        x = x - piece.astype(jnp.float32)
    return pieces


def exact_dot(x, one_hot, contract):
    found = lax.dot_general(
        jnp.concatenate(split(x, 3), axis=0),
        one_hot,
        (contract, ((), ())),
        preferred_element_type=jnp.float32,
    )
    size = x.shape[0]
    return found[:size] + (found[size : 2 * size] + found[2 * size :])


def full_dot(a, b):
    return jnp.dot(a, b, precision=lax.Precision.HIGHEST, preferred_element_type=jnp.float32)


def marks(shape, axis, values):
    return jnp.where(lax.broadcasted_iota(jnp.int32, shape, axis) == values, 1.0, 0.0).astype(
        jnp.bfloat16
    )


def place_of(cell, rows, pencils):
    row = jnp.zeros_like(cell)
    for k in range(1, rows):
        row += (cell >= k * pencils).astype(jnp.int32)
    return row, cell - row * pencils


def tile(t):
    return slice(t * LANES, (t + 1) * LANES)


def turn(ref, x):
    height, pencils = x.shape
    for t in range(pencils // LANES):
        ref[t * height : (t + 1) * height, :] = x[:, tile(t)]


def slab_at(ref, row, height, count):
    return ref[pl.ds(row, count, stride=height), :]


def put_slab(ref, row, height, count, value):
    ref[pl.ds(row, count, stride=height), :] = value


def kept_at(which, i, rows, count):
    return (which * rows + i) * (-(-count // 8) * 8)


def stay_at(rows, count, cells):
    kept = kept_at(4, 0, rows, count) + 40
    return kept, kept, kept + cells, kept + cells + 8


def ready_at(rows, count, cells):
    kept = 2 * cells * count
    return cells * count, kept, kept + stay_at(rows, count, cells)[3]


def done_at(rows, count, cells, var_count):
    x = cells * count
    response = 2 * x
    profile = response + 4 * rows * count
    return x, response, profile, profile + 40, profile + 40 + 2 * var_count * count


def fetch(sources, targets, sems):
    copies = [
        pltpu.make_async_copy(source, target, sems.at[k])
        for k, (source, target) in enumerate(zip(sources, targets))
    ]
    for copy in copies:
        copy.start()
    return copies


def exchange_order(slabs):
    near = sorted(range(slabs), key=lambda p: (abs(p - (slabs * 5) // 8), p))
    upper = [p for p in near if p >= slabs // 2]
    lower = [p for p in reversed(range(slabs // 2))]
    if slabs == 8:
        upper, lower = [5, 4, 6, 7], [2, 3, 1, 0]
    return [p for pair in zip(upper, lower) for p in pair]


class Slices:
    def __init__(self, slabs, count, cross, var_count, images):
        rest = count % slabs
        order = exchange_order(slabs)
        self.place = [order.index(p) for p in range(slabs)]
        self.slabs, self.count, self.cross, self.var_count = slabs, count, cross, var_count
        self.image_rows = var_count * images // LANES
        shared = rest > 0 and slabs % rest == 0 and LANES % (slabs // rest) == 0
        self.full = count // slabs if shared else -(-count // slabs)
        self.rest = rest if shared else 0
        self.per = slabs // rest if shared else 1
        self.width = LANES // self.per
        self.chunk = self.full + (1 if shared else 0)
        self.lines, self.back_lines = 6 * var_count + COEFFICIENTS, 4 * var_count
        self.groups, self.back_groups = (self.group_count(n) for n in (self.lines, self.back_lines))
        self.meta_at = self.lines * self.full
        self.packed_at = self.meta_at + ABOUT
        self.images_at = self.packed_at + self.groups
        self.height = -(-(self.images_at + self.image_rows) // 8) * 8
        self.back_packed_at = self.back_lines * self.full
        self.back_height = -(-(self.back_packed_at + self.back_groups) // 8) * 8

    def group_count(self, lines):
        return -(-lines // self.per) if self.rest else 0

    def row(self, functional, t):
        return (functional * self.full + t) * self.var_count

    def coefficient_row(self, which, t):
        return 6 * self.full * self.var_count + which * self.full + t

    def tiles_at(self, t):
        return t * self.slabs, min(self.count, (t + 1) * self.slabs)


def lane_block(rows, width):
    return lax.broadcasted_iota(jnp.int32, (rows, LANES), 1) // width


def moved_lanes(x, by):
    by %= LANES
    return x if by == 0 else pltpu.roll(x, by, 1)


def image_lines(x, row, pick_ref, weight_ref, rows, var_count):
    pencils, images = pick_ref.shape
    row_at = lax.broadcasted_iota(jnp.int32, (rows, images), 0)
    lower, upper = row_at == row, row_at == row + 1
    total = [jnp.zeros((rows, images), jnp.float32) for _ in range(var_count)]
    pieces = jnp.concatenate(split(x, 2), axis=0)
    for corner, shift in enumerate((0, 1, LINE, LINE + 1)):
        moved = pieces if shift == 0 else pltpu.roll(pieces, pencils - shift, 1)
        found = jnp.dot(moved, pick_ref[...], preferred_element_type=jnp.float32)
        found = found[: var_count * rows] + found[var_count * rows :]
        weight = jnp.where(lower, weight_ref[corner : corner + 1], 0.0) + jnp.where(
            upper, weight_ref[corner + 4 : corner + 5], 0.0
        )
        for v in range(var_count):
            total[v] += found[v * rows : (v + 1) * rows] * weight
    lines = []
    for v in range(var_count):
        value = jnp.sum(total[v], axis=0, keepdims=True)
        lines += [value[:, tile(t)] for t in range(images // LANES)]
    return jnp.concatenate(lines, axis=0)


def ghost_values(slices, blocks, column):
    per = slices.image_rows // slices.var_count
    slabs, cross = slices.slabs, slices.cross
    ghosts = column.shape[1]
    images = per * LANES
    owner = ((column + 0.5) * (1.0 / images)).astype(jnp.int32)
    image = column.astype(jnp.int32) - owner * images
    across = lax.axis_index("cross")
    values = [
        jnp.concatenate(
            [
                jnp.concatenate(
                    [
                        block[pl.ds(v * per + t, slabs, stride=slices.image_rows), :]
                        for t in range(per)
                    ],
                    axis=1,
                )
                for block in blocks
            ],
            axis=0,
        )
        for v in range(slices.var_count)
    ]
    pick = marks((per * LANES, ghosts), 0, image)
    found = exact_dot(jnp.concatenate(values, axis=0), pick, ((1,), (0,)))
    devices = slabs * cross
    at = lax.broadcasted_iota(jnp.int32, (devices, ghosts), 0)
    mine = (at % slabs) * cross + (across ^ (at // slabs)) == owner
    return [
        reflect
        * jnp.sum(
            jnp.where(mine, found[v * devices : (v + 1) * devices], 0.0), axis=0, keepdims=True
        )
        for v, reflect in enumerate(REFLECT)
    ]


def prepare_kernel(
    slices,
    at,
    face_hbm,
    courant_hbm,
    tables_hbm,
    cell_hbm,
    owner_hbm,
    image_hbm,
    mask_hbm,
    base_hbm,
    corner_hbm,
    state_hbm,
    message_ref,
    stay_hbm,
    up_ref,
    down_ref,
    face_ref,
    courant_ref,
    table_ref,
    cell_ref,
    owner_ref,
    image_ref,
    mask_ref,
    base_ref,
    corner_ref,
    state_ref,
    stay_ref,
    turned_ref,
    face_turned_ref,
    courant_turned_ref,
    pair_ref,
    pick_ref,
    matrix_ref,
    adjoint_ref,
    weight_ref,
    cleared_ref,
    rest_ref,
    sems,
    stay_sem,
):
    var_count, rows, pencils = state_ref.shape
    cells = var_count * rows
    count = pencils // LANES
    ghosts = cell_ref.shape[0]
    padded = -(-count // 8) * 8
    p = lax.axis_index("pipe")
    slabs, height = slices.slabs, slices.height
    lines = slices.groups * slices.per
    own_at, reduce_at, adjoint_at, profile_at = at
    copies = fetch(
        (
            face_hbm,
            courant_hbm,
            tables_hbm.at[p],
            cell_hbm,
            owner_hbm,
            image_hbm,
            base_hbm,
            corner_hbm,
            mask_hbm,
            state_hbm,
        ),
        (
            face_ref,
            courant_ref,
            table_ref,
            cell_ref,
            owner_ref,
            image_ref,
            base_ref,
            corner_ref,
            mask_ref,
            state_ref,
        ),
        sems,
    )
    kept, own, about_at, _ = stay_at(rows, count, cells)

    def send(line, rows_at, slab):
        for t, row_at in enumerate(rows_at):
            start, end = slices.tiles_at(t)
            message_ref[pl.ds(row_at, end - start, stride=height), :] = slab[start:end]
        for m in range(slices.rest):
            tail = slices.full * slabs + m
            rest_ref[m * lines + line : m * lines + line + 1, :] = slab[tail : tail + 1]

    def send_value(functional, v, slab):
        rows_at = [slices.row(functional, t) + v for t in range(slices.full)]
        send(functional * var_count + v, rows_at, slab)

    def send_coefficient(which, slab):
        rows_at = [slices.coefficient_row(which, t) for t in range(slices.full)]
        send(6 * var_count + which, rows_at, slab)

    for copy in copies[:8]:
        copy.wait()
    image_row, image_pencil = place_of(base_ref[...].reshape(1, -1), rows, pencils)
    pick_ref[...] = marks(pick_ref.shape, 0, image_pencil)
    turn(face_turned_ref, face_ref[...])

    def face(i):
        return slab_at(face_turned_ref, i, rows, count)

    link = face(0)
    margin = jnp.ones_like(link)
    first_margin = margin
    to_up, to_first = [None] * rows, [None] * rows
    for i in range(1, rows - 1):
        above = face(i)
        inverse = 1.0 / (link + margin + above)
        low, up = link * inverse, above * inverse
        to_up[i], to_first[i] = up, low
        for k, part in enumerate((up, low, inverse)):
            start = kept_at(k, i, rows, count)
            stay_ref[start : start + count, :] = part
        first_margin += low * margin
        link = link * up
        margin = 1.0 + margin * up
    send_coefficient(LINK_IN, link)
    send_coefficient(MARGIN_FIRST, first_margin)
    send_coefficient(MARGIN_LAST, margin)
    send_coefficient(LINK_UP, jnp.where(p == slabs - 1, 0.0, face(rows - 1)))

    zero, one = jnp.zeros_like(margin), jnp.ones_like(margin)
    first, last = [None] * rows, [None] * rows
    first[0], first[rows - 1], last[0], last[rows - 1] = one, zero, zero, one
    for i in range(rows - 2, 0, -1):
        first[i] = to_first[i] + to_up[i] * first[i + 1]
        last[i] = to_up[i] * last[i + 1]
    turn(courant_turned_ref, courant_ref[...])
    for i in range(rows):
        speed = slab_at(courant_turned_ref, i, rows, count)
        start = kept_at(3, i, rows, count)
        stay_ref[start : start + count, :] = speed
        put_slab(pair_ref, i, 2 * rows, count, first[i] * speed)
        put_slab(pair_ref, rows + i, 2 * rows, count, last[i] * speed)
    for t in range(count):
        matrix_ref[:, tile(t)] = pair_ref[t * 2 * rows : (t + 1) * 2 * rows, :]
    stay_ref[kept - 40 : kept, :] = table_ref[profile_at : profile_at + 40, :]
    stay_ref[own : own + cells, :] = table_ref[own_at : own_at + cells, :]
    turn(
        adjoint_ref, full_dot(table_ref[adjoint_at : adjoint_at + 40, : 2 * rows], matrix_ref[...])
    )
    for k in range(6):
        send_coefficient(FIRST_LO + k, slab_at(adjoint_ref, 2 * rows + k, 40, count))
    weight_ref[:, padded - 8 :, :] = jnp.zeros((2 * rows, 8, LANES), jnp.float32)
    for i, share in enumerate(first + last):
        weight_ref[i, :count, :] = share - slab_at(adjoint_ref, i, 40, count)

    row, pencil = place_of(cell_ref[...].reshape(1, ghosts), rows, pencils)
    lane_tile = jnp.right_shift(pencil, 7)
    lane_marks = marks((LANES, ghosts), 0, pencil - lane_tile * LANES)
    picked = exact_dot(
        weight_ref[...].reshape(2 * rows * padded, LANES), lane_marks, ((1,), (0,))
    ).reshape(2, rows, padded, ghosts)
    at_cell = (lax.broadcasted_iota(jnp.int32, (rows, padded, ghosts), 0) == row[None]) & (
        lax.broadcasted_iota(jnp.int32, (rows, padded, ghosts), 1) == lane_tile[None]
    )

    def at_ghosts(values):
        return jnp.sum(jnp.sum(jnp.where(at_cell, values, 0.0), axis=0), axis=0, keepdims=True)

    about = jnp.concatenate(
        [
            cell_ref[...].reshape(1, ghosts).astype(jnp.float32),
            (owner_ref[...] * base_ref.shape[0] + image_ref[...])
            .reshape(1, ghosts)
            .astype(jnp.float32),
            at_ghosts(picked[0]),
            at_ghosts(picked[1]),
        ],
        axis=0,
    )
    for j in range(slabs):
        start = j * height + slices.meta_at
        message_ref[start : start + ABOUT, :] = about
    stay_ref[about_at : about_at + ABOUT, :] = about
    edge = var_count * count
    for ref in (up_ref, down_ref):
        ref[edge : edge + ABOUT, :] = about
    staying = pltpu.make_async_copy(stay_ref, stay_hbm, stay_sem.at[0])
    staying.start()
    for copy in copies[8:]:
        copy.wait()
    values = image_lines(
        state_ref[...].reshape(cells, pencils),
        image_row,
        pick_ref,
        corner_ref,
        rows,
        var_count,
    )
    for j in range(slabs):
        start = j * height + slices.images_at
        message_ref[start : start + slices.image_rows, :] = values
    solid = mask_ref[...] == 1
    for v in range(var_count):
        here = slice(v * rows, (v + 1) * rows)
        cleared_ref[here, :] = jnp.where(solid, 0.0, state_ref[v])
    turn(turned_ref, cleared_ref[...])
    for group in (range(0, 3), range(3, var_count)):
        sums = {v: [zero] * 4 for v in group}
        for i in range(rows):
            up, down = reduce_at + i, reduce_at + rows + i
            weights = (
                table_ref[up : up + 1, :],
                table_ref[down : down + 1, :],
                weight_ref[i, :count, :],
                weight_ref[rows + i, :count, :],
            )
            for v in group:
                cell = slab_at(turned_ref, v * rows + i, cells, count)
                if i == 0:
                    send_value(ROW_FIRST, v, cell)
                    down_ref[v * count : (v + 1) * count, :] = cell
                if i == rows - 1:
                    send_value(ROW_LAST, v, cell)
                    up_ref[v * count : (v + 1) * count, :] = cell
                sums[v] = [x + weight * cell for x, weight in zip(sums[v], weights)]
        for v in group:
            for functional, total in zip((Z_UP, Z_DOWN, RIGHT_FIRST, RIGHT_LAST), sums[v]):
                send_value(functional, v, total)

    block = lane_block(max(slices.groups, 1), slices.width)
    for m in range(slices.rest):
        lined = [
            rest_ref[pl.ds(m * lines + k, slices.groups, stride=slices.per), :]
            for k in range(slices.per)
        ]
        for i in range(slices.per):
            packed = lined[0]
            for k in range(slices.per):
                moved = moved_lanes(lined[k], (k - i) * slices.width)
                packed = moved if k == 0 else jnp.where(block == k, moved, packed)
            start = (m * slices.per + i) * height + slices.packed_at
            message_ref[start : start + slices.groups, :] = packed
    staying.wait()


def chain_kernel(slices, message_ref, rest_ref, chain_ref):
    slabs, chunk, full = slices.slabs, slices.chunk, slices.full
    height, per, width = slices.height, slices.per, slices.width
    if slices.rest:
        for p in range(slabs):
            start = slices.place[p] * height + slices.packed_at
            packed = message_ref[start : start + slices.groups, :]
            for k in range(per):
                rest_ref[pl.ds(p * slices.groups * per + k, slices.groups, stride=per), :] = (
                    moved_lanes(packed, -k * width)
                )
    else:
        rest_ref[...] = jnp.zeros_like(rest_ref)

    def sent(p, which):
        start = slices.place[p] * height + slices.coefficient_row(which, 0)
        slab = message_ref[start : start + full, :]
        if slices.rest:
            start = p * slices.groups * per + 6 * slices.var_count + which
            slab = jnp.concatenate([slab, rest_ref[start : start + 1, :]], axis=0)
        return slab

    nodes = 2 * slabs
    margin = sent(0, MARGIN_FIRST)
    for k in range(nodes):
        link = sent(k // 2, LINK_UP if k % 2 else LINK_IN)
        inverse = 1.0 / (margin + link)
        ratio = link * inverse
        chain_ref[16 * k : 16 * k + chunk, :] = ratio
        chain_ref[16 * k + 8 : 16 * k + 8 + chunk, :] = inverse
        if k < nodes - 1:
            following = sent((k + 1) // 2, MARGIN_FIRST if k % 2 else MARGIN_LAST)
            margin = following + margin * ratio


def solve_kernel(slices, pencils, constants, message_ref, rest_ref, chain_ref, *refs):
    *blocks, back_ref, ghost_ref, back_rest_ref = refs
    slabs, var_count, chunk, full = slices.slabs, slices.var_count, slices.chunk, slices.full
    height, per, width = slices.height, slices.per, slices.width
    along = lax.axis_index("pipe")
    me = sum(jnp.where(along == p, slices.place[p], 0) for p in range(slabs))

    def meta(p, k):
        start = slices.place[p] * height + slices.meta_at + k
        return message_ref[start : start + 1, :]

    def meta_all(k):
        return jnp.concatenate([meta(p, k) for p in range(slabs)], axis=1)

    carry_up, carry_down, ups, downs = constants
    values = ghost_values(slices, blocks, meta_all(COLUMN))
    rows = ups.shape[1]
    row_of, pencil_of = place_of(meta_all(CELL).astype(jnp.int32), rows, pencils)
    ghosts = LANES
    place = lax.broadcasted_iota(jnp.int32, (chunk * LANES, ghosts), 0)
    slot, lane = place // LANES, place % LANES
    pencil_at = jnp.where(
        slot < full,
        (me + slot * slabs) * LANES + lane,
        (full * slabs + me // per) * LANES + (me % per) * width + lane,
    )
    none = jnp.zeros((8 - var_count, ghosts), jnp.float32)
    for p in range(slabs):
        row = row_of[:, tile(p)]
        up = down = jnp.zeros((1, ghosts), jnp.float32)
        for i in range(rows):
            up = jnp.where(row == i, float(ups[p, i]), up)
            down = jnp.where(row == i, float(downs[p, i]), down)
        weights = (
            up,
            down,
            jnp.where(row == 0, 1.0, 0.0),
            jnp.where(row == rows - 1, 1.0, 0.0),
            meta(p, WEIGHT_FIRST),
            meta(p, WEIGHT_LAST),
        )
        here = jnp.concatenate([value[:, tile(p)] for value in values] + [none], axis=0)
        shares = jnp.concatenate([here * weight for weight in weights], axis=0)
        spots = jnp.where(pencil_at == pencil_of[:, tile(p)], 1.0, 0.0)
        share = exact_dot(shares, spots.astype(jnp.bfloat16), ((1,), (1,)))
        for t in range(chunk):
            start = (p * chunk + t) * 48
            ghost_ref[start : start + 48, :] = share[:, tile(t)]

    nodes = 2 * slabs
    zero = jnp.zeros((var_count, LANES), jnp.float32)
    for t in range(chunk):

        def value(p, functional):
            if t < full:
                start = slices.place[p] * height + slices.row(functional, t)
                sent = message_ref[start : start + var_count, :]
            else:
                start = p * slices.groups * per + functional * var_count
                sent = rest_ref[start : start + var_count, :]
            start = (p * chunk + t) * 48 + functional * 8
            return sent + ghost_ref[start : start + var_count, :]

        def coefficient(p, which):
            if t < full:
                start = slices.place[p] * height + slices.coefficient_row(which, t)
                return message_ref[start : start + 1, :]
            start = p * slices.groups * per + 6 * var_count + which
            return rest_ref[start : start + 1, :]

        def give(p, functional, block):
            if t < full:
                start = slices.place[p] * slices.back_height + slices.row(functional, t)
                back_ref[start : start + var_count, :] = block
            else:
                start = p * slices.back_groups * per + functional * var_count
                back_rest_ref[start : start + var_count, :] = block

        def ratio(k):
            return chain_ref[16 * k + t : 16 * k + t + 1, :]

        def scale(k):
            return chain_ref[16 * k + 8 + t : 16 * k + 9 + t, :]

        lo, hi, below, above = ([zero] * slabs for _ in range(4))
        for p in range(1, slabs):
            lo[p] = value(p - 1, Z_UP) + float(carry_up[p]) * lo[p - 1]
            below[p] = value(p - 1, ROW_LAST)
        for p in range(slabs - 2, -1, -1):
            hi[p] = value(p + 1, Z_DOWN) + float(carry_down[p]) * hi[p + 1]
            above[p] = value(p + 1, ROW_FIRST)
        right = []
        for p in range(slabs):
            right.append(
                value(p, RIGHT_FIRST)
                - coefficient(p, FIRST_LO) * lo[p]
                - coefficient(p, FIRST_HI) * hi[p]
                - coefficient(p, FIRST_EDGE) * below[p]
            )
            right.append(
                value(p, RIGHT_LAST)
                - coefficient(p, LAST_LO) * lo[p]
                - coefficient(p, LAST_HI) * hi[p]
                - coefficient(p, LAST_EDGE) * above[p]
            )
            give(p, 2, lo[p])
            give(p, 3, hi[p])
        for k in range(1, nodes):
            right[k] = right[k] + ratio(k - 1) * right[k - 1]
        x = right[nodes - 1] * scale(nodes - 1)
        give(slabs - 1, 1, x)
        for k in range(nodes - 2, -1, -1):
            x = right[k] * scale(k) + ratio(k) * x
            give(k // 2, k % 2, x)
    if slices.rest:
        groups = slices.back_groups
        block = lane_block(groups, width)
        for p in range(slabs):
            for k in range(per):
                lined = back_rest_ref[pl.ds(p * groups * per + k, groups, stride=per), :]
                moved = moved_lanes(lined, k * width)
                packed = moved if k == 0 else jnp.where(block == k, moved, packed)
            start = slices.place[p] * slices.back_height + slices.back_packed_at
            back_ref[start : start + groups, :] = packed


def pick_kernel(slices, message_ref, values_ref):
    size = slices.image_rows
    for p in range(slices.slabs):
        start = slices.place[p] * slices.height + slices.images_at
        values_ref[p * size : (p + 1) * size, :] = message_ref[start : start + size, :]


def own_kernel(stay_ref, mask_ref, state_ref, ready_ref, cleared_ref):
    var_count, rows, pencils = state_ref.shape
    cells = var_count * rows
    count = pencils // LANES
    own_at = stay_at(rows, count, cells)[1]
    cells_at, kept_start, end = ready_at(rows, count, cells)
    solid = mask_ref[...] == 1
    for v in range(var_count):
        cleared_ref[v * rows : (v + 1) * rows, :] = jnp.where(solid, 0.0, state_ref[v])
    turn(ready_ref.at[cells_at:kept_start, :], cleared_ref[...])
    turn(
        ready_ref.at[:cells_at, :],
        full_dot(stay_ref[own_at : own_at + cells, :cells], cleared_ref[...]),
    )
    ready_ref[kept_start:end, :] = stay_ref[...]


def fill_kernel(slices, shape, ready_ref, below_ref, above_ref, *refs):
    *blocks, done_ref, filled_ref, edge_ref = refs
    var_count, rows, pencils = shape
    cells = var_count * rows
    count = pencils // LANES
    _, own_at, about_at, _ = stay_at(rows, count, cells)
    cells_at, kept_start, _ = ready_at(rows, count, cells)

    ghosts = LANES
    about = [ready_ref[kept_start + about_at : kept_start + about_at + ABOUT, :]]
    edge = var_count * count
    about += [ref[edge : edge + ABOUT, :] for ref in (below_ref, above_ref)]

    def known(k):
        return jnp.concatenate([x[k : k + 1] for x in about], axis=1)

    values = ghost_values(slices, blocks, known(COLUMN))
    row, pencil = place_of(known(CELL).astype(jnp.int32), rows, pencils)
    at_row = lax.broadcasted_iota(jnp.int32, (rows, ghosts), 0) == row[:, :ghosts]
    spread = jnp.concatenate([jnp.where(at_row, value[:, :ghosts], 0.0) for value in values], axis=0)
    own = ready_ref[kept_start + own_at : kept_start + own_at + cells, :cells]
    both = jnp.concatenate([full_dot(own, spread), spread], axis=0)
    spots = marks((pencils, ghosts), 0, pencil[:, :ghosts])
    added = exact_dot(both, spots, ((1,), (1,)))
    for t in range(count):
        here = slice(t * cells, (t + 1) * cells)
        there = slice(cells_at + t * cells, cells_at + (t + 1) * cells)
        done_ref[here, :] = ready_ref[here, :] + added[:cells, tile(t)]
        filled_ref[here, :] = ready_ref[there, :] + added[cells:, tile(t)]
    x_at, response_at, profile_at, edge_at, _ = done_at(rows, count, cells, var_count)
    none = jnp.zeros((8 - var_count, ghosts), jnp.float32)
    for k, (ref, wanted) in enumerate(((below_ref, rows - 1), (above_ref, 0))):
        here = slice((k + 1) * ghosts, (k + 2) * ghosts)
        at_edge = row[:, here] == wanted
        spread = [jnp.where(at_edge, value[:, here], 0.0) for value in values] + [none]
        spots = marks((pencils, ghosts), 0, pencil[:, here])
        turn(edge_ref, exact_dot(jnp.concatenate(spread, axis=0), spots, ((1,), (1,))))
        for v in range(var_count):
            start = edge_at + (k * var_count + v) * count
            done_ref[start : start + count, :] = ref[v * count : (v + 1) * count, :] + slab_at(
                edge_ref, v, 8, count
            )

    def kept(which, i):
        start = kept_start + kept_at(which, i, rows, count)
        return ready_ref[start : start + count, :]

    def profile(k):
        start = kept_start + own_at - 40 + k
        return ready_ref[start : start + 1, :]

    def put(at, i, height, value):
        done_ref[pl.ds(at + i, count, stride=height), :] = value

    swept = []
    for i in range(1, rows - 1):
        speed = kept(3, i)
        here = [-speed * profile(i), -speed * profile(rows + i)]
        for v in range(var_count):
            row = v * rows + i
            own_slab = slab_at(done_ref, row, cells, count)
            here.append(slab_at(filled_ref, row, cells, count) - speed * own_slab)
        if swept:
            ratio = kept(0, i - 1)
            here = [x + ratio * y for x, y in zip(here, swept[-1])]
        swept.append(here)
    zero = jnp.zeros((count, LANES), jnp.float32)
    one = jnp.ones((count, LANES), jnp.float32)
    x = [zero] * (2 + var_count)
    first, last = zero, one
    for i in range(rows - 1, -1, -1):
        if 0 < i < rows - 1:
            ratio, inverse = kept(0, i), kept(2, i)
            first, last = kept(1, i) + ratio * first, ratio * last
            x = [inverse * y + ratio * z for y, z in zip(swept[i - 1], x)]
        if i == 0:
            first, last, x = one, zero, [zero] * (2 + var_count)
        for k, value in enumerate([first, last] + x[:2]):
            put(response_at + k * rows * count, i, rows, value)
        for v in range(var_count):
            put(x_at, v * rows + i, cells, x[2 + v])
    done_ref[profile_at : profile_at + 40, :] = ready_ref[
        kept_start + own_at - 40 : kept_start + own_at, :
    ]


def finish_kernel(
    slices, back_ref, done_ref, derivative_hbm, segment_hbm, derivative_ref, segment_ref, tail_ref, sems
):
    var_count, rows, pencils = segment_ref.shape
    count = pencils // LANES
    cells = var_count * rows
    x_at, response_at, profile_at, edge_at, _ = done_at(rows, count, cells, var_count)
    back_height, groups, per = slices.back_height, slices.back_groups, slices.per
    block = lane_block(max(groups, 1), slices.width)
    for m in range(slices.rest):
        packed = []
        for i in range(per):
            start = (m * per + i) * back_height + slices.back_packed_at
            packed.append(back_ref[start : start + groups, :])
        for k in range(per):
            for i in range(per):
                moved = moved_lanes(packed[i], (i - k) * slices.width)
                joined = moved if i == 0 else jnp.where(block == i, moved, joined)
            tail_ref[pl.ds(m * groups * per + k, groups, stride=per), :] = joined

    def got(functional, v, t):
        step, j = t // slices.slabs, t % slices.slabs
        if step < slices.full:
            start = j * back_height + slices.row(functional, step) + v
            return back_ref[start : start + 1, :]
        start = j * groups * per + functional * var_count + v
        return tail_ref[start : start + 1, :]

    lo_profile = done_ref[profile_at : profile_at + rows, :]
    hi_profile = done_ref[profile_at + rows : profile_at + 2 * rows, :]
    row_at = lax.broadcasted_iota(jnp.int32, (rows, LANES), 0)
    edges = profile_at + 2 * rows
    lo_edge = jnp.where(row_at == 0, done_ref[edges : edges + 1, :], 0.0)
    hi_edge = jnp.where(row_at == rows - 1, done_ref[edges + 1 : edges + 2, :], 0.0)

    def edge(k, v, t):
        start = edge_at + (k * var_count + v) * count + t
        return done_ref[start : start + 1, :]

    def response(k, t):
        start = response_at + (k * count + t) * rows
        return done_ref[start : start + rows, :]

    copies = []
    for v in range(var_count):
        for t in range(count):
            start = t * cells + v * rows
            lo, hi = got(2, v, t), got(3, v, t)
            derivative_ref[v, :, tile(t)] = (
                done_ref[start : start + rows, :]
                + (lo_profile * lo + hi_profile * hi)
                + (lo_edge * edge(0, v, t) + hi_edge * edge(1, v, t))
            )
            segment_ref[v, :, tile(t)] = (
                done_ref[x_at + start : x_at + start + rows, :]
                + (response(0, t) * got(0, v, t) + response(1, t) * got(1, v, t))
                + (response(2, t) * lo + response(3, t) * hi)
            )
        for which, (ref, hbm) in enumerate(
            ((derivative_ref, derivative_hbm), (segment_ref, segment_hbm))
        ):
            copies.append(
                pltpu.make_async_copy(ref.at[v], hbm.at[v], sems.at[which * var_count + v])
            )
            copies[-1].start()
    for copy in copies:
        copy.wait()


def call(kernel, outs, scratch, sems, args, near=(), far_out=(), limit=62):
    whole = pl.BlockSpec(memory_space=pltpu.VMEM)
    far = pl.BlockSpec(memory_space=pltpu.HBM)
    buffers = [
        pltpu.VMEM(s.shape, s.dtype) if hasattr(s, "dtype") else pltpu.VMEM(s, jnp.float32)
        for s in scratch
    ]
    buffers += [pltpu.SemaphoreType.DMA((size,)) for size in sems]
    return pl.pallas_call(
        kernel,
        out_shape=[jax.ShapeDtypeStruct(shape, jnp.float32) for shape in outs],
        in_specs=[whole if k in near else far for k in range(len(args))],
        out_specs=[far if k in far_out else whole for k in range(len(outs))],
        scratch_shapes=buffers,
        compiler_params=pltpu.CompilerParams(vmem_limit_bytes=limit * 2**20),
    )(*args)


def exchange(message, axis):
    groups = [exchange_order(lax.axis_size(axis))]
    return lax.all_to_all(message, axis, 0, 0, axis_index_groups=groups, tiled=True)


def local(
    state,
    face_diffusion,
    courant,
    cell_mask,
    ghost_cell,
    ghost_owner,
    ghost_image,
    image_base,
    image_weight,
):
    var_count, rows, pencils = state.shape
    slabs, cross = lax.axis_size("pipe"), lax.axis_size("cross")
    count = pencils // LANES
    cells = var_count * rows
    images = image_base.shape[0]
    tables, at, constants = derivative_tables(slabs, rows, var_count)
    slices = Slices(slabs, count, cross, var_count, images)
    tables = jnp.asarray(tables)
    turned = (cells * count, LANES)
    stay = stay_at(rows, count, cells)[3]
    ready = (ready_at(rows, count, cells)[2], LANES)

    arguments = (
        face_diffusion,
        courant,
        tables,
        ghost_cell,
        ghost_owner,
        ghost_image,
        cell_mask,
        image_base,
        image_weight,
        state,
    )
    buffers = list(arguments)
    buffers[2] = jax.ShapeDtypeStruct(tables.shape[1:], jnp.float32)
    edge = (-(-(var_count * count + ABOUT) // 8) * 8, LANES)
    message, stay, up, down = call(
        functools.partial(prepare_kernel, slices, at),
        [(slabs * slices.height, LANES), (stay, LANES), edge, edge],
        buffers
        + [
            (stay, LANES),
            turned,
            (rows * count, LANES),
            (rows * count, LANES),
            (2 * rows * count, LANES),
            jax.ShapeDtypeStruct((pencils, images), jnp.bfloat16),
            (2 * rows, pencils),
            (40 * count, LANES),
            (2 * rows, -(-count // 8) * 8, LANES),
            (cells, pencils),
            (max(slices.rest, 1) * max(slices.groups, 1) * slices.per, LANES),
        ],
        [len(arguments), 1],
        arguments,
        far_out=(1,),
    )
    message = exchange(message, "pipe")
    forward = [(i, i + 1) for i in range(slabs - 1)]
    below = lax.ppermute(up, "pipe", forward)
    above = lax.ppermute(down, "pipe", [(j, i) for i, j in forward])
    (ready,) = call(
        own_kernel,
        [ready],
        [(cells, pencils)],
        [],
        (stay, cell_mask, state),
        near=range(3),
        limit=48,
    )
    (image_values,) = call(
        functools.partial(pick_kernel, slices),
        [(slabs * slices.image_rows, LANES)],
        [],
        [],
        (message,),
        near=(0,),
        limit=24,
    )
    blocks = [image_values] + [
        lax.ppermute(image_values, "cross", [(i, i ^ u) for i in range(cross)])
        for u in range(1, cross)
    ]

    factored, below, above = lax.optimization_barrier((message, below, above))
    rest, chain = call(
        functools.partial(chain_kernel, slices),
        [(slabs * max(slices.groups, 1) * slices.per, LANES), (2 * slabs * 16, LANES)],
        [],
        [],
        (factored,),
        near=(0,),
        limit=24,
    )
    (back,) = call(
        functools.partial(solve_kernel, slices, pencils, constants),
        [(slabs * slices.back_height, LANES)],
        [
            (slabs * slices.chunk * 48, LANES),
            (slabs * max(slices.back_groups, 1) * slices.per, LANES),
        ],
        [],
        (message, rest, chain, *blocks),
        near=range(3 + cross),
        limit=24,
    )
    back = exchange(back, "pipe")
    (done,) = call(
        functools.partial(fill_kernel, slices, state.shape),
        [(done_at(rows, count, cells, var_count)[4], LANES)],
        [turned, (8 * count, LANES)],
        [],
        (ready, below, above, *blocks),
        near=range(3 + cross),
        limit=48,
    )
    return tuple(
        call(
            functools.partial(finish_kernel, slices),
            [state.shape, state.shape],
            [
                state.shape,
                state.shape,
                (max(slices.rest, 1) * max(slices.back_groups, 1) * slices.per, LANES),
            ],
            [2 * var_count],
            (back, done),
            near=range(2),
            far_out=(0, 1),
            limit=48,
        )
    )


def solution(mesh):
    in_specs = (
        P(None, "pipe", "cross"),
        P("pipe", "cross"),
        P("pipe", "cross"),
        P("pipe", "cross"),
        P(("pipe", "cross")),
        P(("pipe", "cross")),
        P(("pipe", "cross")),
        P(("pipe", "cross")),
        P(None, ("pipe", "cross")),
    )
    out_specs = (P(None, "pipe", "cross"), P(None, "pipe", "cross"))
    return jax.shard_map(local, mesh=mesh, in_specs=in_specs, out_specs=out_specs, check_vma=False)
```

```python
import functools

import numpy as np
import jax
import jax.numpy as jnp
from jax import lax
from jax.experimental import pallas as pl
from jax.experimental.pallas import tpu as pltpu
from jax.sharding import PartitionSpec as P

LINE = 96
LANES = 128
REFLECT = (1.0, -1.0, -1.0, -1.0, 1.0)

Z_UP, Z_DOWN, ROW_FIRST, ROW_LAST, RIGHT_FIRST, RIGHT_LAST = range(6)
LINK_IN, MARGIN_FIRST, MARGIN_LAST, LINK_UP, FIRST_LO, FIRST_HI, LAST_LO, LAST_HI, FIRST_EDGE, LAST_EDGE = range(10)
COEFFICIENTS = 10
CELL, COLUMN, WEIGHT_FIRST, WEIGHT_LAST = range(4)
ABOUT = 4


def derivative_tables(slabs, rows, var_count):
    total = slabs * rows
    A = np.eye(total)
    B = np.zeros((total, total))
    for i in range(2, total - 2):
        A[i, i - 1] = A[i, i + 1] = 1.0 / 3.0
        B[i, i + 1], B[i, i - 1] = 7.0 / 9.0, -7.0 / 9.0
        B[i, i + 2], B[i, i - 2] = 1.0 / 36.0, -1.0 / 36.0
    for i in (1, total - 2):
        A[i, i - 1] = A[i, i + 1] = 0.25
        B[i, i + 1], B[i, i - 1] = 0.75, -0.75
    B[0, :3] = (-1.5, 2.0, -0.5)
    B[-1, -3:] = (0.5, -2.0, 1.5)
    inverse = np.linalg.inv(A)
    M = inverse @ B

    cells = var_count * rows
    own_at, reduce_at, adjoint_at, profile_at = 0, cells, cells + 32, cells + 72
    tables = np.zeros((slabs, cells + 112, LANES))
    carry_up, carry_down = np.zeros(slabs), np.zeros(slabs)
    ups, downs = np.zeros((slabs, rows)), np.zeros((slabs, rows))
    for p in range(slabs):
        table = tables[p]
        base = p * rows
        here = slice(base, base + rows)
        own = M[here, here]
        lo, hi, lo_edge, hi_edge = (np.zeros(rows) for _ in range(4))
        weight_up, weight_down = np.zeros(rows), np.zeros(rows)
        if p > 0:
            lo = inverse[here, base - 8] / inverse[base + 1, base - 8]
            lo_edge[0] = M[base, base - 1] - lo[0] * M[base + 1, base - 1]
            weight_down = M[base - 2, here]
        if p > 1:
            k = base - rows - 8
            carry_up[p] = inverse[base + 1, k] / inverse[base - rows + 1, k]
        if p < slabs - 1:
            k = base + rows + 8
            hi = inverse[here, k] / inverse[base + rows - 2, k]
            hi_edge[-1] = M[base + rows - 1, base + rows] - hi[-1] * M[base + rows - 2, base + rows]
            weight_up = M[base + rows + 1, here]
        if p < slabs - 2:
            k = base + 2 * rows + 8
            carry_down[p] = inverse[base + rows - 2, k] / inverse[base + 2 * rows - 2, k]
        for v in range(var_count):
            at = slice(v * rows, (v + 1) * rows)
            table[own_at + v * rows : own_at + (v + 1) * rows, at] = own
        table[reduce_at : reduce_at + rows] = weight_up[:, None]
        table[reduce_at + rows : reduce_at + 2 * rows] = weight_down[:, None]
        table[adjoint_at : adjoint_at + rows, :rows] = own.T
        table[adjoint_at + rows : adjoint_at + 2 * rows, rows : 2 * rows] = own.T
        more = adjoint_at + 2 * rows
        table[more, :rows] = lo
        table[more + 1, :rows] = hi
        table[more + 2, rows : 2 * rows] = lo
        table[more + 3, rows : 2 * rows] = hi
        table[more + 4, 0] = lo_edge[0]
        table[more + 5, 2 * rows - 1] = hi_edge[-1]
        table[profile_at : profile_at + rows] = lo[:, None]
        table[profile_at + rows : profile_at + 2 * rows] = hi[:, None]
        table[profile_at + 2 * rows] = lo_edge[0]
        table[profile_at + 2 * rows + 1] = hi_edge[-1]
        ups[p], downs[p] = weight_up, weight_down
    at = (own_at, reduce_at, adjoint_at, profile_at)
    return tables.astype(np.float32), at, (carry_up, carry_down, ups, downs)


def split(x, parts):
    pieces = []
    for _ in range(parts):
        piece = x.astype(jnp.bfloat16)
        pieces.append(piece)
        x = x - piece.astype(jnp.float32)
    return pieces


def exact_dot(x, one_hot, contract):
    found = lax.dot_general(
        jnp.concatenate(split(x, 3), axis=0),
        one_hot,
        (contract, ((), ())),
        preferred_element_type=jnp.float32,
    )
    size = x.shape[0]
    return found[:size] + (found[size : 2 * size] + found[2 * size :])


def full_dot(a, b):
    size = a.shape[0]
    stacked = jnp.concatenate(split(a, 3), axis=0)
    terms = []
    for k, part in enumerate(split(b, 3)):
        found = jnp.dot(stacked[: (3 - k) * size], part, preferred_element_type=jnp.float32)
        terms += [found[i * size : (i + 1) * size] for i in range(3 - k)]
    largest, ab, ac, ba, bb, ca = terms
    return largest + ((ab + ba) + (bb + (ac + ca)))


def marks(shape, axis, values):
    return jnp.where(lax.broadcasted_iota(jnp.int32, shape, axis) == values, 1.0, 0.0).astype(
        jnp.bfloat16
    )


def place_of(cell, rows, pencils):
    row = jnp.zeros_like(cell)
    for k in range(1, rows):
        row += (cell >= k * pencils).astype(jnp.int32)
    return row, cell - row * pencils


def tile(t):
    return slice(t * LANES, (t + 1) * LANES)


def turn(ref, x):
    height, pencils = x.shape
    for t in range(pencils // LANES):
        ref[t * height : (t + 1) * height, :] = x[:, tile(t)]


def slab_at(ref, row, height, count):
    return ref[pl.ds(row, count, stride=height), :]


def put_slab(ref, row, height, count, value):
    ref[pl.ds(row, count, stride=height), :] = value


def kept_at(which, i, rows, count):
    return (which * rows + i) * (-(-count // 8) * 8)


def stay_at(rows, count, cells):
    kept = kept_at(4, 0, rows, count) + 40
    return kept, kept, kept + cells, kept + cells + 8


def ready_at(rows, count, cells):
    kept = 2 * cells * count
    return cells * count, kept, kept + stay_at(rows, count, cells)[3]


def done_at(rows, count, cells, var_count):
    x = cells * count
    response = 2 * x
    profile = response + 4 * rows * count
    return x, response, profile, profile + 40, profile + 40 + 2 * var_count * count


def fetch(sources, targets, sems):
    copies = [
        pltpu.make_async_copy(source, target, sems.at[k])
        for k, (source, target) in enumerate(zip(sources, targets))
    ]
    for copy in copies:
        copy.start()
    return copies


def middle_first(slabs):
    return sorted(range(slabs), key=lambda p: (abs(2 * p - slabs + 1), p))


class Slices:
    def __init__(self, slabs, count, cross, var_count, images):
        rest = count % slabs
        order = middle_first(slabs)
        self.place = [order.index(p) for p in range(slabs)]
        self.slabs, self.count, self.cross, self.var_count = slabs, count, cross, var_count
        self.image_rows = var_count * images // LANES
        shared = rest > 0 and slabs % rest == 0 and LANES % (slabs // rest) == 0
        self.full = count // slabs if shared else -(-count // slabs)
        self.rest = rest if shared else 0
        self.per = slabs // rest if shared else 1
        self.width = LANES // self.per
        self.chunk = self.full + (1 if shared else 0)
        self.lines, self.back_lines = 6 * var_count + COEFFICIENTS, 4 * var_count
        self.groups, self.back_groups = (self.group_count(n) for n in (self.lines, self.back_lines))
        self.meta_at = self.lines * self.full
        self.packed_at = self.meta_at + ABOUT
        self.images_at = self.packed_at + self.groups
        self.height = -(-(self.images_at + self.image_rows) // 8) * 8
        self.back_packed_at = self.back_lines * self.full
        self.back_height = -(-(self.back_packed_at + self.back_groups) // 8) * 8

    def group_count(self, lines):
        return -(-lines // self.per) if self.rest else 0

    def row(self, functional, t):
        return (functional * self.full + t) * self.var_count

    def coefficient_row(self, which, t):
        return 6 * self.full * self.var_count + which * self.full + t

    def tiles_at(self, t):
        return t * self.slabs, min(self.count, (t + 1) * self.slabs)


def lane_block(rows, width):
    return lax.broadcasted_iota(jnp.int32, (rows, LANES), 1) // width


def moved_lanes(x, by):
    by %= LANES
    return x if by == 0 else pltpu.roll(x, by, 1)


def image_lines(x, row, pick_ref, weight_ref, rows, var_count):
    pencils, images = pick_ref.shape
    row_at = lax.broadcasted_iota(jnp.int32, (rows, images), 0)
    lower, upper = row_at == row, row_at == row + 1
    total = [jnp.zeros((rows, images), jnp.float32) for _ in range(var_count)]
    cells = var_count * rows
    pieces = jnp.concatenate(split(x, 2), axis=0)
    moved = [pieces] + [pltpu.roll(pieces, pencils - s, 1) for s in (1, LINE, LINE + 1)]
    all_found = jnp.dot(
        jnp.concatenate(moved, axis=0), pick_ref[...], preferred_element_type=jnp.float32
    )
    for corner in range(4):
        start = 2 * corner * cells
        found = all_found[start : start + cells] + all_found[start + cells : start + 2 * cells]
        weight = jnp.where(lower, weight_ref[corner : corner + 1], 0.0) + jnp.where(
            upper, weight_ref[corner + 4 : corner + 5], 0.0
        )
        for v in range(var_count):
            total[v] += found[v * rows : (v + 1) * rows] * weight
    lines = []
    for v in range(var_count):
        value = jnp.sum(total[v], axis=0, keepdims=True)
        lines += [value[:, tile(t)] for t in range(images // LANES)]
    return jnp.concatenate(lines, axis=0)


def ghost_values(slices, blocks, column):
    per = slices.image_rows // slices.var_count
    slabs, cross = slices.slabs, slices.cross
    ghosts = column.shape[1]
    images = per * LANES
    owner = ((column + 0.5) * (1.0 / images)).astype(jnp.int32)
    image = column.astype(jnp.int32) - owner * images
    across = lax.axis_index("cross")
    values = [
        jnp.concatenate(
            [
                jnp.concatenate(
                    [
                        block[pl.ds(v * per + t, slabs, stride=slices.image_rows), :]
                        for t in range(per)
                    ],
                    axis=1,
                )
                for block in blocks
            ],
            axis=0,
        )
        for v in range(slices.var_count)
    ]
    pick = marks((per * LANES, ghosts), 0, image)
    found = exact_dot(jnp.concatenate(values, axis=0), pick, ((1,), (0,)))
    devices = slabs * cross
    at = lax.broadcasted_iota(jnp.int32, (devices, ghosts), 0)
    mine = (at % slabs) * cross + (across ^ (at // slabs)) == owner
    return [
        reflect
        * jnp.sum(
            jnp.where(mine, found[v * devices : (v + 1) * devices], 0.0), axis=0, keepdims=True
        )
        for v, reflect in enumerate(REFLECT)
    ]


def prepare_kernel(
    slices,
    at,
    face_hbm,
    courant_hbm,
    tables_hbm,
    cell_hbm,
    owner_hbm,
    image_hbm,
    mask_hbm,
    base_hbm,
    corner_hbm,
    state_hbm,
    message_ref,
    stay_hbm,
    up_ref,
    down_ref,
    face_ref,
    courant_ref,
    table_ref,
    cell_ref,
    owner_ref,
    image_ref,
    mask_ref,
    base_ref,
    corner_ref,
    state_ref,
    stay_ref,
    turned_ref,
    face_turned_ref,
    courant_turned_ref,
    pair_ref,
    pick_ref,
    matrix_ref,
    adjoint_ref,
    weight_ref,
    cleared_ref,
    rest_ref,
    sems,
    stay_sem,
):
    var_count, rows, pencils = state_ref.shape
    cells = var_count * rows
    count = pencils // LANES
    ghosts = cell_ref.shape[0]
    padded = -(-count // 8) * 8
    p = lax.axis_index("pipe")
    slabs, height = slices.slabs, slices.height
    lines = slices.groups * slices.per
    own_at, reduce_at, adjoint_at, profile_at = at
    copies = fetch(
        (
            face_hbm,
            courant_hbm,
            tables_hbm.at[p],
            cell_hbm,
            owner_hbm,
            image_hbm,
            base_hbm,
            corner_hbm,
            mask_hbm,
            state_hbm,
        ),
        (
            face_ref,
            courant_ref,
            table_ref,
            cell_ref,
            owner_ref,
            image_ref,
            base_ref,
            corner_ref,
            mask_ref,
            state_ref,
        ),
        sems,
    )
    kept, own, about_at, _ = stay_at(rows, count, cells)

    def send(line, rows_at, slab):
        for t, row_at in enumerate(rows_at):
            start, end = slices.tiles_at(t)
            message_ref[pl.ds(row_at, end - start, stride=height), :] = slab[start:end]
        for m in range(slices.rest):
            tail = slices.full * slabs + m
            rest_ref[m * lines + line : m * lines + line + 1, :] = slab[tail : tail + 1]

    def send_value(functional, v, slab):
        rows_at = [slices.row(functional, t) + v for t in range(slices.full)]
        send(functional * var_count + v, rows_at, slab)

    def send_coefficient(which, slab):
        rows_at = [slices.coefficient_row(which, t) for t in range(slices.full)]
        send(6 * var_count + which, rows_at, slab)

    for copy in copies[:8]:
        copy.wait()
    image_row, image_pencil = place_of(base_ref[...].reshape(1, -1), rows, pencils)
    pick_ref[...] = marks(pick_ref.shape, 0, image_pencil)
    turn(face_turned_ref, face_ref[...])

    def face(i):
        return slab_at(face_turned_ref, i, rows, count)

    link = face(0)
    margin = jnp.ones_like(link)
    first_margin = margin
    to_up, to_first = [None] * rows, [None] * rows
    for i in range(1, rows - 1):
        above = face(i)
        inverse = 1.0 / (link + margin + above)
        low, up = link * inverse, above * inverse
        to_up[i], to_first[i] = up, low
        for k, part in enumerate((up, low, inverse)):
            start = kept_at(k, i, rows, count)
            stay_ref[start : start + count, :] = part
        first_margin += low * margin
        link = link * up
        margin = 1.0 + margin * up
    send_coefficient(LINK_IN, link)
    send_coefficient(MARGIN_FIRST, first_margin)
    send_coefficient(MARGIN_LAST, margin)
    send_coefficient(LINK_UP, jnp.where(p == slabs - 1, 0.0, face(rows - 1)))

    zero, one = jnp.zeros_like(margin), jnp.ones_like(margin)
    first, last = [None] * rows, [None] * rows
    first[0], first[rows - 1], last[0], last[rows - 1] = one, zero, zero, one
    for i in range(rows - 2, 0, -1):
        first[i] = to_first[i] + to_up[i] * first[i + 1]
        last[i] = to_up[i] * last[i + 1]
    turn(courant_turned_ref, courant_ref[...])
    for i in range(rows):
        speed = slab_at(courant_turned_ref, i, rows, count)
        start = kept_at(3, i, rows, count)
        stay_ref[start : start + count, :] = speed
        put_slab(pair_ref, i, 2 * rows, count, first[i] * speed)
        put_slab(pair_ref, rows + i, 2 * rows, count, last[i] * speed)
    for t in range(count):
        matrix_ref[:, tile(t)] = pair_ref[t * 2 * rows : (t + 1) * 2 * rows, :]
    stay_ref[kept - 40 : kept, :] = table_ref[profile_at : profile_at + 40, :]
    stay_ref[own : own + cells, :] = table_ref[own_at : own_at + cells, :]
    turn(
        adjoint_ref, full_dot(table_ref[adjoint_at : adjoint_at + 40, : 2 * rows], matrix_ref[...])
    )
    for k in range(6):
        send_coefficient(FIRST_LO + k, slab_at(adjoint_ref, 2 * rows + k, 40, count))
    weight_ref[:, padded - 8 :, :] = jnp.zeros((2 * rows, 8, LANES), jnp.float32)
    for i, share in enumerate(first + last):
        weight_ref[i, :count, :] = share - slab_at(adjoint_ref, i, 40, count)

    row, pencil = place_of(cell_ref[...].reshape(1, ghosts), rows, pencils)
    lane_tile = jnp.right_shift(pencil, 7)
    lane_marks = marks((LANES, ghosts), 0, pencil - lane_tile * LANES)
    picked = exact_dot(
        weight_ref[...].reshape(2 * rows * padded, LANES), lane_marks, ((1,), (0,))
    ).reshape(2, rows, padded, ghosts)
    at_cell = (lax.broadcasted_iota(jnp.int32, (rows, padded, ghosts), 0) == row[None]) & (
        lax.broadcasted_iota(jnp.int32, (rows, padded, ghosts), 1) == lane_tile[None]
    )

    def at_ghosts(values):
        return jnp.sum(jnp.sum(jnp.where(at_cell, values, 0.0), axis=0), axis=0, keepdims=True)

    about = jnp.concatenate(
        [
            cell_ref[...].reshape(1, ghosts).astype(jnp.float32),
            (owner_ref[...] * base_ref.shape[0] + image_ref[...])
            .reshape(1, ghosts)
            .astype(jnp.float32),
            at_ghosts(picked[0]),
            at_ghosts(picked[1]),
        ],
        axis=0,
    )
    for j in range(slabs):
        start = j * height + slices.meta_at
        message_ref[start : start + ABOUT, :] = about
    stay_ref[about_at : about_at + ABOUT, :] = about
    edge = var_count * count
    for ref in (up_ref, down_ref):
        ref[edge : edge + ABOUT, :] = about
    staying = pltpu.make_async_copy(stay_ref, stay_hbm, stay_sem.at[0])
    staying.start()
    for copy in copies[8:]:
        copy.wait()
    values = image_lines(
        state_ref[...].reshape(cells, pencils),
        image_row,
        pick_ref,
        corner_ref,
        rows,
        var_count,
    )
    for j in range(slabs):
        start = j * height + slices.images_at
        message_ref[start : start + slices.image_rows, :] = values
    solid = mask_ref[...] == 1
    for v in range(var_count):
        here = slice(v * rows, (v + 1) * rows)
        cleared_ref[here, :] = jnp.where(solid, 0.0, state_ref[v])
    turn(turned_ref, cleared_ref[...])
    for group in (range(0, 3), range(3, var_count)):
        sums = {v: [zero] * 4 for v in group}
        for i in range(rows):
            up, down = reduce_at + i, reduce_at + rows + i
            weights = (
                table_ref[up : up + 1, :],
                table_ref[down : down + 1, :],
                weight_ref[i, :count, :],
                weight_ref[rows + i, :count, :],
            )
            for v in group:
                cell = slab_at(turned_ref, v * rows + i, cells, count)
                if i == 0:
                    send_value(ROW_FIRST, v, cell)
                    down_ref[v * count : (v + 1) * count, :] = cell
                if i == rows - 1:
                    send_value(ROW_LAST, v, cell)
                    up_ref[v * count : (v + 1) * count, :] = cell
                sums[v] = [x + weight * cell for x, weight in zip(sums[v], weights)]
        for v in group:
            for functional, total in zip((Z_UP, Z_DOWN, RIGHT_FIRST, RIGHT_LAST), sums[v]):
                send_value(functional, v, total)

    block = lane_block(max(slices.groups, 1), slices.width)
    for m in range(slices.rest):
        lined = [
            rest_ref[pl.ds(m * lines + k, slices.groups, stride=slices.per), :]
            for k in range(slices.per)
        ]
        for i in range(slices.per):
            packed = lined[0]
            for k in range(slices.per):
                moved = moved_lanes(lined[k], (k - i) * slices.width)
                packed = moved if k == 0 else jnp.where(block == k, moved, packed)
            start = (m * slices.per + i) * height + slices.packed_at
            message_ref[start : start + slices.groups, :] = packed
    staying.wait()


def chain_kernel(slices, message_ref, rest_ref, chain_ref):
    slabs, chunk, full = slices.slabs, slices.chunk, slices.full
    height, per, width = slices.height, slices.per, slices.width
    if slices.rest:
        for p in range(slabs):
            start = slices.place[p] * height + slices.packed_at
            packed = message_ref[start : start + slices.groups, :]
            for k in range(per):
                rest_ref[pl.ds(p * slices.groups * per + k, slices.groups, stride=per), :] = (
                    moved_lanes(packed, -k * width)
                )
    else:
        rest_ref[...] = jnp.zeros_like(rest_ref)

    def sent(p, which):
        start = slices.place[p] * height + slices.coefficient_row(which, 0)
        slab = message_ref[start : start + full, :]
        if slices.rest:
            start = p * slices.groups * per + 6 * slices.var_count + which
            slab = jnp.concatenate([slab, rest_ref[start : start + 1, :]], axis=0)
        return slab

    nodes = 2 * slabs
    margin = sent(0, MARGIN_FIRST)
    for k in range(nodes):
        link = sent(k // 2, LINK_UP if k % 2 else LINK_IN)
        inverse = 1.0 / (margin + link)
        ratio = link * inverse
        chain_ref[16 * k : 16 * k + chunk, :] = ratio
        chain_ref[16 * k + 8 : 16 * k + 8 + chunk, :] = inverse
        if k < nodes - 1:
            following = sent((k + 1) // 2, MARGIN_FIRST if k % 2 else MARGIN_LAST)
            margin = following + margin * ratio


def solve_kernel(slices, pencils, constants, message_ref, rest_ref, chain_ref, *refs):
    *blocks, back_ref, ghost_ref, back_rest_ref = refs
    slabs, var_count, chunk, full = slices.slabs, slices.var_count, slices.chunk, slices.full
    height, per, width = slices.height, slices.per, slices.width
    along = lax.axis_index("pipe")
    me = sum(jnp.where(along == p, slices.place[p], 0) for p in range(slabs))

    def meta(p, k):
        start = slices.place[p] * height + slices.meta_at + k
        return message_ref[start : start + 1, :]

    def meta_all(k):
        return jnp.concatenate([meta(p, k) for p in range(slabs)], axis=1)

    carry_up, carry_down, ups, downs = constants
    values = ghost_values(slices, blocks, meta_all(COLUMN))
    rows = ups.shape[1]
    row_of, pencil_of = place_of(meta_all(CELL).astype(jnp.int32), rows, pencils)
    ghosts = LANES
    place = lax.broadcasted_iota(jnp.int32, (chunk * LANES, ghosts), 0)
    slot, lane = place // LANES, place % LANES
    pencil_at = jnp.where(
        slot < full,
        (me + slot * slabs) * LANES + lane,
        (full * slabs + me // per) * LANES + (me % per) * width + lane,
    )
    none = jnp.zeros((8 - var_count, ghosts), jnp.float32)
    for p in range(slabs):
        row = row_of[:, tile(p)]
        up = down = jnp.zeros((1, ghosts), jnp.float32)
        for i in range(rows):
            up = jnp.where(row == i, float(ups[p, i]), up)
            down = jnp.where(row == i, float(downs[p, i]), down)
        weights = (
            up,
            down,
            jnp.where(row == 0, 1.0, 0.0),
            jnp.where(row == rows - 1, 1.0, 0.0),
            meta(p, WEIGHT_FIRST),
            meta(p, WEIGHT_LAST),
        )
        here = jnp.concatenate([value[:, tile(p)] for value in values] + [none], axis=0)
        shares = jnp.concatenate([here * weight for weight in weights], axis=0)
        spots = jnp.where(pencil_at == pencil_of[:, tile(p)], 1.0, 0.0)
        share = exact_dot(shares, spots.astype(jnp.bfloat16), ((1,), (1,)))
        for t in range(chunk):
            start = (p * chunk + t) * 48
            ghost_ref[start : start + 48, :] = share[:, tile(t)]

    nodes = 2 * slabs
    zero = jnp.zeros((var_count, LANES), jnp.float32)
    for t in range(chunk):

        def value(p, functional):
            if t < full:
                start = slices.place[p] * height + slices.row(functional, t)
                sent = message_ref[start : start + var_count, :]
            else:
                start = p * slices.groups * per + functional * var_count
                sent = rest_ref[start : start + var_count, :]
            start = (p * chunk + t) * 48 + functional * 8
            return sent + ghost_ref[start : start + var_count, :]

        def coefficient(p, which):
            if t < full:
                start = slices.place[p] * height + slices.coefficient_row(which, t)
                return message_ref[start : start + 1, :]
            start = p * slices.groups * per + 6 * var_count + which
            return rest_ref[start : start + 1, :]

        def give(p, functional, block):
            if t < full:
                start = slices.place[p] * slices.back_height + slices.row(functional, t)
                back_ref[start : start + var_count, :] = block
            else:
                start = p * slices.back_groups * per + functional * var_count
                back_rest_ref[start : start + var_count, :] = block

        def ratio(k):
            return chain_ref[16 * k + t : 16 * k + t + 1, :]

        def scale(k):
            return chain_ref[16 * k + 8 + t : 16 * k + 9 + t, :]

        lo, hi, below, above = ([zero] * slabs for _ in range(4))
        for p in range(1, slabs):
            lo[p] = value(p - 1, Z_UP) + float(carry_up[p]) * lo[p - 1]
            below[p] = value(p - 1, ROW_LAST)
        for p in range(slabs - 2, -1, -1):
            hi[p] = value(p + 1, Z_DOWN) + float(carry_down[p]) * hi[p + 1]
            above[p] = value(p + 1, ROW_FIRST)
        right = []
        for p in range(slabs):
            right.append(
                value(p, RIGHT_FIRST)
                - coefficient(p, FIRST_LO) * lo[p]
                - coefficient(p, FIRST_HI) * hi[p]
                - coefficient(p, FIRST_EDGE) * below[p]
            )
            right.append(
                value(p, RIGHT_LAST)
                - coefficient(p, LAST_LO) * lo[p]
                - coefficient(p, LAST_HI) * hi[p]
                - coefficient(p, LAST_EDGE) * above[p]
            )
            give(p, 2, lo[p])
            give(p, 3, hi[p])
        for k in range(1, nodes):
            right[k] = right[k] + ratio(k - 1) * right[k - 1]
        x = right[nodes - 1] * scale(nodes - 1)
        give(slabs - 1, 1, x)
        for k in range(nodes - 2, -1, -1):
            x = right[k] * scale(k) + ratio(k) * x
            give(k // 2, k % 2, x)
    if slices.rest:
        groups = slices.back_groups
        block = lane_block(groups, width)
        for p in range(slabs):
            for k in range(per):
                lined = back_rest_ref[pl.ds(p * groups * per + k, groups, stride=per), :]
                moved = moved_lanes(lined, k * width)
                packed = moved if k == 0 else jnp.where(block == k, moved, packed)
            start = slices.place[p] * slices.back_height + slices.back_packed_at
            back_ref[start : start + groups, :] = packed


def pick_kernel(slices, message_ref, values_ref):
    size = slices.image_rows
    for p in range(slices.slabs):
        start = slices.place[p] * slices.height + slices.images_at
        values_ref[p * size : (p + 1) * size, :] = message_ref[start : start + size, :]


def own_kernel(stay_ref, mask_ref, state_ref, ready_ref, cleared_ref):
    var_count, rows, pencils = state_ref.shape
    cells = var_count * rows
    count = pencils // LANES
    own_at = stay_at(rows, count, cells)[1]
    cells_at, kept_start, end = ready_at(rows, count, cells)
    solid = mask_ref[...] == 1
    for v in range(var_count):
        cleared_ref[v * rows : (v + 1) * rows, :] = jnp.where(solid, 0.0, state_ref[v])
    turn(ready_ref.at[cells_at:kept_start, :], cleared_ref[...])
    turn(
        ready_ref.at[:cells_at, :],
        full_dot(stay_ref[own_at : own_at + cells, :cells], cleared_ref[...]),
    )
    ready_ref[kept_start:end, :] = stay_ref[...]


def fill_kernel(slices, shape, ready_ref, below_ref, above_ref, *refs):
    *blocks, done_ref, filled_ref, edge_ref = refs
    var_count, rows, pencils = shape
    cells = var_count * rows
    count = pencils // LANES
    _, own_at, about_at, _ = stay_at(rows, count, cells)
    cells_at, kept_start, _ = ready_at(rows, count, cells)

    ghosts = LANES
    about = [ready_ref[kept_start + about_at : kept_start + about_at + ABOUT, :]]
    edge = var_count * count
    about += [ref[edge : edge + ABOUT, :] for ref in (below_ref, above_ref)]

    def known(k):
        return jnp.concatenate([x[k : k + 1] for x in about], axis=1)

    values = ghost_values(slices, blocks, known(COLUMN))
    row, pencil = place_of(known(CELL).astype(jnp.int32), rows, pencils)
    at_row = lax.broadcasted_iota(jnp.int32, (rows, ghosts), 0) == row[:, :ghosts]
    spread = jnp.concatenate([jnp.where(at_row, value[:, :ghosts], 0.0) for value in values], axis=0)
    own = ready_ref[kept_start + own_at : kept_start + own_at + cells, :cells]
    both = jnp.concatenate([full_dot(own, spread), spread], axis=0)
    spots = marks((pencils, ghosts), 0, pencil[:, :ghosts])
    added = exact_dot(both, spots, ((1,), (1,)))
    for t in range(count):
        here = slice(t * cells, (t + 1) * cells)
        there = slice(cells_at + t * cells, cells_at + (t + 1) * cells)
        done_ref[here, :] = ready_ref[here, :] + added[:cells, tile(t)]
        filled_ref[here, :] = ready_ref[there, :] + added[cells:, tile(t)]
    x_at, response_at, profile_at, edge_at, _ = done_at(rows, count, cells, var_count)
    none = jnp.zeros((8 - var_count, ghosts), jnp.float32)
    for k, (ref, wanted) in enumerate(((below_ref, rows - 1), (above_ref, 0))):
        here = slice((k + 1) * ghosts, (k + 2) * ghosts)
        at_edge = row[:, here] == wanted
        spread = [jnp.where(at_edge, value[:, here], 0.0) for value in values] + [none]
        spots = marks((pencils, ghosts), 0, pencil[:, here])
        turn(edge_ref, exact_dot(jnp.concatenate(spread, axis=0), spots, ((1,), (1,))))
        for v in range(var_count):
            start = edge_at + (k * var_count + v) * count
            done_ref[start : start + count, :] = ref[v * count : (v + 1) * count, :] + slab_at(
                edge_ref, v, 8, count
            )

    def kept(which, i):
        start = kept_start + kept_at(which, i, rows, count)
        return ready_ref[start : start + count, :]

    def profile(k):
        start = kept_start + own_at - 40 + k
        return ready_ref[start : start + 1, :]

    def put(at, i, height, value):
        done_ref[pl.ds(at + i, count, stride=height), :] = value

    swept = []
    for i in range(1, rows - 1):
        speed = kept(3, i)
        here = [-speed * profile(i), -speed * profile(rows + i)]
        for v in range(var_count):
            row = v * rows + i
            own_slab = slab_at(done_ref, row, cells, count)
            here.append(slab_at(filled_ref, row, cells, count) - speed * own_slab)
        if swept:
            ratio = kept(0, i - 1)
            here = [x + ratio * y for x, y in zip(here, swept[-1])]
        swept.append(here)
    zero = jnp.zeros((count, LANES), jnp.float32)
    one = jnp.ones((count, LANES), jnp.float32)
    x = [zero] * (2 + var_count)
    first, last = zero, one
    for i in range(rows - 1, -1, -1):
        if 0 < i < rows - 1:
            ratio, inverse = kept(0, i), kept(2, i)
            first, last = kept(1, i) + ratio * first, ratio * last
            x = [inverse * y + ratio * z for y, z in zip(swept[i - 1], x)]
        if i == 0:
            first, last, x = one, zero, [zero] * (2 + var_count)
        for k, value in enumerate([first, last] + x[:2]):
            put(response_at + k * rows * count, i, rows, value)
        for v in range(var_count):
            put(x_at, v * rows + i, cells, x[2 + v])
    done_ref[profile_at : profile_at + 40, :] = ready_ref[
        kept_start + own_at - 40 : kept_start + own_at, :
    ]


def finish_kernel(
    slices, back_ref, done_ref, derivative_hbm, segment_hbm, derivative_ref, segment_ref, tail_ref, sems
):
    var_count, rows, pencils = segment_ref.shape
    count = pencils // LANES
    cells = var_count * rows
    x_at, response_at, profile_at, edge_at, _ = done_at(rows, count, cells, var_count)
    back_height, groups, per = slices.back_height, slices.back_groups, slices.per
    block = lane_block(max(groups, 1), slices.width)
    for m in range(slices.rest):
        packed = []
        for i in range(per):
            start = (m * per + i) * back_height + slices.back_packed_at
            packed.append(back_ref[start : start + groups, :])
        for k in range(per):
            for i in range(per):
                moved = moved_lanes(packed[i], (i - k) * slices.width)
                joined = moved if i == 0 else jnp.where(block == i, moved, joined)
            tail_ref[pl.ds(m * groups * per + k, groups, stride=per), :] = joined

    def got(functional, v, t):
        step, j = t // slices.slabs, t % slices.slabs
        if step < slices.full:
            start = j * back_height + slices.row(functional, step) + v
            return back_ref[start : start + 1, :]
        start = j * groups * per + functional * var_count + v
        return tail_ref[start : start + 1, :]

    lo_profile = done_ref[profile_at : profile_at + rows, :]
    hi_profile = done_ref[profile_at + rows : profile_at + 2 * rows, :]
    row_at = lax.broadcasted_iota(jnp.int32, (rows, LANES), 0)
    edges = profile_at + 2 * rows
    lo_edge = jnp.where(row_at == 0, done_ref[edges : edges + 1, :], 0.0)
    hi_edge = jnp.where(row_at == rows - 1, done_ref[edges + 1 : edges + 2, :], 0.0)

    def edge(k, v, t):
        start = edge_at + (k * var_count + v) * count + t
        return done_ref[start : start + 1, :]

    def response(k, t):
        start = response_at + (k * count + t) * rows
        return done_ref[start : start + rows, :]

    copies = []
    for v in range(var_count):
        for t in range(count):
            start = t * cells + v * rows
            lo, hi = got(2, v, t), got(3, v, t)
            derivative_ref[v, :, tile(t)] = (
                done_ref[start : start + rows, :]
                + (lo_profile * lo + hi_profile * hi)
                + (lo_edge * edge(0, v, t) + hi_edge * edge(1, v, t))
            )
            segment_ref[v, :, tile(t)] = (
                done_ref[x_at + start : x_at + start + rows, :]
                + (response(0, t) * got(0, v, t) + response(1, t) * got(1, v, t))
                + (response(2, t) * lo + response(3, t) * hi)
            )
        for which, (ref, hbm) in enumerate(
            ((derivative_ref, derivative_hbm), (segment_ref, segment_hbm))
        ):
            copies.append(
                pltpu.make_async_copy(ref.at[v], hbm.at[v], sems.at[which * var_count + v])
            )
            copies[-1].start()
    for copy in copies:
        copy.wait()


def call(kernel, outs, scratch, sems, args, near=(), far_out=(), limit=62):
    whole = pl.BlockSpec(memory_space=pltpu.VMEM)
    far = pl.BlockSpec(memory_space=pltpu.HBM)
    buffers = [
        pltpu.VMEM(s.shape, s.dtype) if hasattr(s, "dtype") else pltpu.VMEM(s, jnp.float32)
        for s in scratch
    ]
    buffers += [pltpu.SemaphoreType.DMA((size,)) for size in sems]
    return pl.pallas_call(
        kernel,
        out_shape=[jax.ShapeDtypeStruct(shape, jnp.float32) for shape in outs],
        in_specs=[whole if k in near else far for k in range(len(args))],
        out_specs=[far if k in far_out else whole for k in range(len(outs))],
        scratch_shapes=buffers,
        compiler_params=pltpu.CompilerParams(vmem_limit_bytes=limit * 2**20),
    )(*args)


def exchange(message, axis):
    groups = [middle_first(lax.axis_size(axis))]
    return lax.all_to_all(message, axis, 0, 0, axis_index_groups=groups, tiled=True)


def local(
    state,
    face_diffusion,
    courant,
    cell_mask,
    ghost_cell,
    ghost_owner,
    ghost_image,
    image_base,
    image_weight,
):
    var_count, rows, pencils = state.shape
    slabs, cross = lax.axis_size("pipe"), lax.axis_size("cross")
    count = pencils // LANES
    cells = var_count * rows
    images = image_base.shape[0]
    tables, at, constants = derivative_tables(slabs, rows, var_count)
    slices = Slices(slabs, count, cross, var_count, images)
    tables = jnp.asarray(tables)
    turned = (cells * count, LANES)
    stay = stay_at(rows, count, cells)[3]
    ready = (ready_at(rows, count, cells)[2], LANES)

    arguments = (
        face_diffusion,
        courant,
        tables,
        ghost_cell,
        ghost_owner,
        ghost_image,
        cell_mask,
        image_base,
        image_weight,
        state,
    )
    buffers = list(arguments)
    buffers[2] = jax.ShapeDtypeStruct(tables.shape[1:], jnp.float32)
    edge = (-(-(var_count * count + ABOUT) // 8) * 8, LANES)
    message, stay, up, down = call(
        functools.partial(prepare_kernel, slices, at),
        [(slabs * slices.height, LANES), (stay, LANES), edge, edge],
        buffers
        + [
            (stay, LANES),
            turned,
            (rows * count, LANES),
            (rows * count, LANES),
            (2 * rows * count, LANES),
            jax.ShapeDtypeStruct((pencils, images), jnp.bfloat16),
            (2 * rows, pencils),
            (40 * count, LANES),
            (2 * rows, -(-count // 8) * 8, LANES),
            (cells, pencils),
            (max(slices.rest, 1) * max(slices.groups, 1) * slices.per, LANES),
        ],
        [len(arguments), 1],
        arguments,
        far_out=(1,),
    )
    message = exchange(message, "pipe")
    forward = [(i, i + 1) for i in range(slabs - 1)]
    below = lax.ppermute(up, "pipe", forward)
    above = lax.ppermute(down, "pipe", [(j, i) for i, j in forward])
    (ready,) = call(
        own_kernel,
        [ready],
        [(cells, pencils)],
        [],
        (stay, cell_mask, state),
        near=range(3),
        limit=48,
    )
    (image_values,) = call(
        functools.partial(pick_kernel, slices),
        [(slabs * slices.image_rows, LANES)],
        [],
        [],
        (message,),
        near=(0,),
        limit=24,
    )
    blocks = [image_values] + [
        lax.ppermute(image_values, "cross", [(i, i ^ u) for i in range(cross)])
        for u in range(1, cross)
    ]

    factored, below, above = lax.optimization_barrier((message, below, above))
    rest, chain = call(
        functools.partial(chain_kernel, slices),
        [(slabs * max(slices.groups, 1) * slices.per, LANES), (2 * slabs * 16, LANES)],
        [],
        [],
        (factored,),
        near=(0,),
        limit=24,
    )
    (back,) = call(
        functools.partial(solve_kernel, slices, pencils, constants),
        [(slabs * slices.back_height, LANES)],
        [
            (slabs * slices.chunk * 48, LANES),
            (slabs * max(slices.back_groups, 1) * slices.per, LANES),
        ],
        [],
        (message, rest, chain, *blocks),
        near=range(3 + cross),
        limit=24,
    )
    back = exchange(back, "pipe")
    (done,) = call(
        functools.partial(fill_kernel, slices, state.shape),
        [(done_at(rows, count, cells, var_count)[4], LANES)],
        [turned, (8 * count, LANES)],
        [],
        (ready, below, above, *blocks),
        near=range(3 + cross),
        limit=48,
    )
    return tuple(
        call(
            functools.partial(finish_kernel, slices),
            [state.shape, state.shape],
            [
                state.shape,
                state.shape,
                (max(slices.rest, 1) * max(slices.back_groups, 1) * slices.per, LANES),
            ],
            [2 * var_count],
            (back, done),
            near=range(2),
            far_out=(0, 1),
            limit=48,
        )
    )


def solution(mesh):
    in_specs = (
        P(None, "pipe", "cross"),
        P("pipe", "cross"),
        P("pipe", "cross"),
        P("pipe", "cross"),
        P(("pipe", "cross")),
        P(("pipe", "cross")),
        P(("pipe", "cross")),
        P(("pipe", "cross")),
        P(None, ("pipe", "cross")),
    )
    out_specs = (P(None, "pipe", "cross"), P(None, "pipe", "cross"))
    return jax.shard_map(local, mesh=mesh, in_specs=in_specs, out_specs=out_specs, check_vma=False)
```

```python
import functools

import numpy as np
import jax
import jax.numpy as jnp
from jax import lax
from jax.experimental import pallas as pl
from jax.experimental.pallas import tpu as pltpu
from jax.sharding import PartitionSpec as P

LINE = 96
LANES = 128
REFLECT = (1.0, -1.0, -1.0, -1.0, 1.0)

Z_UP, Z_DOWN, ROW_FIRST, ROW_LAST, RIGHT_FIRST, RIGHT_LAST = range(6)
LINK_IN, MARGIN_FIRST, MARGIN_LAST, LINK_UP, FIRST_LO, FIRST_HI, LAST_LO, LAST_HI, FIRST_EDGE, LAST_EDGE = range(10)
COEFFICIENTS = 10
CELL, COLUMN, WEIGHT_FIRST, WEIGHT_LAST = range(4)
ABOUT = 4


def derivative_tables(slabs, rows, var_count):
    total = slabs * rows
    A = np.eye(total)
    B = np.zeros((total, total))
    for i in range(2, total - 2):
        A[i, i - 1] = A[i, i + 1] = 1.0 / 3.0
        B[i, i + 1], B[i, i - 1] = 7.0 / 9.0, -7.0 / 9.0
        B[i, i + 2], B[i, i - 2] = 1.0 / 36.0, -1.0 / 36.0
    for i in (1, total - 2):
        A[i, i - 1] = A[i, i + 1] = 0.25
        B[i, i + 1], B[i, i - 1] = 0.75, -0.75
    B[0, :3] = (-1.5, 2.0, -0.5)
    B[-1, -3:] = (0.5, -2.0, 1.5)
    inverse = np.linalg.inv(A)
    M = inverse @ B

    cells = var_count * rows
    own_at, reduce_at, adjoint_at, profile_at = 0, cells, cells + 32, cells + 72
    tables = np.zeros((slabs, cells + 112, LANES))
    carry_up, carry_down = np.zeros(slabs), np.zeros(slabs)
    ups, downs = np.zeros((slabs, rows)), np.zeros((slabs, rows))
    for p in range(slabs):
        table = tables[p]
        base = p * rows
        here = slice(base, base + rows)
        own = M[here, here]
        lo, hi, lo_edge, hi_edge = (np.zeros(rows) for _ in range(4))
        weight_up, weight_down = np.zeros(rows), np.zeros(rows)
        if p > 0:
            lo = inverse[here, base - 8] / inverse[base + 1, base - 8]
            lo_edge[0] = M[base, base - 1] - lo[0] * M[base + 1, base - 1]
            weight_down = M[base - 2, here]
        if p > 1:
            k = base - rows - 8
            carry_up[p] = inverse[base + 1, k] / inverse[base - rows + 1, k]
        if p < slabs - 1:
            k = base + rows + 8
            hi = inverse[here, k] / inverse[base + rows - 2, k]
            hi_edge[-1] = M[base + rows - 1, base + rows] - hi[-1] * M[base + rows - 2, base + rows]
            weight_up = M[base + rows + 1, here]
        if p < slabs - 2:
            k = base + 2 * rows + 8
            carry_down[p] = inverse[base + rows - 2, k] / inverse[base + 2 * rows - 2, k]
        for v in range(var_count):
            at = slice(v * rows, (v + 1) * rows)
            table[own_at + v * rows : own_at + (v + 1) * rows, at] = own
        table[reduce_at : reduce_at + rows] = weight_up[:, None]
        table[reduce_at + rows : reduce_at + 2 * rows] = weight_down[:, None]
        table[adjoint_at : adjoint_at + rows, :rows] = own.T
        table[adjoint_at + rows : adjoint_at + 2 * rows, rows : 2 * rows] = own.T
        more = adjoint_at + 2 * rows
        table[more, :rows] = lo
        table[more + 1, :rows] = hi
        table[more + 2, rows : 2 * rows] = lo
        table[more + 3, rows : 2 * rows] = hi
        table[more + 4, 0] = lo_edge[0]
        table[more + 5, 2 * rows - 1] = hi_edge[-1]
        table[profile_at : profile_at + rows] = lo[:, None]
        table[profile_at + rows : profile_at + 2 * rows] = hi[:, None]
        table[profile_at + 2 * rows] = lo_edge[0]
        table[profile_at + 2 * rows + 1] = hi_edge[-1]
        ups[p], downs[p] = weight_up, weight_down
    at = (own_at, reduce_at, adjoint_at, profile_at)
    return tables.astype(np.float32), at, (carry_up, carry_down, ups, downs)


def split(x, parts):
    pieces = []
    for _ in range(parts):
        piece = x.astype(jnp.bfloat16)
        pieces.append(piece)
        x = x - piece.astype(jnp.float32)
    return pieces


def one_hot_dot(x, one_hot, contract, parts):
    found = lax.dot_general(
        jnp.concatenate(split(x, parts), axis=0),
        one_hot,
        (contract, ((), ())),
        preferred_element_type=jnp.float32,
    )
    size = x.shape[0]
    pieces = [found[k * size : (k + 1) * size] for k in range(parts)]
    return sum(pieces[-2::-1], pieces[-1])


def full_dot(a, b):
    return jnp.dot(a, b, precision=lax.Precision.HIGHEST, preferred_element_type=jnp.float32)


def marks(shape, axis, values):
    return jnp.where(lax.broadcasted_iota(jnp.int32, shape, axis) == values, 1.0, 0.0).astype(
        jnp.bfloat16
    )


def place_of(cell, rows, pencils):
    row = jnp.zeros_like(cell)
    for k in range(1, rows):
        row += (cell >= k * pencils).astype(jnp.int32)
    return row, cell - row * pencils


def tile(t):
    return slice(t * LANES, (t + 1) * LANES)


def turn(ref, x):
    height, pencils = x.shape
    for t in range(pencils // LANES):
        ref[t * height : (t + 1) * height, :] = x[:, tile(t)]


def slab_at(ref, row, height, count):
    return ref[pl.ds(row, count, stride=height), :]


def put_slab(ref, row, height, count, value):
    ref[pl.ds(row, count, stride=height), :] = value


def kept_at(which, i, rows, count):
    return (which * rows + i) * (-(-count // 8) * 8)


def stay_at(rows, count, cells):
    kept = kept_at(4, 0, rows, count) + 40
    return kept, kept, kept + cells, kept + cells + 8


def ready_at(rows, count, cells):
    kept = 2 * cells * count
    return cells * count, kept, kept + stay_at(rows, count, cells)[3]


def done_at(rows, count, cells, var_count):
    x = cells * count
    response = 2 * x
    profile = response + 4 * rows * count
    return x, response, profile, profile + 40, profile + 40 + 2 * var_count * count


def fetch(sources, targets, sems):
    copies = [
        pltpu.make_async_copy(source, target, sems.at[k])
        for k, (source, target) in enumerate(zip(sources, targets))
    ]
    for copy in copies:
        copy.start()
    return copies


def middle_first(slabs):
    return sorted(range(slabs), key=lambda p: (abs(2 * p - slabs + 1), p))


class Slices:
    def __init__(self, slabs, count, cross, var_count, images):
        rest = count % slabs
        order = middle_first(slabs)
        self.place = [order.index(p) for p in range(slabs)]
        self.slabs, self.count, self.cross, self.var_count = slabs, count, cross, var_count
        self.image_rows = var_count * images // LANES
        shared = rest > 0 and slabs % rest == 0 and LANES % (slabs // rest) == 0
        self.full = count // slabs if shared else -(-count // slabs)
        self.rest = rest if shared else 0
        self.per = slabs // rest if shared else 1
        self.width = LANES // self.per
        self.chunk = self.full + (1 if shared else 0)
        self.lines, self.back_lines = 6 * var_count + COEFFICIENTS, 4 * var_count
        self.groups, self.back_groups = (self.group_count(n) for n in (self.lines, self.back_lines))
        self.meta_at = self.lines * self.full
        self.packed_at = self.meta_at + ABOUT
        self.images_at = self.packed_at + self.groups
        self.height = -(-(self.images_at + self.image_rows) // 8) * 8
        self.back_packed_at = self.back_lines * self.full
        self.back_height = -(-(self.back_packed_at + self.back_groups) // 8) * 8

    def group_count(self, lines):
        return -(-lines // self.per) if self.rest else 0

    def row(self, functional, t):
        return (functional * self.full + t) * self.var_count

    def coefficient_row(self, which, t):
        return 6 * self.full * self.var_count + which * self.full + t

    def tiles_at(self, t):
        return t * self.slabs, min(self.count, (t + 1) * self.slabs)


def lane_block(rows, width):
    return lax.broadcasted_iota(jnp.int32, (rows, LANES), 1) // width


def moved_lanes(x, by):
    by %= LANES
    return x if by == 0 else pltpu.roll(x, by, 1)


def image_lines(x, row, pick_ref, weight_ref, rows, var_count):
    pencils, images = pick_ref.shape
    row_at = lax.broadcasted_iota(jnp.int32, (rows, images), 0)
    lower, upper = row_at == row, row_at == row + 1
    total = [jnp.zeros((rows, images), jnp.float32) for _ in range(var_count)]
    pieces = jnp.concatenate(split(x, 2), axis=0)
    for corner, shift in enumerate((0, 1, LINE, LINE + 1)):
        moved = pieces if shift == 0 else pltpu.roll(pieces, pencils - shift, 1)
        found = jnp.dot(moved, pick_ref[...], preferred_element_type=jnp.float32)
        found = found[: var_count * rows] + found[var_count * rows :]
        weight = jnp.where(lower, weight_ref[corner : corner + 1], 0.0) + jnp.where(
            upper, weight_ref[corner + 4 : corner + 5], 0.0
        )
        for v in range(var_count):
            total[v] += found[v * rows : (v + 1) * rows] * weight
    lines = []
    for v in range(var_count):
        value = jnp.sum(total[v], axis=0, keepdims=True)
        lines += [value[:, tile(t)] for t in range(images // LANES)]
    return jnp.concatenate(lines, axis=0)


def ghost_values(slices, blocks, column, parts):
    per = slices.image_rows // slices.var_count
    slabs, cross = slices.slabs, slices.cross
    ghosts = column.shape[1]
    images = per * LANES
    owner = ((column + 0.5) * (1.0 / images)).astype(jnp.int32)
    image = column.astype(jnp.int32) - owner * images
    across = lax.axis_index("cross")
    values = [
        jnp.concatenate(
            [
                jnp.concatenate(
                    [
                        block[pl.ds(v * per + t, slabs, stride=slices.image_rows), :]
                        for t in range(per)
                    ],
                    axis=1,
                )
                for block in blocks
            ],
            axis=0,
        )
        for v in range(slices.var_count)
    ]
    pick = marks((per * LANES, ghosts), 0, image)
    found = one_hot_dot(jnp.concatenate(values, axis=0), pick, ((1,), (0,)), parts)
    devices = slabs * cross
    at = lax.broadcasted_iota(jnp.int32, (devices, ghosts), 0)
    mine = (at % slabs) * cross + (across ^ (at // slabs)) == owner
    return [
        reflect
        * jnp.sum(
            jnp.where(mine, found[v * devices : (v + 1) * devices], 0.0), axis=0, keepdims=True
        )
        for v, reflect in enumerate(REFLECT)
    ]


def prepare_kernel(
    slices,
    at,
    face_hbm,
    courant_hbm,
    tables_hbm,
    cell_hbm,
    owner_hbm,
    image_hbm,
    mask_hbm,
    base_hbm,
    corner_hbm,
    state_hbm,
    message_ref,
    stay_hbm,
    up_ref,
    down_ref,
    face_ref,
    courant_ref,
    table_ref,
    cell_ref,
    owner_ref,
    image_ref,
    mask_ref,
    base_ref,
    corner_ref,
    state_ref,
    stay_ref,
    turned_ref,
    face_turned_ref,
    courant_turned_ref,
    pair_ref,
    pick_ref,
    matrix_ref,
    adjoint_ref,
    weight_ref,
    cleared_ref,
    rest_ref,
    sems,
    stay_sem,
):
    var_count, rows, pencils = state_ref.shape
    cells = var_count * rows
    count = pencils // LANES
    ghosts = cell_ref.shape[0]
    padded = -(-count // 8) * 8
    p = lax.axis_index("pipe")
    slabs, height = slices.slabs, slices.height
    lines = slices.groups * slices.per
    own_at, reduce_at, adjoint_at, profile_at = at
    copies = fetch(
        (
            face_hbm,
            courant_hbm,
            tables_hbm.at[p],
            cell_hbm,
            owner_hbm,
            image_hbm,
            base_hbm,
            corner_hbm,
            mask_hbm,
            state_hbm,
        ),
        (
            face_ref,
            courant_ref,
            table_ref,
            cell_ref,
            owner_ref,
            image_ref,
            base_ref,
            corner_ref,
            mask_ref,
            state_ref,
        ),
        sems,
    )
    kept, own, about_at, _ = stay_at(rows, count, cells)

    def send(line, rows_at, slab):
        for t, row_at in enumerate(rows_at):
            start, end = slices.tiles_at(t)
            message_ref[pl.ds(row_at, end - start, stride=height), :] = slab[start:end]
        for m in range(slices.rest):
            tail = slices.full * slabs + m
            rest_ref[m * lines + line : m * lines + line + 1, :] = slab[tail : tail + 1]

    def send_value(functional, v, slab):
        rows_at = [slices.row(functional, t) + v for t in range(slices.full)]
        send(functional * var_count + v, rows_at, slab)

    def send_coefficient(which, slab):
        rows_at = [slices.coefficient_row(which, t) for t in range(slices.full)]
        send(6 * var_count + which, rows_at, slab)

    for copy in copies[:8]:
        copy.wait()
    image_row, image_pencil = place_of(base_ref[...].reshape(1, -1), rows, pencils)
    pick_ref[...] = marks(pick_ref.shape, 0, image_pencil)
    turn(face_turned_ref, face_ref[...])

    def face(i):
        return slab_at(face_turned_ref, i, rows, count)

    link = face(0)
    margin = jnp.ones_like(link)
    first_margin = margin
    to_up, to_first = [None] * rows, [None] * rows
    for i in range(1, rows - 1):
        above = face(i)
        inverse = 1.0 / (link + margin + above)
        low, up = link * inverse, above * inverse
        to_up[i], to_first[i] = up, low
        for k, part in enumerate((up, low, inverse)):
            start = kept_at(k, i, rows, count)
            stay_ref[start : start + count, :] = part
        first_margin += low * margin
        link = link * up
        margin = 1.0 + margin * up
    send_coefficient(LINK_IN, link)
    send_coefficient(MARGIN_FIRST, first_margin)
    send_coefficient(MARGIN_LAST, margin)
    send_coefficient(LINK_UP, jnp.where(p == slabs - 1, 0.0, face(rows - 1)))

    zero, one = jnp.zeros_like(margin), jnp.ones_like(margin)
    first, last = [None] * rows, [None] * rows
    first[0], first[rows - 1], last[0], last[rows - 1] = one, zero, zero, one
    for i in range(rows - 2, 0, -1):
        first[i] = to_first[i] + to_up[i] * first[i + 1]
        last[i] = to_up[i] * last[i + 1]
    turn(courant_turned_ref, courant_ref[...])
    for i in range(rows):
        speed = slab_at(courant_turned_ref, i, rows, count)
        start = kept_at(3, i, rows, count)
        stay_ref[start : start + count, :] = speed
        put_slab(pair_ref, i, 2 * rows, count, first[i] * speed)
        put_slab(pair_ref, rows + i, 2 * rows, count, last[i] * speed)
    for t in range(count):
        matrix_ref[:, tile(t)] = pair_ref[t * 2 * rows : (t + 1) * 2 * rows, :]
    stay_ref[kept - 40 : kept, :] = table_ref[profile_at : profile_at + 40, :]
    stay_ref[own : own + cells, :] = table_ref[own_at : own_at + cells, :]
    turn(
        adjoint_ref, full_dot(table_ref[adjoint_at : adjoint_at + 40, : 2 * rows], matrix_ref[...])
    )
    for k in range(6):
        send_coefficient(FIRST_LO + k, slab_at(adjoint_ref, 2 * rows + k, 40, count))
    weight_ref[:, padded - 8 :, :] = jnp.zeros((2 * rows, 8, LANES), jnp.float32)
    for i, share in enumerate(first + last):
        weight_ref[i, :count, :] = share - slab_at(adjoint_ref, i, 40, count)

    row, pencil = place_of(cell_ref[...].reshape(1, ghosts), rows, pencils)
    lane_tile = jnp.right_shift(pencil, 7)
    lane_marks = marks((LANES, ghosts), 0, pencil - lane_tile * LANES)
    picked = one_hot_dot(
        weight_ref[...].reshape(2 * rows * padded, LANES), lane_marks, ((1,), (0,)), 2
    ).reshape(2, rows, padded, ghosts)
    at_cell = (lax.broadcasted_iota(jnp.int32, (rows, padded, ghosts), 0) == row[None]) & (
        lax.broadcasted_iota(jnp.int32, (rows, padded, ghosts), 1) == lane_tile[None]
    )

    def at_ghosts(values):
        return jnp.sum(jnp.sum(jnp.where(at_cell, values, 0.0), axis=0), axis=0, keepdims=True)

    about = jnp.concatenate(
        [
            cell_ref[...].reshape(1, ghosts).astype(jnp.float32),
            (owner_ref[...] * base_ref.shape[0] + image_ref[...])
            .reshape(1, ghosts)
            .astype(jnp.float32),
            at_ghosts(picked[0]),
            at_ghosts(picked[1]),
        ],
        axis=0,
    )
    for j in range(slabs):
        start = j * height + slices.meta_at
        message_ref[start : start + ABOUT, :] = about
    stay_ref[about_at : about_at + ABOUT, :] = about
    edge = var_count * count
    for ref in (up_ref, down_ref):
        ref[edge : edge + ABOUT, :] = about
    staying = pltpu.make_async_copy(stay_ref, stay_hbm, stay_sem.at[0])
    staying.start()
    for copy in copies[8:]:
        copy.wait()
    values = image_lines(
        state_ref[...].reshape(cells, pencils),
        image_row,
        pick_ref,
        corner_ref,
        rows,
        var_count,
    )
    for j in range(slabs):
        start = j * height + slices.images_at
        message_ref[start : start + slices.image_rows, :] = values
    solid = mask_ref[...] == 1
    for v in range(var_count):
        here = slice(v * rows, (v + 1) * rows)
        cleared_ref[here, :] = jnp.where(solid, 0.0, state_ref[v])
    turn(turned_ref, cleared_ref[...])
    for group in (range(0, 3), range(3, var_count)):
        sums = {v: [zero] * 4 for v in group}
        for i in range(rows):
            up, down = reduce_at + i, reduce_at + rows + i
            weights = (
                table_ref[up : up + 1, :],
                table_ref[down : down + 1, :],
                weight_ref[i, :count, :],
                weight_ref[rows + i, :count, :],
            )
            for v in group:
                cell = slab_at(turned_ref, v * rows + i, cells, count)
                if i == 0:
                    send_value(ROW_FIRST, v, cell)
                    down_ref[v * count : (v + 1) * count, :] = cell
                if i == rows - 1:
                    send_value(ROW_LAST, v, cell)
                    up_ref[v * count : (v + 1) * count, :] = cell
                sums[v] = [x + weight * cell for x, weight in zip(sums[v], weights)]
        for v in group:
            for functional, total in zip((Z_UP, Z_DOWN, RIGHT_FIRST, RIGHT_LAST), sums[v]):
                send_value(functional, v, total)

    block = lane_block(max(slices.groups, 1), slices.width)
    for m in range(slices.rest):
        lined = [
            rest_ref[pl.ds(m * lines + k, slices.groups, stride=slices.per), :]
            for k in range(slices.per)
        ]
        for i in range(slices.per):
            packed = lined[0]
            for k in range(slices.per):
                moved = moved_lanes(lined[k], (k - i) * slices.width)
                packed = moved if k == 0 else jnp.where(block == k, moved, packed)
            start = (m * slices.per + i) * height + slices.packed_at
            message_ref[start : start + slices.groups, :] = packed
    staying.wait()


def chain_kernel(slices, message_ref, rest_ref, chain_ref):
    slabs, chunk, full = slices.slabs, slices.chunk, slices.full
    height, per, width = slices.height, slices.per, slices.width
    if slices.rest:
        for p in range(slabs):
            start = slices.place[p] * height + slices.packed_at
            packed = message_ref[start : start + slices.groups, :]
            for k in range(per):
                rest_ref[pl.ds(p * slices.groups * per + k, slices.groups, stride=per), :] = (
                    moved_lanes(packed, -k * width)
                )
    else:
        rest_ref[...] = jnp.zeros_like(rest_ref)

    def sent(p, which):
        start = slices.place[p] * height + slices.coefficient_row(which, 0)
        slab = message_ref[start : start + full, :]
        if slices.rest:
            start = p * slices.groups * per + 6 * slices.var_count + which
            slab = jnp.concatenate([slab, rest_ref[start : start + 1, :]], axis=0)
        return slab

    nodes = 2 * slabs
    margin = sent(0, MARGIN_FIRST)
    for k in range(nodes):
        link = sent(k // 2, LINK_UP if k % 2 else LINK_IN)
        inverse = 1.0 / (margin + link)
        ratio = link * inverse
        chain_ref[16 * k : 16 * k + chunk, :] = ratio
        chain_ref[16 * k + 8 : 16 * k + 8 + chunk, :] = inverse
        if k < nodes - 1:
            following = sent((k + 1) // 2, MARGIN_FIRST if k % 2 else MARGIN_LAST)
            margin = following + margin * ratio


def solve_kernel(slices, pencils, constants, message_ref, rest_ref, chain_ref, *refs):
    *blocks, back_ref, ghost_ref, back_rest_ref = refs
    slabs, var_count, chunk, full = slices.slabs, slices.var_count, slices.chunk, slices.full
    height, per, width = slices.height, slices.per, slices.width
    along = lax.axis_index("pipe")
    me = sum(jnp.where(along == p, slices.place[p], 0) for p in range(slabs))

    def meta(p, k):
        start = slices.place[p] * height + slices.meta_at + k
        return message_ref[start : start + 1, :]

    def meta_all(k):
        return jnp.concatenate([meta(p, k) for p in range(slabs)], axis=1)

    carry_up, carry_down, ups, downs = constants
    values = ghost_values(slices, blocks, meta_all(COLUMN), 2)
    rows = ups.shape[1]
    row_of, pencil_of = place_of(meta_all(CELL).astype(jnp.int32), rows, pencils)
    ghosts = LANES
    place = lax.broadcasted_iota(jnp.int32, (chunk * LANES, ghosts), 0)
    slot, lane = place // LANES, place % LANES
    pencil_at = jnp.where(
        slot < full,
        (me + slot * slabs) * LANES + lane,
        (full * slabs + me // per) * LANES + (me % per) * width + lane,
    )
    none = jnp.zeros((8 - var_count, ghosts), jnp.float32)
    for p in range(slabs):
        row = row_of[:, tile(p)]
        up = down = jnp.zeros((1, ghosts), jnp.float32)
        for i in range(rows):
            up = jnp.where(row == i, float(ups[p, i]), up)
            down = jnp.where(row == i, float(downs[p, i]), down)
        weights = (
            up,
            down,
            jnp.where(row == 0, 1.0, 0.0),
            jnp.where(row == rows - 1, 1.0, 0.0),
            meta(p, WEIGHT_FIRST),
            meta(p, WEIGHT_LAST),
        )
        here = jnp.concatenate([value[:, tile(p)] for value in values] + [none], axis=0)
        shares = jnp.concatenate([here * weight for weight in weights], axis=0)
        spots = jnp.where(pencil_at == pencil_of[:, tile(p)], 1.0, 0.0)
        share = one_hot_dot(shares, spots.astype(jnp.bfloat16), ((1,), (1,)), 2)
        for t in range(chunk):
            start = (p * chunk + t) * 48
            ghost_ref[start : start + 48, :] = share[:, tile(t)]

    nodes = 2 * slabs
    zero = jnp.zeros((var_count, LANES), jnp.float32)
    for t in range(chunk):

        def value(p, functional):
            if t < full:
                start = slices.place[p] * height + slices.row(functional, t)
                sent = message_ref[start : start + var_count, :]
            else:
                start = p * slices.groups * per + functional * var_count
                sent = rest_ref[start : start + var_count, :]
            start = (p * chunk + t) * 48 + functional * 8
            return sent + ghost_ref[start : start + var_count, :]

        def coefficient(p, which):
            if t < full:
                start = slices.place[p] * height + slices.coefficient_row(which, t)
                return message_ref[start : start + 1, :]
            start = p * slices.groups * per + 6 * var_count + which
            return rest_ref[start : start + 1, :]

        def give(p, functional, block):
            if t < full:
                start = slices.place[p] * slices.back_height + slices.row(functional, t)
                back_ref[start : start + var_count, :] = block
            else:
                start = p * slices.back_groups * per + functional * var_count
                back_rest_ref[start : start + var_count, :] = block

        def ratio(k):
            return chain_ref[16 * k + t : 16 * k + t + 1, :]

        def scale(k):
            return chain_ref[16 * k + 8 + t : 16 * k + 9 + t, :]

        lo, hi, below, above = ([zero] * slabs for _ in range(4))
        for p in range(1, slabs):
            lo[p] = value(p - 1, Z_UP) + float(carry_up[p]) * lo[p - 1]
            below[p] = value(p - 1, ROW_LAST)
        for p in range(slabs - 2, -1, -1):
            hi[p] = value(p + 1, Z_DOWN) + float(carry_down[p]) * hi[p + 1]
            above[p] = value(p + 1, ROW_FIRST)
        right = []
        for p in range(slabs):
            right.append(
                value(p, RIGHT_FIRST)
                - coefficient(p, FIRST_LO) * lo[p]
                - coefficient(p, FIRST_HI) * hi[p]
                - coefficient(p, FIRST_EDGE) * below[p]
            )
            right.append(
                value(p, RIGHT_LAST)
                - coefficient(p, LAST_LO) * lo[p]
                - coefficient(p, LAST_HI) * hi[p]
                - coefficient(p, LAST_EDGE) * above[p]
            )
            give(p, 2, lo[p])
            give(p, 3, hi[p])
        for k in range(1, nodes):
            right[k] = right[k] + ratio(k - 1) * right[k - 1]
        x = right[nodes - 1] * scale(nodes - 1)
        give(slabs - 1, 1, x)
        for k in range(nodes - 2, -1, -1):
            x = right[k] * scale(k) + ratio(k) * x
            give(k // 2, k % 2, x)
    if slices.rest:
        groups = slices.back_groups
        block = lane_block(groups, width)
        for p in range(slabs):
            for k in range(per):
                lined = back_rest_ref[pl.ds(p * groups * per + k, groups, stride=per), :]
                moved = moved_lanes(lined, k * width)
                packed = moved if k == 0 else jnp.where(block == k, moved, packed)
            start = slices.place[p] * slices.back_height + slices.back_packed_at
            back_ref[start : start + groups, :] = packed


def pick_kernel(slices, message_ref, values_ref):
    size = slices.image_rows
    for p in range(slices.slabs):
        start = slices.place[p] * slices.height + slices.images_at
        values_ref[p * size : (p + 1) * size, :] = message_ref[start : start + size, :]


def own_kernel(stay_ref, mask_ref, state_ref, ready_ref, cleared_ref):
    var_count, rows, pencils = state_ref.shape
    cells = var_count * rows
    count = pencils // LANES
    own_at = stay_at(rows, count, cells)[1]
    cells_at, kept_start, end = ready_at(rows, count, cells)
    solid = mask_ref[...] == 1
    for v in range(var_count):
        cleared_ref[v * rows : (v + 1) * rows, :] = jnp.where(solid, 0.0, state_ref[v])
    turn(ready_ref.at[cells_at:kept_start, :], cleared_ref[...])
    turn(
        ready_ref.at[:cells_at, :],
        full_dot(stay_ref[own_at : own_at + cells, :cells], cleared_ref[...]),
    )
    ready_ref[kept_start:end, :] = stay_ref[...]


def fill_kernel(slices, shape, ready_ref, below_ref, above_ref, *refs):
    *blocks, done_ref, filled_ref, edge_ref = refs
    var_count, rows, pencils = shape
    cells = var_count * rows
    count = pencils // LANES
    _, own_at, about_at, _ = stay_at(rows, count, cells)
    cells_at, kept_start, _ = ready_at(rows, count, cells)

    ghosts = LANES
    about = [ready_ref[kept_start + about_at : kept_start + about_at + ABOUT, :]]
    edge = var_count * count
    about += [ref[edge : edge + ABOUT, :] for ref in (below_ref, above_ref)]

    def known(k):
        return jnp.concatenate([x[k : k + 1] for x in about], axis=1)

    values = ghost_values(slices, blocks, known(COLUMN), 3)
    row, pencil = place_of(known(CELL).astype(jnp.int32), rows, pencils)
    at_row = lax.broadcasted_iota(jnp.int32, (rows, ghosts), 0) == row[:, :ghosts]
    spread = jnp.concatenate([jnp.where(at_row, value[:, :ghosts], 0.0) for value in values], axis=0)
    own = ready_ref[kept_start + own_at : kept_start + own_at + cells, :cells]
    both = jnp.concatenate([full_dot(own, spread), spread], axis=0)
    spots = marks((pencils, ghosts), 0, pencil[:, :ghosts])
    added = one_hot_dot(both, spots, ((1,), (1,)), 3)
    for t in range(count):
        here = slice(t * cells, (t + 1) * cells)
        there = slice(cells_at + t * cells, cells_at + (t + 1) * cells)
        done_ref[here, :] = ready_ref[here, :] + added[:cells, tile(t)]
        filled_ref[here, :] = ready_ref[there, :] + added[cells:, tile(t)]
    x_at, response_at, profile_at, edge_at, _ = done_at(rows, count, cells, var_count)
    none = jnp.zeros((8 - var_count, ghosts), jnp.float32)
    for k, (ref, wanted) in enumerate(((below_ref, rows - 1), (above_ref, 0))):
        here = slice((k + 1) * ghosts, (k + 2) * ghosts)
        at_edge = row[:, here] == wanted
        spread = [jnp.where(at_edge, value[:, here], 0.0) for value in values] + [none]
        spots = marks((pencils, ghosts), 0, pencil[:, here])
        turn(edge_ref, one_hot_dot(jnp.concatenate(spread, axis=0), spots, ((1,), (1,)), 3))
        for v in range(var_count):
            start = edge_at + (k * var_count + v) * count
            done_ref[start : start + count, :] = ref[v * count : (v + 1) * count, :] + slab_at(
                edge_ref, v, 8, count
            )

    def kept(which, i):
        start = kept_start + kept_at(which, i, rows, count)
        return ready_ref[start : start + count, :]

    def profile(k):
        start = kept_start + own_at - 40 + k
        return ready_ref[start : start + 1, :]

    def put(at, i, height, value):
        done_ref[pl.ds(at + i, count, stride=height), :] = value

    swept = []
    for i in range(1, rows - 1):
        speed = kept(3, i)
        here = [-speed * profile(i), -speed * profile(rows + i)]
        for v in range(var_count):
            row = v * rows + i
            own_slab = slab_at(done_ref, row, cells, count)
            here.append(slab_at(filled_ref, row, cells, count) - speed * own_slab)
        if swept:
            ratio = kept(0, i - 1)
            here = [x + ratio * y for x, y in zip(here, swept[-1])]
        swept.append(here)
    zero = jnp.zeros((count, LANES), jnp.float32)
    one = jnp.ones((count, LANES), jnp.float32)
    x = [zero] * (2 + var_count)
    first, last = zero, one
    for i in range(rows - 1, -1, -1):
        if 0 < i < rows - 1:
            ratio, inverse = kept(0, i), kept(2, i)
            first, last = kept(1, i) + ratio * first, ratio * last
            x = [inverse * y + ratio * z for y, z in zip(swept[i - 1], x)]
        if i == 0:
            first, last, x = one, zero, [zero] * (2 + var_count)
        for k, value in enumerate([first, last] + x[:2]):
            put(response_at + k * rows * count, i, rows, value)
        for v in range(var_count):
            put(x_at, v * rows + i, cells, x[2 + v])
    done_ref[profile_at : profile_at + 40, :] = ready_ref[
        kept_start + own_at - 40 : kept_start + own_at, :
    ]


def finish_kernel(
    slices, back_ref, done_ref, derivative_hbm, segment_hbm, derivative_ref, segment_ref, tail_ref, sems
):
    var_count, rows, pencils = segment_ref.shape
    count = pencils // LANES
    cells = var_count * rows
    x_at, response_at, profile_at, edge_at, _ = done_at(rows, count, cells, var_count)
    back_height, groups, per = slices.back_height, slices.back_groups, slices.per
    block = lane_block(max(groups, 1), slices.width)
    for m in range(slices.rest):
        packed = []
        for i in range(per):
            start = (m * per + i) * back_height + slices.back_packed_at
            packed.append(back_ref[start : start + groups, :])
        for k in range(per):
            for i in range(per):
                moved = moved_lanes(packed[i], (i - k) * slices.width)
                joined = moved if i == 0 else jnp.where(block == i, moved, joined)
            tail_ref[pl.ds(m * groups * per + k, groups, stride=per), :] = joined

    def got(functional, v, t):
        step, j = t // slices.slabs, t % slices.slabs
        if step < slices.full:
            start = j * back_height + slices.row(functional, step) + v
            return back_ref[start : start + 1, :]
        start = j * groups * per + functional * var_count + v
        return tail_ref[start : start + 1, :]

    lo_profile = done_ref[profile_at : profile_at + rows, :]
    hi_profile = done_ref[profile_at + rows : profile_at + 2 * rows, :]
    row_at = lax.broadcasted_iota(jnp.int32, (rows, LANES), 0)
    edges = profile_at + 2 * rows
    lo_edge = jnp.where(row_at == 0, done_ref[edges : edges + 1, :], 0.0)
    hi_edge = jnp.where(row_at == rows - 1, done_ref[edges + 1 : edges + 2, :], 0.0)

    def edge(k, v, t):
        start = edge_at + (k * var_count + v) * count + t
        return done_ref[start : start + 1, :]

    def response(k, t):
        start = response_at + (k * count + t) * rows
        return done_ref[start : start + rows, :]

    copies = []
    for v in range(var_count):
        for t in range(count):
            start = t * cells + v * rows
            lo, hi = got(2, v, t), got(3, v, t)
            derivative_ref[v, :, tile(t)] = (
                done_ref[start : start + rows, :]
                + (lo_profile * lo + hi_profile * hi)
                + (lo_edge * edge(0, v, t) + hi_edge * edge(1, v, t))
            )
            segment_ref[v, :, tile(t)] = (
                done_ref[x_at + start : x_at + start + rows, :]
                + (response(0, t) * got(0, v, t) + response(1, t) * got(1, v, t))
                + (response(2, t) * lo + response(3, t) * hi)
            )
        for which, (ref, hbm) in enumerate(
            ((derivative_ref, derivative_hbm), (segment_ref, segment_hbm))
        ):
            copies.append(
                pltpu.make_async_copy(ref.at[v], hbm.at[v], sems.at[which * var_count + v])
            )
            copies[-1].start()
    for copy in copies:
        copy.wait()


def call(kernel, outs, scratch, sems, args, near=(), far_out=(), limit=62):
    whole = pl.BlockSpec(memory_space=pltpu.VMEM)
    far = pl.BlockSpec(memory_space=pltpu.HBM)
    buffers = [
        pltpu.VMEM(s.shape, s.dtype) if hasattr(s, "dtype") else pltpu.VMEM(s, jnp.float32)
        for s in scratch
    ]
    buffers += [pltpu.SemaphoreType.DMA((size,)) for size in sems]
    return pl.pallas_call(
        kernel,
        out_shape=[jax.ShapeDtypeStruct(shape, jnp.float32) for shape in outs],
        in_specs=[whole if k in near else far for k in range(len(args))],
        out_specs=[far if k in far_out else whole for k in range(len(outs))],
        scratch_shapes=buffers,
        compiler_params=pltpu.CompilerParams(vmem_limit_bytes=limit * 2**20),
    )(*args)


def exchange(message, axis):
    groups = [middle_first(lax.axis_size(axis))]
    return lax.all_to_all(message, axis, 0, 0, axis_index_groups=groups, tiled=True)


def local(
    state,
    face_diffusion,
    courant,
    cell_mask,
    ghost_cell,
    ghost_owner,
    ghost_image,
    image_base,
    image_weight,
):
    var_count, rows, pencils = state.shape
    slabs, cross = lax.axis_size("pipe"), lax.axis_size("cross")
    count = pencils // LANES
    cells = var_count * rows
    images = image_base.shape[0]
    tables, at, constants = derivative_tables(slabs, rows, var_count)
    slices = Slices(slabs, count, cross, var_count, images)
    tables = jnp.asarray(tables)
    turned = (cells * count, LANES)
    stay = stay_at(rows, count, cells)[3]
    ready = (ready_at(rows, count, cells)[2], LANES)

    arguments = (
        face_diffusion,
        courant,
        tables,
        ghost_cell,
        ghost_owner,
        ghost_image,
        cell_mask,
        image_base,
        image_weight,
        state,
    )
    buffers = list(arguments)
    buffers[2] = jax.ShapeDtypeStruct(tables.shape[1:], jnp.float32)
    edge = (-(-(var_count * count + ABOUT) // 8) * 8, LANES)
    message, stay, up, down = call(
        functools.partial(prepare_kernel, slices, at),
        [(slabs * slices.height, LANES), (stay, LANES), edge, edge],
        buffers
        + [
            (stay, LANES),
            turned,
            (rows * count, LANES),
            (rows * count, LANES),
            (2 * rows * count, LANES),
            jax.ShapeDtypeStruct((pencils, images), jnp.bfloat16),
            (2 * rows, pencils),
            (40 * count, LANES),
            (2 * rows, -(-count // 8) * 8, LANES),
            (cells, pencils),
            (max(slices.rest, 1) * max(slices.groups, 1) * slices.per, LANES),
        ],
        [len(arguments), 1],
        arguments,
        far_out=(1,),
    )
    message = exchange(message, "pipe")
    forward = [(i, i + 1) for i in range(slabs - 1)]
    below = lax.ppermute(up, "pipe", forward)
    above = lax.ppermute(down, "pipe", [(j, i) for i, j in forward])
    (ready,) = call(
        own_kernel,
        [ready],
        [(cells, pencils)],
        [],
        (stay, cell_mask, state),
        near=range(3),
        limit=48,
    )
    (image_values,) = call(
        functools.partial(pick_kernel, slices),
        [(slabs * slices.image_rows, LANES)],
        [],
        [],
        (message,),
        near=(0,),
        limit=24,
    )
    blocks = [image_values] + [
        lax.ppermute(image_values, "cross", [(i, i ^ u) for i in range(cross)])
        for u in range(1, cross)
    ]

    factored, below, above = lax.optimization_barrier((message, below, above))
    rest, chain = call(
        functools.partial(chain_kernel, slices),
        [(slabs * max(slices.groups, 1) * slices.per, LANES), (2 * slabs * 16, LANES)],
        [],
        [],
        (factored,),
        near=(0,),
        limit=24,
    )
    (back,) = call(
        functools.partial(solve_kernel, slices, pencils, constants),
        [(slabs * slices.back_height, LANES)],
        [
            (slabs * slices.chunk * 48, LANES),
            (slabs * max(slices.back_groups, 1) * slices.per, LANES),
        ],
        [],
        (message, rest, chain, *blocks),
        near=range(3 + cross),
        limit=24,
    )
    back = exchange(back, "pipe")
    (done,) = call(
        functools.partial(fill_kernel, slices, state.shape),
        [(done_at(rows, count, cells, var_count)[4], LANES)],
        [turned, (8 * count, LANES)],
        [],
        (ready, below, above, *blocks),
        near=range(3 + cross),
        limit=48,
    )
    return tuple(
        call(
            functools.partial(finish_kernel, slices),
            [state.shape, state.shape],
            [
                state.shape,
                state.shape,
                (max(slices.rest, 1) * max(slices.back_groups, 1) * slices.per, LANES),
            ],
            [2 * var_count],
            (back, done),
            near=range(2),
            far_out=(0, 1),
            limit=48,
        )
    )


def solution(mesh):
    in_specs = (
        P(None, "pipe", "cross"),
        P("pipe", "cross"),
        P("pipe", "cross"),
        P("pipe", "cross"),
        P(("pipe", "cross")),
        P(("pipe", "cross")),
        P(("pipe", "cross")),
        P(("pipe", "cross")),
        P(None, ("pipe", "cross")),
    )
    out_specs = (P(None, "pipe", "cross"), P(None, "pipe", "cross"))
    return jax.shard_map(local, mesh=mesh, in_specs=in_specs, out_specs=out_specs, check_vma=False)
```

```python
import functools

import numpy as np
import jax
import jax.numpy as jnp
from jax import lax
from jax.experimental import pallas as pl
from jax.experimental.pallas import tpu as pltpu
from jax.sharding import PartitionSpec as P

LINE = 96
LANES = 128
REFLECT = (1.0, -1.0, -1.0, -1.0, 1.0)

Z_UP, Z_DOWN, ROW_FIRST, ROW_LAST, RIGHT_FIRST, RIGHT_LAST = range(6)
LINK_IN, MARGIN_FIRST, MARGIN_LAST, LINK_UP, FIRST_LO, FIRST_HI, LAST_LO, LAST_HI, FIRST_EDGE, LAST_EDGE = range(10)
COEFFICIENTS = 10
CELL, COLUMN, WEIGHT_FIRST, WEIGHT_LAST = range(4)
ABOUT = 4


def derivative_tables(slabs, rows, var_count):
    total = slabs * rows
    A = np.eye(total)
    B = np.zeros((total, total))
    for i in range(2, total - 2):
        A[i, i - 1] = A[i, i + 1] = 1.0 / 3.0
        B[i, i + 1], B[i, i - 1] = 7.0 / 9.0, -7.0 / 9.0
        B[i, i + 2], B[i, i - 2] = 1.0 / 36.0, -1.0 / 36.0
    for i in (1, total - 2):
        A[i, i - 1] = A[i, i + 1] = 0.25
        B[i, i + 1], B[i, i - 1] = 0.75, -0.75
    B[0, :3] = (-1.5, 2.0, -0.5)
    B[-1, -3:] = (0.5, -2.0, 1.5)
    inverse = np.linalg.inv(A)
    M = inverse @ B

    cells = var_count * rows
    own_at, reduce_at, adjoint_at, profile_at = 0, cells, cells + 32, cells + 72
    tables = np.zeros((slabs, cells + 112, LANES))
    carry_up, carry_down = np.zeros(slabs), np.zeros(slabs)
    ups, downs = np.zeros((slabs, rows)), np.zeros((slabs, rows))
    for p in range(slabs):
        table = tables[p]
        base = p * rows
        here = slice(base, base + rows)
        own = M[here, here]
        lo, hi, lo_edge, hi_edge = (np.zeros(rows) for _ in range(4))
        weight_up, weight_down = np.zeros(rows), np.zeros(rows)
        if p > 0:
            lo = inverse[here, base - 8] / inverse[base + 1, base - 8]
            lo_edge[0] = M[base, base - 1] - lo[0] * M[base + 1, base - 1]
            weight_down = M[base - 2, here]
        if p > 1:
            k = base - rows - 8
            carry_up[p] = inverse[base + 1, k] / inverse[base - rows + 1, k]
        if p < slabs - 1:
            k = base + rows + 8
            hi = inverse[here, k] / inverse[base + rows - 2, k]
            hi_edge[-1] = M[base + rows - 1, base + rows] - hi[-1] * M[base + rows - 2, base + rows]
            weight_up = M[base + rows + 1, here]
        if p < slabs - 2:
            k = base + 2 * rows + 8
            carry_down[p] = inverse[base + rows - 2, k] / inverse[base + 2 * rows - 2, k]
        for v in range(var_count):
            at = slice(v * rows, (v + 1) * rows)
            table[own_at + v * rows : own_at + (v + 1) * rows, at] = own
        table[reduce_at : reduce_at + rows] = weight_up[:, None]
        table[reduce_at + rows : reduce_at + 2 * rows] = weight_down[:, None]
        table[adjoint_at : adjoint_at + rows, :rows] = own.T
        table[adjoint_at + rows : adjoint_at + 2 * rows, rows : 2 * rows] = own.T
        more = adjoint_at + 2 * rows
        table[more, :rows] = lo
        table[more + 1, :rows] = hi
        table[more + 2, rows : 2 * rows] = lo
        table[more + 3, rows : 2 * rows] = hi
        table[more + 4, 0] = lo_edge[0]
        table[more + 5, 2 * rows - 1] = hi_edge[-1]
        table[profile_at : profile_at + rows] = lo[:, None]
        table[profile_at + rows : profile_at + 2 * rows] = hi[:, None]
        table[profile_at + 2 * rows] = lo_edge[0]
        table[profile_at + 2 * rows + 1] = hi_edge[-1]
        ups[p], downs[p] = weight_up, weight_down
    at = (own_at, reduce_at, adjoint_at, profile_at)
    return tables.astype(np.float32), at, (carry_up, carry_down, ups, downs)


def split(x, parts):
    pieces = []
    for _ in range(parts):
        piece = x.astype(jnp.bfloat16)
        pieces.append(piece)
        x = x - piece.astype(jnp.float32)
    return pieces


def one_hot_dot(x, one_hot, contract, parts):
    found = lax.dot_general(
        jnp.concatenate(split(x, parts), axis=0),
        one_hot,
        (contract, ((), ())),
        preferred_element_type=jnp.float32,
    )
    size = x.shape[0]
    pieces = [found[k * size : (k + 1) * size] for k in range(parts)]
    return sum(pieces[-2::-1], pieces[-1])


def full_dot(a, b):
    return jnp.dot(a, b, precision=lax.Precision.HIGHEST, preferred_element_type=jnp.float32)


def marks(shape, axis, values):
    return jnp.where(lax.broadcasted_iota(jnp.int32, shape, axis) == values, 1.0, 0.0).astype(
        jnp.bfloat16
    )


def place_of(cell, rows, pencils):
    row = jnp.zeros_like(cell)
    for k in range(1, rows):
        row += (cell >= k * pencils).astype(jnp.int32)
    return row, cell - row * pencils


def tile(t):
    return slice(t * LANES, (t + 1) * LANES)


def turn(ref, x):
    height, pencils = x.shape
    for t in range(pencils // LANES):
        ref[t * height : (t + 1) * height, :] = x[:, tile(t)]


def slab_at(ref, row, height, count):
    return ref[pl.ds(row, count, stride=height), :]


def put_slab(ref, row, height, count, value):
    ref[pl.ds(row, count, stride=height), :] = value


def kept_at(which, i, rows, count):
    return (which * rows + i) * (-(-count // 8) * 8)


def stay_at(rows, count, cells):
    kept = kept_at(4, 0, rows, count) + 40
    return kept, kept, kept + cells, kept + cells + 8


def ready_at(rows, count, cells):
    kept = 2 * cells * count
    return cells * count, kept, kept + stay_at(rows, count, cells)[3]


def done_at(rows, count, cells, var_count):
    x = cells * count
    response = 2 * x
    profile = response + 4 * rows * count
    return x, response, profile, profile + 40, profile + 40 + 2 * var_count * count


def fetch(sources, targets, sems):
    copies = [
        pltpu.make_async_copy(source, target, sems.at[k])
        for k, (source, target) in enumerate(zip(sources, targets))
    ]
    for copy in copies:
        copy.start()
    return copies


def middle_first(slabs):
    return sorted(range(slabs), key=lambda p: (abs(2 * p - slabs + 1), p))


class Slices:
    def __init__(self, slabs, count, cross, var_count, images):
        rest = count % slabs
        order = middle_first(slabs)
        self.place = [order.index(p) for p in range(slabs)]
        self.slabs, self.count, self.cross, self.var_count = slabs, count, cross, var_count
        self.image_rows = var_count * images // LANES
        shared = rest > 0 and slabs % rest == 0 and LANES % (slabs // rest) == 0
        self.full = count // slabs if shared else -(-count // slabs)
        self.rest = rest if shared else 0
        self.per = slabs // rest if shared else 1
        self.width = LANES // self.per
        self.chunk = self.full + (1 if shared else 0)
        self.lines, self.back_lines = 6 * var_count + COEFFICIENTS, 4 * var_count
        self.groups, self.back_groups = (self.group_count(n) for n in (self.lines, self.back_lines))
        self.meta_at = self.lines * self.full
        self.packed_at = self.meta_at + ABOUT
        self.images_at = self.packed_at + self.groups
        self.height = -(-(self.images_at + self.image_rows) // 8) * 8
        self.back_packed_at = self.back_lines * self.full
        self.back_height = -(-(self.back_packed_at + self.back_groups) // 8) * 8

    def group_count(self, lines):
        return -(-lines // self.per) if self.rest else 0

    def row(self, functional, t):
        return (functional * self.full + t) * self.var_count

    def coefficient_row(self, which, t):
        return 6 * self.full * self.var_count + which * self.full + t

    def tiles_at(self, t):
        return t * self.slabs, min(self.count, (t + 1) * self.slabs)


def lane_block(rows, width):
    return lax.broadcasted_iota(jnp.int32, (rows, LANES), 1) // width


def moved_lanes(x, by):
    by %= LANES
    return x if by == 0 else pltpu.roll(x, by, 1)


def image_lines(x, row, pick_ref, weight_ref, rows, var_count):
    pencils, images = pick_ref.shape
    row_at = lax.broadcasted_iota(jnp.int32, (rows, images), 0)
    lower, upper = row_at == row, row_at == row + 1
    total = [jnp.zeros((rows, images), jnp.float32) for _ in range(var_count)]
    pieces = jnp.concatenate(split(x, 2), axis=0)
    for corner, shift in enumerate((0, 1, LINE, LINE + 1)):
        moved = pieces if shift == 0 else pltpu.roll(pieces, pencils - shift, 1)
        found = jnp.dot(moved, pick_ref[...], preferred_element_type=jnp.float32)
        found = found[: var_count * rows] + found[var_count * rows :]
        weight = jnp.where(lower, weight_ref[corner : corner + 1], 0.0) + jnp.where(
            upper, weight_ref[corner + 4 : corner + 5], 0.0
        )
        for v in range(var_count):
            total[v] += found[v * rows : (v + 1) * rows] * weight
    lines = []
    for v in range(var_count):
        value = jnp.sum(total[v], axis=0, keepdims=True)
        lines += [value[:, tile(t)] for t in range(images // LANES)]
    return jnp.concatenate(lines, axis=0)


def ghost_values(slices, blocks, column, parts):
    per = slices.image_rows // slices.var_count
    slabs, cross = slices.slabs, slices.cross
    ghosts = column.shape[1]
    images = per * LANES
    owner = ((column + 0.5) * (1.0 / images)).astype(jnp.int32)
    image = column.astype(jnp.int32) - owner * images
    across = lax.axis_index("cross")
    values = [
        jnp.concatenate(
            [
                jnp.concatenate(
                    [
                        block[pl.ds(v * per + t, slabs, stride=slices.image_rows), :]
                        for t in range(per)
                    ],
                    axis=1,
                )
                for block in blocks
            ],
            axis=0,
        )
        for v in range(slices.var_count)
    ]
    pick = marks((per * LANES, ghosts), 0, image)
    found = one_hot_dot(jnp.concatenate(values, axis=0), pick, ((1,), (0,)), parts)
    devices = slabs * cross
    at = lax.broadcasted_iota(jnp.int32, (devices, ghosts), 0)
    mine = (at % slabs) * cross + (across ^ (at // slabs)) == owner
    return [
        reflect
        * jnp.sum(
            jnp.where(mine, found[v * devices : (v + 1) * devices], 0.0), axis=0, keepdims=True
        )
        for v, reflect in enumerate(REFLECT)
    ]


def prepare_kernel(
    slices,
    at,
    face_hbm,
    courant_hbm,
    tables_hbm,
    cell_hbm,
    owner_hbm,
    image_hbm,
    mask_hbm,
    base_hbm,
    corner_hbm,
    state_hbm,
    message_ref,
    stay_hbm,
    up_ref,
    down_ref,
    face_ref,
    courant_ref,
    table_ref,
    cell_ref,
    owner_ref,
    image_ref,
    mask_ref,
    base_ref,
    corner_ref,
    state_ref,
    stay_ref,
    turned_ref,
    face_turned_ref,
    courant_turned_ref,
    pair_ref,
    pick_ref,
    matrix_ref,
    adjoint_ref,
    weight_ref,
    cleared_ref,
    rest_ref,
    sems,
    stay_sem,
):
    var_count, rows, pencils = state_ref.shape
    cells = var_count * rows
    count = pencils // LANES
    ghosts = cell_ref.shape[0]
    padded = -(-count // 8) * 8
    p = lax.axis_index("pipe")
    slabs, height = slices.slabs, slices.height
    lines = slices.groups * slices.per
    own_at, reduce_at, adjoint_at, profile_at = at
    copies = fetch(
        (
            face_hbm,
            courant_hbm,
            tables_hbm.at[p],
            cell_hbm,
            owner_hbm,
            image_hbm,
            base_hbm,
            corner_hbm,
            mask_hbm,
            state_hbm,
        ),
        (
            face_ref,
            courant_ref,
            table_ref,
            cell_ref,
            owner_ref,
            image_ref,
            base_ref,
            corner_ref,
            mask_ref,
            state_ref,
        ),
        sems,
    )
    kept, own, about_at, _ = stay_at(rows, count, cells)

    def send(line, rows_at, slab):
        for t, row_at in enumerate(rows_at):
            start, end = slices.tiles_at(t)
            message_ref[pl.ds(row_at, end - start, stride=height), :] = slab[start:end]
        for m in range(slices.rest):
            tail = slices.full * slabs + m
            rest_ref[m * lines + line : m * lines + line + 1, :] = slab[tail : tail + 1]

    def send_value(functional, v, slab):
        rows_at = [slices.row(functional, t) + v for t in range(slices.full)]
        send(functional * var_count + v, rows_at, slab)

    def send_coefficient(which, slab):
        rows_at = [slices.coefficient_row(which, t) for t in range(slices.full)]
        send(6 * var_count + which, rows_at, slab)

    for copy in copies[:8]:
        copy.wait()
    image_row, image_pencil = place_of(base_ref[...].reshape(1, -1), rows, pencils)
    pick_ref[...] = marks(pick_ref.shape, 0, image_pencil)
    turn(face_turned_ref, face_ref[...])

    def face(i):
        return slab_at(face_turned_ref, i, rows, count)

    link = face(0)
    margin = jnp.ones_like(link)
    first_margin = margin
    to_up, to_first = [None] * rows, [None] * rows
    for i in range(1, rows - 1):
        above = face(i)
        inverse = 1.0 / (link + margin + above)
        low, up = link * inverse, above * inverse
        to_up[i], to_first[i] = up, low
        for k, part in enumerate((up, low, inverse)):
            start = kept_at(k, i, rows, count)
            stay_ref[start : start + count, :] = part
        first_margin += low * margin
        link = link * up
        margin = 1.0 + margin * up
    send_coefficient(LINK_IN, link)
    send_coefficient(MARGIN_FIRST, first_margin)
    send_coefficient(MARGIN_LAST, margin)
    send_coefficient(LINK_UP, jnp.where(p == slabs - 1, 0.0, face(rows - 1)))

    zero, one = jnp.zeros_like(margin), jnp.ones_like(margin)
    first, last = [None] * rows, [None] * rows
    first[0], first[rows - 1], last[0], last[rows - 1] = one, zero, zero, one
    for i in range(rows - 2, 0, -1):
        first[i] = to_first[i] + to_up[i] * first[i + 1]
        last[i] = to_up[i] * last[i + 1]
    turn(courant_turned_ref, courant_ref[...])
    for i in range(rows):
        speed = slab_at(courant_turned_ref, i, rows, count)
        start = kept_at(3, i, rows, count)
        stay_ref[start : start + count, :] = speed
        put_slab(pair_ref, i, 2 * rows, count, first[i] * speed)
        put_slab(pair_ref, rows + i, 2 * rows, count, last[i] * speed)
    for t in range(count):
        matrix_ref[:, tile(t)] = pair_ref[t * 2 * rows : (t + 1) * 2 * rows, :]
    stay_ref[kept - 40 : kept, :] = table_ref[profile_at : profile_at + 40, :]
    stay_ref[own : own + cells, :] = table_ref[own_at : own_at + cells, :]
    turn(
        adjoint_ref, full_dot(table_ref[adjoint_at : adjoint_at + 40, : 2 * rows], matrix_ref[...])
    )
    for k in range(6):
        send_coefficient(FIRST_LO + k, slab_at(adjoint_ref, 2 * rows + k, 40, count))
    weight_ref[:, padded - 8 :, :] = jnp.zeros((2 * rows, 8, LANES), jnp.float32)
    for i, share in enumerate(first + last):
        weight_ref[i, :count, :] = share - slab_at(adjoint_ref, i, 40, count)

    row, pencil = place_of(cell_ref[...].reshape(1, ghosts), rows, pencils)
    lane_tile = jnp.right_shift(pencil, 7)
    lane_marks = marks((LANES, ghosts), 0, pencil - lane_tile * LANES)
    picked = one_hot_dot(
        weight_ref[...].reshape(2 * rows * padded, LANES), lane_marks, ((1,), (0,)), 2
    ).reshape(2, rows, padded, ghosts)
    at_cell = (lax.broadcasted_iota(jnp.int32, (rows, padded, ghosts), 0) == row[None]) & (
        lax.broadcasted_iota(jnp.int32, (rows, padded, ghosts), 1) == lane_tile[None]
    )

    def at_ghosts(values):
        return jnp.sum(jnp.sum(jnp.where(at_cell, values, 0.0), axis=0), axis=0, keepdims=True)

    about = jnp.concatenate(
        [
            cell_ref[...].reshape(1, ghosts).astype(jnp.float32),
            (owner_ref[...] * base_ref.shape[0] + image_ref[...])
            .reshape(1, ghosts)
            .astype(jnp.float32),
            at_ghosts(picked[0]),
            at_ghosts(picked[1]),
        ],
        axis=0,
    )
    for j in range(slabs):
        start = j * height + slices.meta_at
        message_ref[start : start + ABOUT, :] = about
    stay_ref[about_at : about_at + ABOUT, :] = about
    edge = var_count * count
    for ref in (up_ref, down_ref):
        ref[edge : edge + ABOUT, :] = about
    staying = pltpu.make_async_copy(stay_ref, stay_hbm, stay_sem.at[0])
    staying.start()
    for copy in copies[8:]:
        copy.wait()
    values = image_lines(
        state_ref[...].reshape(cells, pencils),
        image_row,
        pick_ref,
        corner_ref,
        rows,
        var_count,
    )
    for j in range(slabs):
        start = j * height + slices.images_at
        message_ref[start : start + slices.image_rows, :] = values
    solid = mask_ref[...] == 1
    for v in range(var_count):
        here = slice(v * rows, (v + 1) * rows)
        cleared_ref[here, :] = jnp.where(solid, 0.0, state_ref[v])
    turn(turned_ref, cleared_ref[...])
    for group in (range(0, 3), range(3, var_count)):
        sums = {v: [zero] * 4 for v in group}
        for i in range(rows):
            up, down = reduce_at + i, reduce_at + rows + i
            weights = (
                table_ref[up : up + 1, :],
                table_ref[down : down + 1, :],
                weight_ref[i, :count, :],
                weight_ref[rows + i, :count, :],
            )
            for v in group:
                cell = slab_at(turned_ref, v * rows + i, cells, count)
                if i == 0:
                    send_value(ROW_FIRST, v, cell)
                    down_ref[v * count : (v + 1) * count, :] = cell
                if i == rows - 1:
                    send_value(ROW_LAST, v, cell)
                    up_ref[v * count : (v + 1) * count, :] = cell
                sums[v] = [x + weight * cell for x, weight in zip(sums[v], weights)]
        for v in group:
            for functional, total in zip((Z_UP, Z_DOWN, RIGHT_FIRST, RIGHT_LAST), sums[v]):
                send_value(functional, v, total)

    block = lane_block(max(slices.groups, 1), slices.width)
    for m in range(slices.rest):
        lined = [
            rest_ref[pl.ds(m * lines + k, slices.groups, stride=slices.per), :]
            for k in range(slices.per)
        ]
        for i in range(slices.per):
            packed = lined[0]
            for k in range(slices.per):
                moved = moved_lanes(lined[k], (k - i) * slices.width)
                packed = moved if k == 0 else jnp.where(block == k, moved, packed)
            start = (m * slices.per + i) * height + slices.packed_at
            message_ref[start : start + slices.groups, :] = packed
    staying.wait()


def chain_kernel(slices, message_ref, rest_ref, chain_ref):
    slabs, chunk, full = slices.slabs, slices.chunk, slices.full
    height, per, width = slices.height, slices.per, slices.width
    if slices.rest:
        for p in range(slabs):
            start = slices.place[p] * height + slices.packed_at
            packed = message_ref[start : start + slices.groups, :]
            for k in range(per):
                rest_ref[pl.ds(p * slices.groups * per + k, slices.groups, stride=per), :] = (
                    moved_lanes(packed, -k * width)
                )
    else:
        rest_ref[...] = jnp.zeros_like(rest_ref)

    def sent(p, which):
        start = slices.place[p] * height + slices.coefficient_row(which, 0)
        slab = message_ref[start : start + full, :]
        if slices.rest:
            start = p * slices.groups * per + 6 * slices.var_count + which
            slab = jnp.concatenate([slab, rest_ref[start : start + 1, :]], axis=0)
        return slab

    nodes = 2 * slabs
    margin = sent(0, MARGIN_FIRST)
    for k in range(nodes):
        link = sent(k // 2, LINK_UP if k % 2 else LINK_IN)
        inverse = 1.0 / (margin + link)
        ratio = link * inverse
        chain_ref[16 * k : 16 * k + chunk, :] = ratio
        chain_ref[16 * k + 8 : 16 * k + 8 + chunk, :] = inverse
        if k < nodes - 1:
            following = sent((k + 1) // 2, MARGIN_FIRST if k % 2 else MARGIN_LAST)
            margin = following + margin * ratio


def solve_kernel(slices, pencils, constants, message_ref, rest_ref, chain_ref, *refs):
    *blocks, back_ref, ghost_ref, back_rest_ref = refs
    slabs, var_count, chunk, full = slices.slabs, slices.var_count, slices.chunk, slices.full
    height, per, width = slices.height, slices.per, slices.width
    along = lax.axis_index("pipe")
    me = sum(jnp.where(along == p, slices.place[p], 0) for p in range(slabs))

    def meta(p, k):
        start = slices.place[p] * height + slices.meta_at + k
        return message_ref[start : start + 1, :]

    def meta_all(k):
        return jnp.concatenate([meta(p, k) for p in range(slabs)], axis=1)

    carry_up, carry_down, ups, downs = constants
    values = ghost_values(slices, blocks, meta_all(COLUMN), 2)
    rows = ups.shape[1]
    row_of, pencil_of = place_of(meta_all(CELL).astype(jnp.int32), rows, pencils)
    ghosts = LANES
    place = lax.broadcasted_iota(jnp.int32, (chunk * LANES, ghosts), 0)
    slot, lane = place // LANES, place % LANES
    pencil_at = jnp.where(
        slot < full,
        (me + slot * slabs) * LANES + lane,
        (full * slabs + me // per) * LANES + (me % per) * width + lane,
    )
    none = jnp.zeros((8 - var_count, ghosts), jnp.float32)
    for p in range(slabs):
        row = row_of[:, tile(p)]
        up = down = jnp.zeros((1, ghosts), jnp.float32)
        for i in range(rows):
            up = jnp.where(row == i, float(ups[p, i]), up)
            down = jnp.where(row == i, float(downs[p, i]), down)
        weights = (
            up,
            down,
            jnp.where(row == 0, 1.0, 0.0),
            jnp.where(row == rows - 1, 1.0, 0.0),
            meta(p, WEIGHT_FIRST),
            meta(p, WEIGHT_LAST),
        )
        here = jnp.concatenate([value[:, tile(p)] for value in values] + [none], axis=0)
        shares = jnp.concatenate([here * weight for weight in weights], axis=0)
        spots = jnp.where(pencil_at == pencil_of[:, tile(p)], 1.0, 0.0)
        share = one_hot_dot(shares, spots.astype(jnp.bfloat16), ((1,), (1,)), 2)
        for t in range(chunk):
            start = (p * chunk + t) * 48
            ghost_ref[start : start + 48, :] = share[:, tile(t)]

    nodes = 2 * slabs
    zero = jnp.zeros((var_count, LANES), jnp.float32)
    for t in range(chunk):

        def value(p, functional):
            if t < full:
                start = slices.place[p] * height + slices.row(functional, t)
                sent = message_ref[start : start + var_count, :]
            else:
                start = p * slices.groups * per + functional * var_count
                sent = rest_ref[start : start + var_count, :]
            start = (p * chunk + t) * 48 + functional * 8
            return sent + ghost_ref[start : start + var_count, :]

        def coefficient(p, which):
            if t < full:
                start = slices.place[p] * height + slices.coefficient_row(which, t)
                return message_ref[start : start + 1, :]
            start = p * slices.groups * per + 6 * var_count + which
            return rest_ref[start : start + 1, :]

        def give(p, functional, block):
            if t < full:
                start = slices.place[p] * slices.back_height + slices.row(functional, t)
                back_ref[start : start + var_count, :] = block
            else:
                start = p * slices.back_groups * per + functional * var_count
                back_rest_ref[start : start + var_count, :] = block

        def ratio(k):
            return chain_ref[16 * k + t : 16 * k + t + 1, :]

        def scale(k):
            return chain_ref[16 * k + 8 + t : 16 * k + 9 + t, :]

        lo, hi, below, above = ([zero] * slabs for _ in range(4))
        for p in range(1, slabs):
            lo[p] = value(p - 1, Z_UP) + float(carry_up[p]) * lo[p - 1]
            below[p] = value(p - 1, ROW_LAST)
        for p in range(slabs - 2, -1, -1):
            hi[p] = value(p + 1, Z_DOWN) + float(carry_down[p]) * hi[p + 1]
            above[p] = value(p + 1, ROW_FIRST)
        right = []
        for p in range(slabs):
            right.append(
                value(p, RIGHT_FIRST)
                - coefficient(p, FIRST_LO) * lo[p]
                - coefficient(p, FIRST_HI) * hi[p]
                - coefficient(p, FIRST_EDGE) * below[p]
            )
            right.append(
                value(p, RIGHT_LAST)
                - coefficient(p, LAST_LO) * lo[p]
                - coefficient(p, LAST_HI) * hi[p]
                - coefficient(p, LAST_EDGE) * above[p]
            )
            give(p, 2, lo[p])
            give(p, 3, hi[p])
        for k in range(1, nodes):
            right[k] = right[k] + ratio(k - 1) * right[k - 1]
        x = right[nodes - 1] * scale(nodes - 1)
        give(slabs - 1, 1, x)
        for k in range(nodes - 2, -1, -1):
            x = right[k] * scale(k) + ratio(k) * x
            give(k // 2, k % 2, x)
    if slices.rest:
        groups = slices.back_groups
        block = lane_block(groups, width)
        for p in range(slabs):
            for k in range(per):
                lined = back_rest_ref[pl.ds(p * groups * per + k, groups, stride=per), :]
                moved = moved_lanes(lined, k * width)
                packed = moved if k == 0 else jnp.where(block == k, moved, packed)
            start = slices.place[p] * slices.back_height + slices.back_packed_at
            back_ref[start : start + groups, :] = packed


def pick_kernel(slices, message_ref, values_ref):
    size = slices.image_rows
    for p in range(slices.slabs):
        start = slices.place[p] * slices.height + slices.images_at
        values_ref[p * size : (p + 1) * size, :] = message_ref[start : start + size, :]


def own_kernel(stay_ref, mask_ref, state_ref, ready_ref, cleared_ref):
    var_count, rows, pencils = state_ref.shape
    cells = var_count * rows
    count = pencils // LANES
    own_at = stay_at(rows, count, cells)[1]
    cells_at, kept_start, end = ready_at(rows, count, cells)
    solid = mask_ref[...] == 1
    for v in range(var_count):
        cleared_ref[v * rows : (v + 1) * rows, :] = jnp.where(solid, 0.0, state_ref[v])
    turn(ready_ref.at[cells_at:kept_start, :], cleared_ref[...])
    turn(
        ready_ref.at[:cells_at, :],
        full_dot(stay_ref[own_at : own_at + cells, :cells], cleared_ref[...]),
    )
    ready_ref[kept_start:end, :] = stay_ref[...]


def fill_kernel(slices, shape, ready_ref, below_ref, above_ref, *refs):
    *blocks, done_ref, filled_ref, edge_ref = refs
    var_count, rows, pencils = shape
    cells = var_count * rows
    count = pencils // LANES
    _, own_at, about_at, _ = stay_at(rows, count, cells)
    cells_at, kept_start, _ = ready_at(rows, count, cells)

    ghosts = LANES
    about = [ready_ref[kept_start + about_at : kept_start + about_at + ABOUT, :]]
    edge = var_count * count
    about += [ref[edge : edge + ABOUT, :] for ref in (below_ref, above_ref)]

    def known(k):
        return jnp.concatenate([x[k : k + 1] for x in about], axis=1)

    values = ghost_values(slices, blocks, known(COLUMN), 3)
    row, pencil = place_of(known(CELL).astype(jnp.int32), rows, pencils)
    at_row = lax.broadcasted_iota(jnp.int32, (rows, ghosts), 0) == row[:, :ghosts]
    spread = jnp.concatenate([jnp.where(at_row, value[:, :ghosts], 0.0) for value in values], axis=0)
    own = ready_ref[kept_start + own_at : kept_start + own_at + cells, :cells]
    both = jnp.concatenate([full_dot(own, spread), spread], axis=0)
    spots = marks((pencils, ghosts), 0, pencil[:, :ghosts])
    added = one_hot_dot(both, spots, ((1,), (1,)), 3)
    for t in range(count):
        here = slice(t * cells, (t + 1) * cells)
        there = slice(cells_at + t * cells, cells_at + (t + 1) * cells)
        done_ref[here, :] = ready_ref[here, :] + added[:cells, tile(t)]
        filled_ref[here, :] = ready_ref[there, :] + added[cells:, tile(t)]
    x_at, response_at, profile_at, edge_at, _ = done_at(rows, count, cells, var_count)
    none = jnp.zeros((8 - var_count, ghosts), jnp.float32)
    for k, (ref, wanted) in enumerate(((below_ref, rows - 1), (above_ref, 0))):
        here = slice((k + 1) * ghosts, (k + 2) * ghosts)
        at_edge = row[:, here] == wanted
        spread = [jnp.where(at_edge, value[:, here], 0.0) for value in values] + [none]
        spots = marks((pencils, ghosts), 0, pencil[:, here])
        turn(edge_ref, one_hot_dot(jnp.concatenate(spread, axis=0), spots, ((1,), (1,)), 3))
        for v in range(var_count):
            start = edge_at + (k * var_count + v) * count
            done_ref[start : start + count, :] = ref[v * count : (v + 1) * count, :] + slab_at(
                edge_ref, v, 8, count
            )

    def kept(which, i):
        start = kept_start + kept_at(which, i, rows, count)
        return ready_ref[start : start + count, :]

    def profile(k):
        start = kept_start + own_at - 40 + k
        return ready_ref[start : start + 1, :]

    def put(at, i, height, value):
        done_ref[pl.ds(at + i, count, stride=height), :] = value

    swept = []
    for i in range(1, rows - 1):
        speed = kept(3, i)
        here = [-speed * profile(i), -speed * profile(rows + i)]
        for v in range(var_count):
            row = v * rows + i
            own_slab = slab_at(done_ref, row, cells, count)
            here.append(slab_at(filled_ref, row, cells, count) - speed * own_slab)
        if swept:
            ratio = kept(0, i - 1)
            here = [x + ratio * y for x, y in zip(here, swept[-1])]
        swept.append(here)
    zero = jnp.zeros((count, LANES), jnp.float32)
    one = jnp.ones((count, LANES), jnp.float32)
    x = [zero] * (2 + var_count)
    first, last = zero, one
    for i in range(rows - 1, -1, -1):
        if 0 < i < rows - 1:
            ratio, inverse = kept(0, i), kept(2, i)
            first, last = kept(1, i) + ratio * first, ratio * last
            x = [inverse * y + ratio * z for y, z in zip(swept[i - 1], x)]
        if i == 0:
            first, last, x = one, zero, [zero] * (2 + var_count)
        for k, value in enumerate([first, last] + x[:2]):
            put(response_at + k * rows * count, i, rows, value)
        for v in range(var_count):
            put(x_at, v * rows + i, cells, x[2 + v])
    done_ref[profile_at : profile_at + 40, :] = ready_ref[
        kept_start + own_at - 40 : kept_start + own_at, :
    ]


def finish_kernel(
    slices, back_ref, done_ref, derivative_hbm, segment_hbm, derivative_ref, segment_ref, tail_ref, sems
):
    var_count, rows, pencils = segment_ref.shape
    count = pencils // LANES
    cells = var_count * rows
    x_at, response_at, profile_at, edge_at, _ = done_at(rows, count, cells, var_count)
    back_height, groups, per = slices.back_height, slices.back_groups, slices.per
    block = lane_block(max(groups, 1), slices.width)
    for m in range(slices.rest):
        packed = []
        for i in range(per):
            start = (m * per + i) * back_height + slices.back_packed_at
            packed.append(back_ref[start : start + groups, :])
        for k in range(per):
            for i in range(per):
                moved = moved_lanes(packed[i], (i - k) * slices.width)
                joined = moved if i == 0 else jnp.where(block == i, moved, joined)
            tail_ref[pl.ds(m * groups * per + k, groups, stride=per), :] = joined

    def got(functional, v, t):
        step, j = t // slices.slabs, t % slices.slabs
        if step < slices.full:
            start = j * back_height + slices.row(functional, step) + v
            return back_ref[start : start + 1, :]
        start = j * groups * per + functional * var_count + v
        return tail_ref[start : start + 1, :]

    lo_profile = done_ref[profile_at : profile_at + rows, :]
    hi_profile = done_ref[profile_at + rows : profile_at + 2 * rows, :]
    row_at = lax.broadcasted_iota(jnp.int32, (rows, LANES), 0)
    edges = profile_at + 2 * rows
    lo_edge = jnp.where(row_at == 0, done_ref[edges : edges + 1, :], 0.0)
    hi_edge = jnp.where(row_at == rows - 1, done_ref[edges + 1 : edges + 2, :], 0.0)

    def edge(k, v, t):
        start = edge_at + (k * var_count + v) * count + t
        return done_ref[start : start + 1, :]

    def response(k, t):
        start = response_at + (k * count + t) * rows
        return done_ref[start : start + rows, :]

    copies = []
    for v in range(var_count):
        for t in range(count):
            start = t * cells + v * rows
            lo, hi = got(2, v, t), got(3, v, t)
            derivative_ref[v, :, tile(t)] = (
                done_ref[start : start + rows, :]
                + (lo_profile * lo + hi_profile * hi)
                + (lo_edge * edge(0, v, t) + hi_edge * edge(1, v, t))
            )
            segment_ref[v, :, tile(t)] = (
                done_ref[x_at + start : x_at + start + rows, :]
                + (response(0, t) * got(0, v, t) + response(1, t) * got(1, v, t))
                + (response(2, t) * lo + response(3, t) * hi)
            )
        for which, (ref, hbm) in enumerate(
            ((derivative_ref, derivative_hbm), (segment_ref, segment_hbm))
        ):
            copies.append(
                pltpu.make_async_copy(ref.at[v], hbm.at[v], sems.at[which * var_count + v])
            )
            copies[-1].start()
    for copy in copies:
        copy.wait()


def call(kernel, outs, scratch, sems, args, near=(), far_out=(), limit=62):
    whole = pl.BlockSpec(memory_space=pltpu.VMEM)
    far = pl.BlockSpec(memory_space=pltpu.HBM)
    buffers = [
        pltpu.VMEM(s.shape, s.dtype) if hasattr(s, "dtype") else pltpu.VMEM(s, jnp.float32)
        for s in scratch
    ]
    buffers += [pltpu.SemaphoreType.DMA((size,)) for size in sems]
    return pl.pallas_call(
        kernel,
        out_shape=[jax.ShapeDtypeStruct(shape, jnp.float32) for shape in outs],
        in_specs=[whole if k in near else far for k in range(len(args))],
        out_specs=[far if k in far_out else whole for k in range(len(outs))],
        scratch_shapes=buffers,
        compiler_params=pltpu.CompilerParams(vmem_limit_bytes=limit * 2**20),
    )(*args)


def exchange(message, axis):
    groups = [middle_first(lax.axis_size(axis))]
    return lax.all_to_all(message, axis, 0, 0, axis_index_groups=groups, tiled=True)


def local(
    state,
    face_diffusion,
    courant,
    cell_mask,
    ghost_cell,
    ghost_owner,
    ghost_image,
    image_base,
    image_weight,
):
    var_count, rows, pencils = state.shape
    slabs, cross = lax.axis_size("pipe"), lax.axis_size("cross")
    count = pencils // LANES
    cells = var_count * rows
    images = image_base.shape[0]
    tables, at, constants = derivative_tables(slabs, rows, var_count)
    slices = Slices(slabs, count, cross, var_count, images)
    tables = jnp.asarray(tables)
    turned = (cells * count, LANES)
    stay = stay_at(rows, count, cells)[3]
    ready = (ready_at(rows, count, cells)[2], LANES)

    arguments = (
        face_diffusion,
        courant,
        tables,
        ghost_cell,
        ghost_owner,
        ghost_image,
        cell_mask,
        image_base,
        image_weight,
        state,
    )
    buffers = list(arguments)
    buffers[2] = jax.ShapeDtypeStruct(tables.shape[1:], jnp.float32)
    edge = (-(-(var_count * count + ABOUT) // 8) * 8, LANES)
    message, stay, up, down = call(
        functools.partial(prepare_kernel, slices, at),
        [(slabs * slices.height, LANES), (stay, LANES), edge, edge],
        buffers
        + [
            (stay, LANES),
            turned,
            (rows * count, LANES),
            (rows * count, LANES),
            (2 * rows * count, LANES),
            jax.ShapeDtypeStruct((pencils, images), jnp.bfloat16),
            (2 * rows, pencils),
            (40 * count, LANES),
            (2 * rows, -(-count // 8) * 8, LANES),
            (cells, pencils),
            (max(slices.rest, 1) * max(slices.groups, 1) * slices.per, LANES),
        ],
        [len(arguments), 1],
        arguments,
        far_out=(1,),
    )
    message = exchange(message, "pipe")
    forward = [(i, i + 1) for i in range(slabs - 1)]
    below = lax.ppermute(up, "pipe", forward)
    above = lax.ppermute(down, "pipe", [(j, i) for i, j in forward])
    (ready,) = call(
        own_kernel,
        [ready],
        [(cells, pencils)],
        [],
        (stay, cell_mask, state),
        near=range(3),
        limit=48,
    )
    (image_values,) = call(
        functools.partial(pick_kernel, slices),
        [(slabs * slices.image_rows, LANES)],
        [],
        [],
        (message,),
        near=(0,),
        limit=24,
    )
    blocks = {0: image_values}
    step = cross // 2
    while step:
        route = [(i, i ^ step) for i in range(cross)]
        passed = {u ^ step: lax.ppermute(x, "cross", route) for u, x in blocks.items()}
        if step == cross // 2:
            passed, below, above = lax.optimization_barrier((passed, below, above))
        blocks.update(passed)
        step //= 2
    blocks = [blocks[u] for u in range(cross)]
    rest, chain = call(
        functools.partial(chain_kernel, slices),
        [(slabs * max(slices.groups, 1) * slices.per, LANES), (2 * slabs * 16, LANES)],
        [],
        [],
        (message,),
        near=(0,),
        limit=24,
    )
    (back,) = call(
        functools.partial(solve_kernel, slices, pencils, constants),
        [(slabs * slices.back_height, LANES)],
        [
            (slabs * slices.chunk * 48, LANES),
            (slabs * max(slices.back_groups, 1) * slices.per, LANES),
        ],
        [],
        (message, rest, chain, *blocks),
        near=range(3 + cross),
        limit=24,
    )
    back = exchange(back, "pipe")
    (done,) = call(
        functools.partial(fill_kernel, slices, state.shape),
        [(done_at(rows, count, cells, var_count)[4], LANES)],
        [turned, (8 * count, LANES)],
        [],
        (ready, below, above, *blocks),
        near=range(3 + cross),
        limit=48,
    )
    return tuple(
        call(
            functools.partial(finish_kernel, slices),
            [state.shape, state.shape],
            [
                state.shape,
                state.shape,
                (max(slices.rest, 1) * max(slices.back_groups, 1) * slices.per, LANES),
            ],
            [2 * var_count],
            (back, done),
            near=range(2),
            far_out=(0, 1),
            limit=48,
        )
    )


def solution(mesh):
    in_specs = (
        P(None, "pipe", "cross"),
        P("pipe", "cross"),
        P("pipe", "cross"),
        P("pipe", "cross"),
        P(("pipe", "cross")),
        P(("pipe", "cross")),
        P(("pipe", "cross")),
        P(("pipe", "cross")),
        P(None, ("pipe", "cross")),
    )
    out_specs = (P(None, "pipe", "cross"), P(None, "pipe", "cross"))
    return jax.shard_map(local, mesh=mesh, in_specs=in_specs, out_specs=out_specs, check_vma=False)
```

```python
import functools

import numpy as np
import jax
import jax.numpy as jnp
from jax import lax
from jax.experimental import pallas as pl
from jax.experimental.pallas import tpu as pltpu
from jax.sharding import PartitionSpec as P

LINE = 96
LANES = 128
REFLECT = (1.0, -1.0, -1.0, -1.0, 1.0)

Z_UP, Z_DOWN, ROW_FIRST, ROW_LAST, RIGHT_FIRST, RIGHT_LAST = range(6)
LINK_IN, MARGIN_FIRST, MARGIN_LAST, LINK_UP, FIRST_LO, FIRST_HI, LAST_LO, LAST_HI, FIRST_EDGE, LAST_EDGE = range(10)
COEFFICIENTS = 10
CELL, COLUMN, WEIGHT_FIRST, WEIGHT_LAST = range(4)
ABOUT = 4


def derivative_tables(slabs, rows, var_count):
    total = slabs * rows
    A = np.eye(total)
    B = np.zeros((total, total))
    for i in range(2, total - 2):
        A[i, i - 1] = A[i, i + 1] = 1.0 / 3.0
        B[i, i + 1], B[i, i - 1] = 7.0 / 9.0, -7.0 / 9.0
        B[i, i + 2], B[i, i - 2] = 1.0 / 36.0, -1.0 / 36.0
    for i in (1, total - 2):
        A[i, i - 1] = A[i, i + 1] = 0.25
        B[i, i + 1], B[i, i - 1] = 0.75, -0.75
    B[0, :3] = (-1.5, 2.0, -0.5)
    B[-1, -3:] = (0.5, -2.0, 1.5)
    inverse = np.linalg.inv(A)
    M = inverse @ B

    cells = var_count * rows
    own_at, reduce_at, adjoint_at, profile_at = 0, cells, cells + 32, cells + 72
    tables = np.zeros((slabs, cells + 112, LANES))
    carry_up, carry_down = np.zeros(slabs), np.zeros(slabs)
    ups, downs = np.zeros((slabs, rows)), np.zeros((slabs, rows))
    for p in range(slabs):
        table = tables[p]
        base = p * rows
        here = slice(base, base + rows)
        own = M[here, here]
        lo, hi, lo_edge, hi_edge = (np.zeros(rows) for _ in range(4))
        weight_up, weight_down = np.zeros(rows), np.zeros(rows)
        if p > 0:
            lo = inverse[here, base - 8] / inverse[base + 1, base - 8]
            lo_edge[0] = M[base, base - 1] - lo[0] * M[base + 1, base - 1]
            weight_down = M[base - 2, here]
        if p > 1:
            k = base - rows - 8
            carry_up[p] = inverse[base + 1, k] / inverse[base - rows + 1, k]
        if p < slabs - 1:
            k = base + rows + 8
            hi = inverse[here, k] / inverse[base + rows - 2, k]
            hi_edge[-1] = M[base + rows - 1, base + rows] - hi[-1] * M[base + rows - 2, base + rows]
            weight_up = M[base + rows + 1, here]
        if p < slabs - 2:
            k = base + 2 * rows + 8
            carry_down[p] = inverse[base + rows - 2, k] / inverse[base + 2 * rows - 2, k]
        for v in range(var_count):
            at = slice(v * rows, (v + 1) * rows)
            table[own_at + v * rows : own_at + (v + 1) * rows, at] = own
        table[reduce_at : reduce_at + rows] = weight_up[:, None]
        table[reduce_at + rows : reduce_at + 2 * rows] = weight_down[:, None]
        table[adjoint_at : adjoint_at + rows, :rows] = own.T
        table[adjoint_at + rows : adjoint_at + 2 * rows, rows : 2 * rows] = own.T
        more = adjoint_at + 2 * rows
        table[more, :rows] = lo
        table[more + 1, :rows] = hi
        table[more + 2, rows : 2 * rows] = lo
        table[more + 3, rows : 2 * rows] = hi
        table[more + 4, 0] = lo_edge[0]
        table[more + 5, 2 * rows - 1] = hi_edge[-1]
        table[profile_at : profile_at + rows] = lo[:, None]
        table[profile_at + rows : profile_at + 2 * rows] = hi[:, None]
        table[profile_at + 2 * rows] = lo_edge[0]
        table[profile_at + 2 * rows + 1] = hi_edge[-1]
        ups[p], downs[p] = weight_up, weight_down
    at = (own_at, reduce_at, adjoint_at, profile_at)
    return tables.astype(np.float32), at, (carry_up, carry_down, ups, downs)


def split(x, parts):
    pieces = []
    for _ in range(parts):
        piece = x.astype(jnp.bfloat16)
        pieces.append(piece)
        x = x - piece.astype(jnp.float32)
    return pieces


def one_hot_dot(x, one_hot, contract, parts):
    found = lax.dot_general(
        jnp.concatenate(split(x, parts), axis=0),
        one_hot,
        (contract, ((), ())),
        preferred_element_type=jnp.float32,
    )
    size = x.shape[0]
    pieces = [found[k * size : (k + 1) * size] for k in range(parts)]
    return sum(pieces[-2::-1], pieces[-1])


def full_dot(a, b):
    return jnp.dot(a, b, precision=lax.Precision.HIGHEST, preferred_element_type=jnp.float32)


def marks(shape, axis, values):
    return jnp.where(lax.broadcasted_iota(jnp.int32, shape, axis) == values, 1.0, 0.0).astype(
        jnp.bfloat16
    )


def place_of(cell, rows, pencils):
    row = jnp.zeros_like(cell)
    for k in range(1, rows):
        row += (cell >= k * pencils).astype(jnp.int32)
    return row, cell - row * pencils


def tile(t):
    return slice(t * LANES, (t + 1) * LANES)


def turn(ref, x):
    height, pencils = x.shape
    for t in range(pencils // LANES):
        ref[t * height : (t + 1) * height, :] = x[:, tile(t)]


def slab_at(ref, row, height, count):
    return ref[pl.ds(row, count, stride=height), :]


def put_slab(ref, row, height, count, value):
    ref[pl.ds(row, count, stride=height), :] = value


def kept_at(which, i, rows, count):
    return (which * rows + i) * (-(-count // 8) * 8)


def stay_at(rows, count, cells):
    kept = kept_at(4, 0, rows, count) + 40
    return kept, kept, kept + cells, kept + cells + 8


def ready_at(rows, count, cells):
    kept = 2 * cells * count
    return cells * count, kept, kept + stay_at(rows, count, cells)[3]


def done_at(rows, count, cells, var_count):
    x = cells * count
    response = 2 * x
    profile = response + 4 * rows * count
    return x, response, profile, profile + 40, profile + 40 + 2 * var_count * count


def fetch(sources, targets, sems):
    copies = [
        pltpu.make_async_copy(source, target, sems.at[k])
        for k, (source, target) in enumerate(zip(sources, targets))
    ]
    for copy in copies:
        copy.start()
    return copies


def middle_first(slabs):
    return sorted(range(slabs), key=lambda p: (abs(2 * p - slabs + 1), -p))


class Slices:
    def __init__(self, slabs, count, cross, var_count, images):
        rest = count % slabs
        order = middle_first(slabs)
        self.place = [order.index(p) for p in range(slabs)]
        self.slabs, self.count, self.cross, self.var_count = slabs, count, cross, var_count
        self.image_rows = var_count * images // LANES
        shared = rest > 0 and slabs % rest == 0 and LANES % (slabs // rest) == 0
        self.full = count // slabs if shared else -(-count // slabs)
        self.rest = rest if shared else 0
        self.per = slabs // rest if shared else 1
        self.width = LANES // self.per
        self.chunk = self.full + (1 if shared else 0)
        self.lines, self.back_lines = 6 * var_count + COEFFICIENTS, 4 * var_count
        self.groups, self.back_groups = (self.group_count(n) for n in (self.lines, self.back_lines))
        self.meta_at = self.lines * self.full
        self.packed_at = self.meta_at + ABOUT
        self.images_at = self.packed_at + self.groups
        self.height = -(-(self.images_at + self.image_rows) // 8) * 8
        self.back_packed_at = self.back_lines * self.full
        self.back_height = -(-(self.back_packed_at + self.back_groups) // 8) * 8

    def group_count(self, lines):
        return -(-lines // self.per) if self.rest else 0

    def row(self, functional, t):
        return (functional * self.full + t) * self.var_count

    def coefficient_row(self, which, t):
        return 6 * self.full * self.var_count + which * self.full + t

    def tiles_at(self, t):
        return t * self.slabs, min(self.count, (t + 1) * self.slabs)


def lane_block(rows, width):
    return lax.broadcasted_iota(jnp.int32, (rows, LANES), 1) // width


def moved_lanes(x, by):
    by %= LANES
    return x if by == 0 else pltpu.roll(x, by, 1)


def image_lines(x, row, pick_ref, weight_ref, rows, var_count):
    pencils, images = pick_ref.shape
    row_at = lax.broadcasted_iota(jnp.int32, (rows, images), 0)
    lower, upper = row_at == row, row_at == row + 1
    total = [jnp.zeros((rows, images), jnp.float32) for _ in range(var_count)]
    pieces = jnp.concatenate(split(x, 2), axis=0)
    for corner, shift in enumerate((0, 1, LINE, LINE + 1)):
        moved = pieces if shift == 0 else pltpu.roll(pieces, pencils - shift, 1)
        found = jnp.dot(moved, pick_ref[...], preferred_element_type=jnp.float32)
        found = found[: var_count * rows] + found[var_count * rows :]
        weight = jnp.where(lower, weight_ref[corner : corner + 1], 0.0) + jnp.where(
            upper, weight_ref[corner + 4 : corner + 5], 0.0
        )
        for v in range(var_count):
            total[v] += found[v * rows : (v + 1) * rows] * weight
    lines = []
    for v in range(var_count):
        value = jnp.sum(total[v], axis=0, keepdims=True)
        lines += [value[:, tile(t)] for t in range(images // LANES)]
    return jnp.concatenate(lines, axis=0)


def ghost_values(slices, blocks, column, parts):
    per = slices.image_rows // slices.var_count
    slabs, cross = slices.slabs, slices.cross
    ghosts = column.shape[1]
    images = per * LANES
    owner = ((column + 0.5) * (1.0 / images)).astype(jnp.int32)
    image = column.astype(jnp.int32) - owner * images
    across = lax.axis_index("cross")
    values = [
        jnp.concatenate(
            [
                jnp.concatenate(
                    [
                        block[pl.ds(v * per + t, slabs, stride=slices.image_rows), :]
                        for t in range(per)
                    ],
                    axis=1,
                )
                for block in blocks
            ],
            axis=0,
        )
        for v in range(slices.var_count)
    ]
    pick = marks((per * LANES, ghosts), 0, image)
    found = one_hot_dot(jnp.concatenate(values, axis=0), pick, ((1,), (0,)), parts)
    devices = slabs * cross
    at = lax.broadcasted_iota(jnp.int32, (devices, ghosts), 0)
    mine = (at % slabs) * cross + (across ^ (at // slabs)) == owner
    return [
        reflect
        * jnp.sum(
            jnp.where(mine, found[v * devices : (v + 1) * devices], 0.0), axis=0, keepdims=True
        )
        for v, reflect in enumerate(REFLECT)
    ]


def prepare_kernel(
    slices,
    at,
    face_hbm,
    courant_hbm,
    tables_hbm,
    cell_hbm,
    owner_hbm,
    image_hbm,
    mask_hbm,
    base_hbm,
    corner_hbm,
    state_hbm,
    message_ref,
    stay_hbm,
    up_ref,
    down_ref,
    face_ref,
    courant_ref,
    table_ref,
    cell_ref,
    owner_ref,
    image_ref,
    mask_ref,
    base_ref,
    corner_ref,
    state_ref,
    stay_ref,
    turned_ref,
    face_turned_ref,
    courant_turned_ref,
    pair_ref,
    pick_ref,
    matrix_ref,
    adjoint_ref,
    weight_ref,
    cleared_ref,
    rest_ref,
    sems,
    stay_sem,
):
    var_count, rows, pencils = state_ref.shape
    cells = var_count * rows
    count = pencils // LANES
    ghosts = cell_ref.shape[0]
    padded = -(-count // 8) * 8
    p = lax.axis_index("pipe")
    slabs, height = slices.slabs, slices.height
    lines = slices.groups * slices.per
    own_at, reduce_at, adjoint_at, profile_at = at
    copies = fetch(
        (
            face_hbm,
            courant_hbm,
            tables_hbm.at[p],
            cell_hbm,
            owner_hbm,
            image_hbm,
            base_hbm,
            corner_hbm,
            mask_hbm,
            state_hbm,
        ),
        (
            face_ref,
            courant_ref,
            table_ref,
            cell_ref,
            owner_ref,
            image_ref,
            base_ref,
            corner_ref,
            mask_ref,
            state_ref,
        ),
        sems,
    )
    kept, own, about_at, _ = stay_at(rows, count, cells)

    def send(line, rows_at, slab):
        for t, row_at in enumerate(rows_at):
            start, end = slices.tiles_at(t)
            message_ref[pl.ds(row_at, end - start, stride=height), :] = slab[start:end]
        for m in range(slices.rest):
            tail = slices.full * slabs + m
            rest_ref[m * lines + line : m * lines + line + 1, :] = slab[tail : tail + 1]

    def send_value(functional, v, slab):
        rows_at = [slices.row(functional, t) + v for t in range(slices.full)]
        send(functional * var_count + v, rows_at, slab)

    def send_coefficient(which, slab):
        rows_at = [slices.coefficient_row(which, t) for t in range(slices.full)]
        send(6 * var_count + which, rows_at, slab)

    for copy in copies[:8]:
        copy.wait()
    image_row, image_pencil = place_of(base_ref[...].reshape(1, -1), rows, pencils)
    pick_ref[...] = marks(pick_ref.shape, 0, image_pencil)
    turn(face_turned_ref, face_ref[...])

    def face(i):
        return slab_at(face_turned_ref, i, rows, count)

    link = face(0)
    margin = jnp.ones_like(link)
    first_margin = margin
    to_up, to_first = [None] * rows, [None] * rows
    for i in range(1, rows - 1):
        above = face(i)
        inverse = 1.0 / (link + margin + above)
        low, up = link * inverse, above * inverse
        to_up[i], to_first[i] = up, low
        for k, part in enumerate((up, low, inverse)):
            start = kept_at(k, i, rows, count)
            stay_ref[start : start + count, :] = part
        first_margin += low * margin
        link = link * up
        margin = 1.0 + margin * up
    send_coefficient(LINK_IN, link)
    send_coefficient(MARGIN_FIRST, first_margin)
    send_coefficient(MARGIN_LAST, margin)
    send_coefficient(LINK_UP, jnp.where(p == slabs - 1, 0.0, face(rows - 1)))

    zero, one = jnp.zeros_like(margin), jnp.ones_like(margin)
    first, last = [None] * rows, [None] * rows
    first[0], first[rows - 1], last[0], last[rows - 1] = one, zero, zero, one
    for i in range(rows - 2, 0, -1):
        first[i] = to_first[i] + to_up[i] * first[i + 1]
        last[i] = to_up[i] * last[i + 1]
    turn(courant_turned_ref, courant_ref[...])
    for i in range(rows):
        speed = slab_at(courant_turned_ref, i, rows, count)
        start = kept_at(3, i, rows, count)
        stay_ref[start : start + count, :] = speed
        put_slab(pair_ref, i, 2 * rows, count, first[i] * speed)
        put_slab(pair_ref, rows + i, 2 * rows, count, last[i] * speed)
    for t in range(count):
        matrix_ref[:, tile(t)] = pair_ref[t * 2 * rows : (t + 1) * 2 * rows, :]
    stay_ref[kept - 40 : kept, :] = table_ref[profile_at : profile_at + 40, :]
    stay_ref[own : own + cells, :] = table_ref[own_at : own_at + cells, :]
    turn(
        adjoint_ref, full_dot(table_ref[adjoint_at : adjoint_at + 40, : 2 * rows], matrix_ref[...])
    )
    for k in range(6):
        send_coefficient(FIRST_LO + k, slab_at(adjoint_ref, 2 * rows + k, 40, count))
    weight_ref[:, padded - 8 :, :] = jnp.zeros((2 * rows, 8, LANES), jnp.float32)
    for i, share in enumerate(first + last):
        weight_ref[i, :count, :] = share - slab_at(adjoint_ref, i, 40, count)

    row, pencil = place_of(cell_ref[...].reshape(1, ghosts), rows, pencils)
    lane_tile = jnp.right_shift(pencil, 7)
    lane_marks = marks((LANES, ghosts), 0, pencil - lane_tile * LANES)
    picked = one_hot_dot(
        weight_ref[...].reshape(2 * rows * padded, LANES), lane_marks, ((1,), (0,)), 2
    ).reshape(2, rows, padded, ghosts)
    at_cell = (lax.broadcasted_iota(jnp.int32, (rows, padded, ghosts), 0) == row[None]) & (
        lax.broadcasted_iota(jnp.int32, (rows, padded, ghosts), 1) == lane_tile[None]
    )

    def at_ghosts(values):
        return jnp.sum(jnp.sum(jnp.where(at_cell, values, 0.0), axis=0), axis=0, keepdims=True)

    about = jnp.concatenate(
        [
            cell_ref[...].reshape(1, ghosts).astype(jnp.float32),
            (owner_ref[...] * base_ref.shape[0] + image_ref[...])
            .reshape(1, ghosts)
            .astype(jnp.float32),
            at_ghosts(picked[0]),
            at_ghosts(picked[1]),
        ],
        axis=0,
    )
    for j in range(slabs):
        start = j * height + slices.meta_at
        message_ref[start : start + ABOUT, :] = about
    stay_ref[about_at : about_at + ABOUT, :] = about
    edge = var_count * count
    for ref in (up_ref, down_ref):
        ref[edge : edge + ABOUT, :] = about
    staying = pltpu.make_async_copy(stay_ref, stay_hbm, stay_sem.at[0])
    staying.start()
    for copy in copies[8:]:
        copy.wait()
    values = image_lines(
        state_ref[...].reshape(cells, pencils),
        image_row,
        pick_ref,
        corner_ref,
        rows,
        var_count,
    )
    for j in range(slabs):
        start = j * height + slices.images_at
        message_ref[start : start + slices.image_rows, :] = values
    solid = mask_ref[...] == 1
    for v in range(var_count):
        here = slice(v * rows, (v + 1) * rows)
        cleared_ref[here, :] = jnp.where(solid, 0.0, state_ref[v])
    turn(turned_ref, cleared_ref[...])
    for group in (range(0, 3), range(3, var_count)):
        sums = {v: [zero] * 4 for v in group}
        for i in range(rows):
            up, down = reduce_at + i, reduce_at + rows + i
            weights = (
                table_ref[up : up + 1, :],
                table_ref[down : down + 1, :],
                weight_ref[i, :count, :],
                weight_ref[rows + i, :count, :],
            )
            for v in group:
                cell = slab_at(turned_ref, v * rows + i, cells, count)
                if i == 0:
                    send_value(ROW_FIRST, v, cell)
                    down_ref[v * count : (v + 1) * count, :] = cell
                if i == rows - 1:
                    send_value(ROW_LAST, v, cell)
                    up_ref[v * count : (v + 1) * count, :] = cell
                sums[v] = [x + weight * cell for x, weight in zip(sums[v], weights)]
        for v in group:
            for functional, total in zip((Z_UP, Z_DOWN, RIGHT_FIRST, RIGHT_LAST), sums[v]):
                send_value(functional, v, total)

    block = lane_block(max(slices.groups, 1), slices.width)
    for m in range(slices.rest):
        lined = [
            rest_ref[pl.ds(m * lines + k, slices.groups, stride=slices.per), :]
            for k in range(slices.per)
        ]
        for i in range(slices.per):
            packed = lined[0]
            for k in range(slices.per):
                moved = moved_lanes(lined[k], (k - i) * slices.width)
                packed = moved if k == 0 else jnp.where(block == k, moved, packed)
            start = (m * slices.per + i) * height + slices.packed_at
            message_ref[start : start + slices.groups, :] = packed
    staying.wait()


def chain_kernel(slices, message_ref, rest_ref, chain_ref):
    slabs, chunk, full = slices.slabs, slices.chunk, slices.full
    height, per, width = slices.height, slices.per, slices.width
    if slices.rest:
        for p in range(slabs):
            start = slices.place[p] * height + slices.packed_at
            packed = message_ref[start : start + slices.groups, :]
            for k in range(per):
                rest_ref[pl.ds(p * slices.groups * per + k, slices.groups, stride=per), :] = (
                    moved_lanes(packed, -k * width)
                )
    else:
        rest_ref[...] = jnp.zeros_like(rest_ref)

    def sent(p, which):
        start = slices.place[p] * height + slices.coefficient_row(which, 0)
        slab = message_ref[start : start + full, :]
        if slices.rest:
            start = p * slices.groups * per + 6 * slices.var_count + which
            slab = jnp.concatenate([slab, rest_ref[start : start + 1, :]], axis=0)
        return slab

    nodes = 2 * slabs
    margin = sent(0, MARGIN_FIRST)
    for k in range(nodes):
        link = sent(k // 2, LINK_UP if k % 2 else LINK_IN)
        inverse = 1.0 / (margin + link)
        ratio = link * inverse
        chain_ref[16 * k : 16 * k + chunk, :] = ratio
        chain_ref[16 * k + 8 : 16 * k + 8 + chunk, :] = inverse
        if k < nodes - 1:
            following = sent((k + 1) // 2, MARGIN_FIRST if k % 2 else MARGIN_LAST)
            margin = following + margin * ratio


def solve_kernel(slices, pencils, constants, message_ref, rest_ref, chain_ref, *refs):
    *blocks, back_ref, ghost_ref, back_rest_ref = refs
    slabs, var_count, chunk, full = slices.slabs, slices.var_count, slices.chunk, slices.full
    height, per, width = slices.height, slices.per, slices.width
    along = lax.axis_index("pipe")
    me = sum(jnp.where(along == p, slices.place[p], 0) for p in range(slabs))

    def meta(p, k):
        start = slices.place[p] * height + slices.meta_at + k
        return message_ref[start : start + 1, :]

    def meta_all(k):
        return jnp.concatenate([meta(p, k) for p in range(slabs)], axis=1)

    carry_up, carry_down, ups, downs = constants
    values = ghost_values(slices, blocks, meta_all(COLUMN), 2)
    rows = ups.shape[1]
    row_of, pencil_of = place_of(meta_all(CELL).astype(jnp.int32), rows, pencils)
    ghosts = LANES
    place = lax.broadcasted_iota(jnp.int32, (chunk * LANES, ghosts), 0)
    slot, lane = place // LANES, place % LANES
    pencil_at = jnp.where(
        slot < full,
        (me + slot * slabs) * LANES + lane,
        (full * slabs + me // per) * LANES + (me % per) * width + lane,
    )
    none = jnp.zeros((8 - var_count, ghosts), jnp.float32)
    for p in range(slabs):
        row = row_of[:, tile(p)]
        up = down = jnp.zeros((1, ghosts), jnp.float32)
        for i in range(rows):
            up = jnp.where(row == i, float(ups[p, i]), up)
            down = jnp.where(row == i, float(downs[p, i]), down)
        weights = (
            up,
            down,
            jnp.where(row == 0, 1.0, 0.0),
            jnp.where(row == rows - 1, 1.0, 0.0),
            meta(p, WEIGHT_FIRST),
            meta(p, WEIGHT_LAST),
        )
        here = jnp.concatenate([value[:, tile(p)] for value in values] + [none], axis=0)
        shares = jnp.concatenate([here * weight for weight in weights], axis=0)
        spots = jnp.where(pencil_at == pencil_of[:, tile(p)], 1.0, 0.0)
        share = one_hot_dot(shares, spots.astype(jnp.bfloat16), ((1,), (1,)), 2)
        for t in range(chunk):
            start = (p * chunk + t) * 48
            ghost_ref[start : start + 48, :] = share[:, tile(t)]

    nodes = 2 * slabs
    zero = jnp.zeros((var_count, LANES), jnp.float32)
    for t in range(chunk):

        def value(p, functional):
            if t < full:
                start = slices.place[p] * height + slices.row(functional, t)
                sent = message_ref[start : start + var_count, :]
            else:
                start = p * slices.groups * per + functional * var_count
                sent = rest_ref[start : start + var_count, :]
            start = (p * chunk + t) * 48 + functional * 8
            return sent + ghost_ref[start : start + var_count, :]

        def coefficient(p, which):
            if t < full:
                start = slices.place[p] * height + slices.coefficient_row(which, t)
                return message_ref[start : start + 1, :]
            start = p * slices.groups * per + 6 * var_count + which
            return rest_ref[start : start + 1, :]

        def give(p, functional, block):
            if t < full:
                start = slices.place[p] * slices.back_height + slices.row(functional, t)
                back_ref[start : start + var_count, :] = block
            else:
                start = p * slices.back_groups * per + functional * var_count
                back_rest_ref[start : start + var_count, :] = block

        def ratio(k):
            return chain_ref[16 * k + t : 16 * k + t + 1, :]

        def scale(k):
            return chain_ref[16 * k + 8 + t : 16 * k + 9 + t, :]

        lo, hi, below, above = ([zero] * slabs for _ in range(4))
        for p in range(1, slabs):
            lo[p] = value(p - 1, Z_UP) + float(carry_up[p]) * lo[p - 1]
            below[p] = value(p - 1, ROW_LAST)
        for p in range(slabs - 2, -1, -1):
            hi[p] = value(p + 1, Z_DOWN) + float(carry_down[p]) * hi[p + 1]
            above[p] = value(p + 1, ROW_FIRST)
        right = []
        for p in range(slabs):
            right.append(
                value(p, RIGHT_FIRST)
                - coefficient(p, FIRST_LO) * lo[p]
                - coefficient(p, FIRST_HI) * hi[p]
                - coefficient(p, FIRST_EDGE) * below[p]
            )
            right.append(
                value(p, RIGHT_LAST)
                - coefficient(p, LAST_LO) * lo[p]
                - coefficient(p, LAST_HI) * hi[p]
                - coefficient(p, LAST_EDGE) * above[p]
            )
            give(p, 2, lo[p])
            give(p, 3, hi[p])
        for k in range(1, nodes):
            right[k] = right[k] + ratio(k - 1) * right[k - 1]
        x = right[nodes - 1] * scale(nodes - 1)
        give(slabs - 1, 1, x)
        for k in range(nodes - 2, -1, -1):
            x = right[k] * scale(k) + ratio(k) * x
            give(k // 2, k % 2, x)
    if slices.rest:
        groups = slices.back_groups
        block = lane_block(groups, width)
        for p in range(slabs):
            for k in range(per):
                lined = back_rest_ref[pl.ds(p * groups * per + k, groups, stride=per), :]
                moved = moved_lanes(lined, k * width)
                packed = moved if k == 0 else jnp.where(block == k, moved, packed)
            start = slices.place[p] * slices.back_height + slices.back_packed_at
            back_ref[start : start + groups, :] = packed


def pick_kernel(slices, message_ref, values_ref):
    size = slices.image_rows
    for p in range(slices.slabs):
        start = slices.place[p] * slices.height + slices.images_at
        values_ref[p * size : (p + 1) * size, :] = message_ref[start : start + size, :]


def own_kernel(stay_ref, mask_ref, state_ref, ready_ref, cleared_ref):
    var_count, rows, pencils = state_ref.shape
    cells = var_count * rows
    count = pencils // LANES
    own_at = stay_at(rows, count, cells)[1]
    cells_at, kept_start, end = ready_at(rows, count, cells)
    solid = mask_ref[...] == 1
    for v in range(var_count):
        cleared_ref[v * rows : (v + 1) * rows, :] = jnp.where(solid, 0.0, state_ref[v])
    turn(ready_ref.at[cells_at:kept_start, :], cleared_ref[...])
    turn(
        ready_ref.at[:cells_at, :],
        full_dot(stay_ref[own_at : own_at + cells, :cells], cleared_ref[...]),
    )
    ready_ref[kept_start:end, :] = stay_ref[...]


def fill_kernel(slices, shape, ready_ref, below_ref, above_ref, *refs):
    *blocks, done_ref, filled_ref, edge_ref = refs
    var_count, rows, pencils = shape
    cells = var_count * rows
    count = pencils // LANES
    _, own_at, about_at, _ = stay_at(rows, count, cells)
    cells_at, kept_start, _ = ready_at(rows, count, cells)

    ghosts = LANES
    about = [ready_ref[kept_start + about_at : kept_start + about_at + ABOUT, :]]
    edge = var_count * count
    about += [ref[edge : edge + ABOUT, :] for ref in (below_ref, above_ref)]

    def known(k):
        return jnp.concatenate([x[k : k + 1] for x in about], axis=1)

    values = ghost_values(slices, blocks, known(COLUMN), 3)
    row, pencil = place_of(known(CELL).astype(jnp.int32), rows, pencils)
    at_row = lax.broadcasted_iota(jnp.int32, (rows, ghosts), 0) == row[:, :ghosts]
    spread = jnp.concatenate([jnp.where(at_row, value[:, :ghosts], 0.0) for value in values], axis=0)
    own = ready_ref[kept_start + own_at : kept_start + own_at + cells, :cells]
    both = jnp.concatenate([full_dot(own, spread), spread], axis=0)
    spots = marks((pencils, ghosts), 0, pencil[:, :ghosts])
    added = one_hot_dot(both, spots, ((1,), (1,)), 3)
    for t in range(count):
        here = slice(t * cells, (t + 1) * cells)
        there = slice(cells_at + t * cells, cells_at + (t + 1) * cells)
        done_ref[here, :] = ready_ref[here, :] + added[:cells, tile(t)]
        filled_ref[here, :] = ready_ref[there, :] + added[cells:, tile(t)]
    x_at, response_at, profile_at, edge_at, _ = done_at(rows, count, cells, var_count)
    none = jnp.zeros((8 - var_count, ghosts), jnp.float32)
    for k, (ref, wanted) in enumerate(((below_ref, rows - 1), (above_ref, 0))):
        here = slice((k + 1) * ghosts, (k + 2) * ghosts)
        at_edge = row[:, here] == wanted
        spread = [jnp.where(at_edge, value[:, here], 0.0) for value in values] + [none]
        spots = marks((pencils, ghosts), 0, pencil[:, here])
        turn(edge_ref, one_hot_dot(jnp.concatenate(spread, axis=0), spots, ((1,), (1,)), 3))
        for v in range(var_count):
            start = edge_at + (k * var_count + v) * count
            done_ref[start : start + count, :] = ref[v * count : (v + 1) * count, :] + slab_at(
                edge_ref, v, 8, count
            )

    def kept(which, i):
        start = kept_start + kept_at(which, i, rows, count)
        return ready_ref[start : start + count, :]

    def profile(k):
        start = kept_start + own_at - 40 + k
        return ready_ref[start : start + 1, :]

    def put(at, i, height, value):
        done_ref[pl.ds(at + i, count, stride=height), :] = value

    swept = []
    for i in range(1, rows - 1):
        speed = kept(3, i)
        here = [-speed * profile(i), -speed * profile(rows + i)]
        for v in range(var_count):
            row = v * rows + i
            own_slab = slab_at(done_ref, row, cells, count)
            here.append(slab_at(filled_ref, row, cells, count) - speed * own_slab)
        if swept:
            ratio = kept(0, i - 1)
            here = [x + ratio * y for x, y in zip(here, swept[-1])]
        swept.append(here)
    zero = jnp.zeros((count, LANES), jnp.float32)
    one = jnp.ones((count, LANES), jnp.float32)
    x = [zero] * (2 + var_count)
    first, last = zero, one
    for i in range(rows - 1, -1, -1):
        if 0 < i < rows - 1:
            ratio, inverse = kept(0, i), kept(2, i)
            first, last = kept(1, i) + ratio * first, ratio * last
            x = [inverse * y + ratio * z for y, z in zip(swept[i - 1], x)]
        if i == 0:
            first, last, x = one, zero, [zero] * (2 + var_count)
        for k, value in enumerate([first, last] + x[:2]):
            put(response_at + k * rows * count, i, rows, value)
        for v in range(var_count):
            put(x_at, v * rows + i, cells, x[2 + v])
    done_ref[profile_at : profile_at + 40, :] = ready_ref[
        kept_start + own_at - 40 : kept_start + own_at, :
    ]


def finish_kernel(
    slices, back_ref, done_ref, derivative_hbm, segment_hbm, derivative_ref, segment_ref, tail_ref, sems
):
    var_count, rows, pencils = segment_ref.shape
    count = pencils // LANES
    cells = var_count * rows
    x_at, response_at, profile_at, edge_at, _ = done_at(rows, count, cells, var_count)
    back_height, groups, per = slices.back_height, slices.back_groups, slices.per
    block = lane_block(max(groups, 1), slices.width)
    for m in range(slices.rest):
        packed = []
        for i in range(per):
            start = (m * per + i) * back_height + slices.back_packed_at
            packed.append(back_ref[start : start + groups, :])
        for k in range(per):
            for i in range(per):
                moved = moved_lanes(packed[i], (i - k) * slices.width)
                joined = moved if i == 0 else jnp.where(block == i, moved, joined)
            tail_ref[pl.ds(m * groups * per + k, groups, stride=per), :] = joined

    def got(functional, v, t):
        step, j = t // slices.slabs, t % slices.slabs
        if step < slices.full:
            start = j * back_height + slices.row(functional, step) + v
            return back_ref[start : start + 1, :]
        start = j * groups * per + functional * var_count + v
        return tail_ref[start : start + 1, :]

    lo_profile = done_ref[profile_at : profile_at + rows, :]
    hi_profile = done_ref[profile_at + rows : profile_at + 2 * rows, :]
    row_at = lax.broadcasted_iota(jnp.int32, (rows, LANES), 0)
    edges = profile_at + 2 * rows
    lo_edge = jnp.where(row_at == 0, done_ref[edges : edges + 1, :], 0.0)
    hi_edge = jnp.where(row_at == rows - 1, done_ref[edges + 1 : edges + 2, :], 0.0)

    def edge(k, v, t):
        start = edge_at + (k * var_count + v) * count + t
        return done_ref[start : start + 1, :]

    def response(k, t):
        start = response_at + (k * count + t) * rows
        return done_ref[start : start + rows, :]

    copies = []
    for v in range(var_count):
        for t in range(count):
            start = t * cells + v * rows
            lo, hi = got(2, v, t), got(3, v, t)
            derivative_ref[v, :, tile(t)] = (
                done_ref[start : start + rows, :]
                + (lo_profile * lo + hi_profile * hi)
                + (lo_edge * edge(0, v, t) + hi_edge * edge(1, v, t))
            )
            segment_ref[v, :, tile(t)] = (
                done_ref[x_at + start : x_at + start + rows, :]
                + (response(0, t) * got(0, v, t) + response(1, t) * got(1, v, t))
                + (response(2, t) * lo + response(3, t) * hi)
            )
        for which, (ref, hbm) in enumerate(
            ((derivative_ref, derivative_hbm), (segment_ref, segment_hbm))
        ):
            copies.append(
                pltpu.make_async_copy(ref.at[v], hbm.at[v], sems.at[which * var_count + v])
            )
            copies[-1].start()
    for copy in copies:
        copy.wait()


def call(kernel, outs, scratch, sems, args, near=(), far_out=(), limit=62):
    whole = pl.BlockSpec(memory_space=pltpu.VMEM)
    far = pl.BlockSpec(memory_space=pltpu.HBM)
    buffers = [
        pltpu.VMEM(s.shape, s.dtype) if hasattr(s, "dtype") else pltpu.VMEM(s, jnp.float32)
        for s in scratch
    ]
    buffers += [pltpu.SemaphoreType.DMA((size,)) for size in sems]
    return pl.pallas_call(
        kernel,
        out_shape=[jax.ShapeDtypeStruct(shape, jnp.float32) for shape in outs],
        in_specs=[whole if k in near else far for k in range(len(args))],
        out_specs=[far if k in far_out else whole for k in range(len(outs))],
        scratch_shapes=buffers,
        compiler_params=pltpu.CompilerParams(vmem_limit_bytes=limit * 2**20),
    )(*args)


def exchange(message, axis):
    groups = [middle_first(lax.axis_size(axis))]
    return lax.all_to_all(message, axis, 0, 0, axis_index_groups=groups, tiled=True)


def local(
    state,
    face_diffusion,
    courant,
    cell_mask,
    ghost_cell,
    ghost_owner,
    ghost_image,
    image_base,
    image_weight,
):
    var_count, rows, pencils = state.shape
    slabs, cross = lax.axis_size("pipe"), lax.axis_size("cross")
    count = pencils // LANES
    cells = var_count * rows
    images = image_base.shape[0]
    tables, at, constants = derivative_tables(slabs, rows, var_count)
    slices = Slices(slabs, count, cross, var_count, images)
    tables = jnp.asarray(tables)
    turned = (cells * count, LANES)
    stay = stay_at(rows, count, cells)[3]
    ready = (ready_at(rows, count, cells)[2], LANES)

    arguments = (
        face_diffusion,
        courant,
        tables,
        ghost_cell,
        ghost_owner,
        ghost_image,
        cell_mask,
        image_base,
        image_weight,
        state,
    )
    buffers = list(arguments)
    buffers[2] = jax.ShapeDtypeStruct(tables.shape[1:], jnp.float32)
    edge = (-(-(var_count * count + ABOUT) // 8) * 8, LANES)
    message, stay, up, down = call(
        functools.partial(prepare_kernel, slices, at),
        [(slabs * slices.height, LANES), (stay, LANES), edge, edge],
        buffers
        + [
            (stay, LANES),
            turned,
            (rows * count, LANES),
            (rows * count, LANES),
            (2 * rows * count, LANES),
            jax.ShapeDtypeStruct((pencils, images), jnp.bfloat16),
            (2 * rows, pencils),
            (40 * count, LANES),
            (2 * rows, -(-count // 8) * 8, LANES),
            (cells, pencils),
            (max(slices.rest, 1) * max(slices.groups, 1) * slices.per, LANES),
        ],
        [len(arguments), 1],
        arguments,
        far_out=(1,),
    )
    message = exchange(message, "pipe")
    forward = [(i, i + 1) for i in range(slabs - 1)]
    below = lax.ppermute(up, "pipe", forward)
    above = lax.ppermute(down, "pipe", [(j, i) for i, j in forward])
    (ready,) = call(
        own_kernel,
        [ready],
        [(cells, pencils)],
        [],
        (stay, cell_mask, state),
        near=range(3),
        limit=48,
    )
    (image_values,) = call(
        functools.partial(pick_kernel, slices),
        [(slabs * slices.image_rows, LANES)],
        [],
        [],
        (message,),
        near=(0,),
        limit=24,
    )
    blocks = [image_values] + [
        lax.ppermute(image_values, "cross", [(i, i ^ u) for i in range(cross)])
        for u in range(1, cross)
    ]

    factored, below, above = lax.optimization_barrier((message, below, above))
    rest, chain = call(
        functools.partial(chain_kernel, slices),
        [(slabs * max(slices.groups, 1) * slices.per, LANES), (2 * slabs * 16, LANES)],
        [],
        [],
        (factored,),
        near=(0,),
        limit=24,
    )
    (back,) = call(
        functools.partial(solve_kernel, slices, pencils, constants),
        [(slabs * slices.back_height, LANES)],
        [
            (slabs * slices.chunk * 48, LANES),
            (slabs * max(slices.back_groups, 1) * slices.per, LANES),
        ],
        [],
        (message, rest, chain, *blocks),
        near=range(3 + cross),
        limit=24,
    )
    back = exchange(back, "pipe")
    (done,) = call(
        functools.partial(fill_kernel, slices, state.shape),
        [(done_at(rows, count, cells, var_count)[4], LANES)],
        [turned, (8 * count, LANES)],
        [],
        (ready, below, above, *blocks),
        near=range(3 + cross),
        limit=48,
    )
    return tuple(
        call(
            functools.partial(finish_kernel, slices),
            [state.shape, state.shape],
            [
                state.shape,
                state.shape,
                (max(slices.rest, 1) * max(slices.back_groups, 1) * slices.per, LANES),
            ],
            [2 * var_count],
            (back, done),
            near=range(2),
            far_out=(0, 1),
            limit=48,
        )
    )


def solution(mesh):
    in_specs = (
        P(None, "pipe", "cross"),
        P("pipe", "cross"),
        P("pipe", "cross"),
        P("pipe", "cross"),
        P(("pipe", "cross")),
        P(("pipe", "cross")),
        P(("pipe", "cross")),
        P(("pipe", "cross")),
        P(None, ("pipe", "cross")),
    )
    out_specs = (P(None, "pipe", "cross"), P(None, "pipe", "cross"))
    return jax.shard_map(local, mesh=mesh, in_specs=in_specs, out_specs=out_specs, check_vma=False)
```

```python
import functools

import numpy as np
import jax
import jax.numpy as jnp
from jax import lax
from jax.experimental import pallas as pl
from jax.experimental.pallas import tpu as pltpu
from jax.sharding import PartitionSpec as P

LINE = 96
LANES = 128
REFLECT = (1.0, -1.0, -1.0, -1.0, 1.0)

Z_UP, Z_DOWN, ROW_FIRST, ROW_LAST, RIGHT_FIRST, RIGHT_LAST = range(6)
LINK_IN, MARGIN_FIRST, MARGIN_LAST, LINK_UP, FIRST_LO, FIRST_HI, LAST_LO, LAST_HI, FIRST_EDGE, LAST_EDGE = range(10)
COEFFICIENTS = 10
CELL, COLUMN, WEIGHT_FIRST, WEIGHT_LAST = range(4)
ABOUT = 4


def derivative_tables(slabs, rows, var_count):
    total = slabs * rows
    A = np.eye(total)
    B = np.zeros((total, total))
    for i in range(2, total - 2):
        A[i, i - 1] = A[i, i + 1] = 1.0 / 3.0
        B[i, i + 1], B[i, i - 1] = 7.0 / 9.0, -7.0 / 9.0
        B[i, i + 2], B[i, i - 2] = 1.0 / 36.0, -1.0 / 36.0
    for i in (1, total - 2):
        A[i, i - 1] = A[i, i + 1] = 0.25
        B[i, i + 1], B[i, i - 1] = 0.75, -0.75
    B[0, :3] = (-1.5, 2.0, -0.5)
    B[-1, -3:] = (0.5, -2.0, 1.5)
    inverse = np.linalg.inv(A)
    M = inverse @ B

    cells = var_count * rows
    own_at, reduce_at, adjoint_at, profile_at = 0, cells, cells + 32, cells + 72
    tables = np.zeros((slabs, cells + 112, LANES))
    carry_up, carry_down = np.zeros(slabs), np.zeros(slabs)
    ups, downs = np.zeros((slabs, rows)), np.zeros((slabs, rows))
    for p in range(slabs):
        table = tables[p]
        base = p * rows
        here = slice(base, base + rows)
        own = M[here, here]
        lo, hi, lo_edge, hi_edge = (np.zeros(rows) for _ in range(4))
        weight_up, weight_down = np.zeros(rows), np.zeros(rows)
        if p > 0:
            lo = inverse[here, base - 8] / inverse[base + 1, base - 8]
            lo_edge[0] = M[base, base - 1] - lo[0] * M[base + 1, base - 1]
            weight_down = M[base - 2, here]
        if p > 1:
            k = base - rows - 8
            carry_up[p] = inverse[base + 1, k] / inverse[base - rows + 1, k]
        if p < slabs - 1:
            k = base + rows + 8
            hi = inverse[here, k] / inverse[base + rows - 2, k]
            hi_edge[-1] = M[base + rows - 1, base + rows] - hi[-1] * M[base + rows - 2, base + rows]
            weight_up = M[base + rows + 1, here]
        if p < slabs - 2:
            k = base + 2 * rows + 8
            carry_down[p] = inverse[base + rows - 2, k] / inverse[base + 2 * rows - 2, k]
        for v in range(var_count):
            at = slice(v * rows, (v + 1) * rows)
            table[own_at + v * rows : own_at + (v + 1) * rows, at] = own
        table[reduce_at : reduce_at + rows] = weight_up[:, None]
        table[reduce_at + rows : reduce_at + 2 * rows] = weight_down[:, None]
        table[adjoint_at : adjoint_at + rows, :rows] = own.T
        table[adjoint_at + rows : adjoint_at + 2 * rows, rows : 2 * rows] = own.T
        more = adjoint_at + 2 * rows
        table[more, :rows] = lo
        table[more + 1, :rows] = hi
        table[more + 2, rows : 2 * rows] = lo
        table[more + 3, rows : 2 * rows] = hi
        table[more + 4, 0] = lo_edge[0]
        table[more + 5, 2 * rows - 1] = hi_edge[-1]
        table[profile_at : profile_at + rows] = lo[:, None]
        table[profile_at + rows : profile_at + 2 * rows] = hi[:, None]
        table[profile_at + 2 * rows] = lo_edge[0]
        table[profile_at + 2 * rows + 1] = hi_edge[-1]
        ups[p], downs[p] = weight_up, weight_down
    at = (own_at, reduce_at, adjoint_at, profile_at)
    return tables.astype(np.float32), at, (carry_up, carry_down, ups, downs)


def split(x, parts):
    pieces = []
    for _ in range(parts):
        piece = x.astype(jnp.bfloat16)
        pieces.append(piece)
        x = x - piece.astype(jnp.float32)
    return pieces


def one_hot_dot(x, one_hot, contract, parts):
    found = lax.dot_general(
        jnp.concatenate(split(x, parts), axis=0),
        one_hot,
        (contract, ((), ())),
        preferred_element_type=jnp.float32,
    )
    size = x.shape[0]
    pieces = [found[k * size : (k + 1) * size] for k in range(parts)]
    return sum(pieces[-2::-1], pieces[-1])


def full_dot(a, b):
    return jnp.dot(a, b, precision=lax.Precision.HIGHEST, preferred_element_type=jnp.float32)


def marks(shape, axis, values):
    return jnp.where(lax.broadcasted_iota(jnp.int32, shape, axis) == values, 1.0, 0.0).astype(
        jnp.bfloat16
    )


def place_of(cell, rows, pencils):
    row = jnp.zeros_like(cell)
    for k in range(1, rows):
        row += (cell >= k * pencils).astype(jnp.int32)
    return row, cell - row * pencils


def tile(t):
    return slice(t * LANES, (t + 1) * LANES)


def turn(ref, x):
    height, pencils = x.shape
    for t in range(pencils // LANES):
        ref[t * height : (t + 1) * height, :] = x[:, tile(t)]


def slab_at(ref, row, height, count):
    return ref[pl.ds(row, count, stride=height), :]


def put_slab(ref, row, height, count, value):
    ref[pl.ds(row, count, stride=height), :] = value


def kept_at(which, i, rows, count):
    return (which * rows + i) * (-(-count // 8) * 8)


def stay_at(rows, count, cells):
    kept = kept_at(4, 0, rows, count) + 40
    return kept, kept, kept + cells, kept + cells + 8


def ready_at(rows, count, cells):
    kept = 2 * cells * count
    return cells * count, kept, kept + stay_at(rows, count, cells)[3]


def done_at(rows, count, cells, var_count):
    x = cells * count
    response = 2 * x
    profile = response + 4 * rows * count
    return x, response, profile, profile + 40, profile + 40 + 2 * var_count * count


def fetch(sources, targets, sems):
    copies = [
        pltpu.make_async_copy(source, target, sems.at[k])
        for k, (source, target) in enumerate(zip(sources, targets))
    ]
    for copy in copies:
        copy.start()
    return copies


def middle_first(slabs):
    half = slabs // 2
    order = []
    for p in range(half - 1, -1, -1):
        mirror = slabs - 1 - p
        order += [p, mirror ^ 1]
    return order


class Slices:
    def __init__(self, slabs, count, cross, var_count, images):
        rest = count % slabs
        order = middle_first(slabs)
        self.place = [order.index(p) for p in range(slabs)]
        self.slabs, self.count, self.cross, self.var_count = slabs, count, cross, var_count
        self.image_rows = var_count * images // LANES
        shared = rest > 0 and slabs % rest == 0 and LANES % (slabs // rest) == 0
        self.full = count // slabs if shared else -(-count // slabs)
        self.rest = rest if shared else 0
        self.per = slabs // rest if shared else 1
        self.width = LANES // self.per
        self.chunk = self.full + (1 if shared else 0)
        self.lines, self.back_lines = 6 * var_count + COEFFICIENTS, 4 * var_count
        self.groups, self.back_groups = (self.group_count(n) for n in (self.lines, self.back_lines))
        self.meta_at = self.lines * self.full
        self.packed_at = self.meta_at + ABOUT
        self.images_at = self.packed_at + self.groups
        self.height = -(-(self.images_at + self.image_rows) // 8) * 8
        self.back_packed_at = self.back_lines * self.full
        self.back_height = -(-(self.back_packed_at + self.back_groups) // 8) * 8

    def group_count(self, lines):
        return -(-lines // self.per) if self.rest else 0

    def row(self, functional, t):
        return (functional * self.full + t) * self.var_count

    def coefficient_row(self, which, t):
        return 6 * self.full * self.var_count + which * self.full + t

    def tiles_at(self, t):
        return t * self.slabs, min(self.count, (t + 1) * self.slabs)


def lane_block(rows, width):
    return lax.broadcasted_iota(jnp.int32, (rows, LANES), 1) // width


def moved_lanes(x, by):
    by %= LANES
    return x if by == 0 else pltpu.roll(x, by, 1)


def image_lines(x, row, pick_ref, weight_ref, rows, var_count):
    pencils, images = pick_ref.shape
    row_at = lax.broadcasted_iota(jnp.int32, (rows, images), 0)
    lower, upper = row_at == row, row_at == row + 1
    total = [jnp.zeros((rows, images), jnp.float32) for _ in range(var_count)]
    pieces = jnp.concatenate(split(x, 2), axis=0)
    for corner, shift in enumerate((0, 1, LINE, LINE + 1)):
        moved = pieces if shift == 0 else pltpu.roll(pieces, pencils - shift, 1)
        found = jnp.dot(moved, pick_ref[...], preferred_element_type=jnp.float32)
        found = found[: var_count * rows] + found[var_count * rows :]
        weight = jnp.where(lower, weight_ref[corner : corner + 1], 0.0) + jnp.where(
            upper, weight_ref[corner + 4 : corner + 5], 0.0
        )
        for v in range(var_count):
            total[v] += found[v * rows : (v + 1) * rows] * weight
    lines = []
    for v in range(var_count):
        value = jnp.sum(total[v], axis=0, keepdims=True)
        lines += [value[:, tile(t)] for t in range(images // LANES)]
    return jnp.concatenate(lines, axis=0)


def ghost_values(slices, blocks, column, parts):
    per = slices.image_rows // slices.var_count
    slabs, cross = slices.slabs, slices.cross
    ghosts = column.shape[1]
    images = per * LANES
    owner = ((column + 0.5) * (1.0 / images)).astype(jnp.int32)
    image = column.astype(jnp.int32) - owner * images
    across = lax.axis_index("cross")
    values = [
        jnp.concatenate(
            [
                jnp.concatenate(
                    [
                        block[pl.ds(v * per + t, slabs, stride=slices.image_rows), :]
                        for t in range(per)
                    ],
                    axis=1,
                )
                for block in blocks
            ],
            axis=0,
        )
        for v in range(slices.var_count)
    ]
    pick = marks((per * LANES, ghosts), 0, image)
    found = one_hot_dot(jnp.concatenate(values, axis=0), pick, ((1,), (0,)), parts)
    devices = slabs * cross
    at = lax.broadcasted_iota(jnp.int32, (devices, ghosts), 0)
    mine = (at % slabs) * cross + (across ^ (at // slabs)) == owner
    return [
        reflect
        * jnp.sum(
            jnp.where(mine, found[v * devices : (v + 1) * devices], 0.0), axis=0, keepdims=True
        )
        for v, reflect in enumerate(REFLECT)
    ]


def prepare_kernel(
    slices,
    at,
    face_hbm,
    courant_hbm,
    tables_hbm,
    cell_hbm,
    owner_hbm,
    image_hbm,
    mask_hbm,
    base_hbm,
    corner_hbm,
    state_hbm,
    message_ref,
    stay_hbm,
    up_ref,
    down_ref,
    face_ref,
    courant_ref,
    table_ref,
    cell_ref,
    owner_ref,
    image_ref,
    mask_ref,
    base_ref,
    corner_ref,
    state_ref,
    stay_ref,
    turned_ref,
    face_turned_ref,
    courant_turned_ref,
    pair_ref,
    pick_ref,
    matrix_ref,
    adjoint_ref,
    weight_ref,
    cleared_ref,
    rest_ref,
    sems,
    stay_sem,
):
    var_count, rows, pencils = state_ref.shape
    cells = var_count * rows
    count = pencils // LANES
    ghosts = cell_ref.shape[0]
    padded = -(-count // 8) * 8
    p = lax.axis_index("pipe")
    slabs, height = slices.slabs, slices.height
    lines = slices.groups * slices.per
    own_at, reduce_at, adjoint_at, profile_at = at
    copies = fetch(
        (
            face_hbm,
            courant_hbm,
            tables_hbm.at[p],
            cell_hbm,
            owner_hbm,
            image_hbm,
            base_hbm,
            corner_hbm,
            mask_hbm,
            state_hbm,
        ),
        (
            face_ref,
            courant_ref,
            table_ref,
            cell_ref,
            owner_ref,
            image_ref,
            base_ref,
            corner_ref,
            mask_ref,
            state_ref,
        ),
        sems,
    )
    kept, own, about_at, _ = stay_at(rows, count, cells)

    def send(line, rows_at, slab):
        for t, row_at in enumerate(rows_at):
            start, end = slices.tiles_at(t)
            message_ref[pl.ds(row_at, end - start, stride=height), :] = slab[start:end]
        for m in range(slices.rest):
            tail = slices.full * slabs + m
            rest_ref[m * lines + line : m * lines + line + 1, :] = slab[tail : tail + 1]

    def send_value(functional, v, slab):
        rows_at = [slices.row(functional, t) + v for t in range(slices.full)]
        send(functional * var_count + v, rows_at, slab)

    def send_coefficient(which, slab):
        rows_at = [slices.coefficient_row(which, t) for t in range(slices.full)]
        send(6 * var_count + which, rows_at, slab)

    for copy in copies[:8]:
        copy.wait()
    image_row, image_pencil = place_of(base_ref[...].reshape(1, -1), rows, pencils)
    pick_ref[...] = marks(pick_ref.shape, 0, image_pencil)
    turn(face_turned_ref, face_ref[...])

    def face(i):
        return slab_at(face_turned_ref, i, rows, count)

    link = face(0)
    margin = jnp.ones_like(link)
    first_margin = margin
    to_up, to_first = [None] * rows, [None] * rows
    for i in range(1, rows - 1):
        above = face(i)
        inverse = 1.0 / (link + margin + above)
        low, up = link * inverse, above * inverse
        to_up[i], to_first[i] = up, low
        for k, part in enumerate((up, low, inverse)):
            start = kept_at(k, i, rows, count)
            stay_ref[start : start + count, :] = part
        first_margin += low * margin
        link = link * up
        margin = 1.0 + margin * up
    send_coefficient(LINK_IN, link)
    send_coefficient(MARGIN_FIRST, first_margin)
    send_coefficient(MARGIN_LAST, margin)
    send_coefficient(LINK_UP, jnp.where(p == slabs - 1, 0.0, face(rows - 1)))

    zero, one = jnp.zeros_like(margin), jnp.ones_like(margin)
    first, last = [None] * rows, [None] * rows
    first[0], first[rows - 1], last[0], last[rows - 1] = one, zero, zero, one
    for i in range(rows - 2, 0, -1):
        first[i] = to_first[i] + to_up[i] * first[i + 1]
        last[i] = to_up[i] * last[i + 1]
    turn(courant_turned_ref, courant_ref[...])
    for i in range(rows):
        speed = slab_at(courant_turned_ref, i, rows, count)
        start = kept_at(3, i, rows, count)
        stay_ref[start : start + count, :] = speed
        put_slab(pair_ref, i, 2 * rows, count, first[i] * speed)
        put_slab(pair_ref, rows + i, 2 * rows, count, last[i] * speed)
    for t in range(count):
        matrix_ref[:, tile(t)] = pair_ref[t * 2 * rows : (t + 1) * 2 * rows, :]
    stay_ref[kept - 40 : kept, :] = table_ref[profile_at : profile_at + 40, :]
    stay_ref[own : own + cells, :] = table_ref[own_at : own_at + cells, :]
    turn(
        adjoint_ref, full_dot(table_ref[adjoint_at : adjoint_at + 40, : 2 * rows], matrix_ref[...])
    )
    for k in range(6):
        send_coefficient(FIRST_LO + k, slab_at(adjoint_ref, 2 * rows + k, 40, count))
    weight_ref[:, padded - 8 :, :] = jnp.zeros((2 * rows, 8, LANES), jnp.float32)
    for i, share in enumerate(first + last):
        weight_ref[i, :count, :] = share - slab_at(adjoint_ref, i, 40, count)

    row, pencil = place_of(cell_ref[...].reshape(1, ghosts), rows, pencils)
    lane_tile = jnp.right_shift(pencil, 7)
    lane_marks = marks((LANES, ghosts), 0, pencil - lane_tile * LANES)
    picked = one_hot_dot(
        weight_ref[...].reshape(2 * rows * padded, LANES), lane_marks, ((1,), (0,)), 2
    ).reshape(2, rows, padded, ghosts)
    at_cell = (lax.broadcasted_iota(jnp.int32, (rows, padded, ghosts), 0) == row[None]) & (
        lax.broadcasted_iota(jnp.int32, (rows, padded, ghosts), 1) == lane_tile[None]
    )

    def at_ghosts(values):
        return jnp.sum(jnp.sum(jnp.where(at_cell, values, 0.0), axis=0), axis=0, keepdims=True)

    about = jnp.concatenate(
        [
            cell_ref[...].reshape(1, ghosts).astype(jnp.float32),
            (owner_ref[...] * base_ref.shape[0] + image_ref[...])
            .reshape(1, ghosts)
            .astype(jnp.float32),
            at_ghosts(picked[0]),
            at_ghosts(picked[1]),
        ],
        axis=0,
    )
    for j in range(slabs):
        start = j * height + slices.meta_at
        message_ref[start : start + ABOUT, :] = about
    stay_ref[about_at : about_at + ABOUT, :] = about
    edge = var_count * count
    for ref in (up_ref, down_ref):
        ref[edge : edge + ABOUT, :] = about
    staying = pltpu.make_async_copy(stay_ref, stay_hbm, stay_sem.at[0])
    staying.start()
    for copy in copies[8:]:
        copy.wait()
    values = image_lines(
        state_ref[...].reshape(cells, pencils),
        image_row,
        pick_ref,
        corner_ref,
        rows,
        var_count,
    )
    for j in range(slabs):
        start = j * height + slices.images_at
        message_ref[start : start + slices.image_rows, :] = values
    solid = mask_ref[...] == 1
    for v in range(var_count):
        here = slice(v * rows, (v + 1) * rows)
        cleared_ref[here, :] = jnp.where(solid, 0.0, state_ref[v])
    turn(turned_ref, cleared_ref[...])
    for group in (range(0, 3), range(3, var_count)):
        sums = {v: [zero] * 4 for v in group}
        for i in range(rows):
            up, down = reduce_at + i, reduce_at + rows + i
            weights = (
                table_ref[up : up + 1, :],
                table_ref[down : down + 1, :],
                weight_ref[i, :count, :],
                weight_ref[rows + i, :count, :],
            )
            for v in group:
                cell = slab_at(turned_ref, v * rows + i, cells, count)
                if i == 0:
                    send_value(ROW_FIRST, v, cell)
                    down_ref[v * count : (v + 1) * count, :] = cell
                if i == rows - 1:
                    send_value(ROW_LAST, v, cell)
                    up_ref[v * count : (v + 1) * count, :] = cell
                sums[v] = [x + weight * cell for x, weight in zip(sums[v], weights)]
        for v in group:
            for functional, total in zip((Z_UP, Z_DOWN, RIGHT_FIRST, RIGHT_LAST), sums[v]):
                send_value(functional, v, total)

    block = lane_block(max(slices.groups, 1), slices.width)
    for m in range(slices.rest):
        lined = [
            rest_ref[pl.ds(m * lines + k, slices.groups, stride=slices.per), :]
            for k in range(slices.per)
        ]
        for i in range(slices.per):
            packed = lined[0]
            for k in range(slices.per):
                moved = moved_lanes(lined[k], (k - i) * slices.width)
                packed = moved if k == 0 else jnp.where(block == k, moved, packed)
            start = (m * slices.per + i) * height + slices.packed_at
            message_ref[start : start + slices.groups, :] = packed
    staying.wait()


def chain_kernel(slices, message_ref, rest_ref, chain_ref):
    slabs, chunk, full = slices.slabs, slices.chunk, slices.full
    height, per, width = slices.height, slices.per, slices.width
    if slices.rest:
        for p in range(slabs):
            start = slices.place[p] * height + slices.packed_at
            packed = message_ref[start : start + slices.groups, :]
            for k in range(per):
                rest_ref[pl.ds(p * slices.groups * per + k, slices.groups, stride=per), :] = (
                    moved_lanes(packed, -k * width)
                )
    else:
        rest_ref[...] = jnp.zeros_like(rest_ref)

    def sent(p, which):
        start = slices.place[p] * height + slices.coefficient_row(which, 0)
        slab = message_ref[start : start + full, :]
        if slices.rest:
            start = p * slices.groups * per + 6 * slices.var_count + which
            slab = jnp.concatenate([slab, rest_ref[start : start + 1, :]], axis=0)
        return slab

    nodes = 2 * slabs
    margin = sent(0, MARGIN_FIRST)
    for k in range(nodes):
        link = sent(k // 2, LINK_UP if k % 2 else LINK_IN)
        inverse = 1.0 / (margin + link)
        ratio = link * inverse
        chain_ref[16 * k : 16 * k + chunk, :] = ratio
        chain_ref[16 * k + 8 : 16 * k + 8 + chunk, :] = inverse
        if k < nodes - 1:
            following = sent((k + 1) // 2, MARGIN_FIRST if k % 2 else MARGIN_LAST)
            margin = following + margin * ratio


def solve_kernel(slices, pencils, constants, message_ref, rest_ref, chain_ref, *refs):
    *blocks, back_ref, ghost_ref, back_rest_ref = refs
    slabs, var_count, chunk, full = slices.slabs, slices.var_count, slices.chunk, slices.full
    height, per, width = slices.height, slices.per, slices.width
    along = lax.axis_index("pipe")
    me = sum(jnp.where(along == p, slices.place[p], 0) for p in range(slabs))

    def meta(p, k):
        start = slices.place[p] * height + slices.meta_at + k
        return message_ref[start : start + 1, :]

    def meta_all(k):
        return jnp.concatenate([meta(p, k) for p in range(slabs)], axis=1)

    carry_up, carry_down, ups, downs = constants
    values = ghost_values(slices, blocks, meta_all(COLUMN), 2)
    rows = ups.shape[1]
    row_of, pencil_of = place_of(meta_all(CELL).astype(jnp.int32), rows, pencils)
    ghosts = LANES
    place = lax.broadcasted_iota(jnp.int32, (chunk * LANES, ghosts), 0)
    slot, lane = place // LANES, place % LANES
    pencil_at = jnp.where(
        slot < full,
        (me + slot * slabs) * LANES + lane,
        (full * slabs + me // per) * LANES + (me % per) * width + lane,
    )
    none = jnp.zeros((8 - var_count, ghosts), jnp.float32)
    for p in range(slabs):
        row = row_of[:, tile(p)]
        up = down = jnp.zeros((1, ghosts), jnp.float32)
        for i in range(rows):
            up = jnp.where(row == i, float(ups[p, i]), up)
            down = jnp.where(row == i, float(downs[p, i]), down)
        weights = (
            up,
            down,
            jnp.where(row == 0, 1.0, 0.0),
            jnp.where(row == rows - 1, 1.0, 0.0),
            meta(p, WEIGHT_FIRST),
            meta(p, WEIGHT_LAST),
        )
        here = jnp.concatenate([value[:, tile(p)] for value in values] + [none], axis=0)
        shares = jnp.concatenate([here * weight for weight in weights], axis=0)
        spots = jnp.where(pencil_at == pencil_of[:, tile(p)], 1.0, 0.0)
        share = one_hot_dot(shares, spots.astype(jnp.bfloat16), ((1,), (1,)), 2)
        for t in range(chunk):
            start = (p * chunk + t) * 48
            ghost_ref[start : start + 48, :] = share[:, tile(t)]

    nodes = 2 * slabs
    zero = jnp.zeros((var_count, LANES), jnp.float32)
    for t in range(chunk):

        def value(p, functional):
            if t < full:
                start = slices.place[p] * height + slices.row(functional, t)
                sent = message_ref[start : start + var_count, :]
            else:
                start = p * slices.groups * per + functional * var_count
                sent = rest_ref[start : start + var_count, :]
            start = (p * chunk + t) * 48 + functional * 8
            return sent + ghost_ref[start : start + var_count, :]

        def coefficient(p, which):
            if t < full:
                start = slices.place[p] * height + slices.coefficient_row(which, t)
                return message_ref[start : start + 1, :]
            start = p * slices.groups * per + 6 * var_count + which
            return rest_ref[start : start + 1, :]

        def give(p, functional, block):
            if t < full:
                start = slices.place[p] * slices.back_height + slices.row(functional, t)
                back_ref[start : start + var_count, :] = block
            else:
                start = p * slices.back_groups * per + functional * var_count
                back_rest_ref[start : start + var_count, :] = block

        def ratio(k):
            return chain_ref[16 * k + t : 16 * k + t + 1, :]

        def scale(k):
            return chain_ref[16 * k + 8 + t : 16 * k + 9 + t, :]

        lo, hi, below, above = ([zero] * slabs for _ in range(4))
        for p in range(1, slabs):
            lo[p] = value(p - 1, Z_UP) + float(carry_up[p]) * lo[p - 1]
            below[p] = value(p - 1, ROW_LAST)
        for p in range(slabs - 2, -1, -1):
            hi[p] = value(p + 1, Z_DOWN) + float(carry_down[p]) * hi[p + 1]
            above[p] = value(p + 1, ROW_FIRST)
        right = []
        for p in range(slabs):
            right.append(
                value(p, RIGHT_FIRST)
                - coefficient(p, FIRST_LO) * lo[p]
                - coefficient(p, FIRST_HI) * hi[p]
                - coefficient(p, FIRST_EDGE) * below[p]
            )
            right.append(
                value(p, RIGHT_LAST)
                - coefficient(p, LAST_LO) * lo[p]
                - coefficient(p, LAST_HI) * hi[p]
                - coefficient(p, LAST_EDGE) * above[p]
            )
            give(p, 2, lo[p])
            give(p, 3, hi[p])
        for k in range(1, nodes):
            right[k] = right[k] + ratio(k - 1) * right[k - 1]
        x = right[nodes - 1] * scale(nodes - 1)
        give(slabs - 1, 1, x)
        for k in range(nodes - 2, -1, -1):
            x = right[k] * scale(k) + ratio(k) * x
            give(k // 2, k % 2, x)
    if slices.rest:
        groups = slices.back_groups
        block = lane_block(groups, width)
        for p in range(slabs):
            for k in range(per):
                lined = back_rest_ref[pl.ds(p * groups * per + k, groups, stride=per), :]
                moved = moved_lanes(lined, k * width)
                packed = moved if k == 0 else jnp.where(block == k, moved, packed)
            start = slices.place[p] * slices.back_height + slices.back_packed_at
            back_ref[start : start + groups, :] = packed


def pick_kernel(slices, message_ref, values_ref):
    size = slices.image_rows
    for p in range(slices.slabs):
        start = slices.place[p] * slices.height + slices.images_at
        values_ref[p * size : (p + 1) * size, :] = message_ref[start : start + size, :]


def own_kernel(stay_ref, mask_ref, state_ref, ready_ref, cleared_ref):
    var_count, rows, pencils = state_ref.shape
    cells = var_count * rows
    count = pencils // LANES
    own_at = stay_at(rows, count, cells)[1]
    cells_at, kept_start, end = ready_at(rows, count, cells)
    solid = mask_ref[...] == 1
    for v in range(var_count):
        cleared_ref[v * rows : (v + 1) * rows, :] = jnp.where(solid, 0.0, state_ref[v])
    turn(ready_ref.at[cells_at:kept_start, :], cleared_ref[...])
    turn(
        ready_ref.at[:cells_at, :],
        full_dot(stay_ref[own_at : own_at + cells, :cells], cleared_ref[...]),
    )
    ready_ref[kept_start:end, :] = stay_ref[...]


def fill_kernel(slices, shape, ready_ref, below_ref, above_ref, *refs):
    *blocks, done_ref, filled_ref, edge_ref = refs
    var_count, rows, pencils = shape
    cells = var_count * rows
    count = pencils // LANES
    _, own_at, about_at, _ = stay_at(rows, count, cells)
    cells_at, kept_start, _ = ready_at(rows, count, cells)

    ghosts = LANES
    about = [ready_ref[kept_start + about_at : kept_start + about_at + ABOUT, :]]
    edge = var_count * count
    about += [ref[edge : edge + ABOUT, :] for ref in (below_ref, above_ref)]

    def known(k):
        return jnp.concatenate([x[k : k + 1] for x in about], axis=1)

    values = ghost_values(slices, blocks, known(COLUMN), 3)
    row, pencil = place_of(known(CELL).astype(jnp.int32), rows, pencils)
    at_row = lax.broadcasted_iota(jnp.int32, (rows, ghosts), 0) == row[:, :ghosts]
    spread = jnp.concatenate([jnp.where(at_row, value[:, :ghosts], 0.0) for value in values], axis=0)
    own = ready_ref[kept_start + own_at : kept_start + own_at + cells, :cells]
    both = jnp.concatenate([full_dot(own, spread), spread], axis=0)
    spots = marks((pencils, ghosts), 0, pencil[:, :ghosts])
    added = one_hot_dot(both, spots, ((1,), (1,)), 3)
    for t in range(count):
        here = slice(t * cells, (t + 1) * cells)
        there = slice(cells_at + t * cells, cells_at + (t + 1) * cells)
        done_ref[here, :] = ready_ref[here, :] + added[:cells, tile(t)]
        filled_ref[here, :] = ready_ref[there, :] + added[cells:, tile(t)]
    x_at, response_at, profile_at, edge_at, _ = done_at(rows, count, cells, var_count)
    none = jnp.zeros((8 - var_count, ghosts), jnp.float32)
    for k, (ref, wanted) in enumerate(((below_ref, rows - 1), (above_ref, 0))):
        here = slice((k + 1) * ghosts, (k + 2) * ghosts)
        at_edge = row[:, here] == wanted
        spread = [jnp.where(at_edge, value[:, here], 0.0) for value in values] + [none]
        spots = marks((pencils, ghosts), 0, pencil[:, here])
        turn(edge_ref, one_hot_dot(jnp.concatenate(spread, axis=0), spots, ((1,), (1,)), 3))
        for v in range(var_count):
            start = edge_at + (k * var_count + v) * count
            done_ref[start : start + count, :] = ref[v * count : (v + 1) * count, :] + slab_at(
                edge_ref, v, 8, count
            )

    def kept(which, i):
        start = kept_start + kept_at(which, i, rows, count)
        return ready_ref[start : start + count, :]

    def profile(k):
        start = kept_start + own_at - 40 + k
        return ready_ref[start : start + 1, :]

    def put(at, i, height, value):
        done_ref[pl.ds(at + i, count, stride=height), :] = value

    swept = []
    for i in range(1, rows - 1):
        speed = kept(3, i)
        here = [-speed * profile(i), -speed * profile(rows + i)]
        for v in range(var_count):
            row = v * rows + i
            own_slab = slab_at(done_ref, row, cells, count)
            here.append(slab_at(filled_ref, row, cells, count) - speed * own_slab)
        if swept:
            ratio = kept(0, i - 1)
            here = [x + ratio * y for x, y in zip(here, swept[-1])]
        swept.append(here)
    zero = jnp.zeros((count, LANES), jnp.float32)
    one = jnp.ones((count, LANES), jnp.float32)
    x = [zero] * (2 + var_count)
    first, last = zero, one
    for i in range(rows - 1, -1, -1):
        if 0 < i < rows - 1:
            ratio, inverse = kept(0, i), kept(2, i)
            first, last = kept(1, i) + ratio * first, ratio * last
            x = [inverse * y + ratio * z for y, z in zip(swept[i - 1], x)]
        if i == 0:
            first, last, x = one, zero, [zero] * (2 + var_count)
        for k, value in enumerate([first, last] + x[:2]):
            put(response_at + k * rows * count, i, rows, value)
        for v in range(var_count):
            put(x_at, v * rows + i, cells, x[2 + v])
    done_ref[profile_at : profile_at + 40, :] = ready_ref[
        kept_start + own_at - 40 : kept_start + own_at, :
    ]


def finish_kernel(
    slices, back_ref, done_ref, derivative_hbm, segment_hbm, derivative_ref, segment_ref, tail_ref, sems
):
    var_count, rows, pencils = segment_ref.shape
    count = pencils // LANES
    cells = var_count * rows
    x_at, response_at, profile_at, edge_at, _ = done_at(rows, count, cells, var_count)
    back_height, groups, per = slices.back_height, slices.back_groups, slices.per
    block = lane_block(max(groups, 1), slices.width)
    for m in range(slices.rest):
        packed = []
        for i in range(per):
            start = (m * per + i) * back_height + slices.back_packed_at
            packed.append(back_ref[start : start + groups, :])
        for k in range(per):
            for i in range(per):
                moved = moved_lanes(packed[i], (i - k) * slices.width)
                joined = moved if i == 0 else jnp.where(block == i, moved, joined)
            tail_ref[pl.ds(m * groups * per + k, groups, stride=per), :] = joined

    def got(functional, v, t):
        step, j = t // slices.slabs, t % slices.slabs
        if step < slices.full:
            start = j * back_height + slices.row(functional, step) + v
            return back_ref[start : start + 1, :]
        start = j * groups * per + functional * var_count + v
        return tail_ref[start : start + 1, :]

    lo_profile = done_ref[profile_at : profile_at + rows, :]
    hi_profile = done_ref[profile_at + rows : profile_at + 2 * rows, :]
    row_at = lax.broadcasted_iota(jnp.int32, (rows, LANES), 0)
    edges = profile_at + 2 * rows
    lo_edge = jnp.where(row_at == 0, done_ref[edges : edges + 1, :], 0.0)
    hi_edge = jnp.where(row_at == rows - 1, done_ref[edges + 1 : edges + 2, :], 0.0)

    def edge(k, v, t):
        start = edge_at + (k * var_count + v) * count + t
        return done_ref[start : start + 1, :]

    def response(k, t):
        start = response_at + (k * count + t) * rows
        return done_ref[start : start + rows, :]

    copies = []
    for v in range(var_count):
        for t in range(count):
            start = t * cells + v * rows
            lo, hi = got(2, v, t), got(3, v, t)
            derivative_ref[v, :, tile(t)] = (
                done_ref[start : start + rows, :]
                + (lo_profile * lo + hi_profile * hi)
                + (lo_edge * edge(0, v, t) + hi_edge * edge(1, v, t))
            )
            segment_ref[v, :, tile(t)] = (
                done_ref[x_at + start : x_at + start + rows, :]
                + (response(0, t) * got(0, v, t) + response(1, t) * got(1, v, t))
                + (response(2, t) * lo + response(3, t) * hi)
            )
        for which, (ref, hbm) in enumerate(
            ((derivative_ref, derivative_hbm), (segment_ref, segment_hbm))
        ):
            copies.append(
                pltpu.make_async_copy(ref.at[v], hbm.at[v], sems.at[which * var_count + v])
            )
            copies[-1].start()
    for copy in copies:
        copy.wait()


def call(kernel, outs, scratch, sems, args, near=(), far_out=(), limit=62):
    whole = pl.BlockSpec(memory_space=pltpu.VMEM)
    far = pl.BlockSpec(memory_space=pltpu.HBM)
    buffers = [
        pltpu.VMEM(s.shape, s.dtype) if hasattr(s, "dtype") else pltpu.VMEM(s, jnp.float32)
        for s in scratch
    ]
    buffers += [pltpu.SemaphoreType.DMA((size,)) for size in sems]
    return pl.pallas_call(
        kernel,
        out_shape=[jax.ShapeDtypeStruct(shape, jnp.float32) for shape in outs],
        in_specs=[whole if k in near else far for k in range(len(args))],
        out_specs=[far if k in far_out else whole for k in range(len(outs))],
        scratch_shapes=buffers,
        compiler_params=pltpu.CompilerParams(vmem_limit_bytes=limit * 2**20),
    )(*args)


def exchange(message, axis):
    groups = [middle_first(lax.axis_size(axis))]
    return lax.all_to_all(message, axis, 0, 0, axis_index_groups=groups, tiled=True)


def local(
    state,
    face_diffusion,
    courant,
    cell_mask,
    ghost_cell,
    ghost_owner,
    ghost_image,
    image_base,
    image_weight,
):
    var_count, rows, pencils = state.shape
    slabs, cross = lax.axis_size("pipe"), lax.axis_size("cross")
    count = pencils // LANES
    cells = var_count * rows
    images = image_base.shape[0]
    tables, at, constants = derivative_tables(slabs, rows, var_count)
    slices = Slices(slabs, count, cross, var_count, images)
    tables = jnp.asarray(tables)
    turned = (cells * count, LANES)
    stay = stay_at(rows, count, cells)[3]
    ready = (ready_at(rows, count, cells)[2], LANES)

    arguments = (
        face_diffusion,
        courant,
        tables,
        ghost_cell,
        ghost_owner,
        ghost_image,
        cell_mask,
        image_base,
        image_weight,
        state,
    )
    buffers = list(arguments)
    buffers[2] = jax.ShapeDtypeStruct(tables.shape[1:], jnp.float32)
    edge = (-(-(var_count * count + ABOUT) // 8) * 8, LANES)
    message, stay, up, down = call(
        functools.partial(prepare_kernel, slices, at),
        [(slabs * slices.height, LANES), (stay, LANES), edge, edge],
        buffers
        + [
            (stay, LANES),
            turned,
            (rows * count, LANES),
            (rows * count, LANES),
            (2 * rows * count, LANES),
            jax.ShapeDtypeStruct((pencils, images), jnp.bfloat16),
            (2 * rows, pencils),
            (40 * count, LANES),
            (2 * rows, -(-count // 8) * 8, LANES),
            (cells, pencils),
            (max(slices.rest, 1) * max(slices.groups, 1) * slices.per, LANES),
        ],
        [len(arguments), 1],
        arguments,
        far_out=(1,),
    )
    message = exchange(message, "pipe")
    forward = [(i, i + 1) for i in range(slabs - 1)]
    below = lax.ppermute(up, "pipe", forward)
    above = lax.ppermute(down, "pipe", [(j, i) for i, j in forward])
    (ready,) = call(
        own_kernel,
        [ready],
        [(cells, pencils)],
        [],
        (stay, cell_mask, state),
        near=range(3),
        limit=48,
    )
    (image_values,) = call(
        functools.partial(pick_kernel, slices),
        [(slabs * slices.image_rows, LANES)],
        [],
        [],
        (message,),
        near=(0,),
        limit=24,
    )
    blocks = [image_values] + [
        lax.ppermute(image_values, "cross", [(i, i ^ u) for i in range(cross)])
        for u in range(1, cross)
    ]

    factored, below, above = lax.optimization_barrier((message, below, above))
    rest, chain = call(
        functools.partial(chain_kernel, slices),
        [(slabs * max(slices.groups, 1) * slices.per, LANES), (2 * slabs * 16, LANES)],
        [],
        [],
        (factored,),
        near=(0,),
        limit=24,
    )
    (back,) = call(
        functools.partial(solve_kernel, slices, pencils, constants),
        [(slabs * slices.back_height, LANES)],
        [
            (slabs * slices.chunk * 48, LANES),
            (slabs * max(slices.back_groups, 1) * slices.per, LANES),
        ],
        [],
        (message, rest, chain, *blocks),
        near=range(3 + cross),
        limit=24,
    )
    back = exchange(back, "pipe")
    (done,) = call(
        functools.partial(fill_kernel, slices, state.shape),
        [(done_at(rows, count, cells, var_count)[4], LANES)],
        [turned, (8 * count, LANES)],
        [],
        (ready, below, above, *blocks),
        near=range(3 + cross),
        limit=48,
    )
    return tuple(
        call(
            functools.partial(finish_kernel, slices),
            [state.shape, state.shape],
            [
                state.shape,
                state.shape,
                (max(slices.rest, 1) * max(slices.back_groups, 1) * slices.per, LANES),
            ],
            [2 * var_count],
            (back, done),
            near=range(2),
            far_out=(0, 1),
            limit=48,
        )
    )


def solution(mesh):
    in_specs = (
        P(None, "pipe", "cross"),
        P("pipe", "cross"),
        P("pipe", "cross"),
        P("pipe", "cross"),
        P(("pipe", "cross")),
        P(("pipe", "cross")),
        P(("pipe", "cross")),
        P(("pipe", "cross")),
        P(None, ("pipe", "cross")),
    )
    out_specs = (P(None, "pipe", "cross"), P(None, "pipe", "cross"))
    return jax.shard_map(local, mesh=mesh, in_specs=in_specs, out_specs=out_specs, check_vma=False)
```
